128 devices in a mesh: row: 16 (over z, x_hi, core), col: 8 (over x_lo, y).
Axes of the slice: x: 4 (x_hi: 2, x_lo: 2; x = x_hi * 2 + x_lo), y: 4, z: 4, core: 2. Of those that a mesh axis runs over, the one named last changes fastest.
Arguments:
- stream_in: bfloat16 [16384, 1280], P('row'), may hold values from -6 to 6
- segments: int32 [16384], replicated, may hold values from 0 to 47, as said below
- head_table: int32 [8, 3], replicated, may hold values from 0 to 20, as said below
- query_key_value: bfloat16 [2, 3, 1280, 1280], P(None, None, 'row', 'col'), may hold values from -0.15625 to 0.15625
- attention_out: bfloat16 [2, 1280, 1280], P(None, 'row', 'col'), may hold values from -0.625 to 0.625
- expand_weight: bfloat16 [2, 1280, 5120], P(None, 'row', 'col'), may hold values from -0.15625 to 0.15625
- contract_weight: bfloat16 [2, 5120, 1280], P(None, 'col', 'row'), may hold values from -0.078125 to 0.078125
- norm_gain: float32 [2, 2, 1280], replicated, may hold values from 0.25 to 1.75
- norm_bias: float32 [2, 2, 1280], replicated, may hold values from -1.2 to 1.2
- attention_bias: float32 [2, 3, 1280], P(None, None, 'col'), may hold values from -1.8 to 1.8
- expand_bias: float32 [2, 5120], P(None, 'col'), may hold values from -1.8 to 1.8
- contract_bias: float32 [2, 1280], replicated, may hold values from -1.8 to 1.8
- cotangent: bfloat16 [16384, 1280], P('row'), may hold values from -6 to 6
Outputs:
- activations: bfloat16 [2, 16384, 1280], P(None, 'row', 'col')
- grad_stream: float32 [16384, 1280], P('row', 'col')
- grad_query_key_value: float32 [2, 3, 1280, 1280], P(None, None, 'row', 'col')
- grad_attention_out: float32 [2, 1280, 1280], P(None, 'row', 'col')
- grad_expand: float32 [2, 1280, 5120], P(None, 'row', 'col')
- grad_contract: float32 [2, 5120, 1280], P(None, 'col', 'row')
- grad_norm_gain: float32 [2, 2, 1280], replicated
- grad_norm_bias: float32 [2, 2, 1280], replicated
- grad_attention_bias: float32 [2, 3, 1280], P(None, None, 'col')
- grad_expand_bias: float32 [2, 5120], P(None, 'col')
- grad_contract_bias: float32 [2, 1280], replicated
The draws below stay inside these ranges and needn't reach their ends.
Inputs may be any that keep to these rules, and one draw needn't show every extreme that they name: `segments`: document numbers start at 0, never fall and rise by at most one from token to token; a new document starts at every multiple of 1024, and each sequence of 1024 tokens holds exactly 3 documents. Apart from the multiples of 1024, no document starts within min(1024, 1024) // 8 tokens of a multiple of 1024. `head_table`: each head number below 20 stands in exactly one slot; 20 marks an empty slot; at least one index of col has all 3 slots filled.
All inputs are finite; a program needn't handle non-finite values.
Results may differ from the reference program's by a relative error of at most 0.03.
Values may be sent and summed in bfloat16 or wider, within the bound.
No kernel may reach another device: no remote copies, remote signals or barrier semaphores. Data moves between devices by JAX's collectives and lax.ppermute only.
A program may use at most 192 MiB of HBM per device.

```python
import jax
import jax.numpy as jnp
from jax import lax

D = 1280
HEADS = 20
HEAD_DIM = 64
FF = 5120
SEQ_LEN = 1024
TOK_ROW = 1024
DOCS = 3
LAYERS = 2
TOKENS = 16384
HSLOT = 3
SLOTS = 24


def draw_segments(key, part):
    key = jax.random.fold_in(key, 11)
    places = jnp.arange(TOKENS, dtype=jnp.int32)
    inner = places % SEQ_LEN
    local = places % TOK_ROW
    margin = min(TOK_ROW, SEQ_LEN) // 8
    barred = (inner == 0) | (local < margin) | (local >= TOK_ROW - margin)
    scores = jax.random.randint(key, (TOKENS,), 0, SEQ_LEN, dtype=jnp.int32) * SEQ_LEN + inner
    scores = jnp.where(barred, -1, scores).reshape(TOKENS // SEQ_LEN, SEQ_LEN)
    unused, picked = lax.top_k(scores, DOCS - 1)
    offsets = (jnp.arange(TOKENS // SEQ_LEN, dtype=jnp.int32) * SEQ_LEN)[:, None]
    starts = (inner == 0).astype(jnp.int32)
    starts = starts.at[(picked.astype(jnp.int32) + offsets).reshape(-1)].set(1)
    return (jnp.cumsum(starts) - 1).astype(jnp.int32)


def draw_head_table(key, part):
    key = jax.random.fold_in(key, 23)
    shuffled = jax.random.permutation(key, SLOTS)
    return jnp.minimum(shuffled, HEADS).astype(jnp.int32).reshape(SLOTS // HSLOT, HSLOT)


def block_levels(own_key, dims, pieces, smallest, high):
    level = 1.0
    for position, parts in pieces:
        steps = jax.random.uniform(jax.random.fold_in(jax.random.fold_in(own_key, 6), position), (parts,), jnp.float32, smallest / len(pieces), high / len(pieces))
        level = level * jnp.repeat(jnp.exp(steps), dims[position] // parts).reshape((-1,) + (1,) * (len(dims) - 1 - position))
    return level


def scatter_about(stream_key, extent, scale, limit, pieces=(), kind=jnp.bfloat16):
    level = block_levels(stream_key, extent, pieces, -0.22, 0.18) if pieces else 1.0
    drawn = jax.random.normal(stream_key, extent, jnp.float32) * scale * level
    return jnp.minimum(jnp.maximum(drawn, -limit), limit).astype(kind)


def setup_inputs(seed: int = 0) -> dict:
    streams_of = jax.random.split(jax.random.key(seed), 14)
    return {
        "stream_in": scatter_about(streams_of[0], (TOKENS, D), 1.0, 6.0, ((0, 16),)),
        "segments": draw_segments(jax.random.fold_in(streams_of[13], 71), 0),
        "head_table": draw_head_table(jax.random.fold_in(streams_of[13], 71), 0),
        "query_key_value": scatter_about(streams_of[3], (LAYERS, 3, D, D), D ** -0.5, 0.15625, ((2, 16), (3, 8))),
        "attention_out": scatter_about(streams_of[4], (LAYERS, D, D), (D // 16) ** -0.5, 0.625, ((1, 16), (2, 8))),
        "expand_weight": scatter_about(streams_of[5], (LAYERS, D, FF), D ** -0.5, 0.15625, ((1, 16), (2, 8))),
        "contract_weight": scatter_about(streams_of[6], (LAYERS, FF, D), FF ** -0.5, 0.078125, ((1, 8), (2, 16))),
        "norm_gain": jnp.clip(1.0 + 0.15 * jax.random.normal(streams_of[7], (LAYERS, 2, D), jnp.float32), 0.25, 1.75),
        "norm_bias": scatter_about(streams_of[8], (LAYERS, 2, D), 0.2, 1.2, (), jnp.float32),
        "attention_bias": scatter_about(streams_of[9], (LAYERS, 3, D), 0.3, 1.8, ((2, 8),), jnp.float32),
        "expand_bias": scatter_about(streams_of[10], (LAYERS, FF), 0.3, 1.8, ((1, 8),), jnp.float32),
        "contract_bias": scatter_about(streams_of[11], (LAYERS, D), 0.3, 1.8, (), jnp.float32),
        "cotangent": scatter_about(streams_of[12], (TOKENS, D), 1.0, 6.0, ((0, 16),)),
    }


@jax.custom_vjp
def low(v):
    return lax.optimization_barrier(v.astype(jnp.bfloat16)).astype(jnp.float32)

@jax.custom_vjp
def low_back(v):
    return v

def low_keep(v):
    return (low(v), None)

def low_pass(kept, grad):
    return (grad,)

def back_keep(v):
    return (v, None)

def back_low(kept, grad):
    return (low(grad),)
low.defvjp(low_keep, low_pass)
low_back.defvjp(back_keep, back_low)
HIGHEST = lax.Precision.HIGHEST

def layer_norm(values, gain, shift):
    row_mean = lax.optimization_barrier(jnp.mean(values, axis=-1, keepdims=True))
    centred = values - row_mean
    variance = lax.optimization_barrier(jnp.mean(centred * centred, axis=-1, keepdims=True))
    return centred * lax.rsqrt(variance + 1e-05) * gain + shift

def split_heads(matrix):
    return matrix.reshape(TOKENS // SEQ_LEN, SEQ_LEN, HEADS, HEAD_DIM).transpose(2, 0, 1, 3)

def reference(stream_in, segments, head_table, query_key_value, attention_out, expand_weight, contract_weight, norm_gain, norm_bias, attention_bias, expand_bias, contract_bias, cotangent):
    seq_segs = segments.reshape(TOKENS // SEQ_LEN, SEQ_LEN)
    places = jnp.arange(SEQ_LEN, dtype=jnp.int32)
    causal = places[None, :] <= places[:, None]
    allowed = (seq_segs[:, None, :] == seq_segs[:, :, None]) & causal[None]
    scale = HEAD_DIM ** (-0.5)
    slot_heads = head_table.reshape(-1)
    filled = (slot_heads < HEADS).astype(jnp.int32)
    order_rank = (jnp.cumsum(filled) - 1).astype(jnp.int32)
    head_ids = jnp.arange(HEADS, dtype=jnp.int32)
    head_rank = lax.optimization_barrier(jnp.sum(jnp.where(slot_heads[None, :] == head_ids[:, None], order_rank[None, :], 0), axis=1)).astype(jnp.int32)

    @jax.checkpoint
    def attend(triple):
        queries, keys, values = triple
        scores = low_back(jnp.einsum('sqd,skd->sqk', queries, keys, precision=HIGHEST) * scale)
        scores = jnp.where(allowed, scores, -1e+30)
        top = lax.optimization_barrier(jnp.max(scores, axis=2, keepdims=True))
        weights = jnp.exp(scores - top)
        weights = low(weights / lax.optimization_barrier(jnp.sum(weights, axis=2, keepdims=True)))
        return jnp.einsum('sqk,skd->sqd', weights, values, precision=HIGHEST)

    def forward(stream, in_weight, out_weight, up_weight, down_weight, gains, shifts, attn_shift, up_shift, down_shift):
        layer_outputs = []
        for layer_idx in range(LAYERS):
            normed = low(layer_norm(stream, gains[layer_idx, 0], shifts[layer_idx, 0]))
            queries = low(low_back(jnp.dot(normed, in_weight[layer_idx, 0], precision=HIGHEST) + attn_shift[layer_idx, 0]))
            keys = low(low_back(jnp.dot(normed, in_weight[layer_idx, 1], precision=HIGHEST)))
            values = low(low_back(jnp.dot(normed, in_weight[layer_idx, 2], precision=HIGHEST) + attn_shift[layer_idx, 1]))
            outputs = lax.map(attend, (split_heads(queries), split_heads(keys), split_heads(values)))
            outputs = low(low_back(outputs.reshape(HEADS, TOKENS, HEAD_DIM)))
            out_rows = jnp.take(out_weight[layer_idx].reshape(HEADS, HEAD_DIM, D), head_rank, axis=0)
            branch = low_back(jnp.einsum('htd,hdf->tf', outputs, out_rows, precision=HIGHEST))
            stream = stream + branch + attn_shift[layer_idx, 2]
            normed_two = low(layer_norm(stream, gains[layer_idx, 1], shifts[layer_idx, 1]))
            hidden = low_back(jnp.dot(normed_two, up_weight[layer_idx], precision=HIGHEST)) + up_shift[layer_idx]
            activated = low(jax.nn.gelu(hidden, approximate=True))
            stream = stream + low_back(jnp.dot(activated, down_weight[layer_idx], precision=HIGHEST)) + down_shift[layer_idx]
            layer_outputs.append(stream)
        return (stream, jnp.stack(layer_outputs))
    primals = (stream_in.astype(jnp.float32), query_key_value.astype(jnp.float32), attention_out.astype(jnp.float32), expand_weight.astype(jnp.float32), contract_weight.astype(jnp.float32), norm_gain.astype(jnp.float32), norm_bias.astype(jnp.float32), attention_bias.astype(jnp.float32), expand_bias.astype(jnp.float32), contract_bias.astype(jnp.float32))
    final, pullback, stacked = jax.vjp(forward, *primals, has_aux=True)
    grads = pullback(cotangent.astype(jnp.float32))
    return (stacked.astype(jnp.bfloat16), grads[0], grads[1], grads[2], grads[3], grads[4], grads[5], grads[6], grads[7], grads[8], grads[9])
```

```python
import functools

import jax
import jax.numpy as jnp
from jax import lax
from jax.experimental import pallas as pl
from jax.experimental.pallas import tpu as pltpu
from jax.sharding import PartitionSpec as P

D = 1280
HEADS = 20
HEAD_DIM = 64
SEQ = 1024
LAYERS = 2
BLOCK = 128
LOCAL = 3 * HEAD_DIM
SCALE = HEAD_DIM ** (-0.5)
AXES = ("row", "col")
BF16 = jnp.bfloat16
F32 = jnp.float32
LIMIT = 48 * 1024 * 1024


def device(z, x, core, y):
    return (z * 4 + (x // 2) * 2 + core) * 8 + (x % 2) * 4 + y


def pairs(target):
    out = []
    for z in range(4):
        for x in range(4):
            for core in range(2):
                for y in range(4):
                    out.append((device(z, x, core, y), device(*target(z, x, core, y))))
    return out


def along_y(k):
    return pairs(lambda z, x, core, y: (z, x, core, (y + k) % 4))


def along_plane(dz, dx):
    return pairs(lambda z, x, core, y: ((z + dz) % 4, (x + dx) % 4, core, y))


def to_feature(z, x, core, y):
    block = (x % 2) * 4 + y
    return (z, (x // 2) * 2 + core, block % 2, block // 2)


CORES = pairs(lambda z, x, core, y: (z, x, 1 - core, y))
TO_FEATURE = pairs(to_feature)
FROM_FEATURE = [(b, a) for a, b in TO_FEATURE]
PLANES = [
    [device(z, x, core, y) for z in range(4) for x in range(4)]
    for y in range(4)
    for core in range(2)
]
GROUPS = [
    [device(z, x, core, y) for y in range(4) for core in range(2)]
    for z in range(4)
    for x in range(4)
]


def send(value, perm):
    return lax.ppermute(value, AXES, perm)


def out_place(j, k):
    return pairs(
        lambda z, x, core, y: (z, (x // 2) * 2 + (core ^ j), x % 2, (y + k) % 4)
    )


def call(kernel, **kwargs):
    return pl.pallas_call(
        kernel, compiler_params=pltpu.CompilerParams(vmem_limit_bytes=LIMIT), **kwargs
    )


def assemble(pieces, places):
    count = len(pieces)
    shape = pieces[0].shape
    rows = shape[-2]

    def kernel(places_ref, *refs):
        sems = refs[count + 1]
        out = refs[count]
        copies = []
        for i in range(count):
            at = pl.ds(pl.multiple_of(places_ref[i] * rows, rows), rows)
            target = out.at[:, at, :] if len(shape) == 3 else out.at[at, :]
            copies.append(pltpu.make_async_copy(refs[i], target, sems.at[i]))
        for copy in copies:
            copy.start()
        for copy in copies:
            copy.wait()

    return call(
        kernel,
        out_shape=jax.ShapeDtypeStruct(
            shape[:-2] + (rows * count, shape[-1]), pieces[0].dtype
        ),
        in_specs=[pl.BlockSpec(memory_space=pltpu.SMEM)]
        + [pl.BlockSpec(memory_space=pl.ANY)] * count,
        out_specs=pl.BlockSpec(memory_space=pl.ANY),
        scratch_shapes=[pltpu.SemaphoreType.DMA((count,))],
    )(places, *pieces)


QB = 256


def allowed_at(start_ref, at, keys):
    key = lax.broadcasted_iota(jnp.int32, (keys, QB), 0)
    query = lax.broadcasted_iota(jnp.int32, (keys, QB), 1) + at
    return (key >= start_ref[:, at : at + QB]) & (key <= query)


def attend_forward_kernel(start_ref, qkv_ref, out_ref, turned_ref, lse_ref):
    heads = []
    for h in range(3):
        lo = h * HEAD_DIM
        q = qkv_ref[:, lo : lo + HEAD_DIM] * jnp.asarray(SCALE, BF16)
        k = qkv_ref[:, LOCAL + lo : LOCAL + lo + HEAD_DIM]
        v = qkv_ref[:, 2 * LOCAL + lo : 2 * LOCAL + lo + HEAD_DIM]
        heads.append((q, k, v.astype(F32).T.astype(BF16)))
    for block in range(SEQ // QB):
        at = block * QB
        keys = at + QB
        allowed = allowed_at(start_ref, at, keys)
        parts = []
        for h, (q, k, vt) in enumerate(heads):
            scores = lax.dot_general(
                k[:keys], q[at : at + QB], (((1,), (1,)), ((), ())), preferred_element_type=F32
            )
            scores = jnp.where(allowed, scores, -1e30)
            top = jnp.max(scores, axis=0, keepdims=True)
            weights = jnp.exp(scores - top)
            total = jnp.sum(weights, axis=0, keepdims=True)
            turned = (
                jnp.dot(vt[:, :keys], weights.astype(BF16), preferred_element_type=F32) / total
            )
            lse_ref[h : h + 1, at : at + QB] = top + jnp.log(total)
            turned_ref[h * HEAD_DIM : (h + 1) * HEAD_DIM, at : at + QB] = turned
            parts.append(turned)
        out_ref[at : at + QB, :] = jnp.concatenate(parts, axis=0).T.astype(BF16)


def attend_forward(start, qkv):
    return call(
        attend_forward_kernel,
        out_shape=(
            jax.ShapeDtypeStruct((SEQ, LOCAL), BF16),
            jax.ShapeDtypeStruct((LOCAL, SEQ), F32),
            jax.ShapeDtypeStruct((8, SEQ), F32),
        ),
    )(start, qkv)


def attend_backward_kernel(
    start_ref, qkv_ref, grad_ref, turned_ref, lse_ref, out_ref, dk_ref, dv_ref
):
    for h in range(3):
        lo = h * HEAD_DIM
        q = qkv_ref[:, lo : lo + HEAD_DIM] * jnp.asarray(SCALE, BF16)
        k = qkv_ref[:, LOCAL + lo : LOCAL + lo + HEAD_DIM]
        v = qkv_ref[:, 2 * LOCAL + lo : 2 * LOCAL + lo + HEAD_DIM]
        g = grad_ref[:, lo : lo + HEAD_DIM]
        kt = k.astype(F32).T.astype(BF16)
        delta = jnp.sum(
            g.astype(F32).T * turned_ref[lo : lo + HEAD_DIM, :], axis=0, keepdims=True
        )
        for block in reversed(range(SEQ // QB)):
            at = block * QB
            keys = at + QB
            allowed = allowed_at(start_ref, at, keys)
            q_part, g_part = q[at : at + QB], g[at : at + QB]
            scores = lax.dot_general(
                k[:keys], q_part, (((1,), (1,)), ((), ())), preferred_element_type=F32
            )
            probs = jnp.where(
                allowed, jnp.exp(scores - lse_ref[h : h + 1, at : at + QB]), 0.0
            )
            grad_probs = lax.dot_general(
                v[:keys], g_part, (((1,), (1,)), ((), ())), preferred_element_type=F32
            )
            grad_scores = (probs * (grad_probs - delta[:, at : at + QB])).astype(BF16)
            dv = jnp.dot(probs.astype(BF16), g_part, preferred_element_type=F32)
            dk = jnp.dot(grad_scores, q_part, preferred_element_type=F32)
            dq = jnp.dot(kt[:, :keys], grad_scores, preferred_element_type=F32) * SCALE
            out_ref[at : at + QB, lo : lo + HEAD_DIM] = dq.T.astype(BF16)
            if keys == SEQ:
                dk_ref[...] = dk
                dv_ref[...] = dv
            else:
                dk_ref[:keys, :] += dk
                dv_ref[:keys, :] += dv
        out_ref[:, LOCAL + lo : LOCAL + lo + HEAD_DIM] = dk_ref[...].astype(BF16)
        out_ref[:, 2 * LOCAL + lo : 2 * LOCAL + lo + HEAD_DIM] = dv_ref[...].astype(BF16)


def attend_backward(start, qkv, grad, turned, lse):
    return call(
        attend_backward_kernel,
        out_shape=jax.ShapeDtypeStruct((SEQ, 3 * LOCAL), BF16),
        scratch_shapes=[pltpu.VMEM((SEQ, HEAD_DIM), F32), pltpu.VMEM((SEQ, HEAD_DIM), F32)],
    )(start, qkv, grad, turned, lse)


def nt(a, b):
    return lax.dot_general(a, b, (((1,), (1,)), ((), ())), preferred_element_type=F32)


def tn(a, b):
    return lax.dot_general(a, b, (((0,), (0,)), ((), ())), preferred_element_type=F32)


def gelu(v):
    inner = 0.7978845608028654 * (v + 0.044715 * v * v * v)
    return 0.5 * v * (1.0 + jnp.tanh(inner))


def gelu_slope(v):
    t = jnp.tanh(0.7978845608028654 * (v + 0.044715 * v * v * v))
    return 0.5 * (1.0 + t) + 0.5 * v * (1.0 - t * t) * 0.7978845608028654 * (
        1.0 + 3 * 0.044715 * v * v
    )


UNITS = 640
TB = 256


def up_down_kernel(x_ref, up_ref, down_ref, bias_ref, hidden_ref, act_ref, out_ref):
    hidden = jnp.dot(x_ref[...], up_ref[...], preferred_element_type=F32) + bias_ref[...]
    hidden_ref[...] = hidden
    act = gelu(hidden).astype(BF16)
    act_ref[...] = act
    out_ref[...] = nt(act, down_ref[...]).astype(BF16)


def row_block(columns):
    return pl.BlockSpec((TB, columns), lambda i: (i, 0))


def whole(rows, columns, at=0):
    return pl.BlockSpec((rows, columns), lambda i: (0, at))


def up_down(x, weights, bias):
    return call(
        up_down_kernel,
        grid=(SEQ // TB,),
        in_specs=[row_block(D), whole(D, UNITS, 0), whole(D, UNITS, 1), whole(1, UNITS)],
        out_specs=[row_block(UNITS), row_block(UNITS), row_block(D)],
        out_shape=(
            jax.ShapeDtypeStruct((SEQ, UNITS), F32),
            jax.ShapeDtypeStruct((SEQ, UNITS), BF16),
            jax.ShapeDtypeStruct((SEQ, D), BF16),
        ),
    )(x, weights, weights, bias)


def up_down_back_kernel(g_ref, up_ref, down_ref, hidden_ref, low_ref, sum_ref, out_ref):
    grad = jnp.dot(g_ref[...], down_ref[...], preferred_element_type=F32)
    grad = grad * gelu_slope(hidden_ref[...])

    @pl.when(pl.program_id(0) == 0)
    def _():
        sum_ref[...] = jnp.zeros_like(sum_ref)

    sum_ref[...] += jnp.sum(grad, axis=0, keepdims=True)
    low = grad.astype(BF16)
    low_ref[...] = low
    out_ref[...] = nt(low, up_ref[...]).astype(BF16)


def up_down_back(g, weights, hidden):
    return call(
        up_down_back_kernel,
        grid=(SEQ // TB,),
        in_specs=[row_block(D), whole(D, UNITS, 0), whole(D, UNITS, 1), row_block(UNITS)],
        out_specs=[row_block(UNITS), whole(1, UNITS), row_block(D)],
        out_shape=(
            jax.ShapeDtypeStruct((SEQ, UNITS), BF16),
            jax.ShapeDtypeStruct((1, UNITS), F32),
            jax.ShapeDtypeStruct((SEQ, D), BF16),
        ),
    )(g, weights, weights, hidden)


def normal(v):
    mean = jnp.mean(v, axis=-1, keepdims=True)
    centred = v - mean
    variance = jnp.mean(centred * centred, axis=-1, keepdims=True)
    scale = lax.rsqrt(variance + 1e-05)
    return centred * scale, scale


def join_norm_kernel(a, b, c, d, old_ref, bias_ref, gain_ref, shift_ref, new_ref, low_ref):
    total = (a[...].astype(F32) + b[...].astype(F32)) + (c[...].astype(F32) + d[...].astype(F32))
    new = old_ref[...] + total + bias_ref[...]
    new_ref[...] = new
    low_ref[...] = (normal(new)[0] * gain_ref[...] + shift_ref[...]).astype(BF16)


def join_norm(parts, old, bias, gain, shift):
    return call(
        join_norm_kernel,
        out_shape=(
            jax.ShapeDtypeStruct((BLOCK, D), F32),
            jax.ShapeDtypeStruct((BLOCK, D), BF16),
        ),
    )(*parts, old, bias, gain, shift)


def norm_back_kernel(a, b, c, d, x_ref, old_ref, gain_ref, new_ref, low_ref, sums_ref):
    dy = (a[...].astype(F32) + b[...].astype(F32)) + (c[...].astype(F32) + d[...].astype(F32))
    unit, scale = normal(x_ref[...])
    slope = dy * gain_ref[...]
    mean_one = jnp.mean(slope, axis=-1, keepdims=True)
    mean_two = jnp.mean(slope * unit, axis=-1, keepdims=True)
    new = old_ref[...] + scale * (slope - mean_one - unit * mean_two)
    new_ref[...] = new
    low_ref[...] = new.astype(BF16)
    sums_ref[...] = jnp.concatenate(
        [
            jnp.sum(dy * unit, axis=0, keepdims=True),
            jnp.sum(dy, axis=0, keepdims=True),
            jnp.sum(new, axis=0, keepdims=True),
            jnp.zeros((5, D), F32),
        ],
        axis=0,
    )


def norm_back(parts, x, old, gain):
    return call(
        norm_back_kernel,
        out_shape=(
            jax.ShapeDtypeStruct((BLOCK, D), F32),
            jax.ShapeDtypeStruct((BLOCK, D), BF16),
            jax.ShapeDtypeStruct((8, D), F32),
        ),
    )(*parts, x, old, gain)


def on_device(
    stream_in,
    segments,
    head_table,
    query_key_value,
    attention_out,
    expand_weight,
    contract_weight,
    norm_gain,
    norm_bias,
    attention_bias,
    expand_bias,
    contract_bias,
    cotangent,
):
    row = lax.axis_index("row")
    col = lax.axis_index("col")
    core = row % 2
    z = row // 4
    y = col % 4
    x = ((row // 2) % 2) * 2 + col // 4
    first = core == 0
    feature = 2 * y + core
    mine = core * 4 + y
    sequence = z * 4 + x

    def spread_core(own, axis=-1):
        half = HEAD_DIM // 2
        low = lax.slice_in_dim(own, 0, half, axis=axis)
        high = lax.slice_in_dim(own, own.shape[axis] - half, own.shape[axis], axis=axis)
        got = send(jnp.where(first, high, low), CORES)
        return jnp.where(
            first,
            jnp.concatenate([own, got], axis=axis),
            jnp.concatenate([got, own], axis=axis),
        )

    def own_columns(value):
        return jnp.where(first, value[..., :160], value[..., 32:])

    packed_a = []
    packed_b = []
    for l in range(LAYERS):
        packed_a.append(
            jnp.concatenate([query_key_value[l, i] for i in range(3)] + [attention_out[l]], axis=1)
        )
        packed_b.append(jnp.concatenate([expand_weight[l], contract_weight[l].T], axis=1))
    biases = jnp.concatenate([attention_bias.reshape(LAYERS, 480), expand_bias], axis=1)
    moved_a = [send(packed_a[0], TO_FEATURE), None]
    biases = send(biases, TO_FEATURE)
    moved_b = [send(packed_b[0], TO_FEATURE), None]
    moved_a[1] = send(packed_a[1], TO_FEATURE)
    moved_b[1] = send(packed_b[1], TO_FEATURE)

    def widen(moved):
        own = moved[:, :480].reshape(80, 3, 160)
        full = spread_core(own).reshape(80, 3 * LOCAL)
        return jnp.concatenate([full, moved[:, 480:]], axis=1)

    def gather_plane(value):
        pieces = [value]
        places = [z * 4 + x]
        for dz in range(4):
            for dx in range(4):
                if dz or dx:
                    pieces.append(send(value, along_plane(dz, dx)))
                    places.append(((z - dz) % 4) * 4 + (x - dx) % 4)
        return assemble(pieces, jnp.stack(places).astype(jnp.int32))

    def gather_plane_far(value):
        return lax.all_gather(value, AXES, axis=0, tiled=True, axis_index_groups=PLANES)

    full_a = [gather_plane(widen(moved_a[0])), None]
    full_b = [gather_plane_far(moved_b[0]), None]
    full_a[1] = gather_plane_far(widen(moved_a[1]))
    full_b[1] = gather_plane_far(moved_b[1])

    query_bias = [spread_core(biases[l : l + 1, :160]) for l in range(LAYERS)]
    value_bias = [spread_core(biases[l : l + 1, 160:320]) for l in range(LAYERS)]
    qkv_bias = [
        jnp.concatenate([query_bias[l], jnp.zeros((1, LOCAL), F32), value_bias[l]], axis=1)
        for l in range(LAYERS)
    ]
    out_bias = []
    for l in range(LAYERS):
        out_bias.append(
            lax.dynamic_update_slice_in_dim(
                jnp.zeros((1, D), F32), biases[l : l + 1, 320:480], feature * 160, 1
            )
        )
    up_bias = [biases[l : l + 1, 480:] for l in range(LAYERS)]

    slot_heads = head_table.reshape(-1)
    filled = (slot_heads < HEADS).astype(jnp.int32)
    places24 = jnp.arange(24, dtype=jnp.int32)
    order = jnp.sum(jnp.where(places24[None, :] < places24[:, None], filled[None, :], 0), axis=1)
    head_ids = jnp.arange(HEADS, dtype=jnp.int32)
    rank = jnp.sum(jnp.where(slot_heads[None, :] == head_ids[:, None], order[None, :], 0), axis=1)
    head_of_rank = jnp.sum(jnp.where(rank[None, :] == head_ids[:, None], head_ids[None, :], 0), axis=1)
    local_heads = jnp.asarray([5 * (f // 2) + 2 * (f % 2) + i for f in range(8) for i in range(3)])
    rank_of_local = jnp.take(rank, local_heads)
    within = head_of_rank % 5
    local_of_rank = 6 * (head_of_rank // 5) + within + (within > 2).astype(jnp.int32)

    def out_weights(gathered):
        chosen = jnp.take(gathered.reshape(HEADS, HEAD_DIM, 160), rank_of_local, axis=0)
        blocks = chosen.reshape(8, LOCAL, 160).transpose(0, 2, 1)
        got = lax.all_to_all(blocks, AXES, 0, 0, tiled=True, axis_index_groups=GROUPS)
        return got.reshape(D, LOCAL)

    def out_weight_grads(local):
        blocks = local.astype(BF16).reshape(8, 160, LOCAL)
        got = lax.all_to_all(blocks, AXES, 0, 0, tiled=True, axis_index_groups=GROUPS)
        slots = got.transpose(0, 2, 1).reshape(24, HEAD_DIM, 160)
        return jnp.take(slots, local_of_rank, axis=0).reshape(D, 160)

    def sequence_of(value):
        return jnp.where(core == x % 2, value, send(value, CORES))

    def own_block(value):
        return lax.dynamic_slice_in_dim(value, mine * BLOCK, BLOCK, 0)

    tokens = sequence_of(stream_in)
    seg = lax.dynamic_slice_in_dim(segments, sequence * SEQ, SEQ)
    start = jnp.sum((seg[:, None] < seg[None, :]).astype(jnp.int32), axis=0, keepdims=True)

    block_places = jnp.stack(
        [core * 4 + (y - k) % 4 for k in (0, 1, 3, 2)]
        + [(1 - core) * 4 + (y - k) % 4 for k in (0, 1, 3, 2)]
    ).astype(jnp.int32)

    def gather_tokens(block):
        near = [block] + [send(block, along_y(k)) for k in (1, 3, 2)]
        far = [send(value, CORES) for value in near]
        return assemble(near + far, block_places)

    def sum_parts(partial):
        halves = partial.reshape(2, 4, BLOCK, D)
        got = send(lax.dynamic_index_in_dim(halves, 1 - core, 0, False), CORES)
        kept = lax.dynamic_index_in_dim(halves, core, 0, False)
        parts = []
        for k in (2, 1, 3, 0):
            at = (y + k) % 4
            part = lax.dynamic_index_in_dim(kept, at, 0, False).astype(F32) + (
                lax.dynamic_index_in_dim(got, at, 0, False).astype(F32)
            )
            part = part.astype(BF16)
            parts.append(send(part, along_y(k)) if k else part)
        return parts

    def scatter_plane(value):
        return lax.psum_scatter(
            value, AXES, scatter_dimension=0, tiled=True, axis_index_groups=PLANES
        )

    result_places = jnp.stack(
        [((x % 2) ^ j) * 4 + (y - k) % 4 for j in range(2) for k in range(4)]
    ).astype(jnp.int32)

    def to_result(value):
        blocks = jnp.moveaxis(value.reshape(value.shape[:-1] + (8, 160)), -2, 0)
        pieces = []
        for j in range(2):
            for k in range(4):
                at = (core ^ j) * 4 + (y + k) % 4
                piece = lax.dynamic_index_in_dim(blocks, at, 0, False)
                pieces.append(send(piece, out_place(j, k)))
        return assemble(pieces, result_places)

    head_column = lax.broadcasted_iota(jnp.int32, (1, LOCAL), 1)
    counted = first | (head_column >= HEAD_DIM)
    counted_all = jnp.concatenate([counted] * 3, axis=1)

    def gain_of(l, i):
        return norm_gain[l, i].reshape(1, D), norm_bias[l, i].reshape(1, D)

    stream = own_block(tokens).astype(F32)
    gain, shift = gain_of(0, 0)
    normed = (normal(tokens.astype(F32))[0] * gain + shift).astype(BF16)
    kept = []
    streams = []
    for l in range(LAYERS):
        w_in = full_a[l][:, : 3 * LOCAL]
        w_out = out_weights(full_a[l][:, 3 * LOCAL :])
        qkv = (jnp.dot(normed, w_in, preferred_element_type=F32) + qkv_bias[l]).astype(BF16)
        outputs, turned, lse = attend_forward(start, qkv)
        partial = nt(jnp.where(counted, outputs, 0).astype(BF16), w_out) + out_bias[l]
        parts = sum_parts(partial.astype(BF16))
        gain, shift = gain_of(l, 1)
        mid, low = join_norm(parts, stream, jnp.zeros((1, D), F32), gain, shift)
        normed_two = gather_tokens(low)
        hidden, act, partial = up_down(normed_two, full_b[l], up_bias[l])
        parts = sum_parts(partial)
        bias = contract_bias[l].reshape(1, D)
        kept.append(
            (stream, mid, normed, normed_two, hidden, act, w_in, w_out, qkv, outputs, turned, lse)
        )
        if l + 1 < LAYERS:
            gain, shift = gain_of(l + 1, 0)
            stream, low = join_norm(parts, mid, bias, gain, shift)
            normed = gather_tokens(low)
            streams.append(stream.astype(BF16))
        else:
            total = (parts[0].astype(F32) + parts[1].astype(F32)) + (
                parts[2].astype(F32) + parts[3].astype(F32)
            )
            streams.append((mid + total + bias).astype(BF16))
    activations = to_result(jnp.stack(streams))

    grad_low = sequence_of(cotangent)
    grad = own_block(grad_low).astype(F32)
    grad_sum = jnp.sum(grad, axis=0, keepdims=True)
    wide_sums = [None] * LAYERS
    plane_sums = [None] * LAYERS
    w_grads = [None] * LAYERS
    for l in reversed(range(LAYERS)):
        stream, mid, normed, normed_two, hidden, act, w_in, w_out, qkv, outputs, turned, lse = kept[l]
        low, up_sum, partial = up_down_back(grad_low, full_b[l], hidden)
        parts = sum_parts(partial)
        grad_down = tn(grad_low, act).astype(BF16)
        grad_up = tn(normed_two, low).astype(BF16)
        mid_grad, mid_low, sums_two = norm_back(parts, mid, grad, gain_of(l, 1)[0])
        mid_low = gather_tokens(mid_low)
        grad_outputs = jnp.dot(mid_low, w_out, preferred_element_type=F32).astype(BF16)
        grad_out = out_weight_grads(tn(mid_low, outputs))
        grad_qkv = attend_backward(start, qkv, grad_outputs, turned, lse)
        partial = nt(jnp.where(counted_all, grad_qkv, 0).astype(BF16), w_in)
        parts = sum_parts(partial.astype(BF16))
        grad_in = tn(normed, grad_qkv)
        grad_in = jnp.concatenate(
            [own_columns(grad_in[:, i * LOCAL : (i + 1) * LOCAL]) for i in range(3)], axis=1
        ).astype(BF16)
        qkv_sum = jnp.sum(grad_qkv.astype(F32), axis=0, keepdims=True)
        grad_new, next_low, sums_one = norm_back(parts, stream, mid_grad, gain_of(l, 0)[0])
        wide_sums[l] = jnp.concatenate(
            [sums_one[:2], sums_two[:3], grad_sum], axis=0
        )
        plane_sums[l] = jnp.concatenate(
            [
                own_columns(qkv_sum[:, :LOCAL]),
                own_columns(qkv_sum[:, 2 * LOCAL :]),
                up_sum,
                jnp.zeros((1, D - 960), F32),
            ],
            axis=1,
        )
        grad_sum = sums_one[2:3]
        grad = grad_new
        if l:
            grad_low = gather_tokens(next_low)
            w_grads[l] = scatter_plane(
                jnp.concatenate([grad_in, grad_out, grad_up, grad_down], axis=1)
            )
        else:
            early = scatter_plane(jnp.concatenate([grad_out, grad_up, grad_down], axis=1))
            late = scatter_plane(grad_in)
            w_grads[l] = jnp.concatenate([late, early], axis=1)
    grad_stream = to_result(grad)

    back = send(jnp.stack(w_grads), FROM_FEATURE).astype(F32)
    grad_query_key_value = back[:, :, :480].reshape(LAYERS, 80, 3, 160).transpose(0, 2, 1, 3)
    grad_attention_out = back[:, :, 480:640]
    grad_expand = back[:, :, 640:1280]
    grad_contract = back[:, :, 1280:].transpose(0, 2, 1)

    def sum_four(value, perms):
        one, two, three = (send(value, perm) for perm in perms)
        return (value + two) + (one + three)

    def sum_y(value):
        value = value + send(value, CORES)
        return sum_four(value, [along_y(k) for k in (1, 2, 3)])

    def sum_plane(value):
        value = sum_four(value, [along_plane(0, k) for k in (1, 2, 3)])
        return sum_four(value, [along_plane(k, 0) for k in (1, 2, 3)])

    wide = sum_y(jnp.concatenate(wide_sums, axis=0))
    sums = sum_plane(jnp.concatenate([wide] + plane_sums, axis=0))
    wide = sums[:12].reshape(LAYERS, 6, D)
    plane = send(sums[12:], FROM_FEATURE)
    grad_norm_gain = jnp.stack([wide[:, 0], wide[:, 2]], axis=1)
    grad_norm_bias = jnp.stack([wide[:, 1], wide[:, 3]], axis=1)
    out_sums = lax.dynamic_slice_in_dim(wide[:, 4], col * 160, 160, 1)
    grad_attention_bias = jnp.stack([plane[:, :160], plane[:, 160:320], out_sums], axis=1)
    grad_expand_bias = plane[:, 320:960]
    grad_contract_bias = wide[:, 5]
    return (
        activations,
        grad_stream,
        grad_query_key_value,
        grad_attention_out,
        grad_expand,
        grad_contract,
        grad_norm_gain,
        grad_norm_bias,
        grad_attention_bias,
        grad_expand_bias,
        grad_contract_bias,
    )


def solution(mesh):
    placed = (
        P("row", None),
        P(),
        P(),
        P(None, None, "row", "col"),
        P(None, "row", "col"),
        P(None, "row", "col"),
        P(None, "col", "row"),
        P(),
        P(),
        P(None, None, "col"),
        P(None, "col"),
        P(),
        P("row", None),
    )
    return jax.shard_map(
        on_device,
        mesh=mesh,
        in_specs=placed,
        out_specs=(
            P(None, "row", "col"),
            P("row", "col"),
            P(None, None, "row", "col"),
            P(None, "row", "col"),
            P(None, "row", "col"),
            P(None, "col", "row"),
            P(),
            P(),
            P(None, None, "col"),
            P(None, "col"),
            P(),
        ),
        check_vma=False,
    )
```

```python
import functools

import jax
import jax.numpy as jnp
from jax import lax
from jax.experimental import pallas as pl
from jax.experimental.pallas import tpu as pltpu
from jax.sharding import PartitionSpec as P

D = 1280
HEADS = 20
HEAD_DIM = 64
SEQ = 1024
LAYERS = 2
BLOCK = 128
LOCAL = 3 * HEAD_DIM
SCALE = HEAD_DIM ** (-0.5)
AXES = ("row", "col")
BF16 = jnp.bfloat16
F32 = jnp.float32
MIB = 1024 * 1024


def device(z, x, core, y):
    return (z * 4 + (x // 2) * 2 + core) * 8 + (x % 2) * 4 + y


def pairs(target):
    out = []
    for z in range(4):
        for x in range(4):
            for core in range(2):
                for y in range(4):
                    out.append((device(z, x, core, y), device(*target(z, x, core, y))))
    return out


def along_y(k):
    return pairs(lambda z, x, core, y: (z, x, core, (y + k) % 4))


def to_step(dy, dc):
    return pairs(lambda z, x, core, y: (z, x, core ^ dc, (y + dy) % 4))


def along_plane(dz, dx):
    return pairs(lambda z, x, core, y: ((z + dz) % 4, (x + dx) % 4, core, y))


def to_feature(z, x, core, y):
    block = (x % 2) * 4 + y
    return (z, (x // 2) * 2 + core, block % 2, block // 2)


CORES = pairs(lambda z, x, core, y: (z, x, 1 - core, y))
TO_FEATURE = pairs(to_feature)
FROM_FEATURE = [(b, a) for a, b in TO_FEATURE]
PLANES = [
    [device(z, x, core, y) for z in range(4) for x in range(4)]
    for y in range(4)
    for core in range(2)
]
BY_FEATURE = [
    [device(z, x, core, y) for y in range(4) for core in range(2)]
    for z in range(4)
    for x in range(4)
]
BY_TOKEN = [
    [device(z, x, core, y) for core in range(2) for y in range(4)]
    for z in range(4)
    for x in range(4)
]
STEPS = [(dy, dc) for dy in (0, 1, 3, 2) for dc in (0, 1)]
HOPS = (0, 1, 3, 2)


def send(value, perm):
    return lax.ppermute(value, AXES, perm)


CORE, TO_BLOCK, TO_SLOT, FROM_BLOCK, FROM_SLOT, HELD = 0, 8, 16, 24, 32, 40
IN_SMEM = pl.BlockSpec(memory_space=pltpu.SMEM)
ANYWHERE = pl.BlockSpec(memory_space=pl.ANY)


def call(kernel, limit=24, **kwargs):
    return pl.pallas_call(
        kernel, compiler_params=pltpu.CompilerParams(vmem_limit_bytes=limit * MIB), **kwargs
    )


def shaped(shape, dtype):
    return jax.ShapeDtypeStruct(shape, dtype)


def full(shape):
    return pl.BlockSpec(shape, lambda i: (0,) * len(shape))


def fetch(pieces, target, sems):
    rows = pieces[0].shape[0]
    copies = []
    for i, piece in enumerate(pieces):
        copies.append(
            pltpu.make_async_copy(piece, target.at[pl.ds(i * rows, rows), :], sems.at[i])
        )
    for copy in copies:
        copy.start()
    return copies


def pieces_of(count, rows=BLOCK, columns=D):
    return [pltpu.VMEM((count * rows, columns), BF16), pltpu.SemaphoreType.DMA((count,))]


def assemble(pieces, places):
    count = len(pieces)
    shape = pieces[0].shape
    rows = shape[-2]

    def kernel(places_ref, *refs):
        sems = refs[count + 1]
        out = refs[count]
        copies = []
        for i in range(count):
            at = pl.ds(pl.multiple_of(places_ref[i] * rows, rows), rows)
            target = out.at[:, at, :] if len(shape) == 3 else out.at[at, :]
            copies.append(pltpu.make_async_copy(refs[i], target, sems.at[i]))
        for copy in copies:
            copy.start()
        for copy in copies:
            copy.wait()

    return call(
        kernel,
        grid=(1,),
        out_shape=shaped(shape[:-2] + (rows * count, shape[-1]), pieces[0].dtype),
        in_specs=[IN_SMEM] + [ANYWHERE] * count,
        out_specs=full(shape[:-2] + (rows * count, shape[-1])),
        scratch_shapes=[pltpu.SemaphoreType.DMA((count,))],
    )(places, *pieces)


def in_order(value, places):
    def kernel(places_ref, in_ref, out, sems):
        copies = []
        for i in range(8):
            at = pl.ds(pl.multiple_of(places_ref[i] * BLOCK, BLOCK), BLOCK)
            copies.append(
                pltpu.make_async_copy(
                    in_ref.at[at, :], out.at[pl.ds(i * BLOCK, BLOCK), :], sems.at[i]
                )
            )
        for copy in copies:
            copy.start()
        for copy in copies:
            copy.wait()

    return call(
        kernel,
        grid=(1,),
        out_shape=shaped(value.shape, value.dtype),
        in_specs=[IN_SMEM, ANYWHERE],
        out_specs=full(value.shape),
        scratch_shapes=[pltpu.SemaphoreType.DMA((8,))],
    )(places, value)


def end_to_end(pieces):
    return assemble(pieces, jnp.arange(len(pieces), dtype=jnp.int32))


def rows_at(meta_ref, index):
    return pl.ds(pl.multiple_of(meta_ref[index] * BLOCK, BLOCK), BLOCK)


def hold(value, *until):
    return lax.optimization_barrier((value,) + until)[0]


def nt(a, b):
    return lax.dot_general(a, b, (((1,), (1,)), ((), ())), preferred_element_type=F32)


def tn(a, b):
    return lax.dot_general(a, b, (((0,), (0,)), ((), ())), preferred_element_type=F32)


QB = 256


def allowed_at(start_ref, at, keys):
    key = lax.broadcasted_iota(jnp.int32, (keys, QB), 0)
    query = lax.broadcasted_iota(jnp.int32, (keys, QB), 1) + at
    return (key >= start_ref[:, at : at + QB]) & (key <= query)


def attend_forward_kernel(meta_ref, start_ref, qkv_ref, *refs):
    pieces = refs[:8]
    turned_ref, lse_ref, own_ref, sems = refs[8:]
    heads = []
    for h in range(3):
        lo = h * HEAD_DIM
        q = qkv_ref[:, lo : lo + HEAD_DIM] * jnp.asarray(SCALE, BF16)
        k = qkv_ref[:, LOCAL + lo : LOCAL + lo + HEAD_DIM]
        v = qkv_ref[:, 2 * LOCAL + lo : 2 * LOCAL + lo + HEAD_DIM]
        heads.append((q, k, v.astype(F32).T.astype(BF16)))
    for block in range(SEQ // QB):
        at = block * QB
        keys = at + QB
        allowed = allowed_at(start_ref, at, keys)
        parts = []
        for h, (q, k, vt) in enumerate(heads):
            scores = nt(k[:keys], q[at : at + QB])
            scores = jnp.where(allowed, scores, -1e30)
            top = jnp.max(scores, axis=0, keepdims=True)
            weights = jnp.exp(scores - top)
            total = jnp.sum(weights, axis=0, keepdims=True)
            turned = (
                jnp.dot(vt[:, :keys], weights.astype(BF16), preferred_element_type=F32) / total
            )
            lse_ref[h : h + 1, at : at + QB] = top + jnp.log(total)
            turned_ref[h * HEAD_DIM : (h + 1) * HEAD_DIM, at : at + QB] = turned
            parts.append(turned)
        out = jnp.concatenate(parts, axis=0).T.astype(BF16)
        own_ref[at : at + QB, :] = jnp.where(meta_ref[CORE] == 0, out[:, :160], out[:, 32:])
    copies = [
        pltpu.make_async_copy(own_ref.at[rows_at(meta_ref, TO_BLOCK + j), :], pieces[j], sems.at[j])
        for j in range(8)
    ]
    for copy in copies:
        copy.start()
    for copy in copies:
        copy.wait()


def attend_forward(meta, start, qkv):
    results = call(
        attend_forward_kernel,
        grid=(1,),
        in_specs=[IN_SMEM, full((1, SEQ)), full((SEQ, 3 * LOCAL))],
        out_specs=[ANYWHERE] * 8
        + [full((LOCAL, SEQ)), full((8, SEQ))],
        out_shape=[shaped((BLOCK, 160), BF16)] * 8
        + [shaped((LOCAL, SEQ), F32), shaped((8, SEQ), F32)],
        scratch_shapes=[pltpu.VMEM((SEQ, 160), BF16), pltpu.SemaphoreType.DMA((8,))],
    )(meta, start, qkv)
    return results[:8], results[8], results[9]


WIDE = LOCAL + 160


def attend_backward_kernel(meta_ref, start_ref, qkv_ref, turned_ref, lse_ref, *refs):
    pieces = refs[:8]
    out_ref, own_ref, sum_ref, mid_ref, grad_ref, sems, dk_ref, dv_ref = refs[8:]
    copies = [
        pltpu.make_async_copy(
            pieces[j], grad_ref.at[rows_at(meta_ref, FROM_BLOCK + j), :], sems.at[j]
        )
        for j in range(8)
    ]
    for copy in copies:
        copy.start()
    for copy in copies:
        copy.wait()
    mid_ref[...] = grad_ref[:, LOCAL:]
    for h in range(3):
        lo = h * HEAD_DIM
        q = qkv_ref[:, lo : lo + HEAD_DIM] * jnp.asarray(SCALE, BF16)
        k = qkv_ref[:, LOCAL + lo : LOCAL + lo + HEAD_DIM]
        v = qkv_ref[:, 2 * LOCAL + lo : 2 * LOCAL + lo + HEAD_DIM]
        g = grad_ref[:, lo : lo + HEAD_DIM]
        kt = k.astype(F32).T.astype(BF16)
        delta = jnp.sum(
            g.astype(F32).T * turned_ref[lo : lo + HEAD_DIM, :], axis=0, keepdims=True
        )
        for block in reversed(range(SEQ // QB)):
            at = block * QB
            keys = at + QB
            allowed = allowed_at(start_ref, at, keys)
            q_part, g_part = q[at : at + QB], g[at : at + QB]
            scores = nt(k[:keys], q_part)
            probs = jnp.where(
                allowed, jnp.exp(scores - lse_ref[h : h + 1, at : at + QB]), 0.0
            )
            grad_probs = nt(v[:keys], g_part)
            grad_scores = (probs * (grad_probs - delta[:, at : at + QB])).astype(BF16)
            dv = jnp.dot(probs.astype(BF16), g_part, preferred_element_type=F32)
            dk = jnp.dot(grad_scores, q_part, preferred_element_type=F32)
            dq = jnp.dot(kt[:, :keys], grad_scores, preferred_element_type=F32) * SCALE
            out_ref[at : at + QB, lo : lo + HEAD_DIM] = dq.T.astype(BF16)
            if keys == SEQ:
                dk_ref[...] = dk
                dv_ref[...] = dv
            else:
                dk_ref[:keys, :] += dk
                dv_ref[:keys, :] += dv
        out_ref[:, LOCAL + lo : LOCAL + lo + HEAD_DIM] = dk_ref[...].astype(BF16)
        out_ref[:, 2 * LOCAL + lo : 2 * LOCAL + lo + HEAD_DIM] = dv_ref[...].astype(BF16)
    for i in range(3):
        part = out_ref[:, i * LOCAL : (i + 1) * LOCAL]
        own = jnp.where(meta_ref[CORE] == 0, part[:, :160], part[:, 32:])
        own_ref[:, i * 160 : (i + 1) * 160] = own
        sum_ref[:, i * 160 : (i + 1) * 160] = jnp.sum(own.astype(F32), axis=0, keepdims=True)


def attend_backward(meta, start, qkv, turned, lse, pieces):
    return call(
        attend_backward_kernel,
        grid=(1,),
        in_specs=[
            IN_SMEM,
            full((1, SEQ)),
            full((SEQ, 3 * LOCAL)),
            full((LOCAL, SEQ)),
            full((8, SEQ)),
        ]
        + [ANYWHERE] * 8,
        out_specs=[full((SEQ, 3 * LOCAL)), full((SEQ, 480)), full((1, 480)), full((SEQ, 160))],
        out_shape=(
            shaped((SEQ, 3 * LOCAL), BF16),
            shaped((SEQ, 480), BF16),
            shaped((1, 480), F32),
            shaped((SEQ, 160), BF16),
        ),
        scratch_shapes=[
            pltpu.VMEM((SEQ, WIDE), BF16),
            pltpu.SemaphoreType.DMA((8,)),
            pltpu.VMEM((SEQ, HEAD_DIM), F32),
            pltpu.VMEM((SEQ, HEAD_DIM), F32),
        ],
    )(meta, start, qkv, turned, lse, *pieces)


def gelu(v):
    inner = 0.7978845608028654 * (v + 0.044715 * v * v * v)
    return 0.5 * v * (1.0 + jnp.tanh(inner))


def gelu_slope(v):
    t = jnp.tanh(0.7978845608028654 * (v + 0.044715 * v * v * v))
    return 0.5 * (1.0 + t) + 0.5 * v * (1.0 - t * t) * 0.7978845608028654 * (
        1.0 + 3 * 0.044715 * v * v
    )


UNITS = 640
HALF = 512
WEIGHT_SPECS = [
    pl.BlockSpec((D, UNITS), lambda i: (0, 0)),
    pl.BlockSpec((D, UNITS), lambda i: (0, 1)),
]


def up_down_kernel(
    a, b, c, d, up_ref, down_ref, bias_ref, hidden_ref, act_ref, out_ref, x_ref, sems, y_ref, done
):
    copies = fetch((a, b, c, d), x_ref, sems)
    outs = []
    for i in range(2):
        at = pl.ds(i * 256, 256)
        copies[2 * i].wait()
        copies[2 * i + 1].wait()
        hidden = jnp.dot(x_ref[at, :], up_ref[...], preferred_element_type=F32) + bias_ref[...]
        hidden_ref[at, :] = hidden
        act = gelu(hidden).astype(BF16)
        act_ref[at, :] = act
        y_ref[at, :] = nt(act, down_ref[...]).astype(BF16)
        outs.append(pltpu.make_async_copy(y_ref.at[at, :], out_ref.at[at, :], done.at[i]))
        outs[i].start()
    for copy in outs:
        copy.wait()


def up_down(pieces, weights, bias):
    return call(
        up_down_kernel,
        grid=(1,),
        in_specs=[ANYWHERE] * 4 + WEIGHT_SPECS + [full((1, UNITS))],
        out_specs=[full((HALF, UNITS)), full((HALF, UNITS)), ANYWHERE],
        scratch_shapes=pieces_of(4) + pieces_of(2, 256),
        out_shape=(
            shaped((HALF, UNITS), F32),
            shaped((HALF, UNITS), BF16),
            shaped((HALF, D), BF16),
        ),
    )(*pieces, weights, weights, bias)


def up_down_back_kernel(first, *refs):
    if first is None:
        ins, refs = refs[:4], refs[4:]
    else:
        ins = [refs[0].at[pl.ds((first + i) * BLOCK, BLOCK), :] for i in range(4)]
        refs = refs[1:]
    up_ref, down_ref, hidden_ref, low_ref, sum_ref, out_ref, g_ref, sems, y_ref, done = refs
    copies = fetch(ins, g_ref, sems)
    outs = []
    total = jnp.zeros((1, UNITS), F32)
    for i in range(2):
        at = pl.ds(i * 256, 256)
        copies[2 * i].wait()
        copies[2 * i + 1].wait()
        grad = jnp.dot(g_ref[at, :], down_ref[...], preferred_element_type=F32)
        grad = grad * gelu_slope(hidden_ref[at, :])
        total += jnp.sum(grad, axis=0, keepdims=True)
        low = grad.astype(BF16)
        low_ref[at, :] = low
        y_ref[at, :] = nt(low, up_ref[...]).astype(BF16)
        outs.append(pltpu.make_async_copy(y_ref.at[at, :], out_ref.at[at, :], done.at[i]))
        outs[i].start()
    sum_ref[...] = total
    for copy in outs:
        copy.wait()


def up_down_back(pieces, weights, hidden, first=None):
    return call(
        functools.partial(up_down_back_kernel, first),
        grid=(1,),
        in_specs=[ANYWHERE] * len(pieces) + WEIGHT_SPECS + [full((HALF, UNITS))],
        out_specs=[full((HALF, UNITS)), full((1, UNITS)), ANYWHERE],
        scratch_shapes=pieces_of(4) + pieces_of(2, 256),
        out_shape=(
            shaped((HALF, UNITS), BF16),
            shaped((1, UNITS), F32),
            shaped((HALF, D), BF16),
        ),
    )(*pieces, weights, weights, hidden)


def add_cores_kernel(near_ref, far_ref, *refs):
    outs, (one, one_sems, two, two_sems, sums, done) = refs[:4], refs[4:]
    at = [pl.ds(i * BLOCK, BLOCK) for i in range(4)]
    order = (3, 1, 2, 0)
    ins = {}
    for i in order:
        ins[i] = (
            pltpu.make_async_copy(near_ref.at[at[i], :], one.at[at[i], :], one_sems.at[i]),
            pltpu.make_async_copy(far_ref.at[at[i], :], two.at[at[i], :], two_sems.at[i]),
        )
        ins[i][0].start()
        ins[i][1].start()
    copies = []
    for i in order:
        ins[i][0].wait()
        ins[i][1].wait()
        sums[at[i], :] = (one[at[i], :].astype(F32) + two[at[i], :].astype(F32)).astype(BF16)
        copies.append(pltpu.make_async_copy(sums.at[at[i], :], outs[i], done.at[i]))
        copies[-1].start()
    for copy in copies:
        copy.wait()


def add_cores(near, far):
    return call(
        add_cores_kernel,
        grid=(1,),
        in_specs=[ANYWHERE] * 2,
        out_specs=[ANYWHERE] * 4,
        out_shape=[shaped((BLOCK, D), BF16)] * 4,
        scratch_shapes=pieces_of(4) * 3,
    )(near, far)


def project_kernel(meta_ref, *refs):
    pieces = refs[:8]
    w_ref, bias_ref, qkv_ref, normed_ref, x_ref, sems = refs[8:]
    copies = fetch(pieces, x_ref, sems)
    for i in range(0, 8, 2):
        copies[i].wait()
        copies[i + 1].wait()
        x = x_ref[i * BLOCK : (i + 2) * BLOCK, :]
        qkv = jnp.dot(x, w_ref[:, : 3 * LOCAL], preferred_element_type=F32) + bias_ref[...]
        qkv = qkv.astype(BF16)
        for k in range(2):
            at = rows_at(meta_ref, HELD + i + k)
            normed_ref[at, :] = x[k * BLOCK : (k + 1) * BLOCK]
            qkv_ref[at, :] = qkv[k * BLOCK : (k + 1) * BLOCK]


def columns_of(at):
    return pl.BlockSpec((D, UNITS), lambda i: (0, at))


def project_first_kernel(x_ref, w_ref, bias_ref, qkv_ref):
    qkv = jnp.dot(x_ref[...], w_ref[:, : 3 * LOCAL], preferred_element_type=F32)
    qkv_ref[...] = (qkv + bias_ref[...]).astype(BF16)


def project_first(normed, weights, bias):
    return call(
        project_first_kernel,
        grid=(4,),
        in_specs=[pl.BlockSpec((256, D), lambda i: (i, 0)), columns_of(0), full((1, 3 * LOCAL))],
        out_specs=pl.BlockSpec((256, 3 * LOCAL), lambda i: (i, 0)),
        out_shape=shaped((SEQ, 3 * LOCAL), BF16),
    )(normed, weights, bias)


def turn_heads_kernel(rank_ref, one_ref, two_ref, terms_ref, out_ref):
    for h in range(0, HEADS, 2):
        parts = []
        for k in range(2):
            at = pl.ds(pl.multiple_of(rank_ref[h + k] * HEAD_DIM, HEAD_DIM), HEAD_DIM)
            parts.append(
                jnp.concatenate(
                    [one_ref[at, 64:].astype(F32), two_ref[at, :96].astype(F32)], axis=1
                )
            )
        out_ref[:, h * HEAD_DIM : (h + 2) * HEAD_DIM] = (
            jnp.concatenate(parts, axis=0).T.astype(BF16)
        )
    out_ref[:, D:] = terms_ref[...]


def turn_heads(rank, weights, at, terms):
    first = at // 128
    return call(
        turn_heads_kernel,
        grid=(1,),
        in_specs=[
            IN_SMEM,
            pl.BlockSpec((D, 128), lambda i: (0, first)),
            pl.BlockSpec((D, 128), lambda i: (0, first + 1)),
            full((160, 128)),
        ],
        out_specs=full((160, D + 128)),
        out_shape=shaped((160, D + 128), BF16),
    )(rank, weights, weights, terms)


def project(meta, pieces, weights, at, bias):
    return call(
        project_kernel,
        grid=(1,),
        in_specs=[IN_SMEM]
        + [ANYWHERE] * 8
        + [columns_of(at), full((1, 3 * LOCAL))],
        out_specs=[full((SEQ, 3 * LOCAL)), full((SEQ, D))],
        scratch_shapes=pieces_of(8),
        out_shape=(shaped((SEQ, 3 * LOCAL), BF16), shaped((SEQ, D), BF16)),
    )(meta, *pieces, weights, bias)


def project_back(meta, grads, weights, column, first):
    def kernel(meta_ref, grad_ref, w_ref, out_ref, y_ref, done):
        outs = []
        column = lax.broadcasted_iota(jnp.int32, (1, 3 * LOCAL), 1)
        twice = jnp.zeros((1, 3 * LOCAL), jnp.int32)
        for i in range(3):
            at = column - i * LOCAL
            twice += jnp.where((at >= 0) & (at < HEAD_DIM), 1, 0)
        counted = twice * meta_ref[CORE] == 0
        for i in range(2):
            x = jnp.concatenate(
                [grad_ref[rows_at(meta_ref, HELD + first + 2 * i + k), :] for k in range(2)],
                axis=0,
            )
            x = jnp.where(counted, x.astype(F32), 0.0).astype(BF16)
            at = pl.ds(i * 256, 256)
            y_ref[at, :] = nt(x, w_ref[:, : 3 * LOCAL]).astype(BF16)
            outs.append(pltpu.make_async_copy(y_ref.at[at, :], out_ref.at[at, :], done.at[i]))
            outs[i].start()
        for copy in outs:
            copy.wait()

    return call(
        kernel,
        grid=(1,),
        in_specs=[IN_SMEM, full((SEQ, 3 * LOCAL)), columns_of(column)],
        out_specs=ANYWHERE,
        out_shape=shaped((HALF, D), BF16),
        scratch_shapes=pieces_of(2, 256),
    )(meta, grads, weights)


def normal(v):
    mean = jnp.mean(v, axis=-1, keepdims=True)
    centred = v - mean
    variance = jnp.mean(centred * centred, axis=-1, keepdims=True)
    scale = lax.rsqrt(variance + 1e-05)
    return centred * scale, scale


def four(pieces, held_ref, sems):
    copies = fetch(pieces, held_ref, sems)
    for copy in copies:
        copy.wait()
    a, b, c, d = (held_ref[i * BLOCK : (i + 1) * BLOCK, :].astype(F32) for i in range(4))
    return (a + b) + (c + d)


def send_out(value, held_ref, out, sem):
    held_ref[...] = value
    copy = pltpu.make_async_copy(held_ref, out, sem)
    copy.start()
    return copy


def join_norm_kernel(
    a, b, c, d, old_ref, bias_ref, gain_ref, shift_ref, new_ref, low_ref, x_ref, sems, y_ref, done
):
    new = old_ref[...] + four((a, b, c, d), x_ref, sems) + bias_ref[...]
    low = (normal(new)[0] * gain_ref[...] + shift_ref[...]).astype(BF16)
    copy = send_out(low, y_ref, low_ref, done.at[0])
    new_ref[...] = new
    copy.wait()


def join_norm(parts, old, bias, gain, shift):
    return call(
        join_norm_kernel,
        grid=(1,),
        in_specs=[ANYWHERE] * 4 + [full((BLOCK, D))] + [full((1, D))] * 3,
        out_specs=[full((BLOCK, D)), ANYWHERE],
        out_shape=(shaped((BLOCK, D), F32), shaped((BLOCK, D), BF16)),
        scratch_shapes=pieces_of(4) + pieces_of(1),
    )(*parts, old, bias, gain, shift)


def join_heads_kernel(meta_ref, *refs):
    pieces = refs[:8]
    w_ref, old_ref, bias_ref, gain_ref, shift_ref, new_ref, low_ref, heads_ref = refs[8:16]
    slots, sems, y_ref, done = refs[16:]
    copies = [
        pltpu.make_async_copy(pieces[j], slots.at[meta_ref[FROM_SLOT + j]], sems.at[j])
        for j in range(8)
    ]
    for copy in copies:
        copy.start()
    for copy in copies:
        copy.wait()
    x = jnp.concatenate([slots[f] for f in range(8)], axis=1)
    new = old_ref[...] + nt(x, w_ref[...]) + bias_ref[...]
    low = (normal(new)[0] * gain_ref[...] + shift_ref[...]).astype(BF16)
    copy = send_out(low, y_ref, low_ref, done.at[0])
    new_ref[...] = new
    heads_ref[...] = x
    copy.wait()


def join_heads(meta, pieces, weights, old, bias, gain, shift):
    return call(
        join_heads_kernel,
        grid=(1,),
        in_specs=[IN_SMEM]
        + [ANYWHERE] * 8
        + [pl.BlockSpec((D, D), lambda i: (0, 0)), full((BLOCK, D))]
        + [full((1, D))] * 3,
        out_specs=[full((BLOCK, D)), ANYWHERE, full((BLOCK, D))],
        out_shape=(shaped((BLOCK, D), F32), shaped((BLOCK, D), BF16), shaped((BLOCK, D), BF16)),
        scratch_shapes=[pltpu.VMEM((8, BLOCK, 160), BF16), pltpu.SemaphoreType.DMA((8,))]
        + pieces_of(1),
    )(meta, *pieces, weights, old, bias, gain, shift)


def norm_back_math(dy, x, old, gain):
    unit, scale = normal(x)
    slope = dy * gain
    mean_one = jnp.mean(slope, axis=-1, keepdims=True)
    mean_two = jnp.mean(slope * unit, axis=-1, keepdims=True)
    new = old + scale * (slope - mean_one - unit * mean_two)
    sums = jnp.concatenate(
        [
            jnp.sum(dy * unit, axis=0, keepdims=True),
            jnp.sum(dy, axis=0, keepdims=True),
            jnp.sum(new, axis=0, keepdims=True),
            jnp.zeros((5, D), F32),
        ],
        axis=0,
    )
    return new, sums


def norm_back_kernel(
    a, b, c, d, x_ref, old_ref, gain_ref, new_ref, low_ref, sums_ref, p_ref, sems, y_ref, done
):
    total = four((a, b, c, d), p_ref, sems)
    new, sums = norm_back_math(total, x_ref[...], old_ref[...], gain_ref[...])
    copy = send_out(new.astype(BF16), y_ref, low_ref, done.at[0])
    new_ref[...] = new
    sums_ref[...] = sums
    copy.wait()


def norm_back(parts, x, old, gain):
    return call(
        norm_back_kernel,
        grid=(1,),
        in_specs=[ANYWHERE] * 4 + [full((BLOCK, D))] * 2 + [full((1, D))],
        out_specs=[full((BLOCK, D)), ANYWHERE, full((8, D))],
        out_shape=(shaped((BLOCK, D), F32), shaped((BLOCK, D), BF16), shaped((8, D), F32)),
        scratch_shapes=pieces_of(4) + pieces_of(1),
    )(*parts, x, old, gain)


def norm_back_heads_kernel(
    meta_ref, a, b, c, d, x_ref, old_ref, gain_ref, w_ref, new_ref, low_ref, sums_ref, *refs
):
    pieces, (slots, sent, p_ref, sems, y_ref, done) = refs[:8], refs[8:]
    total = four((a, b, c, d), p_ref, sems)
    new, sums = norm_back_math(total, x_ref[...], old_ref[...], gain_ref[...])
    new_ref[...] = new
    low = new.astype(BF16)
    copies = [send_out(low, y_ref, low_ref, done.at[0])]
    sums_ref[...] = sums
    grads = jnp.dot(low, w_ref[...], preferred_element_type=F32)
    for f in range(8):
        at = 320 * (f // 2) + 128 * (f % 2)
        slots[f, :, :LOCAL] = grads[:, at : at + LOCAL].astype(BF16)
        slots[f, :, LOCAL:] = low[:, f * 160 : (f + 1) * 160]
    for j in range(8):
        copies.append(
            pltpu.make_async_copy(slots.at[meta_ref[TO_SLOT + j]], pieces[j], sent.at[j])
        )
        copies[-1].start()
    for copy in copies:
        copy.wait()


def norm_back_heads(meta, parts, x, old, gain, weights):
    results = call(
        norm_back_heads_kernel,
        grid=(1,),
        in_specs=[IN_SMEM]
        + [ANYWHERE] * 4
        + [full((BLOCK, D))] * 2
        + [full((1, D)), pl.BlockSpec((D, D), lambda i: (0, 0))],
        out_specs=[full((BLOCK, D)), ANYWHERE, full((8, D))] + [ANYWHERE] * 8,
        out_shape=[shaped((BLOCK, D), F32), shaped((BLOCK, D), BF16), shaped((8, D), F32)]
        + [shaped((BLOCK, WIDE), BF16)] * 8,
        scratch_shapes=[pltpu.VMEM((8, BLOCK, WIDE), BF16), pltpu.SemaphoreType.DMA((8,))]
        + pieces_of(4)
        + pieces_of(1),
    )(meta, *parts, x, old, gain, weights)
    return results[0], results[2], results[3:]


def on_device(
    stream_in,
    segments,
    head_table,
    query_key_value,
    attention_out,
    expand_weight,
    contract_weight,
    norm_gain,
    norm_bias,
    attention_bias,
    expand_bias,
    contract_bias,
    cotangent,
):
    row = lax.axis_index("row")
    col = lax.axis_index("col")
    core = row % 2
    z = row // 4
    y = col % 4
    x = ((row // 2) % 2) * 2 + col // 4
    first = core == 0
    mine = core * 4 + y
    sequence = z * 4 + x

    to_devices = [(core ^ dc, (y + dy) % 4) for dy, dc in STEPS]
    from_devices = [(core ^ dc, (y - dy) % 4) for dy, dc in STEPS]
    held = [core * 4 + (y - k) % 4 for k in HOPS] + [(1 - core) * 4 + (y - k) % 4 for k in HOPS]
    meta = (
        [core] * 8
        + [c * 4 + at for c, at in to_devices]
        + [2 * at + c for c, at in to_devices]
        + [c * 4 + at for c, at in from_devices]
        + [2 * at + c for c, at in from_devices]
        + held
    )
    meta = jnp.stack(meta).astype(jnp.int32)

    def spread_core(own, axis=-1):
        half = HEAD_DIM // 2
        low = lax.slice_in_dim(own, 0, half, axis=axis)
        high = lax.slice_in_dim(own, own.shape[axis] - half, own.shape[axis], axis=axis)
        got = send(jnp.where(first, high, low), CORES)
        return jnp.where(
            first,
            jnp.concatenate([own, got], axis=axis),
            jnp.concatenate([got, own], axis=axis),
        )

    packed_a = [
        jnp.concatenate([query_key_value[l, i] for i in range(3)] + [attention_out[l]], axis=1)
        for l in range(LAYERS)
    ]
    packed_b = [
        jnp.concatenate([expand_weight[l], contract_weight[l].T], axis=1) for l in range(LAYERS)
    ]
    biases = jnp.concatenate([attention_bias.reshape(LAYERS, 480), expand_bias], axis=1)
    moved_a = send(packed_a[0], TO_FEATURE)
    biases = send(biases, TO_FEATURE)
    moved_b = send(packed_b[0], TO_FEATURE)
    moved_late = send(jnp.concatenate([packed_b[1], packed_a[1]], axis=1), TO_FEATURE)

    def widen(moved):
        own = moved[:, :480].reshape(80, 3, 160)
        whole = spread_core(own).reshape(80, 3 * LOCAL)
        return jnp.concatenate([whole, moved[:, 480:]], axis=1)

    def gather_plane(value):
        return lax.all_gather(value, AXES, axis=0, tiled=True, axis_index_groups=PLANES)

    wide_a = widen(moved_a)
    spread = jnp.broadcast_to(wide_a[None], (16,) + wide_a.shape)
    first_a = lax.all_to_all(
        spread, AXES, 0, 0, tiled=True, axis_index_groups=PLANES
    ).reshape(D, 736)
    first_b = gather_plane(hold(moved_b, first_a))
    late_shard = jnp.concatenate([moved_late[:, :D], widen(moved_late[:, D:])], axis=1)
    w_in = [(first_a, 0)]
    w_out = [(first_a, 3 * LOCAL)]
    w_units = [first_b]

    query_bias = spread_core(biases[:, :160])
    value_bias = spread_core(biases[:, 160:320])
    qkv_bias = jnp.concatenate(
        [query_bias, jnp.zeros((LAYERS, LOCAL), F32), value_bias], axis=1
    ).reshape(LAYERS, 1, 3 * LOCAL)
    up_bias = biases[:, 480:].reshape(LAYERS, 1, UNITS)

    slot_heads = head_table.reshape(-1)
    filled = (slot_heads < HEADS).astype(jnp.int32)
    places24 = jnp.arange(24, dtype=jnp.int32)
    order = jnp.sum(jnp.where(places24[None, :] < places24[:, None], filled[None, :], 0), axis=1)
    head_ids = jnp.arange(HEADS, dtype=jnp.int32)
    rank = jnp.sum(jnp.where(slot_heads[None, :] == head_ids[:, None], order[None, :], 0), axis=1)
    head_of_rank = jnp.sum(
        jnp.where(rank[None, :] == head_ids[:, None], head_ids[None, :], 0), axis=1
    )

    def pick(value, index):
        return jnp.take(value, index, axis=0, mode="clip")

    def exchange(pieces):
        return [
            send(piece, to_step(dy, dc)) if dy or dc else piece
            for piece, (dy, dc) in zip(pieces, STEPS)
        ]

    def gather_pieces(block, until=()):
        near = [block] + [send(block, along_y(k)) for k in HOPS[1:]]
        if until:
            near = lax.optimization_barrier((*near, *until))[:4]
        return [*near] + [send(value, CORES) for value in near]

    bias_terms = []
    left = biases[:, 320:480]
    for _ in range(3):
        term = left.astype(BF16)
        bias_terms.append(term)
        left = left - term.astype(F32)
    bias_terms = jnp.stack(bias_terms, axis=1)
    feature_places = jnp.stack(
        [2 * ((y - k) % 4) + core for k in HOPS] + [2 * ((y - k) % 4) + 1 - core for k in HOPS]
    ).astype(jnp.int32)

    def out_block(l):
        terms = jnp.concatenate([bias_terms[l].T, jnp.zeros((160, 125), BF16)], axis=1)
        return turn_heads(rank, *w_out[l], terms)

    def out_weights(block, until):
        whole = assemble(gather_pieces(block, until), feature_places)
        terms = whole[:, D : D + 3].astype(F32)
        bias = (terms[:, 0] + terms[:, 1]) + terms[:, 2]
        return whole, bias.reshape(1, D)

    def out_weight_grads(heads, grads):
        local = tn(heads, grads).astype(BF16)
        return pick(local.reshape(HEADS, HEAD_DIM, 160), head_of_rank).reshape(D, 160)

    def sequence_of(value):
        return jnp.where(core == x % 2, value, send(value, CORES))

    def block_of(value, at):
        return lax.dynamic_slice_in_dim(value, at * BLOCK, BLOCK, 0)

    tokens = sequence_of(stream_in)
    seg = lax.dynamic_slice_in_dim(segments, sequence * SEQ, SEQ)
    start = jnp.sum((seg[:, None] < seg[None, :]).astype(jnp.int32), axis=0, keepdims=True)
    held_places = meta[HELD : HELD + 8]

    def gather_tokens(value):
        return lax.all_gather(value, AXES, axis=0, tiled=True, axis_index_groups=BY_TOKEN)

    def sum_parts(far, near):
        parts = add_cores(near, send(far, CORES))
        return [send(part, along_y(-k)) if k else part for part, k in zip(parts, HOPS)], parts[1]

    def scatter_plane(value):
        return lax.psum_scatter(
            value, AXES, scatter_dimension=0, tiled=True, axis_index_groups=PLANES
        )

    def to_result(value):
        blocks = jnp.moveaxis(value.reshape(value.shape[:-1] + (8, 160)), -2, 0)
        got = lax.all_to_all(blocks, AXES, 0, 0, tiled=True, axis_index_groups=BY_FEATURE)
        got = got.reshape((4, 2) + got.shape[1:])
        got = jnp.moveaxis(got, (1, 0), (-4, -3))
        return send(got.reshape(value.shape[:-2] + (SEQ, 160)), FROM_FEATURE)

    def gain_of(l, i):
        return norm_gain[l, i].reshape(1, D), norm_bias[l, i].reshape(1, D)

    stream = block_of(tokens, mine).astype(F32)
    gain, shift = gain_of(0, 0)
    normed = (normal(tokens.astype(F32))[0] * gain + shift).astype(BF16)
    grad_all = sequence_of(cotangent)
    grad = block_of(grad_all, mine).astype(F32)
    grad_sum = jnp.sum(grad, axis=0, keepdims=True)
    grad_held = in_order(grad_all, held_places)
    pieces = None
    kept = []
    streams = []
    for l in range(LAYERS):
        if l:
            block = out_block(l)
            pieces = lax.optimization_barrier((*pieces, block))[:8]
            qkv, normed = project(meta, pieces, *w_in[l], qkv_bias[l])
            all_heads[0] = gather_tokens(hold(all_heads[0], qkv))
        else:
            block = out_block(l)
            qkv = project_first(normed, first_a, qkv_bias[l])
            all_heads = []
        pieces, turned, lse = attend_forward(meta, start, qkv)
        w_heads, out_bias = out_weights(block, pieces[:1])
        gain, shift = gain_of(l, 1)
        mid, low, heads = join_heads(
            meta, exchange(pieces), w_heads, stream, out_bias, gain, shift
        )
        if not l:
            late = gather_plane(hold(late_shard, low))
            w_in.append((late, 2))
            w_out.append((late, D + 3 * LOCAL))
            w_units.append(late)
        pieces_two = gather_pieces(low)
        all_heads.append(heads if not l else gather_tokens(hold(heads, *pieces_two)))
        far = up_down(pieces_two[4:], w_units[l], up_bias[l])
        near = up_down(pieces_two[:4], w_units[l], up_bias[l])
        bias = contract_bias[l].reshape(1, D)
        kept.append((stream, mid, normed, pieces_two, far, near, w_heads, qkv, turned, lse))
        if l + 1 < LAYERS:
            parts, _ = sum_parts(far[2], near[2])
            gain, shift = gain_of(l + 1, 0)
            stream, low = join_norm(parts, mid, bias, gain, shift)
            pieces = gather_pieces(low)
            streams.append(stream.astype(BF16))
        else:
            last = (far[2], near[2], mid, bias)

    grad_pieces = None
    wide_sums = [None] * LAYERS
    plane_sums = [None] * LAYERS
    unit_grads = [None] * LAYERS
    head_grads = [None] * LAYERS
    for l in reversed(range(LAYERS)):
        stream, mid, normed, pieces_two, far, near, w_heads, qkv, turned, lse = kept[l]
        if grad_pieces is None:
            back = [
                up_down_back((grad_held,), w_units[l], part[0], first)
                for part, first in ((far, 4), (near, 0))
            ]
        else:
            grad_pieces = lax.optimization_barrier((*grad_pieces, unit_grads[1]))[:8]
            back = [
                up_down_back(pieces, w_units[l], part[0])
                for part, pieces in ((far, grad_pieces[4:]), (near, grad_pieces[:4]))
            ]
        (low_far, sum_far, back_far), (low_near, sum_near, back_near) = back
        parts, sent = sum_parts(back_far, back_near)
        held = lax.optimization_barrier(
            (pieces_two, (near[1], far[1]), (low_near, low_far), grad_pieces, sent)
        )
        if l == 0:
            grad_held = end_to_end(held[3])
        grad_down = tn(grad_held, end_to_end(held[1])).astype(BF16)
        grad_up = tn(end_to_end(held[0]), end_to_end(held[2])).astype(BF16)
        units = jnp.concatenate([grad_up, grad_down], axis=1)
        parts[0] = hold(parts[0], units)
        mid_grad, sums_two, pieces = norm_back_heads(
            meta, parts, mid, grad, gain_of(l, 1)[0], w_heads
        )
        if l:
            unit_grads[l] = scatter_plane(units)
        else:
            spare = jnp.zeros((D, 128), BF16)
            both = scatter_plane(jnp.concatenate([units, head_grads[1], spare], axis=1))
            unit_grads[l], head_grads[1] = both[:, : 2 * UNITS], both[:, 2 * UNITS : 3 * UNITS]
        pieces = exchange(pieces)
        if not l:
            last_far, last_near, last_mid, bias = last
            last_far = hold(last_far, *pieces)
        grad_qkv, grad_own, qkv_sum, mid_all = attend_backward(
            meta, start, qkv, turned, lse, pieces
        )
        back_far = project_back(meta, grad_qkv, *w_in[l], 4)
        back_near = project_back(meta, grad_qkv, *w_in[l], 0)
        parts, sent = sum_parts(back_far, back_near)
        normed, mid_all = lax.optimization_barrier((normed, mid_all, sent))[:2]
        grad_in = tn(normed, grad_own).astype(BF16)
        grad_out = out_weight_grads(all_heads[l], mid_all)
        heads = jnp.concatenate([grad_in, grad_out], axis=1)
        parts[0] = hold(parts[0], heads)
        grad_new, next_low, sums_one = norm_back(parts, stream, mid_grad, gain_of(l, 0)[0])
        wide_sums[l] = jnp.concatenate([sums_one[:2], sums_two[:3], grad_sum], axis=0)
        plane_sums[l] = jnp.concatenate(
            [
                qkv_sum[:, :160],
                qkv_sum[:, 320:],
                sum_far + sum_near,
                jnp.zeros((1, D - 960), F32),
            ],
            axis=1,
        )
        grad_sum = sums_one[2:3]
        grad = grad_new
        if l:
            grad_pieces = gather_pieces(next_low)
            head_grads[l] = heads
        else:
            got = lax.all_to_all(
                heads.reshape(16, 80, 640), AXES, 0, 0, tiled=True, axis_index_groups=PLANES
            )
            head_grads[l] = jnp.sum(got.astype(F32), axis=0).astype(BF16)
    grad_stream = to_result(grad)

    parts, _ = sum_parts(last_far, last_near)
    parts = lax.optimization_barrier((*parts, sent))[:4]
    total = (parts[0].astype(F32) + parts[1].astype(F32)) + (
        parts[2].astype(F32) + parts[3].astype(F32)
    )
    streams.append((last_mid + total + bias).astype(BF16))
    activations = to_result(jnp.stack(streams))

    unit_back = jnp.stack([send(v, FROM_FEATURE) for v in unit_grads]).astype(F32)
    head_back = jnp.stack([send(v, FROM_FEATURE) for v in head_grads]).astype(F32)
    grad_query_key_value = head_back[:, :, :480].reshape(LAYERS, 80, 3, 160).transpose(0, 2, 1, 3)
    grad_attention_out = head_back[:, :, 480:]
    grad_expand = unit_back[:, :, :UNITS]
    grad_contract = unit_back[:, :, UNITS:].transpose(0, 2, 1)

    def sum_four(value, perms):
        one, two, three = (send(value, perm) for perm in perms)
        return (value + two) + (one + three)

    def sum_y(value):
        value = value + send(value, CORES)
        return sum_four(value, [along_y(k) for k in (1, 2, 3)])

    def sum_plane(value):
        value = sum_four(value, [along_plane(0, k) for k in (1, 2, 3)])
        return sum_four(value, [along_plane(k, 0) for k in (1, 2, 3)])

    wide = sum_y(jnp.concatenate(wide_sums, axis=0))
    sums = sum_plane(jnp.concatenate([wide] + plane_sums, axis=0))
    wide = sums[:12].reshape(LAYERS, 6, D)
    plane = send(sums[12:], FROM_FEATURE)
    grad_norm_gain = jnp.stack([wide[:, 0], wide[:, 2]], axis=1)
    grad_norm_bias = jnp.stack([wide[:, 1], wide[:, 3]], axis=1)
    out_sums = lax.dynamic_slice_in_dim(wide[:, 4], col * 160, 160, 1)
    grad_attention_bias = jnp.stack([plane[:, :160], plane[:, 160:320], out_sums], axis=1)
    grad_expand_bias = plane[:, 320:960]
    grad_contract_bias = wide[:, 5]
    return (
        activations,
        grad_stream,
        grad_query_key_value,
        grad_attention_out,
        grad_expand,
        grad_contract,
        grad_norm_gain,
        grad_norm_bias,
        grad_attention_bias,
        grad_expand_bias,
        grad_contract_bias,
    )


def solution(mesh):
    placed = (
        P("row", None),
        P(),
        P(),
        P(None, None, "row", "col"),
        P(None, "row", "col"),
        P(None, "row", "col"),
        P(None, "col", "row"),
        P(),
        P(),
        P(None, None, "col"),
        P(None, "col"),
        P(),
        P("row", None),
    )
    return jax.shard_map(
        on_device,
        mesh=mesh,
        in_specs=placed,
        out_specs=(
            P(None, "row", "col"),
            P("row", "col"),
            P(None, None, "row", "col"),
            P(None, "row", "col"),
            P(None, "row", "col"),
            P(None, "col", "row"),
            P(),
            P(),
            P(None, None, "col"),
            P(None, "col"),
            P(),
        ),
        check_vma=False,
    )
```

```python
import functools

import jax
import jax.numpy as jnp
from jax import lax
from jax.experimental import pallas as pl
from jax.experimental.pallas import tpu as pltpu
from jax.sharding import PartitionSpec as P

D = 1280
HEADS = 20
HEAD_DIM = 64
SEQ = 1024
LAYERS = 2
BLOCK = 128
LOCAL = 3 * HEAD_DIM
SCALE = HEAD_DIM ** (-0.5)
AXES = ("row", "col")
BF16 = jnp.bfloat16
F32 = jnp.float32
MIB = 1024 * 1024


def device(z, x, core, y):
    return (z * 4 + (x // 2) * 2 + core) * 8 + (x % 2) * 4 + y


def pairs(target):
    out = []
    for z in range(4):
        for x in range(4):
            for core in range(2):
                for y in range(4):
                    out.append((device(z, x, core, y), device(*target(z, x, core, y))))
    return out


def along_y(k):
    return pairs(lambda z, x, core, y: (z, x, core, (y + k) % 4))


def to_step(dy, dc):
    return pairs(lambda z, x, core, y: (z, x, core ^ dc, (y + dy) % 4))


def along_plane(dz, dx):
    return pairs(lambda z, x, core, y: ((z + dz) % 4, (x + dx) % 4, core, y))


def to_feature(z, x, core, y):
    block = (x % 2) * 4 + y
    return (z, (x // 2) * 2 + core, block % 2, block // 2)


CORES = pairs(lambda z, x, core, y: (z, x, 1 - core, y))
TO_FEATURE = pairs(to_feature)
FROM_FEATURE = [(b, a) for a, b in TO_FEATURE]
PLANES = [
    [device(z, x, core, y) for z in range(4) for x in range(4)]
    for y in range(4)
    for core in range(2)
]
BY_FEATURE = [
    [device(z, x, core, y) for y in range(4) for core in range(2)]
    for z in range(4)
    for x in range(4)
]
BY_TOKEN = [
    [device(z, x, core, y) for core in range(2) for y in range(4)]
    for z in range(4)
    for x in range(4)
]
STEPS = [(dy, dc) for dy in (0, 1, 3, 2) for dc in (0, 1)]
HOPS = (0, 1, 3, 2)


NAMES = {tuple(CORES): "cores", tuple(TO_FEATURE): "to_feature", tuple(FROM_FEATURE): "from_feature"}


def send(value, perm):
    with jax.named_scope("send_" + NAMES.get(tuple(perm), "far")):
        return lax.ppermute(value, AXES, perm)


CORE, SAME, TO_BLOCK, TO_SLOT, FROM_BLOCK, FROM_SLOT, HELD, HEAD_OF = 0, 1, 8, 16, 24, 32, 40, 48
IN_SMEM = pl.BlockSpec(memory_space=pltpu.SMEM)
ANYWHERE = pl.BlockSpec(memory_space=pl.ANY)
IN_HBM = pl.BlockSpec(memory_space=pltpu.HBM)


LIGHT = pl.CostEstimate(flops=1000, bytes_accessed=1000, transcendentals=0)


def call(kernel, in_specs, limit=16, after=(), light=False, **kwargs):
    count = len(after)

    def waiting(*refs):
        kernel(*refs[count:])

    specs = [IN_HBM] * count + list(in_specs)
    run = pl.pallas_call(
        waiting,
        in_specs=specs,
        compiler_params=pltpu.CompilerParams(vmem_limit_bytes=limit * MIB),
        cost_estimate=LIGHT if light else None,
        **kwargs,
    )
    label = getattr(kernel, "func", kernel).__name__

    def named(*operands):
        with jax.named_scope(label):
            placed = [
                pltpu.with_memory_space_constraint(value, pltpu.HBM) if spec is IN_HBM else value
                for value, spec in zip((*after, *operands), specs)
            ]
            return run(*placed)

    return named


def shaped(shape, dtype):
    return jax.ShapeDtypeStruct(shape, dtype)


def in_hbm(shape, dtype):
    return pltpu.HBM(shape, dtype)


def full(shape):
    return pl.BlockSpec(shape, lambda i: (0,) * len(shape))


TOKEN = full((8, 128))
TOKEN_SHAPE = in_hbm((8, 128), F32)


def mark(token_ref):
    token_ref[...] = jnp.zeros((8, 128), F32)


def fetch(pieces, target, sems):
    rows = target.shape[0] // len(pieces)
    copies = []
    for i, piece in enumerate(pieces):
        copies.append(
            pltpu.make_async_copy(
                piece.at[pl.ds(0, rows), :], target.at[pl.ds(i * rows, rows), :], sems.at[i]
            )
        )
    for copy in copies:
        copy.start()
    return copies


def load(ref, columns, targets, sems, rows=None):
    copies = []
    for i, target in enumerate(targets):
        width = target.shape[1]
        at = pl.ds(columns + i * width, width)
        copies.append(pltpu.make_async_copy(ref.at[:, at], target, sems.at[i]))
        copies[i].start()
    return copies


def held_rows(count):
    return [pltpu.VMEM((BLOCK, D), F32)] * count + [pltpu.SemaphoreType.DMA((count,))]


def weights_of(count):
    return [pltpu.VMEM((D, UNITS), BF16)] * count + [pltpu.SemaphoreType.DMA((count,))]


UNITS = 640


def pieces_of(count, rows=BLOCK, columns=D):
    return [pltpu.VMEM((count * rows, columns), BF16), pltpu.SemaphoreType.DMA((count,))]


def assemble(pieces, places, after=()):
    count = len(pieces)
    shape = pieces[0].shape
    rows = shape[-2]

    def assemble_kernel(places_ref, *refs):
        sems = refs[count + 1]
        out = refs[count]
        copies = []
        for i in range(count):
            at = pl.ds(pl.multiple_of(places_ref[i] * rows, rows), rows)
            target = out.at[:, at, :] if len(shape) == 3 else out.at[at, :]
            copies.append(pltpu.make_async_copy(refs[i], target, sems.at[i]))
        for copy in copies:
            copy.start()
        for copy in copies:
            copy.wait()

    return call(
        assemble_kernel,
        grid=(1,),
        out_shape=in_hbm(shape[:-2] + (rows * count, shape[-1]), pieces[0].dtype),
        in_specs=[IN_SMEM] + [IN_HBM] * count,
        out_specs=full(shape[:-2] + (rows * count, shape[-1])),
        scratch_shapes=[pltpu.SemaphoreType.DMA((count,))],
        after=after,
    )(places, *pieces)


def take_in(meta_ref, own_ref, got_ref, copies_of):
    for flag, ref in ((1, own_ref), (0, got_ref)):

        @pl.when(meta_ref[SAME] == flag)
        def _():
            copies = copies_of(ref)
            for copy in copies:
                copy.start()
            for copy in copies:
                copy.wait()


def hold_grads_kernel(meta_ref, own_ref, got_ref, held_ref, first_ref, sum_ref, token_ref, sems):
    def copies_of(ref):
        return [
            pltpu.make_async_copy(
                ref.at[rows_at(meta_ref, HELD + i), :],
                held_ref.at[pl.ds(i * BLOCK, BLOCK), :],
                sems.at[i],
            )
            for i in range(8)
        ]

    take_in(meta_ref, own_ref, got_ref, copies_of)
    first = held_ref[:BLOCK, :].astype(F32)
    first_ref[...] = first
    sum_ref[...] = jnp.sum(first, axis=0, keepdims=True)
    mark(token_ref)


def hold_grads(meta, own, got):
    return call(
        hold_grads_kernel,
        [IN_SMEM, IN_HBM, IN_HBM],
        light=True,
        grid=(1,),
        out_specs=[full((SEQ, D)), full((BLOCK, D)), full((1, D)), TOKEN],
        out_shape=(
            in_hbm((SEQ, D), BF16),
            in_hbm((BLOCK, D), F32),
            shaped((1, D), F32),
            TOKEN_SHAPE,
        ),
        scratch_shapes=[pltpu.SemaphoreType.DMA((8,))],
    )(meta, own, got)


def first_norm_kernel(
    meta_ref, own_ref, got_ref, gain_ref, shift_ref, normed_ref, first_ref, token_ref, x_ref, sems
):
    def copies_of(ref):
        return [
            pltpu.make_async_copy(ref.at[pl.ds(i * 256, 256), :], x_ref.at[pl.ds(i * 256, 256), :], sems.at[i])
            for i in range(4)
        ]

    take_in(meta_ref, own_ref, got_ref, copies_of)
    for i in range(4):
        at = pl.ds(i * 256, 256)
        unit = normal(x_ref[at, :].astype(F32))[0]
        normed_ref[at, :] = (unit * gain_ref[...] + shift_ref[...]).astype(BF16)
    first_ref[...] = x_ref[rows_at(meta_ref, HELD), :].astype(F32)
    mark(token_ref)


def first_norm(meta, own, got, gain, shift):
    return call(
        first_norm_kernel,
        [IN_SMEM, IN_HBM, IN_HBM, full((1, D)), full((1, D))],
        grid=(1,),
        out_specs=[full((SEQ, D)), full((BLOCK, D)), TOKEN],
        out_shape=(in_hbm((SEQ, D), BF16), in_hbm((BLOCK, D), F32), TOKEN_SHAPE),
        scratch_shapes=pieces_of(4, 256),
    )(meta, own, got, gain, shift)


def later(values, after):
    count = len(values)

    def later_kernel(*refs):
        pass

    return call(
        later_kernel,
        [IN_HBM] * count,
        after=after,
        out_specs=[IN_HBM] * count,
        out_shape=[in_hbm(value.shape, value.dtype) for value in values],
        input_output_aliases={len(after) + i: i for i in range(count)},
    )(*values)


def spread_out(value, after):
    def spread_out_kernel(value_ref, out_ref):
        for i in range(16):
            out_ref[i] = value_ref[...]

    shape = (16,) + value.shape
    return call(
        spread_out_kernel,
        [full(value.shape)],
        grid=(1,),
        out_specs=full(shape),
        out_shape=in_hbm(shape, value.dtype),
        after=after,
    )(value)


def rows_at(meta_ref, index):
    return pl.ds(pl.multiple_of(meta_ref[index] * BLOCK, BLOCK), BLOCK)


def nt(a, b):
    return lax.dot_general(a, b, (((1,), (1,)), ((), ())), preferred_element_type=F32)


def tn(a, b):
    return lax.dot_general(a, b, (((0,), (0,)), ((), ())), preferred_element_type=F32)


QB = 256


def allowed_at(start_ref, at, keys):
    key = lax.broadcasted_iota(jnp.int32, (keys, QB), 0)
    query = lax.broadcasted_iota(jnp.int32, (keys, QB), 1) + at
    return (key >= start_ref[:, at : at + QB]) & (key <= query)


def attend_forward_kernel(meta_ref, start_ref, qkv_ref, *refs):
    pieces = refs[:8]
    turned_ref, lse_ref, token_ref, own_ref, sems = refs[8:]
    mark(token_ref)
    heads = []
    for h in range(3):
        lo = h * HEAD_DIM
        q = qkv_ref[:, lo : lo + HEAD_DIM] * jnp.asarray(SCALE, BF16)
        k = qkv_ref[:, LOCAL + lo : LOCAL + lo + HEAD_DIM]
        v = qkv_ref[:, 2 * LOCAL + lo : 2 * LOCAL + lo + HEAD_DIM]
        heads.append((q, k, v.astype(F32).T.astype(BF16)))
    for block in range(SEQ // QB):
        at = block * QB
        keys = at + QB
        allowed = allowed_at(start_ref, at, keys)
        parts = []
        for h, (q, k, vt) in enumerate(heads):
            scores = nt(k[:keys], q[at : at + QB])
            scores = jnp.where(allowed, scores, -1e30)
            top = jnp.max(scores, axis=0, keepdims=True)
            weights = jnp.exp(scores - top)
            total = jnp.sum(weights, axis=0, keepdims=True)
            turned = (
                jnp.dot(vt[:, :keys], weights.astype(BF16), preferred_element_type=F32) / total
            )
            lse_ref[h : h + 1, at : at + QB] = top + jnp.log(total)
            turned_ref[h * HEAD_DIM : (h + 1) * HEAD_DIM, at : at + QB] = turned
            parts.append(turned)
        out = jnp.concatenate(parts, axis=0).T.astype(BF16)
        own_ref[at : at + QB, :] = jnp.where(meta_ref[CORE] == 0, out[:, :160], out[:, 32:])
    copies = [
        pltpu.make_async_copy(own_ref.at[rows_at(meta_ref, TO_BLOCK + j), :], pieces[j], sems.at[j])
        for j in range(8)
    ]
    for copy in copies:
        copy.start()
    for copy in copies:
        copy.wait()


def attend_forward(meta, start, qkv):
    results = call(
        attend_forward_kernel,
        grid=(1,),
        in_specs=[IN_SMEM, full((1, SEQ)), full((SEQ, 3 * LOCAL))],
        out_specs=[ANYWHERE] * 8
        + [full((LOCAL, SEQ)), full((8, SEQ)), TOKEN],
        out_shape=[in_hbm((BLOCK, 160), BF16)] * 8
        + [shaped((LOCAL, SEQ), F32), shaped((8, SEQ), F32), TOKEN_SHAPE],
        scratch_shapes=[pltpu.VMEM((SEQ, 160), BF16), pltpu.SemaphoreType.DMA((8,))],
    )(meta, start, qkv)
    return results[:8], results[8], results[9], results[10]


WIDE = LOCAL + 160


def attend_backward_kernel(meta_ref, start_ref, qkv_ref, turned_ref, lse_ref, *refs):
    pieces = refs[:8]
    out_ref, own_ref, sum_ref, mid_ref, grad_ref, sems, dk_ref, dv_ref = refs[8:]
    copies = [
        pltpu.make_async_copy(
            pieces[j], grad_ref.at[rows_at(meta_ref, FROM_BLOCK + j), :], sems.at[j]
        )
        for j in range(8)
    ]
    for copy in copies:
        copy.start()
    for copy in copies:
        copy.wait()
    mid_ref[...] = grad_ref[:, LOCAL:]
    for h in range(3):
        lo = h * HEAD_DIM
        q = qkv_ref[:, lo : lo + HEAD_DIM] * jnp.asarray(SCALE, BF16)
        k = qkv_ref[:, LOCAL + lo : LOCAL + lo + HEAD_DIM]
        v = qkv_ref[:, 2 * LOCAL + lo : 2 * LOCAL + lo + HEAD_DIM]
        g = grad_ref[:, lo : lo + HEAD_DIM]
        kt = k.astype(F32).T.astype(BF16)
        delta = jnp.sum(
            g.astype(F32).T * turned_ref[lo : lo + HEAD_DIM, :], axis=0, keepdims=True
        )
        for block in reversed(range(SEQ // QB)):
            at = block * QB
            keys = at + QB
            allowed = allowed_at(start_ref, at, keys)
            q_part, g_part = q[at : at + QB], g[at : at + QB]
            scores = nt(k[:keys], q_part)
            probs = jnp.where(
                allowed, jnp.exp(scores - lse_ref[h : h + 1, at : at + QB]), 0.0
            )
            grad_probs = nt(v[:keys], g_part)
            grad_scores = (probs * (grad_probs - delta[:, at : at + QB])).astype(BF16)
            dv = jnp.dot(probs.astype(BF16), g_part, preferred_element_type=F32)
            dk = jnp.dot(grad_scores, q_part, preferred_element_type=F32)
            dq = jnp.dot(kt[:, :keys], grad_scores, preferred_element_type=F32) * SCALE
            out_ref[at : at + QB, lo : lo + HEAD_DIM] = dq.T.astype(BF16)
            if keys == SEQ:
                dk_ref[...] = dk
                dv_ref[...] = dv
            else:
                dk_ref[:keys, :] += dk
                dv_ref[:keys, :] += dv
        out_ref[:, LOCAL + lo : LOCAL + lo + HEAD_DIM] = dk_ref[...].astype(BF16)
        out_ref[:, 2 * LOCAL + lo : 2 * LOCAL + lo + HEAD_DIM] = dv_ref[...].astype(BF16)
    for i in range(3):
        part = out_ref[:, i * LOCAL : (i + 1) * LOCAL]
        own = jnp.where(meta_ref[CORE] == 0, part[:, :160], part[:, 32:])
        own_ref[:, i * 160 : (i + 1) * 160] = own
        sum_ref[:, i * 160 : (i + 1) * 160] = jnp.sum(own.astype(F32), axis=0, keepdims=True)


def attend_backward(meta, start, qkv, turned, lse, pieces):
    return call(
        attend_backward_kernel,
        grid=(1,),
        in_specs=[
            IN_SMEM,
            full((1, SEQ)),
            full((SEQ, 3 * LOCAL)),
            full((LOCAL, SEQ)),
            full((8, SEQ)),
        ]
        + [IN_HBM] * 8,
        out_specs=[full((SEQ, 3 * LOCAL)), full((SEQ, 480)), full((1, 480)), full((SEQ, 160))],
        out_shape=(
            shaped((SEQ, 3 * LOCAL), BF16),
            in_hbm((SEQ, 480), BF16),
            shaped((1, 480), F32),
            in_hbm((SEQ, 160), BF16),
        ),
        scratch_shapes=[
            pltpu.VMEM((SEQ, WIDE), BF16),
            pltpu.SemaphoreType.DMA((8,)),
            pltpu.VMEM((SEQ, HEAD_DIM), F32),
            pltpu.VMEM((SEQ, HEAD_DIM), F32),
        ],
    )(meta, start, qkv, turned, lse, *pieces)


def gelu(v):
    inner = 0.7978845608028654 * (v + 0.044715 * v * v * v)
    return 0.5 * v * (1.0 + jnp.tanh(inner))


def gelu_slope(v):
    t = jnp.tanh(0.7978845608028654 * (v + 0.044715 * v * v * v))
    return 0.5 * (1.0 + t) + 0.5 * v * (1.0 - t * t) * 0.7978845608028654 * (
        1.0 + 3 * 0.044715 * v * v
    )


HALF = 512
def up_down_kernel(
    a, b, c, d, w_ref, bias_ref, hidden_ref, act_ref, out_ref, *refs
):
    x_ref, sems, y_ref, done, up_ref, down_ref, w_sems = refs
    copies = fetch((a, b, c, d), x_ref, sems)
    weights = load(w_ref, 0, (up_ref, down_ref), w_sems)
    outs = []
    for i in range(2):
        at = pl.ds(i * 256, 256)
        copies[2 * i].wait()
        copies[2 * i + 1].wait()
        if not i:
            weights[0].wait()
        hidden = jnp.dot(x_ref[at, :], up_ref[...], preferred_element_type=F32) + bias_ref[...]
        hidden_ref[at, :] = hidden
        act = gelu(hidden).astype(BF16)
        act_ref[at, :] = act
        if not i:
            weights[1].wait()
        y_ref[at, :] = nt(act, down_ref[...]).astype(BF16)
        outs.append(pltpu.make_async_copy(y_ref.at[at, :], out_ref.at[at, :], done.at[i]))
        outs[i].start()
    for copy in outs:
        copy.wait()


def up_down(pieces, weights, bias):
    return call(
        up_down_kernel,
        grid=(1,),
        in_specs=[IN_HBM] * 5 + [full((1, UNITS))],
        out_specs=[full((HALF, UNITS)), full((HALF, UNITS)), ANYWHERE],
        scratch_shapes=pieces_of(4) + pieces_of(2, 256) + weights_of(2),
        out_shape=(
            in_hbm((HALF, UNITS), F32),
            in_hbm((HALF, UNITS), BF16),
            shaped((HALF, D), BF16),
        ),
    )(*pieces, weights, bias)


def up_down_back_kernel(a, b, c, d, w_ref, hidden_ref, low_ref, sum_ref, out_ref, *refs):
    g_ref, sems, y_ref, done, down_ref, up_ref, w_sems, kept_ref, kept_sems = refs
    copies = fetch((a, b, c, d), g_ref, sems)
    kept = pltpu.make_async_copy(hidden_ref, kept_ref, kept_sems.at[0])
    kept.start()
    weights = load(w_ref, UNITS, (down_ref,), w_sems)
    weights.append(pltpu.make_async_copy(w_ref.at[:, pl.ds(0, UNITS)], up_ref, w_sems.at[1]))
    weights[1].start()
    outs = []
    total = jnp.zeros((1, UNITS), F32)
    for i in range(2):
        at = pl.ds(i * 256, 256)
        copies[2 * i].wait()
        copies[2 * i + 1].wait()
        if not i:
            weights[0].wait()
            kept.wait()
        grad = jnp.dot(g_ref[at, :], down_ref[...], preferred_element_type=F32)
        grad = grad * gelu_slope(kept_ref[at, :])
        total += jnp.sum(grad, axis=0, keepdims=True)
        low = grad.astype(BF16)
        low_ref[at, :] = low
        if not i:
            weights[1].wait()
        y_ref[at, :] = nt(low, up_ref[...]).astype(BF16)
        outs.append(pltpu.make_async_copy(y_ref.at[at, :], out_ref.at[at, :], done.at[i]))
        outs[i].start()
    sum_ref[...] = total
    for copy in outs:
        copy.wait()


def up_down_back(pieces, weights, hidden):
    return call(
        up_down_back_kernel,
        grid=(1,),
        in_specs=[IN_HBM] * 6,
        out_specs=[full((HALF, UNITS)), full((1, UNITS)), ANYWHERE],
        scratch_shapes=pieces_of(4)
        + pieces_of(2, 256)
        + weights_of(2)
        + [pltpu.VMEM((HALF, UNITS), F32), pltpu.SemaphoreType.DMA((1,))],
        out_shape=(
            shaped((HALF, UNITS), BF16),
            shaped((1, UNITS), F32),
            shaped((HALF, D), BF16),
        ),
    )(*pieces, weights, hidden)


def up_down_both_kernel(first, a, b, c, d, grad_ref, w_ref, bias_ref, *refs):
    act_ref, low_ref, sum_ref, back_ref, out_ref = refs[:5]
    x_ref, sems, g_ref, g_sems, back, back_done, out, out_done = refs[5:13]
    up_ref, down_ref, w_sems = refs[13:]
    copies = fetch((a, b, c, d), x_ref, sems)
    weights = load(w_ref, 0, (up_ref, down_ref), w_sems)
    grads = [grad_ref.at[pl.ds((first + 2 * i) * BLOCK, 256), :] for i in range(2)]
    grads = fetch(grads, g_ref, g_sems)
    total = jnp.zeros((1, UNITS), F32)
    done = []
    for i in range(2):
        at = pl.ds(i * 256, 256)
        copies[2 * i].wait()
        copies[2 * i + 1].wait()
        grads[i].wait()
        if not i:
            weights[0].wait()
        hidden = jnp.dot(x_ref[at, :], up_ref[...], preferred_element_type=F32) + bias_ref[...]
        act = gelu(hidden).astype(BF16)
        act_ref[at, :] = act
        if not i:
            weights[1].wait()
        grad = jnp.dot(g_ref[at, :], down_ref[...], preferred_element_type=F32)
        grad = grad * gelu_slope(hidden)
        total += jnp.sum(grad, axis=0, keepdims=True)
        low = grad.astype(BF16)
        low_ref[at, :] = low
        back[at, :] = nt(low, up_ref[...]).astype(BF16)
        done.append(pltpu.make_async_copy(back.at[at, :], back_ref.at[at, :], back_done.at[i]))
        done[-1].start()
        out[at, :] = nt(act, down_ref[...]).astype(BF16)
        done.append(pltpu.make_async_copy(out.at[at, :], out_ref.at[at, :], out_done.at[i]))
        done[-1].start()
    sum_ref[...] = total
    for copy in done:
        copy.wait()


def up_down_both(pieces, grads, first, weights, bias):
    return call(
        functools.partial(up_down_both_kernel, first),
        [IN_HBM] * 6 + [full((1, UNITS))],
        grid=(1,),
        out_specs=[full((HALF, UNITS)), full((HALF, UNITS)), full((1, UNITS)), ANYWHERE, ANYWHERE],
        out_shape=(
            shaped((HALF, UNITS), BF16),
            shaped((HALF, UNITS), BF16),
            shaped((1, UNITS), F32),
            shaped((HALF, D), BF16),
            in_hbm((HALF, D), BF16),
        ),
        scratch_shapes=pieces_of(4) + pieces_of(2, 256) * 3 + weights_of(2),
    )(*pieces, grads, weights, bias)


def unit_grads_kernel(x_count, g_count, extra, *refs):
    xs, gs = refs[:x_count], refs[x_count : x_count + g_count]
    halves = refs[x_count + g_count : x_count + g_count + 4]
    refs = refs[x_count + g_count + 4 :]
    if extra:
        heads_ref, refs = refs[0], refs[1:]
    out_ref, token_ref, x_ref, x_sems, g_ref, g_sems, low_ref, low_sems, act_ref, act_sems = refs[:10]
    if extra:
        rest = pltpu.make_async_copy(
            heads_ref, out_ref.at[:, pl.ds(2 * UNITS, UNITS + 128)], refs[10].at[0]
        )
        rest.start()
    ups = fetch(xs, x_ref, x_sems) + fetch(halves[:2], low_ref, low_sems)
    downs = fetch(gs, g_ref, g_sems) + fetch(halves[2:], act_ref, act_sems)
    for copies, left, right, column in (
        (ups, x_ref, low_ref, 0),
        (downs, g_ref, act_ref, UNITS),
    ):
        for copy in copies:
            copy.wait()
        for t in range(5):
            at = pl.ds(t * 256, 256)
            out_ref[at, column : column + UNITS] = tn(left[:, at], right[...]).astype(BF16)
    if extra:
        rest.wait()
    mark(token_ref)


def unit_grads(pieces, lows, grads, acts, after, heads=None):
    extra = [] if heads is None else [heads]
    columns = 2 * UNITS + (768 if extra else 0)
    return call(
        functools.partial(unit_grads_kernel, len(pieces), len(grads), bool(extra)),
        [IN_HBM] * (len(pieces) + len(grads)) + [ANYWHERE] * 4 + [IN_HBM] * len(extra),
        limit=24,
        after=after,
        light=True,
        grid=(1,),
        out_specs=[full((D, columns)), TOKEN],
        out_shape=(in_hbm((D, columns), BF16), TOKEN_SHAPE),
        scratch_shapes=pieces_of(len(pieces), SEQ // len(pieces))
        + pieces_of(len(grads), SEQ // len(grads))
        + pieces_of(2, HALF, UNITS) * 2
        + [pltpu.SemaphoreType.DMA((1,))],
    )(*pieces, *grads, *lows, *acts, *extra)


def head_grads_kernel(*refs):
    ins, (out_ref, token_ref), refs = refs[:4], refs[4:6], refs[6:]
    held, sems = refs[:4], refs[4]
    copies = [pltpu.make_async_copy(ins[i], held[i], sems.at[i]) for i in range(4)]
    for copy in copies:
        copy.start()
    for copy in copies:
        copy.wait()
    normed_ref, own_ref, heads_ref, mid_ref = held
    for t in range(5):
        at = pl.ds(t * 256, 256)
        one = tn(normed_ref[:, at], own_ref[...]).astype(BF16)
        two = tn(heads_ref[:, at], mid_ref[...]).astype(BF16)
        out_ref[at, :UNITS] = jnp.concatenate([one, two], axis=1)
    out_ref[:, UNITS:] = jnp.zeros((D, 128), BF16)
    mark(token_ref)


def head_grads(normed, own, heads, mid, after):
    return call(
        head_grads_kernel,
        [IN_HBM] * 4,
        limit=20,
        after=after,
        light=True,
        grid=(1,),
        out_specs=[full((D, UNITS + 128)), TOKEN],
        out_shape=(in_hbm((D, UNITS + 128), BF16), TOKEN_SHAPE),
        scratch_shapes=[pltpu.VMEM((SEQ, n), BF16) for n in (D, 480, D, 160)]
        + [pltpu.SemaphoreType.DMA((4,))],
    )(normed, own, heads, mid)


def add_cores_kernel(near_ref, far_ref, *refs):
    outs, token_ref, (one, one_sems, two, two_sems, sums, done) = refs[:4], refs[4], refs[5:]
    mark(token_ref)
    at = [pl.ds(i * BLOCK, BLOCK) for i in range(4)]
    order = (3, 1, 2, 0)
    ins = {}
    for i in order:
        ins[i] = (
            pltpu.make_async_copy(near_ref.at[at[i], :], one.at[at[i], :], one_sems.at[i]),
            pltpu.make_async_copy(far_ref.at[at[i], :], two.at[at[i], :], two_sems.at[i]),
        )
        ins[i][0].start()
        ins[i][1].start()
    copies = []
    for i in order:
        ins[i][0].wait()
        ins[i][1].wait()
        sums[at[i], :] = (one[at[i], :].astype(F32) + two[at[i], :].astype(F32)).astype(BF16)
        copies.append(pltpu.make_async_copy(sums.at[at[i], :], outs[i], done.at[i]))
        copies[-1].start()
    for copy in copies:
        copy.wait()


def add_cores(near, far, after=()):
    return call(
        add_cores_kernel,
        after=after,
        grid=(1,),
        in_specs=[ANYWHERE] * 2,
        out_specs=[ANYWHERE] * 4 + [TOKEN],
        out_shape=[in_hbm((BLOCK, D), BF16)] * 4 + [TOKEN_SHAPE],
        scratch_shapes=pieces_of(4) * 3,
    )(near, far)


def project_kernel(column, meta_ref, *refs):
    pieces = refs[:8]
    full_ref, bias_ref, qkv_ref, normed_ref, x_ref, sems, w_ref, w_sems = refs[8:]
    copies = fetch(pieces, x_ref, sems)
    load(full_ref, column * UNITS, (w_ref,), w_sems)[0].wait()
    for i in range(0, 8, 2):
        copies[i].wait()
        copies[i + 1].wait()
        x = x_ref[i * BLOCK : (i + 2) * BLOCK, :]
        qkv = jnp.dot(x, w_ref[:, : 3 * LOCAL], preferred_element_type=F32) + bias_ref[...]
        qkv = qkv.astype(BF16)
        for k in range(2):
            at = rows_at(meta_ref, HELD + i + k)
            normed_ref[at, :] = x[k * BLOCK : (k + 1) * BLOCK]
            qkv_ref[at, :] = qkv[k * BLOCK : (k + 1) * BLOCK]


def columns_of(at):
    return pl.BlockSpec((D, UNITS), lambda i: (0, at))


def project_first_kernel(x_ref, w_ref, bias_ref, qkv_ref):
    qkv = jnp.dot(x_ref[...], w_ref[:, : 3 * LOCAL], preferred_element_type=F32)
    qkv_ref[...] = (qkv + bias_ref[...]).astype(BF16)


def project_first(normed, weights, bias, after):
    return call(
        project_first_kernel,
        after=after,
        grid=(4,),
        in_specs=[pl.BlockSpec((256, D), lambda i: (i, 0)), columns_of(0), full((1, 3 * LOCAL))],
        out_specs=pl.BlockSpec((256, 3 * LOCAL), lambda i: (i, 0)),
        out_shape=shaped((SEQ, 3 * LOCAL), BF16),
    )(normed, weights, bias)


def gathered_rows_kernel(step_ref, *refs):
    pieces, out_ref, held, sems = refs[:8], refs[8], refs[9], refs[10]
    copies = [
        pltpu.make_async_copy(
            piece.at[pl.ds(BLOCK, EXTRA), :], held.at[i], sems.at[i]
        )
        for i, piece in enumerate(pieces)
    ]
    for copy in copies:
        copy.start()
    for copy in copies:
        copy.wait()
    for f in range(8):
        rows = held[step_ref[f]].astype(F32)
        parts = [rows[:10, j * 160 : (j + 1) * 160] for j in range(8)]
        out_ref[:, f * 160 : (f + 1) * 160] = jnp.concatenate(parts, axis=0).astype(BF16)


def gathered_rows(steps, pieces):
    return call(
        gathered_rows_kernel,
        grid=(1,),
        light=True,
        in_specs=[IN_SMEM] + [IN_HBM] * 8,
        out_specs=full((80, D)),
        out_shape=shaped((80, D), BF16),
        scratch_shapes=[pltpu.VMEM((8, EXTRA, D), BF16), pltpu.SemaphoreType.DMA((8,))],
    )(steps, *pieces)


EXTRA = 16


def turn_kernel(one_ref, two_ref, terms_ref, out_ref):
    out_ref[:, D:] = terms_ref[...]
    for i in range(10):
        at = pl.ds(i * 128, 128)
        rows = jnp.concatenate(
            [one_ref[at, 64:].astype(F32), two_ref[at, :96].astype(F32)], axis=1
        )
        out_ref[:, at] = rows.T.astype(BF16)


def turn(weights, terms):
    first = 3 * LOCAL // 128
    return call(
        turn_kernel,
        grid=(1,),
        in_specs=[
            pl.BlockSpec((D, 128), lambda i: (0, first)),
            pl.BlockSpec((D, 128), lambda i: (0, first + 1)),
            full((160, 128)),
        ],
        out_specs=full((160, D + 128)),
        out_shape=in_hbm((160, D + 128), BF16),
    )(weights, weights, terms)


def project(meta, pieces, weights, at, bias):
    return call(
        functools.partial(project_kernel, at),
        grid=(1,),
        in_specs=[IN_SMEM]
        + [IN_HBM] * 9
        + [full((1, 3 * LOCAL))],
        out_specs=[full((SEQ, 3 * LOCAL)), full((SEQ, D))],
        scratch_shapes=pieces_of(8) + weights_of(1),
        out_shape=(shaped((SEQ, 3 * LOCAL), BF16), in_hbm((SEQ, D), BF16)),
    )(meta, *pieces, weights, bias)


def project_back(meta, grads, weights, column_at, first):
    def project_back_kernel(meta_ref, grad_ref, full_ref, out_ref, y_ref, done, w_ref, w_sems):
        weights = load(full_ref, column_at * UNITS, (w_ref,), w_sems)
        outs = []
        column = lax.broadcasted_iota(jnp.int32, (1, 3 * LOCAL), 1)
        twice = jnp.zeros((1, 3 * LOCAL), jnp.int32)
        for i in range(3):
            at = column - i * LOCAL
            twice += jnp.where((at >= 0) & (at < HEAD_DIM), 1, 0)
        counted = twice * meta_ref[CORE] == 0
        for i in range(2):
            x = jnp.concatenate(
                [grad_ref[rows_at(meta_ref, HELD + first + 2 * i + k), :] for k in range(2)],
                axis=0,
            )
            x = jnp.where(counted, x.astype(F32), 0.0).astype(BF16)
            at = pl.ds(i * 256, 256)
            if not i:
                weights[0].wait()
            y_ref[at, :] = nt(x, w_ref[:, : 3 * LOCAL]).astype(BF16)
            outs.append(pltpu.make_async_copy(y_ref.at[at, :], out_ref.at[at, :], done.at[i]))
            outs[i].start()
        for copy in outs:
            copy.wait()

    return call(
        project_back_kernel,
        grid=(1,),
        in_specs=[IN_SMEM, full((SEQ, 3 * LOCAL)), IN_HBM],
        out_specs=ANYWHERE,
        out_shape=shaped((HALF, D), BF16),
        scratch_shapes=pieces_of(2, 256) + weights_of(1),
    )(meta, grads, weights)


def normal(v):
    mean = jnp.mean(v, axis=-1, keepdims=True)
    centred = v - mean
    variance = jnp.mean(centred * centred, axis=-1, keepdims=True)
    scale = lax.rsqrt(variance + 1e-05)
    return centred * scale, scale


def four(pieces, held_ref, sems):
    copies = fetch(pieces, held_ref, sems)
    for copy in copies:
        copy.wait()
    a, b, c, d = (held_ref[i * BLOCK : (i + 1) * BLOCK, :].astype(F32) for i in range(4))
    return (a + b) + (c + d)


def send_out(value, held_ref, out, sem):
    held_ref[...] = value
    copy = pltpu.make_async_copy(held_ref, out, sem)
    copy.start()
    return copy


def join_norm_kernel(
    a, b, c, d, old_ref, bias_ref, gain_ref, shift_ref, new_ref, low_ref, *refs
):
    x_ref, sems, y_ref, done, held_ref, held_sems = refs
    old = pltpu.make_async_copy(old_ref, held_ref, held_sems.at[0])
    old.start()
    total = four((a, b, c, d), x_ref, sems)
    old.wait()
    new = held_ref[...] + total + bias_ref[...]
    low = (normal(new)[0] * gain_ref[...] + shift_ref[...]).astype(BF16)
    copy = send_out(low, y_ref, low_ref, done.at[0])
    new_ref[...] = new
    copy.wait()


def join_norm(parts, old, bias, gain, shift, after=()):
    return call(
        join_norm_kernel,
        after=after,
        grid=(1,),
        in_specs=[IN_HBM] * 5 + [full((1, D))] * 3,
        out_specs=[full((BLOCK, D)), ANYWHERE],
        out_shape=(in_hbm((BLOCK, D), F32), in_hbm((BLOCK, D), BF16)),
        scratch_shapes=pieces_of(4) + pieces_of(1) + held_rows(1),
    )(*parts, old, bias, gain, shift)


def join_heads_kernel(turned, meta_ref, *refs):
    pieces = refs[:8]
    w_ref, old_ref, gain_ref, shift_ref, more_ref, new_ref, low_ref, heads_ref, bias_ref = refs[8:17]
    slots, sems, ordered, y_ref, done, one_ref, two_ref, w_sems, held_ref, held_sems = refs[17:27]
    weights = load_halves(turned, w_ref, (one_ref, two_ref), w_sems)
    old = pltpu.make_async_copy(old_ref, held_ref, held_sems.at[0])
    old.start()
    copies = [
        pltpu.make_async_copy(pieces[j], slots.at[meta_ref[FROM_SLOT + j]], sems.at[j])
        for j in range(8)
    ]
    if turned:
        terms_ref, terms_sem = refs[27:]
        copies.append(
            pltpu.make_async_copy(w_ref.at[:, pl.ds(D, 128)], terms_ref, terms_sem.at[0])
        )
    for copy in copies:
        copy.start()
    for copy in copies:
        copy.wait()
    if turned:
        terms = terms_ref[...].astype(F32).T
        terms = [
            (terms[l : l + 1] + terms[l + 2 : l + 3]) + terms[l + 4 : l + 5] for l in range(LAYERS)
        ]
        bias_ref[...] = jnp.concatenate(terms + [jnp.zeros((6, D), F32)], axis=0)
        bias = terms[0]
    else:
        bias = more_ref[1:2, :]
        bias_ref[...] = more_ref[...]
    for chip in range(4):
        five = jnp.concatenate([slots[2 * chip], slots[2 * chip + 1]], axis=1)
        for i in range(5):
            ordered[5 * chip + i] = five[:, i * HEAD_DIM : (i + 1) * HEAD_DIM]
    x = jnp.concatenate([ordered[meta_ref[HEAD_OF + r]] for r in range(HEADS)], axis=1)
    product = nt if turned else lambda a, b: jnp.dot(a, b, preferred_element_type=F32)
    for copy in weights:
        copy.wait()
    branch = jnp.concatenate([product(x, one_ref[...]), product(x, two_ref[...])], axis=1)
    old.wait()
    new = held_ref[...] + branch + bias
    low = (normal(new)[0] * gain_ref[...] + shift_ref[...]).astype(BF16)
    if turned:
        y_ref[BLOCK:, :] = more_ref[...]
    y_ref[:BLOCK, :] = low
    copy = pltpu.make_async_copy(y_ref, low_ref, done.at[0])
    copy.start()
    new_ref[...] = new
    heads_ref[...] = x
    copy.wait()


def load_halves(turned, ref, targets, sems):
    if not turned:
        return load(ref, UNITS, targets, sems)
    copies = [
        pltpu.make_async_copy(ref.at[pl.ds(i * UNITS, UNITS), pl.ds(0, D)], target, sems.at[i])
        for i, target in enumerate(targets)
    ]
    for copy in copies:
        copy.start()
    return copies


def halves_of(turned):
    shape = (UNITS, D) if turned else (D, UNITS)
    return [pltpu.VMEM(shape, BF16)] * 2 + [pltpu.SemaphoreType.DMA((2,))]


def join_heads(meta, pieces, weights, turned, old, gain, shift, more):
    rows = BLOCK + EXTRA if turned else BLOCK
    return call(
        functools.partial(join_heads_kernel, turned),
        grid=(1,),
        in_specs=[IN_SMEM] + [IN_HBM] * 10 + [full((1, D))] * 2 + [full(more.shape)],
        out_specs=[full((BLOCK, D)), ANYWHERE, full((BLOCK, D)), full((8, D))],
        out_shape=(
            in_hbm((BLOCK, D), F32),
            in_hbm((rows, D), BF16),
            in_hbm((BLOCK, D), BF16),
            shaped((8, D), F32),
        ),
        scratch_shapes=[
            pltpu.VMEM((8, BLOCK, 160), BF16),
            pltpu.SemaphoreType.DMA((8,)),
            pltpu.VMEM((HEADS, BLOCK, HEAD_DIM), BF16),
        ]
        + pieces_of(1, rows)
        + halves_of(turned)
        + held_rows(1)
        + ([pltpu.VMEM((D, 128), BF16), pltpu.SemaphoreType.DMA((1,))] if turned else []),
    )(meta, *pieces, weights, old, gain, shift, more)


def norm_back_math(dy, x, old, gain):
    unit, scale = normal(x)
    slope = dy * gain
    mean_one = jnp.mean(slope, axis=-1, keepdims=True)
    mean_two = jnp.mean(slope * unit, axis=-1, keepdims=True)
    new = old + scale * (slope - mean_one - unit * mean_two)
    sums = jnp.concatenate(
        [
            jnp.sum(dy * unit, axis=0, keepdims=True),
            jnp.sum(dy, axis=0, keepdims=True),
            jnp.sum(new, axis=0, keepdims=True),
            jnp.zeros((5, D), F32),
        ],
        axis=0,
    )
    return new, sums


def hold_rows(refs, targets, sems):
    copies = []
    for i, (ref, target) in enumerate(zip(refs, targets)):
        copies.append(pltpu.make_async_copy(ref, target, sems.at[i]))
        copies[i].start()
    return copies


def norm_back_kernel(
    a, b, c, d, x_ref, old_ref, gain_ref, new_ref, low_ref, sums_ref, token_ref, *refs
):
    mark(token_ref)
    p_ref, sems, y_ref, done, x_held, old_held, held_sems = refs
    held = hold_rows((x_ref, old_ref), (x_held, old_held), held_sems)
    total = four((a, b, c, d), p_ref, sems)
    for copy in held:
        copy.wait()
    new, sums = norm_back_math(total, x_held[...], old_held[...], gain_ref[...])
    copy = send_out(new.astype(BF16), y_ref, low_ref, done.at[0])
    new_ref[...] = new
    sums_ref[...] = sums
    copy.wait()


def norm_back(parts, x, old, gain, after):
    return call(
        norm_back_kernel,
        after=after,
        grid=(1,),
        in_specs=[IN_HBM] * 6 + [full((1, D))],
        out_specs=[full((BLOCK, D)), ANYWHERE, full((8, D)), TOKEN],
        out_shape=(
            in_hbm((BLOCK, D), F32),
            in_hbm((BLOCK, D), BF16),
            shaped((8, D), F32),
            TOKEN_SHAPE,
        ),
        scratch_shapes=pieces_of(4) + pieces_of(1) + held_rows(2),
    )(*parts, x, old, gain)


def norm_back_heads_kernel(turned, meta_ref, a, b, c, d, x_ref, old_ref, gain_ref, *refs):
    w_ref, new_ref, low_ref, sums_ref = refs[:4]
    pieces, token_ref, refs = refs[4:12], refs[12], refs[13:]
    slots, sent, ordered, p_ref, sems, y_ref, done = refs[:7]
    one_ref, two_ref, w_sems, x_held, old_held, held_sems = refs[7:]
    mark(token_ref)
    held = hold_rows((x_ref, old_ref), (x_held, old_held), held_sems)
    total = four((a, b, c, d), p_ref, sems)
    weights = load_halves(turned, w_ref, (one_ref, two_ref), w_sems)
    for copy in held:
        copy.wait()
    new, sums = norm_back_math(total, x_held[...], old_held[...], gain_ref[...])
    new_ref[...] = new
    low = new.astype(BF16)
    copies = [send_out(low, y_ref, low_ref, done.at[0])]
    sums_ref[...] = sums
    product = (lambda p, q: jnp.dot(p, q, preferred_element_type=F32)) if turned else nt
    for copy in weights:
        copy.wait()
    grads = product(low[:, :UNITS], one_ref[...]) + product(low[:, UNITS:], two_ref[...])
    for r in range(HEADS):
        ordered[meta_ref[HEAD_OF + r]] = grads[:, r * HEAD_DIM : (r + 1) * HEAD_DIM].astype(BF16)
    for f in range(8):
        h = 5 * (f // 2) + 2 * (f % 2)
        slots[f, :, :LOCAL] = jnp.concatenate([ordered[h + i] for i in range(3)], axis=1)
        slots[f, :, LOCAL:] = low[:, f * 160 : (f + 1) * 160]
    for j in range(8):
        copies.append(
            pltpu.make_async_copy(slots.at[meta_ref[TO_SLOT + j]], pieces[j], sent.at[j])
        )
        copies[-1].start()
    for copy in copies:
        copy.wait()


def norm_back_heads(meta, parts, x, old, gain, weights, turned, after):
    results = call(
        functools.partial(norm_back_heads_kernel, turned),
        after=after,
        grid=(1,),
        in_specs=[IN_SMEM] + [IN_HBM] * 6 + [full((1, D)), IN_HBM],
        out_specs=[full((BLOCK, D)), ANYWHERE, full((8, D))] + [ANYWHERE] * 8 + [TOKEN],
        out_shape=[in_hbm((BLOCK, D), F32), in_hbm((BLOCK, D), BF16), shaped((8, D), F32)]
        + [in_hbm((BLOCK, WIDE), BF16)] * 8
        + [TOKEN_SHAPE],
        scratch_shapes=[
            pltpu.VMEM((8, BLOCK, WIDE), BF16),
            pltpu.SemaphoreType.DMA((8,)),
            pltpu.VMEM((HEADS, BLOCK, HEAD_DIM), BF16),
        ]
        + pieces_of(4)
        + pieces_of(1)
        + halves_of(turned)
        + held_rows(2),
    )(meta, *parts, x, old, gain, weights)
    return results[0], results[2], results[3:11], results[11]


def on_device(
    stream_in,
    segments,
    head_table,
    query_key_value,
    attention_out,
    expand_weight,
    contract_weight,
    norm_gain,
    norm_bias,
    attention_bias,
    expand_bias,
    contract_bias,
    cotangent,
):
    row = lax.axis_index("row")
    col = lax.axis_index("col")
    core = row % 2
    z = row // 4
    y = col % 4
    x = ((row // 2) % 2) * 2 + col // 4
    first = core == 0
    sequence = z * 4 + x

    to_devices = [(core ^ dc, (y + dy) % 4) for dy, dc in STEPS]
    from_devices = [(core ^ dc, (y - dy) % 4) for dy, dc in STEPS]
    held = [core * 4 + (y - k) % 4 for k in HOPS] + [(1 - core) * 4 + (y - k) % 4 for k in HOPS]
    meta = (
        [core, (core == x % 2).astype(jnp.int32)]
        + [core] * 6
        + [c * 4 + at for c, at in to_devices]
        + [2 * at + c for c, at in to_devices]
        + [c * 4 + at for c, at in from_devices]
        + [2 * at + c for c, at in from_devices]
        + held
    )
    slot_heads = head_table.reshape(-1)
    filled = (slot_heads < HEADS).astype(jnp.int32)
    places24 = jnp.arange(24, dtype=jnp.int32)
    order = jnp.sum(jnp.where(places24[None, :] < places24[:, None], filled[None, :], 0), axis=1)
    head_ids = jnp.arange(HEADS, dtype=jnp.int32)
    ranked = (order[None, :] == head_ids[:, None]) & (slot_heads[None, :] < HEADS)
    head_of_rank = jnp.sum(jnp.where(ranked, slot_heads[None, :], 0), axis=1)
    meta = jnp.concatenate([jnp.stack(meta), head_of_rank]).astype(jnp.int32)

    def spread_core(own, axis=-1):
        half = HEAD_DIM // 2
        low = lax.slice_in_dim(own, 0, half, axis=axis)
        high = lax.slice_in_dim(own, own.shape[axis] - half, own.shape[axis], axis=axis)
        got = send(jnp.where(first, high, low), CORES)
        return jnp.where(
            first,
            jnp.concatenate([own, got], axis=axis),
            jnp.concatenate([got, own], axis=axis),
        )

    packed_a = [
        jnp.concatenate([query_key_value[l, i] for i in range(3)] + [attention_out[l]], axis=1)
        for l in range(LAYERS)
    ]
    packed_b = [
        jnp.concatenate([expand_weight[l], contract_weight[l].T], axis=1) for l in range(LAYERS)
    ]
    biases = jnp.concatenate([attention_bias.reshape(LAYERS, 480), expand_bias], axis=1)
    moved_a = send(packed_a[0], TO_FEATURE)
    packed_late = jnp.concatenate([packed_b[1], packed_a[1]], axis=1)

    def widen_heads(own):
        return spread_core(own.reshape(80, 3, 160)).reshape(80, 3 * LOCAL)

    def widen(moved):
        return jnp.concatenate([widen_heads(moved[:, :480]), moved[:, 480:]], axis=1)

    def gather_plane(value):
        return lax.all_gather(value, AXES, axis=0, tiled=True, axis_index_groups=PLANES)

    def gain_of(l, i):
        return norm_gain[l, i].reshape(1, D), norm_bias[l, i].reshape(1, D)

    normed, stream, token = first_norm(meta, stream_in, send(stream_in, CORES), *gain_of(0, 0))
    biases, packed_first, packed_late = later((biases, packed_b[0], packed_late), (token,))
    biases = send(biases, TO_FEATURE)
    wide_a = widen(moved_a)
    first_a = lax.all_to_all(
        spread_out(wide_a, (token,)), AXES, 0, 0, tiled=True, axis_index_groups=PLANES
    ).reshape(D, 736)

    terms = []
    left = biases[:, 320:480]
    for _ in range(3):
        terms.append(left.astype(BF16))
        left = left - terms[-1].astype(F32)
    terms = jnp.concatenate(terms + [jnp.zeros((122, 160), BF16)], axis=0).T
    block = turn(first_a, terms)
    moved_late = send(packed_late, TO_FEATURE)
    (packed_first,) = later((packed_first,), (block,))
    first_b = gather_plane(send(packed_first, TO_FEATURE))
    more = moved_late[:, D + 480 :].reshape(8, 10, 160).transpose(1, 0, 2).reshape(10, D)
    more = jnp.pad(more, ((0, EXTRA - 10), (0, 0)))
    step_of_feature = jnp.sum(
        jnp.where(
            jnp.stack([2 * ((y - k) % 4) + c for c in (core, 1 - core) for k in HOPS])[None, :]
            == jnp.arange(8)[:, None],
            jnp.arange(8)[None, :],
            0,
        ),
        axis=1,
    )

    w_in = [(first_a, 0)]
    w_units = [first_b]

    query_bias = spread_core(biases[:, :160])
    value_bias = spread_core(biases[:, 160:320])
    qkv_bias = jnp.concatenate(
        [query_bias, jnp.zeros((LAYERS, LOCAL), F32), value_bias], axis=1
    ).reshape(LAYERS, 1, 3 * LOCAL)
    up_bias = biases[:, 480:].reshape(LAYERS, 1, UNITS)

    def exchange(pieces):
        return [
            send(piece, to_step(dy, dc)) if dy or dc else piece
            for piece, (dy, dc) in zip(pieces, STEPS)
        ]

    def gather_pieces(block):
        near = [block] + [send(block, along_y(k)) for k in HOPS[1:]]
        return near + [send(value, CORES) for value in near]

    feature_places = jnp.stack(
        [2 * ((y - k) % 4) + core for k in HOPS] + [2 * ((y - k) % 4) + 1 - core for k in HOPS]
    ).astype(jnp.int32)

    seg = lax.dynamic_slice_in_dim(segments, sequence * SEQ, SEQ)
    start = jnp.sum((seg[:, None] < seg[None, :]).astype(jnp.int32), axis=0, keepdims=True)
    def gather_tokens(value):
        return lax.all_gather(value, AXES, axis=0, tiled=True, axis_index_groups=BY_TOKEN)

    def sum_parts(far, near, after=()):
        *parts, token = add_cores(near, send(far, CORES), after)
        return [send(part, along_y(-k)) if k else part for part, k in zip(parts, HOPS)], token

    def scatter_plane(value):
        return lax.psum_scatter(
            value, AXES, scatter_dimension=0, tiled=True, axis_index_groups=PLANES
        )

    def to_result(value):
        blocks = jnp.moveaxis(value.reshape(value.shape[:-1] + (8, 160)), -2, 0)
        got = lax.all_to_all(blocks, AXES, 0, 0, tiled=True, axis_index_groups=BY_FEATURE)
        got = got.reshape((4, 2) + got.shape[1:])
        got = jnp.moveaxis(got, (1, 0), (-4, -3))
        return send(got.reshape(value.shape[:-2] + (SEQ, 160)), FROM_FEATURE)

    grad_held, grad, grad_sum, held_token = hold_grads(meta, cotangent, send(cotangent, CORES))
    pieces = None
    kept = []
    streams = []
    for l in range(LAYERS):
        first_layer = l == 0
        if first_layer:
            qkv = project_first(normed, first_a, qkv_bias[l], (more,))
            turned_out = [block] + [send(block, along_y(k)) for k in HOPS[1:]]
        else:
            qkv, normed = project(meta, pieces, *w_in[l], qkv_bias[l])
        pieces, turned, lse, token = attend_forward(meta, start, qkv)
        pieces = exchange(pieces)
        if first_layer:
            turned_out = later(turned_out, (pieces[1],))
            turned_out = [*turned_out] + [send(value, CORES) for value in turned_out]
        if first_layer:
            w_heads = assemble(turned_out, feature_places, (pieces[1],))
        else:
            w_heads = late
        gain, shift = gain_of(l, 1)
        mid, low, heads, more = join_heads(
            meta, pieces, w_heads, first_layer, stream, gain, shift, more
        )
        pieces = gather_pieces(low)
        if first_layer:
            rows = gathered_rows(step_of_feature.astype(jnp.int32), pieces)
            late = gather_plane(
                jnp.concatenate(
                    [
                        widen_heads(moved_late[:, D : D + 480]),
                        jnp.zeros((80, 64), BF16),
                        rows,
                    ],
                    axis=1,
                )
            )
            w_in.append((late, 0))
            moved_units, _ = later((moved_late[:, :D], rows), (mid,))
            w_units.append(gather_plane(moved_units))
        bias = contract_bias[l].reshape(1, D)
        state = (stream, mid, normed, pieces, w_heads, qkv, turned, lse, heads)
        if first_layer:
            far = up_down(pieces[4:], w_units[l], up_bias[l])
            near = up_down(pieces[:4], w_units[l], up_bias[l])
            kept.append(state + (far, near))
            parts, _ = sum_parts(far[2], near[2])
            gain, shift = gain_of(l + 1, 0)
            stream, low = join_norm(parts, mid, bias, gain, shift, (held_token,))
            pieces = gather_pieces(low)
            streams.append(stream.astype(BF16))
        else:
            far = up_down_both(pieces[4:], grad_held, 4, w_units[l], up_bias[l])
            near = up_down_both(pieces[:4], grad_held, 0, w_units[l], up_bias[l])
            kept.append(state + (far, near))
            last = (far[4], near[4], mid, bias)

    grad_pieces = None
    wide_sums = [None] * LAYERS
    plane_sums = [None] * LAYERS
    for l in reversed(range(LAYERS)):
        stream, mid, normed, pieces, w_heads, qkv, turned, lse, own_heads, far, near = kept[l]
        if l:
            act_far, low_far, sum_far, back_far, _ = far
            act_near, low_near, sum_near, back_near, _ = near
        else:
            low_far, sum_far, back_far = up_down_back(grad_pieces[4:], w_units[l], far[0])
            low_near, sum_near, back_near = up_down_back(grad_pieces[:4], w_units[l], near[0])
            act_far, act_near = far[1], near[1]
        parts, token = sum_parts(back_far, back_near)
        units, token = unit_grads(
            pieces,
            (low_near, low_far),
            (grad_held,) if l else grad_pieces,
            (act_near, act_far),
            (token,),
            None if l else heads,
        )
        mid_grad, sums_two, pieces, token = norm_back_heads(
            meta,
            parts,
            mid,
            grad,
            gain_of(l, 1)[0],
            w_heads,
            l == 0,
            (token,) if l else (token, units_one),
        )
        units, own_heads = later((units, own_heads), (token,))
        all_heads = gather_tokens(own_heads)
        summed = scatter_plane(units)
        if l:
            units_one = summed
        else:
            units_both = summed
        grad_qkv, grad_own, qkv_sum, mid_all = attend_backward(
            meta, start, qkv, turned, lse, exchange(pieces)
        )
        back_far = project_back(meta, grad_qkv, *w_in[l], 4)
        back_near = project_back(meta, grad_qkv, *w_in[l], 0)
        parts, token = sum_parts(back_far, back_near)
        heads, token = head_grads(normed, grad_own, all_heads, mid_all, (token,))
        grad_new, next_low, sums_one, token = norm_back(
            parts, stream, mid_grad, gain_of(l, 0)[0], (token,)
        )
        wide_sums[l] = jnp.concatenate([sums_one[:2], sums_two[:3], grad_sum], axis=0)
        plane_sums[l] = jnp.concatenate(
            [
                qkv_sum[:, :160],
                qkv_sum[:, 320:],
                sum_far + sum_near,
                jnp.zeros((1, D - 960), F32),
            ],
            axis=1,
        )
        grad_sum = sums_one[2:3]
        grad = grad_new
        if l:
            grad_pieces = gather_pieces(next_low)
    heads_zero = lax.all_to_all(
        heads.reshape(16, 80, UNITS + 128), AXES, 0, 0, tiled=True, axis_index_groups=PLANES
    )
    grad, _ = later((grad, next_low), (heads_zero,))
    heads_zero = jnp.sum(heads_zero[:, :, :UNITS].astype(F32), axis=0).astype(BF16)
    heads_zero = send(heads_zero, FROM_FEATURE)
    grad_stream = to_result(grad)

    last_far, last_near, mid, bias = last
    parts, _ = sum_parts(last_far, last_near, (token,))
    total = (parts[0].astype(F32) + parts[1].astype(F32)) + (
        parts[2].astype(F32) + parts[3].astype(F32)
    )
    streams.append((mid + total + bias).astype(BF16))
    activations = to_result(jnp.stack(streams))

    units_one = send(units_one, FROM_FEATURE)
    units_both = send(units_both, FROM_FEATURE)
    unit_back = jnp.stack([units_both[:, : 2 * UNITS], units_one]).astype(F32)
    head_back = jnp.stack([heads_zero, units_both[:, 2 * UNITS : 3 * UNITS]]).astype(F32)
    grad_query_key_value = head_back[:, :, :480].reshape(LAYERS, 80, 3, 160).transpose(0, 2, 1, 3)
    grad_attention_out = head_back[:, :, 480:]
    grad_expand = unit_back[:, :, :UNITS]
    grad_contract = unit_back[:, :, UNITS:].transpose(0, 2, 1)

    def sum_four(value, perms):
        one, two, three = (send(value, perm) for perm in perms)
        return (value + two) + (one + three)

    def sum_y(value):
        value = value + send(value, CORES)
        return sum_four(value, [along_y(k) for k in (1, 2, 3)])

    def sum_plane(value):
        value = sum_four(value, [along_plane(0, k) for k in (1, 2, 3)])
        return sum_four(value, [along_plane(k, 0) for k in (1, 2, 3)])

    wide = sum_y(jnp.concatenate(wide_sums, axis=0))
    sums = sum_plane(jnp.concatenate([wide] + plane_sums, axis=0))
    wide = sums[:12].reshape(LAYERS, 6, D)
    plane = send(sums[12:], FROM_FEATURE)
    grad_norm_gain = jnp.stack([wide[:, 0], wide[:, 2]], axis=1)
    grad_norm_bias = jnp.stack([wide[:, 1], wide[:, 3]], axis=1)
    out_sums = lax.dynamic_slice_in_dim(wide[:, 4], col * 160, 160, 1)
    grad_attention_bias = jnp.stack([plane[:, :160], plane[:, 160:320], out_sums], axis=1)
    grad_expand_bias = plane[:, 320:960]
    grad_contract_bias = wide[:, 5]
    return (
        activations,
        grad_stream,
        grad_query_key_value,
        grad_attention_out,
        grad_expand,
        grad_contract,
        grad_norm_gain,
        grad_norm_bias,
        grad_attention_bias,
        grad_expand_bias,
        grad_contract_bias,
    )


def solution(mesh):
    placed = (
        P("row", None),
        P(),
        P(),
        P(None, None, "row", "col"),
        P(None, "row", "col"),
        P(None, "row", "col"),
        P(None, "col", "row"),
        P(),
        P(),
        P(None, None, "col"),
        P(None, "col"),
        P(),
        P("row", None),
    )
    return jax.shard_map(
        on_device,
        mesh=mesh,
        in_specs=placed,
        out_specs=(
            P(None, "row", "col"),
            P("row", "col"),
            P(None, None, "row", "col"),
            P(None, "row", "col"),
            P(None, "row", "col"),
            P(None, "col", "row"),
            P(),
            P(),
            P(None, None, "col"),
            P(None, "col"),
            P(),
        ),
        check_vma=False,
    )
```

```python
import functools

import jax
import jax.numpy as jnp
from jax import lax
from jax.experimental import pallas as pl
from jax.experimental.pallas import tpu as pltpu
from jax.sharding import PartitionSpec as P

D = 1280
HEADS = 20
HEAD_DIM = 64
SEQ = 1024
LAYERS = 2
BLOCK = 128
LOCAL = 3 * HEAD_DIM
SCALE = HEAD_DIM ** (-0.5)
AXES = ("row", "col")
BF16 = jnp.bfloat16
F32 = jnp.float32
MIB = 1024 * 1024


def device(z, x, core, y):
    return (z * 4 + (x // 2) * 2 + core) * 8 + (x % 2) * 4 + y


def pairs(target):
    out = []
    for z in range(4):
        for x in range(4):
            for core in range(2):
                for y in range(4):
                    out.append((device(z, x, core, y), device(*target(z, x, core, y))))
    return out


def along_y(k):
    return pairs(lambda z, x, core, y: (z, x, core, (y + k) % 4))


def along_plane(dz, dx):
    return pairs(lambda z, x, core, y: ((z + dz) % 4, (x + dx) % 4, core, y))


def to_feature(z, x, core, y):
    block = (x % 2) * 4 + y
    return (z, (x // 2) * 2 + core, block % 2, block // 2)


CORES = pairs(lambda z, x, core, y: (z, x, 1 - core, y))
TO_FEATURE = pairs(to_feature)
FROM_FEATURE = [(b, a) for a, b in TO_FEATURE]
HOME = pairs(lambda z, x, core, y: (z, (x // 2) * 2 + core, x % 2, y))
PLANES = [
    [device(z, x, core, y) for z in range(4) for x in range(4)]
    for y in range(4)
    for core in range(2)
]
BY_FEATURE = [
    [device(z, x, core, y) for y in range(4) for core in range(2)]
    for z in range(4)
    for x in range(4)
]
BY_TOKEN = [
    [device(z, x, core, y) for core in range(2) for y in range(4)]
    for z in range(4)
    for x in range(4)
]
STEPS = [(dy, dc) for dy in (0, 1, 3, 2) for dc in (0, 1)]
HOPS = (0, 1, 3, 2)


NAMES = {tuple(CORES): "cores", tuple(TO_FEATURE): "to_feature", tuple(FROM_FEATURE): "from_feature"}


def send(value, perm):
    with jax.named_scope("send_" + NAMES.get(tuple(perm), "far")):
        return lax.ppermute(value, AXES, perm)


CORE, SAME, TO_BLOCK, TO_SLOT, FROM_BLOCK, FROM_SLOT, HELD, HEAD_OF = 0, 1, 8, 16, 24, 32, 40, 48
HELD_SLOT = HEAD_OF + HEADS
IN_SMEM = pl.BlockSpec(memory_space=pltpu.SMEM)
ANYWHERE = pl.BlockSpec(memory_space=pl.ANY)
IN_HBM = pl.BlockSpec(memory_space=pltpu.HBM)


LIGHT = pl.CostEstimate(flops=1000, bytes_accessed=1000, transcendentals=0)


def call(kernel, in_specs, limit=16, after=(), light=False, aliases=None, **kwargs):
    count = len(after)

    def waiting(*refs):
        kernel(*refs[count:])

    specs = [IN_HBM] * count + list(in_specs)
    run = pl.pallas_call(
        waiting,
        in_specs=specs,
        compiler_params=pltpu.CompilerParams(vmem_limit_bytes=limit * MIB),
        cost_estimate=LIGHT if light else None,
        input_output_aliases={count + i: out for i, out in (aliases or {}).items()},
        **kwargs,
    )
    label = getattr(kernel, "func", kernel).__name__

    def named(*operands):
        with jax.named_scope(label):
            placed = [
                pltpu.with_memory_space_constraint(value, pltpu.HBM) if spec is IN_HBM else value
                for value, spec in zip((*after, *operands), specs)
            ]
            return run(*placed)

    return named


def shaped(shape, dtype):
    return jax.ShapeDtypeStruct(shape, dtype)


def in_hbm(shape, dtype):
    return pltpu.HBM(shape, dtype)


def full(shape):
    return pl.BlockSpec(shape, lambda i: (0,) * len(shape))


TOKEN = full((8, 128))
TOKEN_SHAPE = in_hbm((8, 128), F32)


def mark(token_ref):
    token_ref[...] = jnp.zeros((8, 128), F32)


def fetch(pieces, target, sems):
    rows = target.shape[0] // len(pieces)
    copies = []
    for i, piece in enumerate(pieces):
        copies.append(
            pltpu.make_async_copy(
                piece.at[pl.ds(0, rows), :], target.at[pl.ds(i * rows, rows), :], sems.at[i]
            )
        )
    for copy in copies:
        copy.start()
    return copies


def load(ref, columns, targets, sems, rows=None):
    copies = []
    for i, target in enumerate(targets):
        width = target.shape[1]
        at = pl.ds(columns + i * width, width)
        copies.append(pltpu.make_async_copy(ref.at[:, at], target, sems.at[i]))
        copies[i].start()
    return copies


def held_rows(count):
    return [pltpu.VMEM((BLOCK, D), F32)] * count + [pltpu.SemaphoreType.DMA((count,))]


def weights_of(count):
    return [pltpu.VMEM((D, UNITS), BF16)] * count + [pltpu.SemaphoreType.DMA((count,))]


UNITS = 640


def pieces_of(count, rows=BLOCK, columns=D):
    return [pltpu.VMEM((count * rows, columns), BF16), pltpu.SemaphoreType.DMA((count,))]


def take_in(meta_ref, own_ref, got_ref, copies_of):
    for flag, ref in ((1, own_ref), (0, got_ref)):

        @pl.when(meta_ref[SAME] == flag)
        def _():
            copies = copies_of(ref)
            for copy in copies:
                copy.start()
            for copy in copies:
                copy.wait()


def hold_grads_kernel(meta_ref, own_ref, got_ref, held_ref, first_ref, sum_ref, token_ref, sems):
    def copies_of(ref):
        return [
            pltpu.make_async_copy(
                ref.at[rows_at(meta_ref, HELD + i), :],
                held_ref.at[pl.ds(i * BLOCK, BLOCK), :],
                sems.at[i],
            )
            for i in range(8)
        ]

    take_in(meta_ref, own_ref, got_ref, copies_of)
    first = held_ref[:BLOCK, :].astype(F32)
    first_ref[...] = first
    sum_ref[...] = jnp.sum(first, axis=0, keepdims=True)
    mark(token_ref)


def hold_grads(meta, own, got):
    return call(
        hold_grads_kernel,
        [IN_SMEM, IN_HBM, IN_HBM],
        light=True,
        grid=(1,),
        out_specs=[full((SEQ, D)), full((BLOCK, D)), full((1, D)), TOKEN],
        out_shape=(
            in_hbm((SEQ, D), BF16),
            in_hbm((BLOCK, D), F32),
            shaped((1, D), F32),
            TOKEN_SHAPE,
        ),
        scratch_shapes=[pltpu.SemaphoreType.DMA((8,))],
    )(meta, own, got)


def first_norm_kernel(
    meta_ref, own_ref, got_ref, gain_ref, shift_ref, normed_ref, first_ref, token_ref, x_ref, sems
):
    def copies_of(ref):
        return [
            pltpu.make_async_copy(ref.at[pl.ds(i * 256, 256), :], x_ref.at[pl.ds(i * 256, 256), :], sems.at[i])
            for i in range(4)
        ]

    take_in(meta_ref, own_ref, got_ref, copies_of)
    for i in range(4):
        at = pl.ds(i * 256, 256)
        unit = normal(x_ref[at, :].astype(F32))[0]
        normed_ref[at, :] = (unit * gain_ref[...] + shift_ref[...]).astype(BF16)
    first_ref[...] = x_ref[rows_at(meta_ref, HELD), :].astype(F32)
    mark(token_ref)


def first_norm(meta, own, got, gain, shift):
    return call(
        first_norm_kernel,
        [IN_SMEM, IN_HBM, IN_HBM, full((1, D)), full((1, D))],
        grid=(1,),
        out_specs=[full((SEQ, D)), full((BLOCK, D)), TOKEN],
        out_shape=(in_hbm((SEQ, D), BF16), in_hbm((BLOCK, D), F32), TOKEN_SHAPE),
        scratch_shapes=pieces_of(4, 256),
    )(meta, own, got, gain, shift)


def later(values, after):
    count = len(values)

    def later_kernel(*refs):
        pass

    return call(
        later_kernel,
        [IN_HBM] * count,
        after=after,
        out_specs=[IN_HBM] * count,
        out_shape=[in_hbm(value.shape, value.dtype) for value in values],
        aliases={i: i for i in range(count)},
    )(*values)


def spread_out(value, rows, after):
    def spread_out_kernel(value_ref, out_ref):
        for i in range(16):
            out_ref[i] = value_ref[:rows, :]

    shape = (16, rows, value.shape[1])
    return call(
        spread_out_kernel,
        [full(value.shape)],
        grid=(1,),
        out_specs=full(shape),
        out_shape=in_hbm(shape, value.dtype),
        after=after,
    )(value)


def rows_at(meta_ref, index):
    return pl.ds(pl.multiple_of(meta_ref[index] * BLOCK, BLOCK), BLOCK)


def nt(a, b):
    return lax.dot_general(a, b, (((1,), (1,)), ((), ())), preferred_element_type=F32)


def tn(a, b):
    return lax.dot_general(a, b, (((0,), (0,)), ((), ())), preferred_element_type=F32)


QB = 256


def allowed_at(start_ref, at, keys):
    key = lax.broadcasted_iota(jnp.int32, (keys, QB), 0)
    query = lax.broadcasted_iota(jnp.int32, (keys, QB), 1) + at
    return (key >= start_ref[:, at : at + QB]) & (key <= query)


def attend_forward_kernel(meta_ref, start_ref, qkv_ref, *refs):
    pieces = refs[:4]
    turned_ref, lse_ref, token_ref, own_ref, sems = refs[4:]
    mark(token_ref)
    heads = []
    for h in range(3):
        lo = h * HEAD_DIM
        q = qkv_ref[:, lo : lo + HEAD_DIM] * jnp.asarray(SCALE, BF16)
        k = qkv_ref[:, LOCAL + lo : LOCAL + lo + HEAD_DIM]
        v = qkv_ref[:, 2 * LOCAL + lo : 2 * LOCAL + lo + HEAD_DIM]
        heads.append((q, k, v.astype(F32).T.astype(BF16)))
    for block in range(SEQ // QB):
        at = block * QB
        keys = at + QB
        allowed = allowed_at(start_ref, at, keys)
        parts = []
        for h, (q, k, vt) in enumerate(heads):
            scores = nt(k[:keys], q[at : at + QB])
            scores = jnp.where(allowed, scores, -1e30)
            top = jnp.max(scores, axis=0, keepdims=True)
            weights = jnp.exp(scores - top)
            total = jnp.sum(weights, axis=0, keepdims=True)
            turned = (
                jnp.dot(vt[:, :keys], weights.astype(BF16), preferred_element_type=F32) / total
            )
            lse_ref[h : h + 1, at : at + QB] = top + jnp.log(total)
            turned_ref[h * HEAD_DIM : (h + 1) * HEAD_DIM, at : at + QB] = turned
            parts.append(turned)
        out = jnp.concatenate(parts, axis=0).T.astype(BF16)
        own_ref[at : at + QB, :] = jnp.where(meta_ref[CORE] == 0, out[:, :160], out[:, 32:])
    copies = [
        pltpu.make_async_copy(
            own_ref.at[rows_at(meta_ref, TO_BLOCK + j), :],
            pieces[j // 2].at[pl.ds(j % 2 * BLOCK, BLOCK), :],
            sems.at[j],
        )
        for j in range(8)
    ]
    for copy in copies:
        copy.start()
    for copy in copies:
        copy.wait()


def attend_forward(meta, start, qkv):
    results = call(
        attend_forward_kernel,
        grid=(1,),
        in_specs=[IN_SMEM, full((1, SEQ)), full((SEQ, 3 * LOCAL))],
        out_specs=[ANYWHERE] * 4
        + [full((LOCAL, SEQ)), full((8, SEQ)), TOKEN],
        out_shape=[in_hbm((2 * BLOCK, 160), BF16)] * 4
        + [shaped((LOCAL, SEQ), F32), shaped((8, SEQ), F32), TOKEN_SHAPE],
        scratch_shapes=[pltpu.VMEM((SEQ, 160), BF16), pltpu.SemaphoreType.DMA((8,))],
    )(meta, start, qkv)
    return results[:4], results[4], results[5], results[6]


WIDE = LOCAL + 160


def attend_backward_kernel(meta_ref, start_ref, qkv_ref, turned_ref, lse_ref, *refs):
    pieces = refs[:8]
    out_ref, own_ref, sum_ref, mid_ref, grad_ref, sems, dk_ref, dv_ref = refs[8:]
    copies = [
        pltpu.make_async_copy(
            pieces[j].at[pl.ds(j % 2 * BLOCK, BLOCK), :],
            grad_ref.at[rows_at(meta_ref, FROM_BLOCK + j), :],
            sems.at[j],
        )
        for j in range(8)
    ]
    for copy in copies:
        copy.start()
    for copy in copies:
        copy.wait()
    mid_ref[...] = grad_ref[:, LOCAL:]
    for h in range(3):
        lo = h * HEAD_DIM
        q = qkv_ref[:, lo : lo + HEAD_DIM] * jnp.asarray(SCALE, BF16)
        k = qkv_ref[:, LOCAL + lo : LOCAL + lo + HEAD_DIM]
        v = qkv_ref[:, 2 * LOCAL + lo : 2 * LOCAL + lo + HEAD_DIM]
        g = grad_ref[:, lo : lo + HEAD_DIM]
        kt = k.astype(F32).T.astype(BF16)
        delta = jnp.sum(
            g.astype(F32).T * turned_ref[lo : lo + HEAD_DIM, :], axis=0, keepdims=True
        )
        for block in reversed(range(SEQ // QB)):
            at = block * QB
            keys = at + QB
            allowed = allowed_at(start_ref, at, keys)
            q_part, g_part = q[at : at + QB], g[at : at + QB]
            scores = nt(k[:keys], q_part)
            probs = jnp.where(
                allowed, jnp.exp(scores - lse_ref[h : h + 1, at : at + QB]), 0.0
            )
            grad_probs = nt(v[:keys], g_part)
            grad_scores = (probs * (grad_probs - delta[:, at : at + QB])).astype(BF16)
            dv = jnp.dot(probs.astype(BF16), g_part, preferred_element_type=F32)
            dk = jnp.dot(grad_scores, q_part, preferred_element_type=F32)
            dq = jnp.dot(kt[:, :keys], grad_scores, preferred_element_type=F32) * SCALE
            out_ref[at : at + QB, lo : lo + HEAD_DIM] = dq.T.astype(BF16)
            if keys == SEQ:
                dk_ref[...] = dk
                dv_ref[...] = dv
            else:
                dk_ref[:keys, :] += dk
                dv_ref[:keys, :] += dv
        out_ref[:, LOCAL + lo : LOCAL + lo + HEAD_DIM] = dk_ref[...].astype(BF16)
        out_ref[:, 2 * LOCAL + lo : 2 * LOCAL + lo + HEAD_DIM] = dv_ref[...].astype(BF16)
    for i in range(3):
        part = out_ref[:, i * LOCAL : (i + 1) * LOCAL]
        own = jnp.where(meta_ref[CORE] == 0, part[:, :160], part[:, 32:])
        own_ref[:, i * 160 : (i + 1) * 160] = own
        sum_ref[:, i * 160 : (i + 1) * 160] = jnp.sum(own.astype(F32), axis=0, keepdims=True)


def gelu(v):
    inner = 0.7978845608028654 * (v + 0.044715 * v * v * v)
    return 0.5 * v * (1.0 + jnp.tanh(inner))


def gelu_slope(v):
    t = jnp.tanh(0.7978845608028654 * (v + 0.044715 * v * v * v))
    return 0.5 * (1.0 + t) + 0.5 * v * (1.0 - t * t) * 0.7978845608028654 * (
        1.0 + 3 * 0.044715 * v * v
    )


HALF = 512
def up_down_kernel(
    a, b, c, d, w_ref, bias_ref, hidden_ref, act_ref, out_ref, *refs
):
    x_ref, sems, y_ref, done, up_ref, down_ref, w_sems = refs
    copies = fetch((a, b, c, d), x_ref, sems)
    weights = load(w_ref, 0, (up_ref, down_ref), w_sems)
    outs = []
    for i in range(2):
        at = pl.ds(i * 256, 256)
        copies[2 * i].wait()
        copies[2 * i + 1].wait()
        if not i:
            weights[0].wait()
        hidden = jnp.dot(x_ref[at, :], up_ref[...], preferred_element_type=F32) + bias_ref[...]
        hidden_ref[at, :] = hidden
        act = gelu(hidden).astype(BF16)
        act_ref[at, :] = act
        if not i:
            weights[1].wait()
        y_ref[at, :] = nt(act, down_ref[...]).astype(BF16)
        outs.append(pltpu.make_async_copy(y_ref.at[at, :], out_ref.at[at, :], done.at[i]))
        outs[i].start()
    for copy in outs:
        copy.wait()


def up_down(pieces, weights, bias):
    return call(
        up_down_kernel,
        grid=(1,),
        in_specs=[IN_HBM] * 5 + [full((1, UNITS))],
        out_specs=[full((HALF, UNITS)), full((HALF, UNITS)), ANYWHERE],
        scratch_shapes=pieces_of(4) + pieces_of(2, 256) + weights_of(2),
        out_shape=(
            in_hbm((HALF, UNITS), F32),
            in_hbm((HALF, UNITS), BF16),
            shaped((HALF, D), BF16),
        ),
    )(*pieces, weights, bias)


def up_down_back_kernel(a, b, c, d, w_ref, hidden_ref, low_ref, sum_ref, out_ref, *refs):
    g_ref, sems, y_ref, done, down_ref, up_ref, w_sems, kept_ref, kept_sems = refs
    copies = fetch((a, b, c, d), g_ref, sems)
    kept = pltpu.make_async_copy(hidden_ref, kept_ref, kept_sems.at[0])
    kept.start()
    weights = load(w_ref, UNITS, (down_ref,), w_sems)
    weights.append(pltpu.make_async_copy(w_ref.at[:, pl.ds(0, UNITS)], up_ref, w_sems.at[1]))
    weights[1].start()
    outs = []
    total = jnp.zeros((1, UNITS), F32)
    for i in range(2):
        at = pl.ds(i * 256, 256)
        copies[2 * i].wait()
        copies[2 * i + 1].wait()
        if not i:
            weights[0].wait()
            kept.wait()
        grad = jnp.dot(g_ref[at, :], down_ref[...], preferred_element_type=F32)
        grad = grad * gelu_slope(kept_ref[at, :])
        total += jnp.sum(grad, axis=0, keepdims=True)
        low = grad.astype(BF16)
        low_ref[at, :] = low
        if not i:
            weights[1].wait()
        y_ref[at, :] = nt(low, up_ref[...]).astype(BF16)
        outs.append(pltpu.make_async_copy(y_ref.at[at, :], out_ref.at[at, :], done.at[i]))
        outs[i].start()
    sum_ref[...] = total
    for copy in outs:
        copy.wait()


def up_down_back(pieces, weights, hidden):
    return call(
        up_down_back_kernel,
        grid=(1,),
        in_specs=[IN_HBM] * 4 + [ANYWHERE, IN_HBM],
        out_specs=[full((HALF, UNITS)), full((1, UNITS)), ANYWHERE],
        scratch_shapes=pieces_of(4)
        + pieces_of(2, 256)
        + weights_of(2)
        + [pltpu.VMEM((HALF, UNITS), F32), pltpu.SemaphoreType.DMA((1,))],
        out_shape=(
            in_hbm((HALF, UNITS), BF16),
            shaped((1, UNITS), F32),
            shaped((HALF, D), BF16),
        ),
    )(*pieces, weights, hidden)


def up_down_both_kernel(first, meta_ref, a, b, c, d, grad_ref, w_ref, bias_ref, *refs):
    if not first:
        refs = refs[1:]
    act_ref, low_ref, sum_ref, back_ref, out_ref = refs[:5]
    x_ref, sems, g_ref, g_sems, back, back_done, out, out_done = refs[5:13]
    up_ref, down_ref, w_sems = refs[13:]
    copies = fetch((a, b, c, d), x_ref, sems)
    weights = load(w_ref, 0, (up_ref, down_ref), w_sems)
    grads = [grad_ref.at[pl.ds((first + 2 * i) * BLOCK, 256), :] for i in range(2)]
    grads = fetch(grads, g_ref, g_sems)
    total = jnp.zeros((1, UNITS), F32)
    done = []
    for i in range(2):
        at = pl.ds(i * 256, 256)
        copies[2 * i].wait()
        copies[2 * i + 1].wait()
        grads[i].wait()
        if not i:
            weights[0].wait()
        hidden = jnp.dot(x_ref[at, :], up_ref[...], preferred_element_type=F32) + bias_ref[...]
        act = gelu(hidden).astype(BF16)
        act_ref[at, :] = act
        if not i:
            weights[1].wait()
        grad = jnp.dot(g_ref[at, :], down_ref[...], preferred_element_type=F32)
        grad = grad * gelu_slope(hidden)
        total += jnp.sum(grad, axis=0, keepdims=True)
        low = grad.astype(BF16)
        low_ref[at, :] = low
        back[at, :] = nt(low, up_ref[...]).astype(BF16)
        done.append(pltpu.make_async_copy(back.at[at, :], back_ref.at[at, :], back_done.at[i]))
        done[-1].start()
        out[at, :] = nt(act, down_ref[...]).astype(BF16)
        for k in range(2 * i, 2 * i + 2):
            rows = rows_at(meta_ref, HELD + first + k)
            done.append(
                pltpu.make_async_copy(
                    out.at[pl.ds(k * BLOCK, BLOCK), :], out_ref.at[rows, :], out_done.at[k]
                )
            )
            done[-1].start()
    sum_ref[...] = total
    for copy in done:
        copy.wait()


def up_down_both(meta, pieces, grads, first, weights, bias, outs=None):
    extra = [] if outs is None else [outs]
    return call(
        functools.partial(up_down_both_kernel, first),
        [IN_SMEM] + [IN_HBM] * 6 + [full((1, UNITS))] + [IN_HBM] * len(extra),
        aliases={8: 4} if extra else None,
        grid=(1,),
        out_specs=[full((HALF, UNITS)), full((HALF, UNITS)), full((1, UNITS)), ANYWHERE, ANYWHERE],
        out_shape=(
            in_hbm((HALF, UNITS), BF16),
            in_hbm((HALF, UNITS), BF16),
            shaped((1, UNITS), F32),
            shaped((HALF, D), BF16),
            in_hbm((SEQ, D), BF16),
        ),
        scratch_shapes=pieces_of(4)
        + pieces_of(2, 256) * 2
        + pieces_of(4)
        + weights_of(2),
    )(meta, *pieces, grads, weights, bias, *extra)


def unit_grads_kernel(x_count, g_count, extra, *refs):
    xs, gs = refs[:x_count], refs[x_count : x_count + g_count]
    halves = refs[x_count + g_count : x_count + g_count + 4]
    refs = refs[x_count + g_count + 4 :]
    if extra:
        heads_ref, refs = refs[0], refs[1:]
    out_ref, token_ref, x_ref, x_sems, g_ref, g_sems, low_ref, low_sems, act_ref, act_sems = refs[:10]
    if extra:
        rest = pltpu.make_async_copy(
            heads_ref, out_ref.at[:, pl.ds(2 * UNITS, UNITS)], refs[10].at[0]
        )
        rest.start()
    ups = fetch(xs, x_ref, x_sems) + fetch(halves[:2], low_ref, low_sems)
    downs = fetch(gs, g_ref, g_sems) + fetch(halves[2:], act_ref, act_sems)
    for copies, left, right, column in (
        (ups, x_ref, low_ref, 0),
        (downs, g_ref, act_ref, UNITS),
    ):
        for copy in copies:
            copy.wait()
        for t in range(5):
            at = pl.ds(t * 256, 256)
            out_ref[at, column : column + UNITS] = tn(left[:, at], right[...]).astype(BF16)
    if extra:
        out_ref[:, 3 * UNITS :] = jnp.zeros((D, 128), BF16)
        rest.wait()
    mark(token_ref)


def unit_grads(pieces, lows, grads, acts, after, heads=None):
    extra = [] if heads is None else [heads]
    columns = 2 * UNITS + (UNITS + 128 if extra else 0)
    return call(
        functools.partial(unit_grads_kernel, len(pieces), len(grads), bool(extra)),
        [IN_HBM] * (len(pieces) + len(grads) + 4 + len(extra)),
        limit=28,
        after=after,
        light=True,
        grid=(1,),
        out_specs=[full((D, columns)), TOKEN],
        out_shape=(in_hbm((D, columns), BF16), TOKEN_SHAPE),
        scratch_shapes=pieces_of(len(pieces), SEQ // len(pieces))
        + pieces_of(len(grads), SEQ // len(grads))
        + pieces_of(2, HALF, UNITS) * 2
        + [pltpu.SemaphoreType.DMA((1,))],
    )(*pieces, *grads, *lows, *acts, *extra)


def head_grads_kernel(layer, *refs):
    ins, (out_ref, token_ref), refs = refs[:4], refs[4:6], refs[6:]
    held, sems = refs[:4], refs[4]
    copies = [pltpu.make_async_copy(ins[i], held[i], sems.at[i]) for i in (0, 1, 3)]
    for d in range(8):
        copies.append(
            pltpu.make_async_copy(
                ins[2].at[pl.ds((LAYERS * d + layer) * BLOCK, BLOCK), :],
                held[2].at[pl.ds(d * BLOCK, BLOCK), :],
                sems.at[4 + d],
            )
        )
    for copy in copies:
        copy.start()
    for copy in copies:
        copy.wait()
    normed_ref, own_ref, heads_ref, mid_ref = held
    for t in range(5):
        at = pl.ds(t * 256, 256)
        one = tn(normed_ref[:, at], own_ref[...]).astype(BF16)
        two = tn(heads_ref[:, at], mid_ref[...]).astype(BF16)
        out_ref[at, :] = jnp.concatenate([one, two], axis=1)
    mark(token_ref)


def head_grads(normed, own, heads, mid, layer, after):
    return call(
        functools.partial(head_grads_kernel, layer),
        [IN_HBM] * 4,
        limit=20,
        after=after,
        light=True,
        grid=(1,),
        out_specs=[full((D, UNITS)), TOKEN],
        out_shape=(in_hbm((D, UNITS), BF16), TOKEN_SHAPE),
        scratch_shapes=[pltpu.VMEM((SEQ, n), BF16) for n in (D, 480, D, 160)]
        + [pltpu.SemaphoreType.DMA((12,))],
    )(normed, own, heads, mid)


def add_cores_kernel(near_ref, far_ref, *refs):
    outs, token_ref, (one, one_sems, two, two_sems, sums, done) = refs[:4], refs[4], refs[5:]
    mark(token_ref)
    at = [pl.ds(i * BLOCK, BLOCK) for i in range(4)]
    order = (3, 1, 2, 0)
    ins = {}
    for i in order:
        ins[i] = (
            pltpu.make_async_copy(near_ref.at[at[i], :], one.at[at[i], :], one_sems.at[i]),
            pltpu.make_async_copy(far_ref.at[at[i], :], two.at[at[i], :], two_sems.at[i]),
        )
        ins[i][0].start()
        ins[i][1].start()
    copies = []
    for i in order:
        ins[i][0].wait()
        ins[i][1].wait()
        sums[at[i], :] = (one[at[i], :].astype(F32) + two[at[i], :].astype(F32)).astype(BF16)
        copies.append(pltpu.make_async_copy(sums.at[at[i], :], outs[i], done.at[i]))
        copies[-1].start()
    for copy in copies:
        copy.wait()


def add_cores(near, far, after=()):
    return call(
        add_cores_kernel,
        after=after,
        grid=(1,),
        in_specs=[ANYWHERE] * 2,
        out_specs=[ANYWHERE] * 4 + [TOKEN],
        out_shape=[in_hbm((BLOCK, D), BF16)] * 4 + [TOKEN_SHAPE],
        scratch_shapes=pieces_of(4) * 3,
    )(near, far)


def project_kernel(column, meta_ref, *refs):
    pieces = refs[:8]
    full_ref, bias_ref, qkv_ref, normed_ref, x_ref, sems, w_ref, w_sems = refs[8:]
    copies = fetch(pieces, x_ref, sems)
    load(full_ref, column * UNITS, (w_ref,), w_sems)[0].wait()
    for i in range(0, 8, 2):
        copies[i].wait()
        copies[i + 1].wait()
        x = x_ref[i * BLOCK : (i + 2) * BLOCK, :]
        qkv = jnp.dot(x, w_ref[:, : 3 * LOCAL], preferred_element_type=F32) + bias_ref[...]
        qkv = qkv.astype(BF16)
        for k in range(2):
            at = rows_at(meta_ref, HELD + i + k)
            normed_ref[at, :] = x[k * BLOCK : (k + 1) * BLOCK]
            qkv_ref[at, :] = qkv[k * BLOCK : (k + 1) * BLOCK]


def columns_of(at):
    return pl.BlockSpec((D, UNITS), lambda i: (0, at))


def project_first_kernel(x_ref, w_ref, bias_ref, qkv_ref):
    qkv = jnp.dot(x_ref[...], w_ref[:, : 3 * LOCAL], preferred_element_type=F32)
    qkv_ref[...] = (qkv + bias_ref[...]).astype(BF16)


def project_first(normed, weights, bias):
    return call(
        project_first_kernel,
        grid=(4,),
        in_specs=[pl.BlockSpec((256, D), lambda i: (i, 0)), columns_of(0), full((1, 3 * LOCAL))],
        out_specs=pl.BlockSpec((256, 3 * LOCAL), lambda i: (i, 0)),
        out_shape=shaped((SEQ, 3 * LOCAL), BF16),
    )(normed, weights, bias)


def gathered_rows_kernel(step_ref, *refs):
    pieces, wide_ref, out_ref, held, sems = refs[:8], refs[8], refs[9], refs[10], refs[11]
    copies = [
        pltpu.make_async_copy(
            piece.at[pl.ds(BLOCK, EXTRA), :], held.at[i], sems.at[i]
        )
        for i, piece in enumerate(pieces)
    ]
    for copy in copies:
        copy.start()
    for copy in copies:
        copy.wait()
    out_ref[:, : 3 * LOCAL] = wide_ref[...]
    out_ref[:, 3 * LOCAL : UNITS] = jnp.zeros((80, UNITS - 3 * LOCAL), BF16)
    for f in range(8):
        rows = held[step_ref[f]].astype(F32)
        parts = [rows[:10, j * 160 : (j + 1) * 160] for j in range(8)]
        at = UNITS + f * 160
        out_ref[:, at : at + 160] = jnp.concatenate(parts, axis=0).astype(BF16)


def gathered_rows(steps, pieces, wide):
    return call(
        gathered_rows_kernel,
        grid=(1,),
        light=True,
        in_specs=[IN_SMEM] + [IN_HBM] * 8 + [full((80, 3 * LOCAL))],
        out_specs=full((80, UNITS + D)),
        out_shape=in_hbm((80, UNITS + D), BF16),
        scratch_shapes=[pltpu.VMEM((8, EXTRA, D), BF16), pltpu.SemaphoreType.DMA((8,))],
    )(steps, *pieces, wide)


EXTRA = 16


def turn_kernel(one_ref, two_ref, terms_ref, out_ref):
    out_ref[:, D:] = terms_ref[...]
    for i in range(10):
        at = pl.ds(i * 128, 128)
        rows = jnp.concatenate(
            [one_ref[at, 64:].astype(F32), two_ref[at, :96].astype(F32)], axis=1
        )
        out_ref[:, at] = rows.T.astype(BF16)


def turn(weights, terms):
    first = 3 * LOCAL // 128
    return call(
        turn_kernel,
        grid=(1,),
        in_specs=[
            pl.BlockSpec((D, 128), lambda i: (0, first)),
            pl.BlockSpec((D, 128), lambda i: (0, first + 1)),
            full((160, 128)),
        ],
        out_specs=full((160, D + 128)),
        out_shape=in_hbm((160, D + 128), BF16),
    )(weights, weights, terms)


def project_attend_kernel(column, meta_ref, *refs):
    ins, (start_ref, qkv_ref, normed_ref), refs = refs[:10], refs[10:13], refs[13:]
    project_kernel(column, meta_ref, *ins, qkv_ref, normed_ref, *refs[7:11])
    attend_forward_kernel(meta_ref, start_ref, qkv_ref, *refs[:7], *refs[11:])


def project_attend(meta, pieces, weights, at, bias, start):
    results = call(
        functools.partial(project_attend_kernel, at),
        limit=24,
        grid=(1,),
        in_specs=[IN_SMEM] + [IN_HBM] * 9 + [full((1, 3 * LOCAL)), full((1, SEQ))],
        out_specs=[full((SEQ, 3 * LOCAL)), full((SEQ, D))]
        + [ANYWHERE] * 4
        + [full((LOCAL, SEQ)), full((8, SEQ)), TOKEN],
        out_shape=[in_hbm((SEQ, 3 * LOCAL), BF16), in_hbm((SEQ, D), BF16)]
        + [in_hbm((2 * BLOCK, 160), BF16)] * 4
        + [in_hbm((LOCAL, SEQ), F32), in_hbm((8, SEQ), F32), TOKEN_SHAPE],
        scratch_shapes=pieces_of(8)
        + weights_of(1)
        + [pltpu.VMEM((SEQ, 160), BF16), pltpu.SemaphoreType.DMA((8,))],
    )(meta, *pieces, weights, bias, start)
    return results[0], results[1], results[2:6], results[6], results[7]


def project_back(meta_ref, grad_ref, w_ref, y_ref, out_ref, done, first):
    column = lax.broadcasted_iota(jnp.int32, (1, 3 * LOCAL), 1)
    twice = jnp.zeros((1, 3 * LOCAL), jnp.int32)
    for i in range(3):
        at = column - i * LOCAL
        twice += jnp.where((at >= 0) & (at < HEAD_DIM), 1, 0)
    counted = twice * meta_ref[CORE] == 0
    outs = []
    for i in range(2):
        x = jnp.concatenate(
            [grad_ref[rows_at(meta_ref, HELD + first + 2 * i + k), :] for k in range(2)],
            axis=0,
        )
        x = jnp.where(counted, x.astype(F32), 0.0).astype(BF16)
        at = pl.ds(i * 256, 256)
        y_ref[at, :] = nt(x, w_ref[:, : 3 * LOCAL]).astype(BF16)
        outs.append(pltpu.make_async_copy(y_ref.at[at, :], out_ref.at[at, :], done.at[i]))
        outs[i].start()
    return outs


def attend_project_back_kernel(column_at, meta_ref, start_ref, qkv_ref, turned_ref, lse_ref, *refs):
    pieces, full_ref = refs[:8], refs[8]
    own_ref, sum_ref, mid_ref, far_ref, near_ref = refs[9:14]
    out_ref, grad_ref, sems, dk_ref, dv_ref, w_ref, w_sems = refs[14:21]
    far, far_done, near, near_done = refs[21:]
    weights = load(full_ref, column_at * UNITS, (w_ref,), w_sems)
    attend_backward_kernel(
        meta_ref,
        start_ref,
        qkv_ref,
        turned_ref,
        lse_ref,
        *pieces,
        out_ref,
        own_ref,
        sum_ref,
        mid_ref,
        grad_ref,
        sems,
        dk_ref,
        dv_ref,
    )
    weights[0].wait()
    copies = project_back(meta_ref, out_ref, w_ref, far, far_ref, far_done, 4)
    copies += project_back(meta_ref, out_ref, w_ref, near, near_ref, near_done, 0)
    for copy in copies:
        copy.wait()


def attend_project_back(meta, start, qkv, turned, lse, pieces, weights, column_at):
    return call(
        functools.partial(attend_project_back_kernel, column_at),
        limit=28,
        grid=(1,),
        in_specs=[
            IN_SMEM,
            full((1, SEQ)),
            full((SEQ, 3 * LOCAL)),
            full((LOCAL, SEQ)),
            full((8, SEQ)),
        ]
        + [IN_HBM] * 9,
        out_specs=[full((SEQ, 480)), full((1, 480)), full((SEQ, 160)), ANYWHERE, ANYWHERE],
        out_shape=(
            in_hbm((SEQ, 480), BF16),
            shaped((1, 480), F32),
            in_hbm((SEQ, 160), BF16),
            shaped((HALF, D), BF16),
            shaped((HALF, D), BF16),
        ),
        scratch_shapes=[
            pltpu.VMEM((SEQ, 3 * LOCAL), BF16),
            pltpu.VMEM((SEQ, WIDE), BF16),
            pltpu.SemaphoreType.DMA((8,)),
            pltpu.VMEM((SEQ, HEAD_DIM), F32),
            pltpu.VMEM((SEQ, HEAD_DIM), F32),
        ]
        + weights_of(1)
        + pieces_of(2, 256) * 2,
    )(meta, start, qkv, turned, lse, *pieces, weights)


def normal(v):
    mean = jnp.mean(v, axis=-1, keepdims=True)
    centred = v - mean
    variance = jnp.mean(centred * centred, axis=-1, keepdims=True)
    scale = lax.rsqrt(variance + 1e-05)
    return centred * scale, scale


def four(pieces, held_ref, sems):
    copies = fetch(pieces, held_ref, sems)
    for copy in copies:
        copy.wait()
    a, b, c, d = (held_ref[i * BLOCK : (i + 1) * BLOCK, :].astype(F32) for i in range(4))
    return (a + b) + (c + d)


def send_out(value, held_ref, out, sem):
    held_ref[...] = value
    copy = pltpu.make_async_copy(held_ref, out, sem)
    copy.start()
    return copy


def join_norm_kernel(
    a, b, c, d, old_ref, bias_ref, gain_ref, shift_ref, new_ref, low_ref, *refs
):
    x_ref, sems, y_ref, done, held_ref, held_sems = refs
    old = pltpu.make_async_copy(old_ref, held_ref, held_sems.at[0])
    old.start()
    total = four((a, b, c, d), x_ref, sems)
    old.wait()
    new = held_ref[...] + total + bias_ref[...]
    low = (normal(new)[0] * gain_ref[...] + shift_ref[...]).astype(BF16)
    copy = send_out(low, y_ref, low_ref, done.at[0])
    new_ref[...] = new
    copy.wait()


def join_norm(parts, old, bias, gain, shift, after=()):
    return call(
        join_norm_kernel,
        after=after,
        grid=(1,),
        in_specs=[IN_HBM] * 5 + [full((1, D))] * 3,
        out_specs=[full((BLOCK, D)), ANYWHERE],
        out_shape=(in_hbm((BLOCK, D), F32), in_hbm((BLOCK, D), BF16)),
        scratch_shapes=pieces_of(4) + pieces_of(1) + held_rows(1),
    )(*parts, old, bias, gain, shift)


def join_heads_kernel(turned, meta_ref, *refs):
    pieces, refs = refs[:8], refs[8:]
    w_refs, refs = (refs[:8], refs[8:]) if turned else (refs[:1], refs[1:])
    old_ref, gain_ref, shift_ref, more_ref, new_ref, low_ref, heads_ref, bias_ref = refs[:8]
    slots, sems, ordered, y_ref, done, held_ref, held_sems = refs[8:15]
    *w_held, w_sems = refs[15:17] if turned else refs[15:18]
    old = pltpu.make_async_copy(old_ref, held_ref, held_sems.at[0])
    old.start()
    copies = [
        pltpu.make_async_copy(
            pieces[j].at[pl.ds(j % 2 * BLOCK, BLOCK), :],
            slots.at[meta_ref[FROM_SLOT + j]],
            sems.at[j],
        )
        for j in range(8)
    ]
    for copy in copies:
        copy.start()
    weights = load_halves(meta_ref, w_refs, w_held, w_sems)
    if turned:
        terms_ref, terms_sems = refs[17:]
        for i, ref in enumerate(w_refs):
            at = pl.ds(pl.multiple_of(meta_ref[HELD_SLOT + i] * 160, 160), 160)
            copies.append(
                pltpu.make_async_copy(
                    ref.at[:, pl.ds(D, 128)], terms_ref.at[at, :], terms_sems.at[i]
                )
            )
            copies[-1].start()
    for copy in copies:
        copy.wait()
    if turned:
        terms = terms_ref[...].astype(F32).T
        terms = [
            (terms[l : l + 1] + terms[l + 2 : l + 3]) + terms[l + 4 : l + 5] for l in range(LAYERS)
        ]
        bias_ref[...] = jnp.concatenate(terms + [jnp.zeros((6, D), F32)], axis=0)
        bias = terms[0]
    else:
        bias = more_ref[1:2, :]
        bias_ref[...] = more_ref[...]
    for chip in range(4):
        five = jnp.concatenate([slots[2 * chip], slots[2 * chip + 1]], axis=1)
        for i in range(5):
            ordered[5 * chip + i] = five[:, i * HEAD_DIM : (i + 1) * HEAD_DIM]
    x = jnp.concatenate([ordered[meta_ref[HEAD_OF + r]] for r in range(HEADS)], axis=1)
    product = nt if turned else lambda a, b: jnp.dot(a, b, preferred_element_type=F32)
    for copy in weights:
        copy.wait()
    branch = [product(x, ref[...]) for ref in w_held]
    branch = branch[0] if turned else jnp.concatenate(branch, axis=1)
    old.wait()
    new = held_ref[...] + branch + bias
    low = (normal(new)[0] * gain_ref[...] + shift_ref[...]).astype(BF16)
    if turned:
        y_ref[BLOCK:, :] = more_ref[...]
    y_ref[:BLOCK, :] = low
    copy = pltpu.make_async_copy(y_ref, low_ref, done.at[0])
    copy.start()
    new_ref[...] = new
    heads_ref[...] = x
    copy.wait()


def load_halves(meta_ref, refs, targets, sems):
    if len(refs) == 1:
        return load(refs[0], UNITS, targets, sems)
    copies = []
    for i, ref in enumerate(refs):
        at = pl.ds(pl.multiple_of(meta_ref[HELD_SLOT + i] * 160, 160), 160)
        copies.append(
            pltpu.make_async_copy(ref.at[:, pl.ds(0, D)], targets[0].at[at, :], sems.at[i])
        )
        copies[i].start()
    return copies


def halves_of(turned):
    if turned:
        return [pltpu.VMEM((D, D), BF16), pltpu.SemaphoreType.DMA((8,))]
    return [pltpu.VMEM((D, UNITS), BF16)] * 2 + [pltpu.SemaphoreType.DMA((2,))]


def join_heads(meta, pieces, weights, turned, old, gain, shift, more):
    rows = BLOCK + EXTRA if turned else BLOCK
    return call(
        functools.partial(join_heads_kernel, turned),
        grid=(1,),
        in_specs=[IN_SMEM]
        + [IN_HBM] * (9 + len(weights))
        + [full((1, D))] * 2
        + [full(more.shape)],
        out_specs=[full((BLOCK, D)), ANYWHERE, full((BLOCK, D)), full((8, D))],
        out_shape=(
            in_hbm((BLOCK, D), F32),
            in_hbm((rows, D), BF16),
            in_hbm((BLOCK, D), BF16),
            shaped((8, D), F32),
        ),
        scratch_shapes=[
            pltpu.VMEM((8, BLOCK, 160), BF16),
            pltpu.SemaphoreType.DMA((8,)),
            pltpu.VMEM((HEADS, BLOCK, HEAD_DIM), BF16),
        ]
        + pieces_of(1, rows)
        + held_rows(1)
        + halves_of(turned)
        + ([pltpu.VMEM((D, 128), BF16), pltpu.SemaphoreType.DMA((8,))] if turned else []),
    )(meta, *pieces, *weights, old, gain, shift, more)


def norm_back_math(dy, x, old, gain):
    unit, scale = normal(x)
    slope = dy * gain
    mean_one = jnp.mean(slope, axis=-1, keepdims=True)
    mean_two = jnp.mean(slope * unit, axis=-1, keepdims=True)
    new = old + scale * (slope - mean_one - unit * mean_two)
    sums = jnp.concatenate(
        [
            jnp.sum(dy * unit, axis=0, keepdims=True),
            jnp.sum(dy, axis=0, keepdims=True),
            jnp.sum(new, axis=0, keepdims=True),
            jnp.zeros((5, D), F32),
        ],
        axis=0,
    )
    return new, sums


def hold_rows(refs, targets, sems):
    copies = []
    for i, (ref, target) in enumerate(zip(refs, targets)):
        copies.append(pltpu.make_async_copy(ref, target, sems.at[i]))
        copies[i].start()
    return copies


def norm_back_kernel(
    a, b, c, d, x_ref, old_ref, gain_ref, new_ref, low_ref, sums_ref, token_ref, *refs
):
    mark(token_ref)
    p_ref, sems, y_ref, done, x_held, old_held, held_sems = refs
    held = hold_rows((x_ref, old_ref), (x_held, old_held), held_sems)
    total = four((a, b, c, d), p_ref, sems)
    for copy in held:
        copy.wait()
    new, sums = norm_back_math(total, x_held[...], old_held[...], gain_ref[...])
    copy = send_out(new.astype(BF16), y_ref, low_ref, done.at[0])
    new_ref[...] = new
    sums_ref[...] = sums
    copy.wait()


def finish_kernel(sum_ref, first_ref, old_ref, bias_ref, out_ref):
    out_ref[:BLOCK, :] = first_ref[...].astype(BF16)
    last = old_ref[...] + sum_ref[...].astype(F32) + bias_ref[...]
    out_ref[BLOCK:, :] = last.astype(BF16)


def finish(total, first, old, bias):
    return call(
        finish_kernel,
        [full((BLOCK, D))] * 3 + [full((1, D))],
        light=True,
        grid=(1,),
        out_specs=full((2 * BLOCK, D)),
        out_shape=in_hbm((2 * BLOCK, D), BF16),
    )(total, first, old, bias)


def norm_back(parts, x, old, gain, after):
    return call(
        norm_back_kernel,
        after=after,
        grid=(1,),
        in_specs=[IN_HBM] * 6 + [full((1, D))],
        out_specs=[full((BLOCK, D)), ANYWHERE, full((8, D)), TOKEN],
        out_shape=(
            in_hbm((BLOCK, D), F32),
            in_hbm((BLOCK, D), BF16),
            shaped((8, D), F32),
            TOKEN_SHAPE,
        ),
        scratch_shapes=pieces_of(4) + pieces_of(1) + held_rows(2),
    )(*parts, x, old, gain)


def norm_back_heads_kernel(turned, meta_ref, a, b, c, d, x_ref, old_ref, gain_ref, *refs):
    w_refs, refs = (refs[:8], refs[8:]) if turned else (refs[:1], refs[1:])
    new_ref, low_ref, sums_ref = refs[:3]
    pieces, token_ref, refs = refs[3:7], refs[7], refs[8:]
    slots, sent, ordered, p_ref, sems, y_ref, done, x_held, old_held, held_sems = refs[:10]
    *w_held, w_sems = refs[10:]
    mark(token_ref)
    held = hold_rows((x_ref, old_ref), (x_held, old_held), held_sems)
    total = four((a, b, c, d), p_ref, sems)
    weights = load_halves(meta_ref, w_refs, w_held, w_sems)
    for copy in held:
        copy.wait()
    new, sums = norm_back_math(total, x_held[...], old_held[...], gain_ref[...])
    new_ref[...] = new
    low = new.astype(BF16)
    copies = [send_out(low, y_ref, low_ref, done.at[0])]
    sums_ref[...] = sums
    for copy in weights:
        copy.wait()
    if turned:
        grads = jnp.dot(low, w_held[0][...], preferred_element_type=F32)
    else:
        grads = nt(low[:, :UNITS], w_held[0][...]) + nt(low[:, UNITS:], w_held[1][...])
    for r in range(HEADS):
        ordered[meta_ref[HEAD_OF + r]] = grads[:, r * HEAD_DIM : (r + 1) * HEAD_DIM].astype(BF16)
    for f in range(8):
        h = 5 * (f // 2) + 2 * (f % 2)
        slots[f, :, :LOCAL] = jnp.concatenate([ordered[h + i] for i in range(3)], axis=1)
        slots[f, :, LOCAL:] = low[:, f * 160 : (f + 1) * 160]
    for j in range(8):
        target = pieces[j // 2].at[pl.ds(j % 2 * BLOCK, BLOCK), :]
        copies.append(
            pltpu.make_async_copy(slots.at[meta_ref[TO_SLOT + j]], target, sent.at[j])
        )
        copies[-1].start()
    for copy in copies:
        copy.wait()


def norm_back_heads(meta, parts, x, old, gain, weights, turned, after):
    results = call(
        functools.partial(norm_back_heads_kernel, turned),
        after=after,
        grid=(1,),
        in_specs=[IN_SMEM] + [IN_HBM] * 6 + [full((1, D))] + [IN_HBM] * len(weights),
        out_specs=[full((BLOCK, D)), ANYWHERE, full((8, D))] + [ANYWHERE] * 4 + [TOKEN],
        out_shape=[in_hbm((BLOCK, D), F32), in_hbm((BLOCK, D), BF16), shaped((8, D), F32)]
        + [in_hbm((2 * BLOCK, WIDE), BF16)] * 4
        + [TOKEN_SHAPE],
        scratch_shapes=[
            pltpu.VMEM((8, BLOCK, WIDE), BF16),
            pltpu.SemaphoreType.DMA((8,)),
            pltpu.VMEM((HEADS, BLOCK, HEAD_DIM), BF16),
        ]
        + pieces_of(4)
        + pieces_of(1)
        + held_rows(2)
        + halves_of(turned),
    )(meta, *parts, x, old, gain, *weights)
    return results[0], results[2], results[3:7], results[7]


def on_device(
    stream_in,
    segments,
    head_table,
    query_key_value,
    attention_out,
    expand_weight,
    contract_weight,
    norm_gain,
    norm_bias,
    attention_bias,
    expand_bias,
    contract_bias,
    cotangent,
):
    row = lax.axis_index("row")
    col = lax.axis_index("col")
    core = row % 2
    z = row // 4
    y = col % 4
    x = ((row // 2) % 2) * 2 + col // 4
    first = core == 0
    sequence = z * 4 + x

    to_devices = [(core ^ dc, (y + dy) % 4) for dy, dc in STEPS]
    from_devices = [(core ^ dc, (y - dy) % 4) for dy, dc in STEPS]
    held = [core * 4 + (y - k) % 4 for k in HOPS] + [(1 - core) * 4 + (y - k) % 4 for k in HOPS]
    meta = (
        [core, (core == x % 2).astype(jnp.int32)]
        + [core] * 6
        + [c * 4 + at for c, at in to_devices]
        + [2 * at + c for c, at in to_devices]
        + [c * 4 + at for c, at in from_devices]
        + [2 * at + c for c, at in from_devices]
        + held
    )
    slot_heads = head_table.reshape(-1)
    filled = (slot_heads < HEADS).astype(jnp.int32)
    places24 = jnp.arange(24, dtype=jnp.int32)
    order = jnp.sum(jnp.where(places24[None, :] < places24[:, None], filled[None, :], 0), axis=1)
    head_ids = jnp.arange(HEADS, dtype=jnp.int32)
    ranked = (order[None, :] == head_ids[:, None]) & (slot_heads[None, :] < HEADS)
    head_of_rank = jnp.sum(jnp.where(ranked, slot_heads[None, :], 0), axis=1)
    held_slots = [2 * ((y - k) % 4) + c for c in (core, 1 - core) for k in HOPS]
    meta = jnp.concatenate([jnp.stack(meta), head_of_rank, jnp.stack(held_slots)])
    meta = meta.astype(jnp.int32)

    def spread_core(own, axis=-1):
        half = HEAD_DIM // 2
        low = lax.slice_in_dim(own, 0, half, axis=axis)
        high = lax.slice_in_dim(own, own.shape[axis] - half, own.shape[axis], axis=axis)
        got = send(jnp.where(first, high, low), CORES)
        return jnp.where(
            first,
            jnp.concatenate([own, got], axis=axis),
            jnp.concatenate([got, own], axis=axis),
        )

    packed_a = [
        jnp.concatenate([query_key_value[l, i] for i in range(3)] + [attention_out[l]], axis=1)
        for l in range(LAYERS)
    ]
    packed_b = [
        jnp.concatenate([expand_weight[l], contract_weight[l].T], axis=1) for l in range(LAYERS)
    ]

    def three(value):
        parts = []
        for _ in range(3):
            parts.append(value.astype(BF16))
            value = value - parts[-1].astype(F32)
        return jnp.concatenate(parts, axis=0)

    def added(rows):
        rows = rows.astype(F32).reshape(3, LAYERS, -1)
        return (rows[0] + rows[1]) + rows[2]

    none = jnp.zeros((LAYERS, 160), F32)
    head_bias = jnp.concatenate(
        [attention_bias[:, 0], none, attention_bias[:, 1], attention_bias[:, 2]], axis=1
    )
    packed_a[0] = jnp.concatenate(
        [packed_a[0], three(head_bias), three(expand_bias), jnp.zeros((4, UNITS), BF16)], axis=0
    )
    packed_a[0] = jnp.concatenate(
        [packed_a[0], jnp.pad(attention_out[1], ((0, 16), (0, 0)))], axis=1
    )
    shards = jnp.concatenate(
        [jnp.pad(value, ((0, 16), (0, 0))) for value in packed_b]
        + [packed_a[0], jnp.pad(packed_a[1][:, :480], ((0, 16), (0, 0)))],
        axis=1,
    )
    stream_got = send(stream_in, CORES)
    (shards,) = later((shards,), (stream_got,))
    shards = send(shards, TO_FEATURE)
    def gain_of(l, i):
        return norm_gain[l, i].reshape(1, D), norm_bias[l, i].reshape(1, D)

    normed, stream, token = first_norm(meta, stream_in, stream_got, *gain_of(0, 0))
    (shards,) = later((shards,), (token,))
    moved_a = shards[:, 2 * D : 2 * D + 800]
    moved_heads = shards[:80, 2 * D + 800 :]

    def widen_heads(own):
        return spread_core(own.reshape(-1, 3, 160)).reshape(-1, 3 * LOCAL)

    def widen(moved):
        return jnp.concatenate([widen_heads(moved[:, :480]), moved[:, 480:UNITS]], axis=1)

    def gather_plane(value):
        return lax.all_gather(value, AXES, axis=0, tiled=True, axis_index_groups=PLANES)

    wide_a = widen(moved_a)
    first_a = lax.all_to_all(
        spread_out(wide_a, 80, (token,)), AXES, 0, 0, tiled=True, axis_index_groups=PLANES
    ).reshape(D, 736)

    terms = jnp.pad(wide_a[80:86, 3 * LOCAL :], ((0, 122), (0, 0))).T
    qkv_bias = added(wide_a[80:86, : 3 * LOCAL]).reshape(LAYERS, 1, 3 * LOCAL)
    up_bias = added(moved_a[86:92, :UNITS]).reshape(LAYERS, 1, UNITS)
    block = turn(first_a, terms)
    (moved_first,) = later((shards[:80, :D],), (block,))
    first_b = gather_plane(moved_first)
    wide_late = widen_heads(moved_heads)
    more = moved_a[:80, UNITS:].reshape(8, 10, 160).transpose(1, 0, 2).reshape(10, D)
    more = jnp.pad(more, ((0, EXTRA - 10), (0, 0)))
    step_of_feature = jnp.sum(
        jnp.where(
            jnp.stack([2 * ((y - k) % 4) + c for c in (core, 1 - core) for k in HOPS])[None, :]
            == jnp.arange(8)[:, None],
            jnp.arange(8)[None, :],
            0,
        ),
        axis=1,
    )

    w_in = [(first_a, 0)]
    w_units = [first_b]

    def exchange(pieces):
        near = [send(piece, along_y(k)) if k else piece for piece, k in zip(pieces, HOPS)]
        return [value for piece in near for value in (piece, send(piece, CORES))]

    def gather_pieces(block):
        near = [block] + [send(block, along_y(k)) for k in HOPS[1:]]
        return near + [send(value, CORES) for value in near]

    seg = lax.dynamic_slice_in_dim(segments, sequence * SEQ, SEQ)
    start = jnp.sum((seg[:, None] < seg[None, :]).astype(jnp.int32), axis=0, keepdims=True)
    def gather_tokens(value):
        return lax.all_gather(value, AXES, axis=0, tiled=True, axis_index_groups=BY_TOKEN)

    def sum_parts(far, near, after=()):
        *parts, token = add_cores(near, send(far, CORES), after)
        return [send(part, along_y(-k)) if k else part for part, k in zip(parts, HOPS)], token

    def scatter_plane(value):
        return lax.psum_scatter(
            value, AXES, scatter_dimension=0, tiled=True, axis_index_groups=PLANES
        )

    def to_result(value, until=()):
        value = send(value, HOME)
        if until:
            (value,) = later((value,), until)
        layers = value.shape[0] // BLOCK
        blocks = jnp.moveaxis(value.reshape(layers, BLOCK, 8, 160), 2, 0)
        blocks = lax.all_to_all(blocks, "col", 0, 0, tiled=True)
        return jnp.moveaxis(blocks, 0, 1).reshape(layers, SEQ, 160)

    grad_held, grad, grad_sum, held_token = hold_grads(meta, cotangent, send(cotangent, CORES))
    pieces = None
    kept = []
    for l in range(LAYERS):
        first_layer = l == 0
        if first_layer:
            qkv = project_first(normed, first_a, qkv_bias[l])
            turned_out = [block] + [send(block, along_y(k)) for k in HOPS[1:]]
            pieces, turned, lse, token = attend_forward(meta, start, qkv)
        else:
            qkv, normed, pieces, turned, lse = project_attend(
                meta, pieces, *w_in[l], qkv_bias[l], start
            )
        pieces = exchange(pieces)
        if first_layer:
            turned_out = later(turned_out, (pieces[1],))
            turned_out = [*turned_out] + [send(value, CORES) for value in turned_out]
        if first_layer:
            w_heads = turned_out
        else:
            w_heads = [late]
        gain, shift = gain_of(l, 1)
        mid, low, heads, more = join_heads(
            meta, pieces, w_heads, first_layer, stream, gain, shift, more
        )
        pieces = gather_pieces(low)
        if first_layer:
            rows = gathered_rows(step_of_feature.astype(jnp.int32), pieces, wide_late)
            late = gather_plane(rows)
            w_in.append((late, 0))
            (moved_units,) = later((shards[:80, D : 2 * D],), (rows,))
            w_units.append(gather_plane(moved_units))
        bias = contract_bias[l].reshape(1, D)
        state = (stream, mid, normed, pieces, w_heads, qkv, turned, lse, heads)
        if first_layer:
            far = up_down(pieces[4:], w_units[l], up_bias[l])
            near = up_down(pieces[:4], w_units[l], up_bias[l])
            kept.append(state + (far, near))
            parts, _ = sum_parts(far[2], near[2])
            gain, shift = gain_of(l + 1, 0)
            stream, low = join_norm(parts, mid, bias, gain, shift, (held_token,))
            pieces = gather_pieces(low)
        else:
            both_heads = jnp.concatenate([kept[0][8], heads], axis=0)
            (both_heads,) = later((both_heads,), (pieces[1], pieces[2], pieces[3]))
            all_heads = gather_tokens(both_heads)
            far = up_down_both(meta, pieces[4:], grad_held, 4, w_units[l], up_bias[l])
            near = up_down_both(meta, pieces[:4], grad_held, 0, w_units[l], up_bias[l], far[4])
            kept.append(state + (far, near))
            last = (near[4], mid, bias)

    grad_pieces = None
    wide_sums = [None] * LAYERS
    plane_sums = [None] * LAYERS
    for l in reversed(range(LAYERS)):
        stream, mid, normed, pieces, w_heads, qkv, turned, lse, _, far, near = kept[l]
        if l:
            act_far, low_far, sum_far, back_far, _ = far
            act_near, low_near, sum_near, back_near, _ = near
        else:
            low_far, sum_far, back_far = up_down_back(grad_pieces[4:], w_units[l], far[0])
            low_near, sum_near, back_near = up_down_back(grad_pieces[:4], w_units[l], near[0])
            act_far, act_near = far[1], near[1]
        parts, token = sum_parts(back_far, back_near)
        units, token = unit_grads(
            pieces,
            (low_near, low_far),
            (grad_held,) if l else grad_pieces,
            (act_near, act_far),
            (token, all_heads) if l else (token, last_rows),
            None if l else heads,
        )
        mid_grad, sums_two, pieces, token = norm_back_heads(
            meta,
            parts,
            mid,
            grad,
            gain_of(l, 1)[0],
            w_heads,
            l == 0,
            (token,) if l else (token, units_one),
        )
        if l:
            last_sum, last_mid, last_bias = last
            units, last_sum = later((units, last_sum), (token,))
            last_sum = lax.psum_scatter(
                last_sum, AXES, scatter_dimension=0, tiled=True, axis_index_groups=BY_TOKEN
            )
            last_rows = finish(last_sum, stream, last_mid, last_bias)
            units_one = scatter_plane(units)
        else:
            (units,) = later((units,), (token,))
            units_both = scatter_plane(units)
        grad_own, qkv_sum, mid_all, back_far, back_near = attend_project_back(
            meta, start, qkv, turned, lse, exchange(pieces), *w_in[l]
        )
        parts, token = sum_parts(back_far, back_near)
        heads, token = head_grads(normed, grad_own, all_heads, mid_all, l, (token,))
        grad_new, next_low, sums_one, token = norm_back(
            parts, stream, mid_grad, gain_of(l, 0)[0], (token,)
        )
        wide_sums[l] = jnp.concatenate([sums_one[:2], sums_two[:3], grad_sum], axis=0)
        plane_sums[l] = jnp.concatenate(
            [
                qkv_sum[:, :160],
                qkv_sum[:, 320:],
                sum_far + sum_near,
                jnp.zeros((1, D - 960), F32),
            ],
            axis=1,
        )
        if l:
            grad_sum = sums_one[2:3]
            grad_pieces = gather_pieces(next_low)
        grad = grad_new
    heads_zero = lax.all_to_all(
        heads.reshape(16, 80, UNITS), AXES, 0, 0, tiled=True, axis_index_groups=PLANES
    )
    heads_added = jnp.sum(heads_zero.astype(F32), axis=0).astype(BF16)
    grad_stream = to_result(grad, (heads_zero,))[0]

    activations = to_result(last_rows)

    back = jnp.concatenate([units_one, units_both, heads_added], axis=1)
    back = send(back, FROM_FEATURE)
    units_one, units_both = back[:, : 2 * UNITS], back[:, 2 * UNITS : 4 * UNITS]
    heads_one, heads_zero = back[:, 4 * UNITS : 5 * UNITS], back[:, 5 * UNITS + 128 :]
    unit_back = jnp.stack([units_both, units_one]).astype(F32)
    head_back = jnp.stack([heads_zero, heads_one]).astype(F32)
    grad_query_key_value = head_back[:, :, :480].reshape(LAYERS, 80, 3, 160).transpose(0, 2, 1, 3)
    grad_attention_out = head_back[:, :, 480:]
    grad_expand = unit_back[:, :, :UNITS]
    grad_contract = unit_back[:, :, UNITS:].transpose(0, 2, 1)

    def sum_four(value, perms):
        one, two, three = (send(value, perm) for perm in perms)
        return (value + two) + (one + three)

    wide = jnp.concatenate(wide_sums, axis=0)
    wide = sum_four(wide + send(wide, CORES), [along_y(k) for k in (1, 2, 3)])
    sums = jnp.concatenate([wide] + plane_sums, axis=0)
    sums = sum_four(sums, [along_plane(0, k) for k in (1, 2, 3)])
    sums = sum_four(sums, [along_plane(k, 0) for k in (1, 2, 3)])
    wide = sums[:12].reshape(LAYERS, 6, D)
    plane = send(sums[12:], FROM_FEATURE)
    grad_norm_gain = jnp.stack([wide[:, 0], wide[:, 2]], axis=1)
    grad_norm_bias = jnp.stack([wide[:, 1], wide[:, 3]], axis=1)
    out_sums = lax.dynamic_slice_in_dim(wide[:, 4], col * 160, 160, 1)
    grad_attention_bias = jnp.stack([plane[:, :160], plane[:, 160:320], out_sums], axis=1)
    grad_expand_bias = plane[:, 320:960]
    grad_contract_bias = wide[:, 5]
    return (
        activations,
        grad_stream,
        grad_query_key_value,
        grad_attention_out,
        grad_expand,
        grad_contract,
        grad_norm_gain,
        grad_norm_bias,
        grad_attention_bias,
        grad_expand_bias,
        grad_contract_bias,
    )


def solution(mesh):
    placed = (
        P("row", None),
        P(),
        P(),
        P(None, None, "row", "col"),
        P(None, "row", "col"),
        P(None, "row", "col"),
        P(None, "col", "row"),
        P(),
        P(),
        P(None, None, "col"),
        P(None, "col"),
        P(),
        P("row", None),
    )
    return jax.shard_map(
        on_device,
        mesh=mesh,
        in_specs=placed,
        out_specs=(
            P(None, "row", "col"),
            P("row", "col"),
            P(None, None, "row", "col"),
            P(None, "row", "col"),
            P(None, "row", "col"),
            P(None, "col", "row"),
            P(),
            P(),
            P(None, None, "col"),
            P(None, "col"),
            P(),
        ),
        check_vma=False,
    )
```

```python
import functools

import jax
import jax.numpy as jnp
from jax import lax
from jax.experimental import pallas as pl
from jax.experimental.pallas import tpu as pltpu
from jax.sharding import PartitionSpec as P

D = 1280
HEADS = 20
HEAD_DIM = 64
SEQ = 1024
LAYERS = 2
BLOCK = 128
LOCAL = 3 * HEAD_DIM
SCALE = HEAD_DIM ** (-0.5)
AXES = ("row", "col")
BF16 = jnp.bfloat16
F32 = jnp.float32
MIB = 1024 * 1024


def device(z, x, core, y):
    return (z * 4 + (x // 2) * 2 + core) * 8 + (x % 2) * 4 + y


def pairs(target):
    out = []
    for z in range(4):
        for x in range(4):
            for core in range(2):
                for y in range(4):
                    out.append((device(z, x, core, y), device(*target(z, x, core, y))))
    return out


def along_y(k):
    return pairs(lambda z, x, core, y: (z, x, core, (y + k) % 4))


def along_plane(dz, dx):
    return pairs(lambda z, x, core, y: ((z + dz) % 4, (x + dx) % 4, core, y))


def to_feature(z, x, core, y):
    block = (x % 2) * 4 + y
    return (z, (x // 2) * 2 + core, block % 2, block // 2)


CORES = pairs(lambda z, x, core, y: (z, x, 1 - core, y))
TO_FEATURE = pairs(to_feature)
FROM_FEATURE = [(b, a) for a, b in TO_FEATURE]
HOME = pairs(lambda z, x, core, y: (z, (x // 2) * 2 + core, x % 2, y))
PLANES = [
    [device(z, x, core, y) for z in range(4) for x in range(4)]
    for y in range(4)
    for core in range(2)
]
BY_FEATURE = [
    [device(z, x, core, y) for y in range(4) for core in range(2)]
    for z in range(4)
    for x in range(4)
]
BY_TOKEN = [
    [device(z, x, core, y) for core in range(2) for y in range(4)]
    for z in range(4)
    for x in range(4)
]
STEPS = [(dy, dc) for dy in (0, 1, 3, 2) for dc in (0, 1)]
HOPS = (0, 1, 3, 2)


NAMES = {tuple(CORES): "cores", tuple(TO_FEATURE): "to_feature", tuple(FROM_FEATURE): "from_feature"}


def send(value, perm):
    with jax.named_scope("send_" + NAMES.get(tuple(perm), "far")):
        return lax.ppermute(value, AXES, perm)


CORE, SAME, TO_BLOCK, TO_SLOT, FROM_BLOCK, FROM_SLOT, HELD, HEAD_OF = 0, 1, 8, 16, 24, 32, 40, 48
HELD_SLOT = HEAD_OF + HEADS
IN_SMEM = pl.BlockSpec(memory_space=pltpu.SMEM)
ANYWHERE = pl.BlockSpec(memory_space=pl.ANY)
IN_HBM = pl.BlockSpec(memory_space=pltpu.HBM)


LIGHT = pl.CostEstimate(flops=1000, bytes_accessed=1000, transcendentals=0)


def call(kernel, in_specs, limit=16, after=(), light=False, aliases=None, **kwargs):
    count = len(after)

    def waiting(*refs):
        kernel(*refs[count:])

    specs = [IN_HBM] * count + list(in_specs)
    run = pl.pallas_call(
        waiting,
        in_specs=specs,
        compiler_params=pltpu.CompilerParams(vmem_limit_bytes=limit * MIB),
        cost_estimate=LIGHT if light else None,
        input_output_aliases={count + i: out for i, out in (aliases or {}).items()},
        **kwargs,
    )
    label = getattr(kernel, "func", kernel).__name__

    def named(*operands):
        with jax.named_scope(label):
            placed = [
                pltpu.with_memory_space_constraint(value, pltpu.HBM) if spec is IN_HBM else value
                for value, spec in zip((*after, *operands), specs)
            ]
            return run(*placed)

    return named


def shaped(shape, dtype):
    return jax.ShapeDtypeStruct(shape, dtype)


def in_hbm(shape, dtype):
    return pltpu.HBM(shape, dtype)


def full(shape):
    return pl.BlockSpec(shape, lambda i: (0,) * len(shape))


TOKEN = full((8, 128))
TOKEN_SHAPE = in_hbm((8, 128), F32)


def mark(token_ref):
    token_ref[...] = jnp.zeros((8, 128), F32)


def fetch(pieces, target, sems):
    rows = target.shape[0] // len(pieces)
    copies = []
    for i, piece in enumerate(pieces):
        copies.append(
            pltpu.make_async_copy(
                piece.at[pl.ds(0, rows), :], target.at[pl.ds(i * rows, rows), :], sems.at[i]
            )
        )
    for copy in copies:
        copy.start()
    return copies


def load(ref, columns, targets, sems, rows=None):
    copies = []
    for i, target in enumerate(targets):
        width = target.shape[1]
        at = pl.ds(columns + i * width, width)
        copies.append(pltpu.make_async_copy(ref.at[:, at], target, sems.at[i]))
        copies[i].start()
    return copies


def held_rows(count):
    return [pltpu.VMEM((BLOCK, D), F32)] * count + [pltpu.SemaphoreType.DMA((count,))]


def weights_of(count):
    return [pltpu.VMEM((D, UNITS), BF16)] * count + [pltpu.SemaphoreType.DMA((count,))]


UNITS = 640


def pieces_of(count, rows=BLOCK, columns=D):
    return [pltpu.VMEM((count * rows, columns), BF16), pltpu.SemaphoreType.DMA((count,))]


def take_in(meta_ref, own_ref, got_ref, copies_of):
    for flag, ref in ((1, own_ref), (0, got_ref)):

        @pl.when(meta_ref[SAME] == flag)
        def _():
            copies = copies_of(ref)
            for copy in copies:
                copy.start()
            for copy in copies:
                copy.wait()


def hold_grads_kernel(meta_ref, own_ref, got_ref, held_ref, first_ref, sum_ref, token_ref, sems):
    def copies_of(ref):
        return [
            pltpu.make_async_copy(
                ref.at[rows_at(meta_ref, HELD + i), :],
                held_ref.at[pl.ds(i * BLOCK, BLOCK), :],
                sems.at[i],
            )
            for i in range(8)
        ]

    take_in(meta_ref, own_ref, got_ref, copies_of)
    first = held_ref[:BLOCK, :].astype(F32)
    first_ref[...] = first
    sum_ref[...] = jnp.sum(first, axis=0, keepdims=True)
    mark(token_ref)


def hold_grads(meta, own, got):
    return call(
        hold_grads_kernel,
        [IN_SMEM, IN_HBM, IN_HBM],
        light=True,
        grid=(1,),
        out_specs=[full((SEQ, D)), full((BLOCK, D)), full((1, D)), TOKEN],
        out_shape=(
            in_hbm((SEQ, D), BF16),
            in_hbm((BLOCK, D), F32),
            shaped((1, D), F32),
            TOKEN_SHAPE,
        ),
        scratch_shapes=[pltpu.SemaphoreType.DMA((8,))],
    )(meta, own, got)


def first_norm_kernel(
    meta_ref, own_ref, got_ref, gain_ref, shift_ref, normed_ref, first_ref, token_ref, x_ref, sems
):
    def copies_of(ref):
        return [
            pltpu.make_async_copy(ref.at[pl.ds(i * 256, 256), :], x_ref.at[pl.ds(i * 256, 256), :], sems.at[i])
            for i in range(4)
        ]

    take_in(meta_ref, own_ref, got_ref, copies_of)
    for i in range(4):
        at = pl.ds(i * 256, 256)
        unit = normal(x_ref[at, :].astype(F32))[0]
        normed_ref[at, :] = (unit * gain_ref[...] + shift_ref[...]).astype(BF16)
    first_ref[...] = x_ref[rows_at(meta_ref, HELD), :].astype(F32)
    mark(token_ref)


def first_norm(meta, own, got, gain, shift):
    return call(
        first_norm_kernel,
        [IN_SMEM, IN_HBM, IN_HBM, full((1, D)), full((1, D))],
        grid=(1,),
        out_specs=[full((SEQ, D)), full((BLOCK, D)), TOKEN],
        out_shape=(in_hbm((SEQ, D), BF16), in_hbm((BLOCK, D), F32), TOKEN_SHAPE),
        scratch_shapes=pieces_of(4, 256),
    )(meta, own, got, gain, shift)


def later(values, after):
    count = len(values)

    def later_kernel(*refs):
        pass

    return call(
        later_kernel,
        [IN_HBM] * count,
        after=after,
        out_specs=[IN_HBM] * count,
        out_shape=[in_hbm(value.shape, value.dtype) for value in values],
        aliases={i: i for i in range(count)},
    )(*values)


def spread_out(value, rows, after):
    def spread_out_kernel(value_ref, out_ref):
        for i in range(16):
            out_ref[i] = value_ref[:rows, :]

    shape = (16, rows, value.shape[1])
    return call(
        spread_out_kernel,
        [full(value.shape)],
        grid=(1,),
        out_specs=full(shape),
        out_shape=in_hbm(shape, value.dtype),
        after=after,
    )(value)


def rows_at(meta_ref, index):
    return pl.ds(pl.multiple_of(meta_ref[index] * BLOCK, BLOCK), BLOCK)


def nt(a, b):
    return lax.dot_general(a, b, (((1,), (1,)), ((), ())), preferred_element_type=F32)


def tn(a, b):
    return lax.dot_general(a, b, (((0,), (0,)), ((), ())), preferred_element_type=F32)


QB = 256


def allowed_at(start_ref, at, keys):
    key = lax.broadcasted_iota(jnp.int32, (keys, QB), 0)
    query = lax.broadcasted_iota(jnp.int32, (keys, QB), 1) + at
    return (key >= start_ref[:, at : at + QB]) & (key <= query)


def attend_forward_kernel(meta_ref, start_ref, qkv_ref, *refs):
    pieces = refs[:4]
    turned_ref, lse_ref, token_ref, own_ref, sems = refs[4:]
    mark(token_ref)
    heads = []
    for h in range(3):
        lo = h * HEAD_DIM
        q = qkv_ref[:, lo : lo + HEAD_DIM] * jnp.asarray(SCALE, BF16)
        k = qkv_ref[:, LOCAL + lo : LOCAL + lo + HEAD_DIM]
        v = qkv_ref[:, 2 * LOCAL + lo : 2 * LOCAL + lo + HEAD_DIM]
        heads.append((q, k, v.astype(F32).T.astype(BF16)))
    for block in range(SEQ // QB):
        at = block * QB
        keys = at + QB
        allowed = allowed_at(start_ref, at, keys)
        parts = []
        for h, (q, k, vt) in enumerate(heads):
            scores = nt(k[:keys], q[at : at + QB])
            scores = jnp.where(allowed, scores, -1e30)
            top = jnp.max(scores, axis=0, keepdims=True)
            weights = jnp.exp(scores - top)
            total = jnp.sum(weights, axis=0, keepdims=True)
            turned = (
                jnp.dot(vt[:, :keys], weights.astype(BF16), preferred_element_type=F32) / total
            )
            lse_ref[h : h + 1, at : at + QB] = top + jnp.log(total)
            turned_ref[h * HEAD_DIM : (h + 1) * HEAD_DIM, at : at + QB] = turned
            parts.append(turned)
        out = jnp.concatenate(parts, axis=0).T.astype(BF16)
        own_ref[at : at + QB, :] = jnp.where(meta_ref[CORE] == 0, out[:, :160], out[:, 32:])
    copies = [
        pltpu.make_async_copy(
            own_ref.at[rows_at(meta_ref, TO_BLOCK + j), :],
            pieces[j // 2].at[pl.ds(j % 2 * BLOCK, BLOCK), :],
            sems.at[j],
        )
        for j in range(8)
    ]
    for copy in copies:
        copy.start()
    for copy in copies:
        copy.wait()


def attend_forward(meta, start, qkv):
    results = call(
        attend_forward_kernel,
        grid=(1,),
        in_specs=[IN_SMEM, full((1, SEQ)), full((SEQ, 3 * LOCAL))],
        out_specs=[ANYWHERE] * 4
        + [full((LOCAL, SEQ)), full((8, SEQ)), TOKEN],
        out_shape=[in_hbm((2 * BLOCK, 160), BF16)] * 4
        + [shaped((LOCAL, SEQ), F32), shaped((8, SEQ), F32), TOKEN_SHAPE],
        scratch_shapes=[pltpu.VMEM((SEQ, 160), BF16), pltpu.SemaphoreType.DMA((8,))],
    )(meta, start, qkv)
    return results[:4], results[4], results[5], results[6]


WIDE = LOCAL + 160


def attend_backward_kernel(meta_ref, start_ref, qkv_ref, turned_ref, lse_ref, *refs):
    pieces = refs[:8]
    out_ref, own_ref, sum_ref, mid_ref, grad_ref, sems, dk_ref, dv_ref = refs[8:]
    copies = [
        pltpu.make_async_copy(
            pieces[j].at[pl.ds(j % 2 * BLOCK, BLOCK), :],
            grad_ref.at[rows_at(meta_ref, FROM_BLOCK + j), :],
            sems.at[j],
        )
        for j in range(8)
    ]
    for copy in copies:
        copy.start()
    for copy in copies:
        copy.wait()
    mid_ref[...] = grad_ref[:, LOCAL:]
    for h in range(3):
        lo = h * HEAD_DIM
        q = qkv_ref[:, lo : lo + HEAD_DIM] * jnp.asarray(SCALE, BF16)
        k = qkv_ref[:, LOCAL + lo : LOCAL + lo + HEAD_DIM]
        v = qkv_ref[:, 2 * LOCAL + lo : 2 * LOCAL + lo + HEAD_DIM]
        g = grad_ref[:, lo : lo + HEAD_DIM]
        kt = k.astype(F32).T.astype(BF16)
        delta = jnp.sum(
            g.astype(F32).T * turned_ref[lo : lo + HEAD_DIM, :], axis=0, keepdims=True
        )
        for block in reversed(range(SEQ // QB)):
            at = block * QB
            keys = at + QB
            allowed = allowed_at(start_ref, at, keys)
            q_part, g_part = q[at : at + QB], g[at : at + QB]
            scores = nt(k[:keys], q_part)
            probs = jnp.where(
                allowed, jnp.exp(scores - lse_ref[h : h + 1, at : at + QB]), 0.0
            )
            grad_probs = nt(v[:keys], g_part)
            grad_scores = (probs * (grad_probs - delta[:, at : at + QB])).astype(BF16)
            dv = jnp.dot(probs.astype(BF16), g_part, preferred_element_type=F32)
            dk = jnp.dot(grad_scores, q_part, preferred_element_type=F32)
            dq = jnp.dot(kt[:, :keys], grad_scores, preferred_element_type=F32) * SCALE
            out_ref[at : at + QB, lo : lo + HEAD_DIM] = dq.T.astype(BF16)
            if keys == SEQ:
                dk_ref[...] = dk
                dv_ref[...] = dv
            else:
                dk_ref[:keys, :] += dk
                dv_ref[:keys, :] += dv
        out_ref[:, LOCAL + lo : LOCAL + lo + HEAD_DIM] = dk_ref[...].astype(BF16)
        out_ref[:, 2 * LOCAL + lo : 2 * LOCAL + lo + HEAD_DIM] = dv_ref[...].astype(BF16)
    for i in range(3):
        part = out_ref[:, i * LOCAL : (i + 1) * LOCAL]
        own = jnp.where(meta_ref[CORE] == 0, part[:, :160], part[:, 32:])
        own_ref[:, i * 160 : (i + 1) * 160] = own
        sum_ref[:, i * 160 : (i + 1) * 160] = jnp.sum(own.astype(F32), axis=0, keepdims=True)


def gelu(v):
    inner = 0.7978845608028654 * (v + 0.044715 * v * v * v)
    return 0.5 * v * (1.0 + jnp.tanh(inner))


def gelu_slope(v):
    t = jnp.tanh(0.7978845608028654 * (v + 0.044715 * v * v * v))
    return 0.5 * (1.0 + t) + 0.5 * v * (1.0 - t * t) * 0.7978845608028654 * (
        1.0 + 3 * 0.044715 * v * v
    )


HALF = 512
def up_down_kernel(
    a, b, c, d, w_ref, bias_ref, hidden_ref, act_ref, out_ref, *refs
):
    x_ref, sems, y_ref, done, up_ref, down_ref, w_sems = refs
    copies = fetch((a, b, c, d), x_ref, sems)
    weights = load(w_ref, 0, (up_ref, down_ref), w_sems)
    outs = []
    for i in range(2):
        at = pl.ds(i * 256, 256)
        copies[2 * i].wait()
        copies[2 * i + 1].wait()
        if not i:
            weights[0].wait()
        hidden = jnp.dot(x_ref[at, :], up_ref[...], preferred_element_type=F32) + bias_ref[...]
        hidden_ref[at, :] = hidden
        act = gelu(hidden).astype(BF16)
        act_ref[at, :] = act
        if not i:
            weights[1].wait()
        y_ref[at, :] = nt(act, down_ref[...]).astype(BF16)
        outs.append(pltpu.make_async_copy(y_ref.at[at, :], out_ref.at[at, :], done.at[i]))
        outs[i].start()
    for copy in outs:
        copy.wait()


def up_down(pieces, weights, bias):
    return call(
        up_down_kernel,
        grid=(1,),
        in_specs=[IN_HBM] * 5 + [full((1, UNITS))],
        out_specs=[full((HALF, UNITS)), full((HALF, UNITS)), ANYWHERE],
        scratch_shapes=pieces_of(4) + pieces_of(2, 256) + weights_of(2),
        out_shape=(
            in_hbm((HALF, UNITS), F32),
            in_hbm((HALF, UNITS), BF16),
            shaped((HALF, D), BF16),
        ),
    )(*pieces, weights, bias)


def up_down_back_kernel(a, b, c, d, w_ref, hidden_ref, low_ref, sum_ref, out_ref, *refs):
    g_ref, sems, y_ref, done, down_ref, up_ref, w_sems, kept_ref, kept_sems = refs
    copies = fetch((a, b, c, d), g_ref, sems)
    kept = pltpu.make_async_copy(hidden_ref, kept_ref, kept_sems.at[0])
    kept.start()
    weights = load(w_ref, UNITS, (down_ref,), w_sems)
    weights.append(pltpu.make_async_copy(w_ref.at[:, pl.ds(0, UNITS)], up_ref, w_sems.at[1]))
    weights[1].start()
    outs = []
    total = jnp.zeros((1, UNITS), F32)
    for i in range(2):
        at = pl.ds(i * 256, 256)
        copies[2 * i].wait()
        copies[2 * i + 1].wait()
        if not i:
            weights[0].wait()
            kept.wait()
        grad = jnp.dot(g_ref[at, :], down_ref[...], preferred_element_type=F32)
        grad = grad * gelu_slope(kept_ref[at, :])
        total += jnp.sum(grad, axis=0, keepdims=True)
        low = grad.astype(BF16)
        low_ref[at, :] = low
        if not i:
            weights[1].wait()
        y_ref[at, :] = nt(low, up_ref[...]).astype(BF16)
        outs.append(pltpu.make_async_copy(y_ref.at[at, :], out_ref.at[at, :], done.at[i]))
        outs[i].start()
    sum_ref[...] = total
    for copy in outs:
        copy.wait()


def up_down_back(pieces, weights, hidden):
    return call(
        up_down_back_kernel,
        grid=(1,),
        in_specs=[IN_HBM] * 4 + [ANYWHERE, IN_HBM],
        out_specs=[full((HALF, UNITS)), full((1, UNITS)), ANYWHERE],
        scratch_shapes=pieces_of(4)
        + pieces_of(2, 256)
        + weights_of(2)
        + [pltpu.VMEM((HALF, UNITS), F32), pltpu.SemaphoreType.DMA((1,))],
        out_shape=(
            in_hbm((HALF, UNITS), BF16),
            shaped((1, UNITS), F32),
            shaped((HALF, D), BF16),
        ),
    )(*pieces, weights, hidden)


def up_down_both_kernel(first, meta_ref, a, b, c, d, grad_ref, w_ref, bias_ref, *refs):
    if not first:
        refs = refs[1:]
    act_ref, low_ref, sum_ref, back_ref, out_ref = refs[:5]
    x_ref, sems, g_ref, g_sems, back, back_done, out, out_done = refs[5:13]
    up_ref, down_ref, w_sems = refs[13:]
    copies = fetch((a, b, c, d), x_ref, sems)
    weights = load(w_ref, 0, (up_ref, down_ref), w_sems)
    grads = [grad_ref.at[pl.ds((first + 2 * i) * BLOCK, 256), :] for i in range(2)]
    grads = fetch(grads, g_ref, g_sems)
    total = jnp.zeros((1, UNITS), F32)
    done = []
    for i in range(2):
        at = pl.ds(i * 256, 256)
        copies[2 * i].wait()
        copies[2 * i + 1].wait()
        grads[i].wait()
        if not i:
            weights[0].wait()
        hidden = jnp.dot(x_ref[at, :], up_ref[...], preferred_element_type=F32) + bias_ref[...]
        act = gelu(hidden).astype(BF16)
        act_ref[at, :] = act
        if not i:
            weights[1].wait()
        grad = jnp.dot(g_ref[at, :], down_ref[...], preferred_element_type=F32)
        grad = grad * gelu_slope(hidden)
        total += jnp.sum(grad, axis=0, keepdims=True)
        low = grad.astype(BF16)
        low_ref[at, :] = low
        back[at, :] = nt(low, up_ref[...]).astype(BF16)
        done.append(pltpu.make_async_copy(back.at[at, :], back_ref.at[at, :], back_done.at[i]))
        done[-1].start()
        out[at, :] = nt(act, down_ref[...]).astype(BF16)
        for k in range(2 * i, 2 * i + 2):
            rows = rows_at(meta_ref, HELD + first + k)
            done.append(
                pltpu.make_async_copy(
                    out.at[pl.ds(k * BLOCK, BLOCK), :], out_ref.at[rows, :], out_done.at[k]
                )
            )
            done[-1].start()
    sum_ref[...] = total
    for copy in done:
        copy.wait()


def up_down_both(meta, pieces, grads, first, weights, bias, outs=None):
    extra = [] if outs is None else [outs]
    return call(
        functools.partial(up_down_both_kernel, first),
        [IN_SMEM] + [IN_HBM] * 6 + [full((1, UNITS))] + [IN_HBM] * len(extra),
        aliases={8: 4} if extra else None,
        grid=(1,),
        out_specs=[full((HALF, UNITS)), full((HALF, UNITS)), full((1, UNITS)), ANYWHERE, ANYWHERE],
        out_shape=(
            in_hbm((HALF, UNITS), BF16),
            in_hbm((HALF, UNITS), BF16),
            shaped((1, UNITS), F32),
            shaped((HALF, D), BF16),
            in_hbm((SEQ, D), BF16),
        ),
        scratch_shapes=pieces_of(4)
        + pieces_of(2, 256) * 2
        + pieces_of(4)
        + weights_of(2),
    )(meta, *pieces, grads, weights, bias, *extra)


def unit_grads_kernel(x_count, g_count, extra, *refs):
    xs, gs = refs[:x_count], refs[x_count : x_count + g_count]
    halves = refs[x_count + g_count : x_count + g_count + 4]
    refs = refs[x_count + g_count + 4 :]
    if extra:
        heads_ref, refs = refs[0], refs[1:]
    out_ref, token_ref, x_ref, x_sems, g_ref, g_sems, low_ref, low_sems, act_ref, act_sems = refs[:10]
    if extra:
        rest = pltpu.make_async_copy(
            heads_ref, out_ref.at[:, pl.ds(2 * UNITS, UNITS)], refs[10].at[0]
        )
        rest.start()
    ups = fetch(xs, x_ref, x_sems) + fetch(halves[:2], low_ref, low_sems)
    downs = fetch(gs, g_ref, g_sems) + fetch(halves[2:], act_ref, act_sems)
    for copies, left, right, column in (
        (ups, x_ref, low_ref, 0),
        (downs, g_ref, act_ref, UNITS),
    ):
        for copy in copies:
            copy.wait()
        for t in range(5):
            at = pl.ds(t * 256, 256)
            out_ref[at, column : column + UNITS] = tn(left[:, at], right[...]).astype(BF16)
    if extra:
        out_ref[:, 3 * UNITS :] = jnp.zeros((D, 128), BF16)
        rest.wait()
    mark(token_ref)


def unit_grads(pieces, lows, grads, acts, after, heads=None):
    extra = [] if heads is None else [heads]
    columns = 2 * UNITS + (UNITS + 128 if extra else 0)
    return call(
        functools.partial(unit_grads_kernel, len(pieces), len(grads), bool(extra)),
        [IN_HBM] * (len(pieces) + len(grads) + 4 + len(extra)),
        limit=28,
        after=after,
        light=True,
        grid=(1,),
        out_specs=[full((D, columns)), TOKEN],
        out_shape=(in_hbm((D, columns), BF16), TOKEN_SHAPE),
        scratch_shapes=pieces_of(len(pieces), SEQ // len(pieces))
        + pieces_of(len(grads), SEQ // len(grads))
        + pieces_of(2, HALF, UNITS) * 2
        + [pltpu.SemaphoreType.DMA((1,))],
    )(*pieces, *grads, *lows, *acts, *extra)


def head_grads_kernel(layer, *refs):
    ins, (out_ref, token_ref), refs = refs[:4], refs[4:6], refs[6:]
    held, sems = refs[:4], refs[4]
    copies = [pltpu.make_async_copy(ins[i], held[i], sems.at[i]) for i in (0, 1, 3)]
    for d in range(8):
        copies.append(
            pltpu.make_async_copy(
                ins[2].at[pl.ds((LAYERS * d + layer) * BLOCK, BLOCK), :],
                held[2].at[pl.ds(d * BLOCK, BLOCK), :],
                sems.at[4 + d],
            )
        )
    for copy in copies:
        copy.start()
    for copy in copies:
        copy.wait()
    normed_ref, own_ref, heads_ref, mid_ref = held
    for t in range(5):
        at = pl.ds(t * 256, 256)
        one = tn(normed_ref[:, at], own_ref[...]).astype(BF16)
        two = tn(heads_ref[:, at], mid_ref[...]).astype(BF16)
        out_ref[at, :] = jnp.concatenate([one, two], axis=1)
    mark(token_ref)


def head_grads(normed, own, heads, mid, layer, after):
    return call(
        functools.partial(head_grads_kernel, layer),
        [IN_HBM] * 4,
        limit=20,
        after=after,
        light=True,
        grid=(1,),
        out_specs=[full((D, UNITS)), TOKEN],
        out_shape=(in_hbm((D, UNITS), BF16), TOKEN_SHAPE),
        scratch_shapes=[pltpu.VMEM((SEQ, n), BF16) for n in (D, 480, D, 160)]
        + [pltpu.SemaphoreType.DMA((12,))],
    )(normed, own, heads, mid)


def add_cores_kernel(near_ref, far_ref, *refs):
    outs, token_ref, (one, one_sems, two, two_sems, sums, done) = refs[:4], refs[4], refs[5:]
    mark(token_ref)
    at = [pl.ds(i * BLOCK, BLOCK) for i in range(4)]
    order = (3, 1, 2, 0)
    ins = {}
    for i in order:
        ins[i] = (
            pltpu.make_async_copy(near_ref.at[at[i], :], one.at[at[i], :], one_sems.at[i]),
            pltpu.make_async_copy(far_ref.at[at[i], :], two.at[at[i], :], two_sems.at[i]),
        )
        ins[i][0].start()
        ins[i][1].start()
    copies = []
    for i in order:
        ins[i][0].wait()
        ins[i][1].wait()
        sums[at[i], :] = (one[at[i], :].astype(F32) + two[at[i], :].astype(F32)).astype(BF16)
        copies.append(pltpu.make_async_copy(sums.at[at[i], :], outs[i], done.at[i]))
        copies[-1].start()
    for copy in copies:
        copy.wait()


def add_cores(near, far, after=()):
    return call(
        add_cores_kernel,
        after=after,
        grid=(1,),
        in_specs=[ANYWHERE] * 2,
        out_specs=[ANYWHERE] * 4 + [TOKEN],
        out_shape=[in_hbm((BLOCK, D), BF16)] * 4 + [TOKEN_SHAPE],
        scratch_shapes=pieces_of(4) * 3,
    )(near, far)


def project_kernel(column, meta_ref, *refs):
    pieces = refs[:8]
    full_ref, bias_ref, qkv_ref, normed_ref, x_ref, sems, w_ref, w_sems = refs[8:]
    copies = fetch(pieces, x_ref, sems)
    load(full_ref, column * UNITS, (w_ref,), w_sems)[0].wait()
    for i in range(0, 8, 2):
        copies[i].wait()
        copies[i + 1].wait()
        x = x_ref[i * BLOCK : (i + 2) * BLOCK, :]
        qkv = jnp.dot(x, w_ref[:, : 3 * LOCAL], preferred_element_type=F32) + bias_ref[...]
        qkv = qkv.astype(BF16)
        for k in range(2):
            at = rows_at(meta_ref, HELD + i + k)
            normed_ref[at, :] = x[k * BLOCK : (k + 1) * BLOCK]
            qkv_ref[at, :] = qkv[k * BLOCK : (k + 1) * BLOCK]


def columns_of(at):
    return pl.BlockSpec((D, UNITS), lambda i: (0, at))


def project_first_kernel(x_ref, w_ref, bias_ref, qkv_ref):
    qkv = jnp.dot(x_ref[...], w_ref[:, : 3 * LOCAL], preferred_element_type=F32)
    qkv_ref[...] = (qkv + bias_ref[...]).astype(BF16)


def project_first(normed, weights, bias):
    return call(
        project_first_kernel,
        grid=(4,),
        in_specs=[pl.BlockSpec((256, D), lambda i: (i, 0)), columns_of(0), full((1, 3 * LOCAL))],
        out_specs=pl.BlockSpec((256, 3 * LOCAL), lambda i: (i, 0)),
        out_shape=shaped((SEQ, 3 * LOCAL), BF16),
    )(normed, weights, bias)


def gathered_rows_kernel(step_ref, *refs):
    pieces, wide_ref, out_ref, held, sems = refs[:8], refs[8], refs[9], refs[10], refs[11]
    copies = [
        pltpu.make_async_copy(
            piece.at[pl.ds(BLOCK, EXTRA), :], held.at[i], sems.at[i]
        )
        for i, piece in enumerate(pieces)
    ]
    for copy in copies:
        copy.start()
    for copy in copies:
        copy.wait()
    out_ref[:, : 3 * LOCAL] = wide_ref[...]
    out_ref[:, 3 * LOCAL : UNITS] = jnp.zeros((80, UNITS - 3 * LOCAL), BF16)
    for f in range(8):
        rows = held[step_ref[f]].astype(F32)
        parts = [rows[:10, j * 160 : (j + 1) * 160] for j in range(8)]
        at = UNITS + f * 160
        out_ref[:, at : at + 160] = jnp.concatenate(parts, axis=0).astype(BF16)


def gathered_rows(steps, pieces, wide):
    return call(
        gathered_rows_kernel,
        grid=(1,),
        light=True,
        in_specs=[IN_SMEM] + [IN_HBM] * 8 + [full((80, 3 * LOCAL))],
        out_specs=full((80, UNITS + D)),
        out_shape=in_hbm((80, UNITS + D), BF16),
        scratch_shapes=[pltpu.VMEM((8, EXTRA, D), BF16), pltpu.SemaphoreType.DMA((8,))],
    )(steps, *pieces, wide)


EXTRA = 16


def turn_kernel(one_ref, two_ref, terms_ref, out_ref):
    out_ref[:, D:] = terms_ref[...]
    for i in range(10):
        at = pl.ds(i * 128, 128)
        rows = jnp.concatenate(
            [one_ref[at, 64:].astype(F32), two_ref[at, :96].astype(F32)], axis=1
        )
        out_ref[:, at] = rows.T.astype(BF16)


def turn(weights, terms):
    first = 3 * LOCAL // 128
    return call(
        turn_kernel,
        grid=(1,),
        in_specs=[
            pl.BlockSpec((D, 128), lambda i: (0, first)),
            pl.BlockSpec((D, 128), lambda i: (0, first + 1)),
            full((160, 128)),
        ],
        out_specs=full((160, D + 128)),
        out_shape=in_hbm((160, D + 128), BF16),
    )(weights, weights, terms)


def project_attend_kernel(column, meta_ref, *refs):
    ins, (start_ref, qkv_ref, normed_ref), refs = refs[:10], refs[10:13], refs[13:]
    project_kernel(column, meta_ref, *ins, qkv_ref, normed_ref, *refs[7:11])
    attend_forward_kernel(meta_ref, start_ref, qkv_ref, *refs[:7], *refs[11:])


def project_attend(meta, pieces, weights, at, bias, start):
    results = call(
        functools.partial(project_attend_kernel, at),
        limit=24,
        grid=(1,),
        in_specs=[IN_SMEM] + [IN_HBM] * 9 + [full((1, 3 * LOCAL)), full((1, SEQ))],
        out_specs=[full((SEQ, 3 * LOCAL)), full((SEQ, D))]
        + [ANYWHERE] * 4
        + [full((LOCAL, SEQ)), full((8, SEQ)), TOKEN],
        out_shape=[in_hbm((SEQ, 3 * LOCAL), BF16), in_hbm((SEQ, D), BF16)]
        + [in_hbm((2 * BLOCK, 160), BF16)] * 4
        + [in_hbm((LOCAL, SEQ), F32), in_hbm((8, SEQ), F32), TOKEN_SHAPE],
        scratch_shapes=pieces_of(8)
        + weights_of(1)
        + [pltpu.VMEM((SEQ, 160), BF16), pltpu.SemaphoreType.DMA((8,))],
    )(meta, *pieces, weights, bias, start)
    return results[0], results[1], results[2:6], results[6], results[7]


def project_back(meta_ref, grad_ref, w_ref, y_ref, out_ref, done, first):
    column = lax.broadcasted_iota(jnp.int32, (1, 3 * LOCAL), 1)
    twice = jnp.zeros((1, 3 * LOCAL), jnp.int32)
    for i in range(3):
        at = column - i * LOCAL
        twice += jnp.where((at >= 0) & (at < HEAD_DIM), 1, 0)
    counted = twice * meta_ref[CORE] == 0
    outs = []
    for i in range(2):
        x = jnp.concatenate(
            [grad_ref[rows_at(meta_ref, HELD + first + 2 * i + k), :] for k in range(2)],
            axis=0,
        )
        x = jnp.where(counted, x.astype(F32), 0.0).astype(BF16)
        at = pl.ds(i * 256, 256)
        y_ref[at, :] = nt(x, w_ref[:, : 3 * LOCAL]).astype(BF16)
        outs.append(pltpu.make_async_copy(y_ref.at[at, :], out_ref.at[at, :], done.at[i]))
        outs[i].start()
    return outs


def attend_project_back_kernel(column_at, meta_ref, start_ref, qkv_ref, turned_ref, lse_ref, *refs):
    pieces, full_ref = refs[:8], refs[8]
    own_ref, sum_ref, mid_ref, far_ref, near_ref = refs[9:14]
    out_ref, grad_ref, sems, dk_ref, dv_ref, w_ref, w_sems = refs[14:21]
    far, far_done, near, near_done = refs[21:]
    weights = load(full_ref, column_at * UNITS, (w_ref,), w_sems)
    attend_backward_kernel(
        meta_ref,
        start_ref,
        qkv_ref,
        turned_ref,
        lse_ref,
        *pieces,
        out_ref,
        own_ref,
        sum_ref,
        mid_ref,
        grad_ref,
        sems,
        dk_ref,
        dv_ref,
    )
    weights[0].wait()
    copies = project_back(meta_ref, out_ref, w_ref, far, far_ref, far_done, 4)
    copies += project_back(meta_ref, out_ref, w_ref, near, near_ref, near_done, 0)
    for copy in copies:
        copy.wait()


def attend_project_back(meta, start, qkv, turned, lse, pieces, weights, column_at):
    return call(
        functools.partial(attend_project_back_kernel, column_at),
        limit=28,
        grid=(1,),
        in_specs=[
            IN_SMEM,
            full((1, SEQ)),
            full((SEQ, 3 * LOCAL)),
            full((LOCAL, SEQ)),
            full((8, SEQ)),
        ]
        + [IN_HBM] * 9,
        out_specs=[full((SEQ, 480)), full((1, 480)), full((SEQ, 160)), ANYWHERE, ANYWHERE],
        out_shape=(
            in_hbm((SEQ, 480), BF16),
            shaped((1, 480), F32),
            in_hbm((SEQ, 160), BF16),
            shaped((HALF, D), BF16),
            shaped((HALF, D), BF16),
        ),
        scratch_shapes=[
            pltpu.VMEM((SEQ, 3 * LOCAL), BF16),
            pltpu.VMEM((SEQ, WIDE), BF16),
            pltpu.SemaphoreType.DMA((8,)),
            pltpu.VMEM((SEQ, HEAD_DIM), F32),
            pltpu.VMEM((SEQ, HEAD_DIM), F32),
        ]
        + weights_of(1)
        + pieces_of(2, 256) * 2,
    )(meta, start, qkv, turned, lse, *pieces, weights)


def normal(v):
    mean = jnp.mean(v, axis=-1, keepdims=True)
    centred = v - mean
    variance = jnp.mean(centred * centred, axis=-1, keepdims=True)
    scale = lax.rsqrt(variance + 1e-05)
    return centred * scale, scale


def four(pieces, held_ref, sems):
    copies = fetch(pieces, held_ref, sems)
    for copy in copies:
        copy.wait()
    a, b, c, d = (held_ref[i * BLOCK : (i + 1) * BLOCK, :].astype(F32) for i in range(4))
    return (a + b) + (c + d)


def send_out(value, held_ref, out, sem):
    held_ref[...] = value
    copy = pltpu.make_async_copy(held_ref, out, sem)
    copy.start()
    return copy


def join_norm_kernel(
    a, b, c, d, old_ref, bias_ref, gain_ref, shift_ref, new_ref, low_ref, *refs
):
    x_ref, sems, y_ref, done, held_ref, held_sems = refs
    old = pltpu.make_async_copy(old_ref, held_ref, held_sems.at[0])
    old.start()
    total = four((a, b, c, d), x_ref, sems)
    old.wait()
    new = held_ref[...] + total + bias_ref[...]
    low = (normal(new)[0] * gain_ref[...] + shift_ref[...]).astype(BF16)
    copy = send_out(low, y_ref, low_ref, done.at[0])
    new_ref[...] = new
    copy.wait()


def join_norm(parts, old, bias, gain, shift, after=()):
    return call(
        join_norm_kernel,
        after=after,
        grid=(1,),
        in_specs=[IN_HBM] * 5 + [full((1, D))] * 3,
        out_specs=[full((BLOCK, D)), ANYWHERE],
        out_shape=(in_hbm((BLOCK, D), F32), in_hbm((BLOCK, D), BF16)),
        scratch_shapes=pieces_of(4) + pieces_of(1) + held_rows(1),
    )(*parts, old, bias, gain, shift)


def join_heads_kernel(turned, meta_ref, *refs):
    pieces, refs = refs[:8], refs[8:]
    w_refs, refs = (refs[:8], refs[8:]) if turned else (refs[:1], refs[1:])
    old_ref, gain_ref, shift_ref, more_ref, new_ref, low_ref, heads_ref, bias_ref = refs[:8]
    slots, sems, ordered, y_ref, done, held_ref, held_sems = refs[8:15]
    *w_held, w_sems = refs[15:17] if turned else refs[15:18]
    old = pltpu.make_async_copy(old_ref, held_ref, held_sems.at[0])
    old.start()
    copies = [
        pltpu.make_async_copy(
            pieces[j].at[pl.ds(j % 2 * BLOCK, BLOCK), :],
            slots.at[meta_ref[FROM_SLOT + j]],
            sems.at[j],
        )
        for j in range(8)
    ]
    for copy in copies:
        copy.start()
    weights = load_halves(meta_ref, w_refs, w_held, w_sems)
    if turned:
        terms_ref, terms_sems = refs[17:]
        for i, ref in enumerate(w_refs):
            at = pl.ds(pl.multiple_of(meta_ref[HELD_SLOT + i] * 160, 160), 160)
            copies.append(
                pltpu.make_async_copy(
                    ref.at[:, pl.ds(D, 128)], terms_ref.at[at, :], terms_sems.at[i]
                )
            )
            copies[-1].start()
    for copy in copies:
        copy.wait()
    if turned:
        terms = terms_ref[...].astype(F32).T
        terms = [
            (terms[l : l + 1] + terms[l + 2 : l + 3]) + terms[l + 4 : l + 5] for l in range(LAYERS)
        ]
        bias_ref[...] = jnp.concatenate(terms + [jnp.zeros((6, D), F32)], axis=0)
        bias = terms[0]
    else:
        bias = more_ref[1:2, :]
        bias_ref[...] = more_ref[...]
    for chip in range(4):
        five = jnp.concatenate([slots[2 * chip], slots[2 * chip + 1]], axis=1)
        for i in range(5):
            ordered[5 * chip + i] = five[:, i * HEAD_DIM : (i + 1) * HEAD_DIM]
    x = jnp.concatenate([ordered[meta_ref[HEAD_OF + r]] for r in range(HEADS)], axis=1)
    product = nt if turned else lambda a, b: jnp.dot(a, b, preferred_element_type=F32)
    for copy in weights:
        copy.wait()
    branch = [product(x, ref[...]) for ref in w_held]
    branch = branch[0] if turned else jnp.concatenate(branch, axis=1)
    old.wait()
    new = held_ref[...] + branch + bias
    low = (normal(new)[0] * gain_ref[...] + shift_ref[...]).astype(BF16)
    if turned:
        y_ref[BLOCK:, :] = more_ref[...]
    y_ref[:BLOCK, :] = low
    copy = pltpu.make_async_copy(y_ref, low_ref, done.at[0])
    copy.start()
    new_ref[...] = new
    heads_ref[...] = x
    copy.wait()


def load_halves(meta_ref, refs, targets, sems):
    if len(refs) == 1:
        return load(refs[0], UNITS, targets, sems)
    copies = []
    for i, ref in enumerate(refs):
        at = pl.ds(pl.multiple_of(meta_ref[HELD_SLOT + i] * 160, 160), 160)
        copies.append(
            pltpu.make_async_copy(ref.at[:, pl.ds(0, D)], targets[0].at[at, :], sems.at[i])
        )
        copies[i].start()
    return copies


def halves_of(turned):
    if turned:
        return [pltpu.VMEM((D, D), BF16), pltpu.SemaphoreType.DMA((8,))]
    return [pltpu.VMEM((D, UNITS), BF16)] * 2 + [pltpu.SemaphoreType.DMA((2,))]


def join_heads(meta, pieces, weights, turned, old, gain, shift, more):
    rows = BLOCK + EXTRA if turned else BLOCK
    return call(
        functools.partial(join_heads_kernel, turned),
        grid=(1,),
        in_specs=[IN_SMEM]
        + [IN_HBM] * (9 + len(weights))
        + [full((1, D))] * 2
        + [full(more.shape)],
        out_specs=[full((BLOCK, D)), ANYWHERE, full((BLOCK, D)), full((8, D))],
        out_shape=(
            in_hbm((BLOCK, D), F32),
            in_hbm((rows, D), BF16),
            in_hbm((BLOCK, D), BF16),
            shaped((8, D), F32),
        ),
        scratch_shapes=[
            pltpu.VMEM((8, BLOCK, 160), BF16),
            pltpu.SemaphoreType.DMA((8,)),
            pltpu.VMEM((HEADS, BLOCK, HEAD_DIM), BF16),
        ]
        + pieces_of(1, rows)
        + held_rows(1)
        + halves_of(turned)
        + ([pltpu.VMEM((D, 128), BF16), pltpu.SemaphoreType.DMA((8,))] if turned else []),
    )(meta, *pieces, *weights, old, gain, shift, more)


def norm_back_math(dy, x, old, gain):
    unit, scale = normal(x)
    slope = dy * gain
    mean_one = jnp.mean(slope, axis=-1, keepdims=True)
    mean_two = jnp.mean(slope * unit, axis=-1, keepdims=True)
    new = old + scale * (slope - mean_one - unit * mean_two)
    sums = jnp.concatenate(
        [
            jnp.sum(dy * unit, axis=0, keepdims=True),
            jnp.sum(dy, axis=0, keepdims=True),
            jnp.sum(new, axis=0, keepdims=True),
            jnp.zeros((5, D), F32),
        ],
        axis=0,
    )
    return new, sums


def hold_rows(refs, targets, sems):
    copies = []
    for i, (ref, target) in enumerate(zip(refs, targets)):
        copies.append(pltpu.make_async_copy(ref, target, sems.at[i]))
        copies[i].start()
    return copies


def norm_back_kernel(
    a, b, c, d, x_ref, old_ref, gain_ref, new_ref, low_ref, sums_ref, token_ref, *refs
):
    mark(token_ref)
    p_ref, sems, y_ref, done, x_held, old_held, held_sems = refs
    held = hold_rows((x_ref, old_ref), (x_held, old_held), held_sems)
    total = four((a, b, c, d), p_ref, sems)
    for copy in held:
        copy.wait()
    new, sums = norm_back_math(total, x_held[...], old_held[...], gain_ref[...])
    copy = send_out(new.astype(BF16), y_ref, low_ref, done.at[0])
    new_ref[...] = new
    sums_ref[...] = sums
    copy.wait()


def finish_kernel(sum_ref, first_ref, old_ref, bias_ref, out_ref):
    out_ref[:BLOCK, :] = first_ref[...].astype(BF16)
    last = old_ref[...] + sum_ref[...].astype(F32) + bias_ref[...]
    out_ref[BLOCK:, :] = last.astype(BF16)


def finish(total, first, old, bias):
    return call(
        finish_kernel,
        [full((BLOCK, D))] * 3 + [full((1, D))],
        light=True,
        grid=(1,),
        out_specs=full((2 * BLOCK, D)),
        out_shape=in_hbm((2 * BLOCK, D), BF16),
    )(total, first, old, bias)


def norm_back(parts, x, old, gain, after):
    return call(
        norm_back_kernel,
        after=after,
        grid=(1,),
        in_specs=[IN_HBM] * 6 + [full((1, D))],
        out_specs=[full((BLOCK, D)), ANYWHERE, full((8, D)), TOKEN],
        out_shape=(
            in_hbm((BLOCK, D), F32),
            in_hbm((BLOCK, D), BF16),
            shaped((8, D), F32),
            TOKEN_SHAPE,
        ),
        scratch_shapes=pieces_of(4) + pieces_of(1) + held_rows(2),
    )(*parts, x, old, gain)


def norm_back_heads_kernel(turned, meta_ref, a, b, c, d, x_ref, old_ref, gain_ref, *refs):
    w_refs, refs = (refs[:8], refs[8:]) if turned else (refs[:1], refs[1:])
    new_ref, low_ref, sums_ref = refs[:3]
    pieces, token_ref, refs = refs[3:7], refs[7], refs[8:]
    slots, sent, ordered, p_ref, sems, y_ref, done, x_held, old_held, held_sems = refs[:10]
    *w_held, w_sems = refs[10:]
    mark(token_ref)
    held = hold_rows((x_ref, old_ref), (x_held, old_held), held_sems)
    total = four((a, b, c, d), p_ref, sems)
    weights = load_halves(meta_ref, w_refs, w_held, w_sems)
    for copy in held:
        copy.wait()
    new, sums = norm_back_math(total, x_held[...], old_held[...], gain_ref[...])
    new_ref[...] = new
    low = new.astype(BF16)
    copies = [send_out(low, y_ref, low_ref, done.at[0])]
    sums_ref[...] = sums
    for copy in weights:
        copy.wait()
    if turned:
        grads = jnp.dot(low, w_held[0][...], preferred_element_type=F32)
    else:
        grads = nt(low[:, :UNITS], w_held[0][...]) + nt(low[:, UNITS:], w_held[1][...])
    for r in range(HEADS):
        ordered[meta_ref[HEAD_OF + r]] = grads[:, r * HEAD_DIM : (r + 1) * HEAD_DIM].astype(BF16)
    for f in range(8):
        h = 5 * (f // 2) + 2 * (f % 2)
        slots[f, :, :LOCAL] = jnp.concatenate([ordered[h + i] for i in range(3)], axis=1)
        slots[f, :, LOCAL:] = low[:, f * 160 : (f + 1) * 160]
    for j in range(8):
        target = pieces[j // 2].at[pl.ds(j % 2 * BLOCK, BLOCK), :]
        copies.append(
            pltpu.make_async_copy(slots.at[meta_ref[TO_SLOT + j]], target, sent.at[j])
        )
        copies[-1].start()
    for copy in copies:
        copy.wait()


def norm_back_heads(meta, parts, x, old, gain, weights, turned, after):
    results = call(
        functools.partial(norm_back_heads_kernel, turned),
        after=after,
        grid=(1,),
        in_specs=[IN_SMEM] + [IN_HBM] * 6 + [full((1, D))] + [IN_HBM] * len(weights),
        out_specs=[full((BLOCK, D)), ANYWHERE, full((8, D))] + [ANYWHERE] * 4 + [TOKEN],
        out_shape=[in_hbm((BLOCK, D), F32), in_hbm((BLOCK, D), BF16), shaped((8, D), F32)]
        + [in_hbm((2 * BLOCK, WIDE), BF16)] * 4
        + [TOKEN_SHAPE],
        scratch_shapes=[
            pltpu.VMEM((8, BLOCK, WIDE), BF16),
            pltpu.SemaphoreType.DMA((8,)),
            pltpu.VMEM((HEADS, BLOCK, HEAD_DIM), BF16),
        ]
        + pieces_of(4)
        + pieces_of(1)
        + held_rows(2)
        + halves_of(turned),
    )(meta, *parts, x, old, gain, *weights)
    return results[0], results[2], results[3:7], results[7]


def on_device(
    stream_in,
    segments,
    head_table,
    query_key_value,
    attention_out,
    expand_weight,
    contract_weight,
    norm_gain,
    norm_bias,
    attention_bias,
    expand_bias,
    contract_bias,
    cotangent,
):
    row = lax.axis_index("row")
    col = lax.axis_index("col")
    core = row % 2
    z = row // 4
    y = col % 4
    x = ((row // 2) % 2) * 2 + col // 4
    first = core == 0
    sequence = z * 4 + x

    to_devices = [(core ^ dc, (y + dy) % 4) for dy, dc in STEPS]
    from_devices = [(core ^ dc, (y - dy) % 4) for dy, dc in STEPS]
    held = [core * 4 + (y - k) % 4 for k in HOPS] + [(1 - core) * 4 + (y - k) % 4 for k in HOPS]
    meta = (
        [core, (core == x % 2).astype(jnp.int32)]
        + [core] * 6
        + [c * 4 + at for c, at in to_devices]
        + [2 * at + c for c, at in to_devices]
        + [c * 4 + at for c, at in from_devices]
        + [2 * at + c for c, at in from_devices]
        + held
    )
    slot_heads = head_table.reshape(-1)
    filled = (slot_heads < HEADS).astype(jnp.int32)
    places24 = jnp.arange(24, dtype=jnp.int32)
    order = jnp.sum(jnp.where(places24[None, :] < places24[:, None], filled[None, :], 0), axis=1)
    head_ids = jnp.arange(HEADS, dtype=jnp.int32)
    ranked = (order[None, :] == head_ids[:, None]) & (slot_heads[None, :] < HEADS)
    head_of_rank = jnp.sum(jnp.where(ranked, slot_heads[None, :], 0), axis=1)
    held_slots = [2 * ((y - k) % 4) + c for c in (core, 1 - core) for k in HOPS]
    meta = jnp.concatenate([jnp.stack(meta), head_of_rank, jnp.stack(held_slots)])
    meta = meta.astype(jnp.int32)

    def spread_core(own, axis=-1):
        half = HEAD_DIM // 2
        low = lax.slice_in_dim(own, 0, half, axis=axis)
        high = lax.slice_in_dim(own, own.shape[axis] - half, own.shape[axis], axis=axis)
        got = send(jnp.where(first, high, low), CORES)
        return jnp.where(
            first,
            jnp.concatenate([own, got], axis=axis),
            jnp.concatenate([got, own], axis=axis),
        )

    packed_a = [
        jnp.concatenate([query_key_value[l, i] for i in range(3)] + [attention_out[l]], axis=1)
        for l in range(LAYERS)
    ]
    packed_b = [
        jnp.concatenate([expand_weight[l], contract_weight[l].T], axis=1) for l in range(LAYERS)
    ]

    def three(value):
        parts = []
        for _ in range(3):
            parts.append(value.astype(BF16))
            value = value - parts[-1].astype(F32)
        return jnp.concatenate(parts, axis=0)

    def added(rows):
        rows = rows.astype(F32).reshape(3, LAYERS, -1)
        return (rows[0] + rows[1]) + rows[2]

    none = jnp.zeros((LAYERS, 160), F32)
    head_bias = jnp.concatenate(
        [attention_bias[:, 0], none, attention_bias[:, 1], attention_bias[:, 2]], axis=1
    )
    packed_a[0] = jnp.concatenate(
        [packed_a[0], three(head_bias), three(expand_bias), jnp.zeros((4, UNITS), BF16)], axis=0
    )
    packed_a[0] = jnp.concatenate(
        [packed_a[0], jnp.pad(attention_out[1], ((0, 16), (0, 0)))], axis=1
    )
    shards = jnp.concatenate(
        [jnp.pad(value, ((0, 16), (0, 0))) for value in packed_b]
        + [packed_a[0], jnp.pad(packed_a[1][:, :480], ((0, 16), (0, 0)))],
        axis=1,
    )
    stream_got = send(stream_in, CORES)
    (shards,) = later((shards,), (stream_got,))
    shards = send(shards, TO_FEATURE)
    def gain_of(l, i):
        return norm_gain[l, i].reshape(1, D), norm_bias[l, i].reshape(1, D)

    normed, stream, token = first_norm(meta, stream_in, stream_got, *gain_of(0, 0))
    (shards,) = later((shards,), (token,))
    moved_a = shards[:, 2 * D : 2 * D + 800]
    moved_heads = shards[:80, 2 * D + 800 :]

    def widen_heads(own):
        return spread_core(own.reshape(-1, 3, 160)).reshape(-1, 3 * LOCAL)

    def widen(moved):
        return jnp.concatenate([widen_heads(moved[:, :480]), moved[:, 480:UNITS]], axis=1)

    def gather_plane(value):
        return lax.all_gather(value, AXES, axis=0, tiled=True, axis_index_groups=PLANES)

    wide_a = widen(moved_a)
    first_a = lax.all_to_all(
        spread_out(wide_a, 80, (token,)), AXES, 0, 0, tiled=True, axis_index_groups=PLANES
    ).reshape(D, 736)

    terms = jnp.pad(wide_a[80:86, 3 * LOCAL :], ((0, 122), (0, 0))).T
    qkv_bias = added(wide_a[80:86, : 3 * LOCAL]).reshape(LAYERS, 1, 3 * LOCAL)
    up_bias = added(moved_a[86:92, :UNITS]).reshape(LAYERS, 1, UNITS)
    block = turn(first_a, terms)
    (moved_first,) = later((shards[:80, :D],), (block,))
    first_b = gather_plane(moved_first)
    wide_late = widen_heads(moved_heads)
    more = moved_a[:80, UNITS:].reshape(8, 10, 160).transpose(1, 0, 2).reshape(10, D)
    more = jnp.pad(more, ((0, EXTRA - 10), (0, 0)))
    step_of_feature = jnp.sum(
        jnp.where(
            jnp.stack([2 * ((y - k) % 4) + c for c in (core, 1 - core) for k in HOPS])[None, :]
            == jnp.arange(8)[:, None],
            jnp.arange(8)[None, :],
            0,
        ),
        axis=1,
    )

    w_in = [(first_a, 0)]
    w_units = [first_b]

    def exchange(pieces):
        near = [send(piece, along_y(k)) if k else piece for piece, k in zip(pieces, HOPS)]
        return [value for piece in near for value in (piece, send(piece, CORES))]

    def gather_pieces(block):
        near = [block] + [send(block, along_y(k)) for k in HOPS[1:]]
        return near + [send(value, CORES) for value in near]

    seg = lax.dynamic_slice_in_dim(segments, sequence * SEQ, SEQ)
    start = jnp.sum((seg[:, None] < seg[None, :]).astype(jnp.int32), axis=0, keepdims=True)
    def gather_tokens(value):
        return lax.all_gather(value, AXES, axis=0, tiled=True, axis_index_groups=BY_TOKEN)

    def sum_parts(far, near, after=()):
        *parts, token = add_cores(near, send(far, CORES), after)
        return [send(part, along_y(-k)) if k else part for part, k in zip(parts, HOPS)], token

    def scatter_plane(value):
        return lax.psum_scatter(
            value, AXES, scatter_dimension=0, tiled=True, axis_index_groups=PLANES
        )

    def to_result(value, until=()):
        value = send(value, HOME)
        if until:
            (value,) = later((value,), until)
        layers = value.shape[0] // BLOCK
        blocks = jnp.moveaxis(value.reshape(layers, BLOCK, 8, 160), 2, 0)
        blocks = lax.all_to_all(blocks, "col", 0, 0, tiled=True)
        return jnp.moveaxis(blocks, 0, 1).reshape(layers, SEQ, 160)

    grad_held, grad, grad_sum, held_token = hold_grads(meta, cotangent, send(cotangent, CORES))
    pieces = None
    kept = []
    for l in range(LAYERS):
        first_layer = l == 0
        if first_layer:
            qkv = project_first(normed, first_a, qkv_bias[l])
            turned_out = [block] + [send(block, along_y(k)) for k in HOPS[1:]]
            pieces, turned, lse, token = attend_forward(meta, start, qkv)
        else:
            qkv, normed, pieces, turned, lse = project_attend(
                meta, pieces, *w_in[l], qkv_bias[l], start
            )
        pieces = exchange(pieces)
        if first_layer:
            turned_out = later(turned_out, (pieces[1],))
            turned_out = [*turned_out] + [send(value, CORES) for value in turned_out]
        if first_layer:
            w_heads = turned_out
        else:
            w_heads = [late]
        gain, shift = gain_of(l, 1)
        mid, low, heads, more = join_heads(
            meta, pieces, w_heads, first_layer, stream, gain, shift, more
        )
        pieces = gather_pieces(low)
        if first_layer:
            rows = gathered_rows(step_of_feature.astype(jnp.int32), pieces, wide_late)
            late = gather_plane(rows)
            w_in.append((late, 0))
            (moved_units,) = later((shards[:80, D : 2 * D],), (rows,))
            w_units.append(gather_plane(moved_units))
        bias = contract_bias[l].reshape(1, D)
        state = (stream, mid, normed, pieces, w_heads, qkv, turned, lse, heads)
        if first_layer:
            far = up_down(pieces[4:], w_units[l], up_bias[l])
            near = up_down(pieces[:4], w_units[l], up_bias[l])
            kept.append(state + (far, near))
            parts, _ = sum_parts(far[2], near[2])
            gain, shift = gain_of(l + 1, 0)
            stream, low = join_norm(parts, mid, bias, gain, shift, (held_token,))
            pieces = gather_pieces(low)
        else:
            both_heads = jnp.concatenate([kept[0][8], heads], axis=0)
            (both_heads,) = later((both_heads,), (pieces[1], pieces[2], pieces[3]))
            all_heads = gather_tokens(both_heads)
            far = up_down_both(meta, pieces[4:], grad_held, 4, w_units[l], up_bias[l])
            near = up_down_both(meta, pieces[:4], grad_held, 0, w_units[l], up_bias[l], far[4])
            kept.append(state + (far, near))
            last = (near[4], mid, bias)

    grad_pieces = None
    wide_sums = [None] * LAYERS
    plane_sums = [None] * LAYERS
    for l in reversed(range(LAYERS)):
        stream, mid, normed, pieces, w_heads, qkv, turned, lse, _, far, near = kept[l]
        if l:
            act_far, low_far, sum_far, back_far, _ = far
            act_near, low_near, sum_near, back_near, _ = near
        else:
            low_far, sum_far, back_far = up_down_back(grad_pieces[4:], w_units[l], far[0])
            low_near, sum_near, back_near = up_down_back(grad_pieces[:4], w_units[l], near[0])
            act_far, act_near = far[1], near[1]
        parts, token = sum_parts(back_far, back_near)
        units, token = unit_grads(
            pieces,
            (low_near, low_far),
            (grad_held,) if l else grad_pieces,
            (act_near, act_far),
            (token, all_heads) if l else (token, last_rows),
            None if l else heads,
        )
        mid_grad, sums_two, pieces, token = norm_back_heads(
            meta,
            parts,
            mid,
            grad,
            gain_of(l, 1)[0],
            w_heads,
            l == 0,
            (token,) if l else (token, units_one),
        )
        if l:
            last_sum, last_mid, last_bias = last
            units, last_sum = later((units, last_sum), (token,))
            last_sum = lax.psum_scatter(
                last_sum, AXES, scatter_dimension=0, tiled=True, axis_index_groups=BY_TOKEN
            )
            last_rows = finish(last_sum, stream, last_mid, last_bias)
            units_one = scatter_plane(units)
        else:
            (units,) = later((units,), (token,))
            units_both = scatter_plane(units)
        grad_own, qkv_sum, mid_all, back_far, back_near = attend_project_back(
            meta, start, qkv, turned, lse, exchange(pieces), *w_in[l]
        )
        parts, token = sum_parts(back_far, back_near)
        heads, token = head_grads(normed, grad_own, all_heads, mid_all, l, (token,))
        grad_new, next_low, sums_one, token = norm_back(
            parts, stream, mid_grad, gain_of(l, 0)[0], (token,)
        )
        wide_sums[l] = jnp.concatenate([sums_one[:2], sums_two[:3], grad_sum], axis=0)
        plane_sums[l] = jnp.concatenate(
            [
                qkv_sum[:, :160],
                qkv_sum[:, 320:],
                sum_far + sum_near,
                jnp.zeros((1, D - 960), F32),
            ],
            axis=1,
        )
        if l:
            grad_sum = sums_one[2:3]
            grad_pieces = gather_pieces(next_low)
        grad = grad_new
    heads_zero = lax.all_to_all(
        heads.reshape(16, 80, UNITS), AXES, 0, 0, tiled=True, axis_index_groups=PLANES
    )
    heads_added = jnp.sum(heads_zero.astype(F32), axis=0).astype(BF16)
    results = to_result(jnp.concatenate([last_rows, next_low], axis=0), (heads_zero,))
    activations = results[:LAYERS]
    grad_stream = results[LAYERS].astype(F32)


    back = jnp.concatenate([units_one, units_both, heads_added], axis=1)
    back = send(back, FROM_FEATURE)
    units_one, units_both = back[:, : 2 * UNITS], back[:, 2 * UNITS : 4 * UNITS]
    heads_one, heads_zero = back[:, 4 * UNITS : 5 * UNITS], back[:, 5 * UNITS + 128 :]
    unit_back = jnp.stack([units_both, units_one]).astype(F32)
    head_back = jnp.stack([heads_zero, heads_one]).astype(F32)
    grad_query_key_value = head_back[:, :, :480].reshape(LAYERS, 80, 3, 160).transpose(0, 2, 1, 3)
    grad_attention_out = head_back[:, :, 480:]
    grad_expand = unit_back[:, :, :UNITS]
    grad_contract = unit_back[:, :, UNITS:].transpose(0, 2, 1)

    def sum_four(value, perms):
        one, two, three = (send(value, perm) for perm in perms)
        return (value + two) + (one + three)

    wide = jnp.concatenate(wide_sums, axis=0)
    wide = sum_four(wide + send(wide, CORES), [along_y(k) for k in (1, 2, 3)])
    sums = jnp.concatenate([wide] + plane_sums, axis=0)
    sums = sum_four(sums, [along_plane(0, k) for k in (1, 2, 3)])
    sums = sum_four(sums, [along_plane(k, 0) for k in (1, 2, 3)])
    wide = sums[:12].reshape(LAYERS, 6, D)
    plane = send(sums[12:], FROM_FEATURE)
    grad_norm_gain = jnp.stack([wide[:, 0], wide[:, 2]], axis=1)
    grad_norm_bias = jnp.stack([wide[:, 1], wide[:, 3]], axis=1)
    out_sums = lax.dynamic_slice_in_dim(wide[:, 4], col * 160, 160, 1)
    grad_attention_bias = jnp.stack([plane[:, :160], plane[:, 160:320], out_sums], axis=1)
    grad_expand_bias = plane[:, 320:960]
    grad_contract_bias = wide[:, 5]
    return (
        activations,
        grad_stream,
        grad_query_key_value,
        grad_attention_out,
        grad_expand,
        grad_contract,
        grad_norm_gain,
        grad_norm_bias,
        grad_attention_bias,
        grad_expand_bias,
        grad_contract_bias,
    )


def solution(mesh):
    placed = (
        P("row", None),
        P(),
        P(),
        P(None, None, "row", "col"),
        P(None, "row", "col"),
        P(None, "row", "col"),
        P(None, "col", "row"),
        P(),
        P(),
        P(None, None, "col"),
        P(None, "col"),
        P(),
        P("row", None),
    )
    return jax.shard_map(
        on_device,
        mesh=mesh,
        in_specs=placed,
        out_specs=(
            P(None, "row", "col"),
            P("row", "col"),
            P(None, None, "row", "col"),
            P(None, "row", "col"),
            P(None, "row", "col"),
            P(None, "col", "row"),
            P(),
            P(),
            P(None, None, "col"),
            P(None, "col"),
            P(),
        ),
        check_vma=False,
    )
```

```python
import functools

import jax
import jax.numpy as jnp
from jax import lax
from jax.experimental import pallas as pl
from jax.experimental.pallas import tpu as pltpu
from jax.sharding import PartitionSpec as P

D = 1280
HEADS = 20
HEAD_DIM = 64
SEQ = 1024
LAYERS = 2
BLOCK = 128
LOCAL = 3 * HEAD_DIM
SCALE = HEAD_DIM ** (-0.5)
AXES = ("row", "col")
BF16 = jnp.bfloat16
F32 = jnp.float32
MIB = 1024 * 1024


def device(z, x, core, y):
    return (z * 4 + (x // 2) * 2 + core) * 8 + (x % 2) * 4 + y


def pairs(target):
    out = []
    for z in range(4):
        for x in range(4):
            for core in range(2):
                for y in range(4):
                    out.append((device(z, x, core, y), device(*target(z, x, core, y))))
    return out


def along_y(k):
    return pairs(lambda z, x, core, y: (z, x, core, (y + k) % 4))


def along_plane(dz, dx):
    return pairs(lambda z, x, core, y: ((z + dz) % 4, (x + dx) % 4, core, y))


def to_feature(z, x, core, y):
    block = (x % 2) * 4 + y
    return (z, (x // 2) * 2 + core, block % 2, block // 2)


CORES = pairs(lambda z, x, core, y: (z, x, 1 - core, y))
TO_FEATURE = pairs(to_feature)
FROM_FEATURE = [(b, a) for a, b in TO_FEATURE]
HOME = pairs(lambda z, x, core, y: (z, (x // 2) * 2 + core, x % 2, y))
PLANES = [
    [device(z, x, core, y) for z in range(4) for x in range(4)]
    for y in range(4)
    for core in range(2)
]
BY_FEATURE = [
    [device(z, x, core, y) for y in range(4) for core in range(2)]
    for z in range(4)
    for x in range(4)
]
BY_TOKEN = [
    [device(z, x, core, y) for core in range(2) for y in range(4)]
    for z in range(4)
    for x in range(4)
]
STEPS = [(dy, dc) for dy in (0, 1, 3, 2) for dc in (0, 1)]
HOPS = (0, 1, 3, 2)


NAMES = {tuple(CORES): "cores", tuple(TO_FEATURE): "to_feature", tuple(FROM_FEATURE): "from_feature"}


def send(value, perm):
    with jax.named_scope("send_" + NAMES.get(tuple(perm), "far")):
        return lax.ppermute(value, AXES, perm)


CORE, SAME, TO_BLOCK, TO_SLOT, FROM_BLOCK, FROM_SLOT, HELD, HEAD_OF = 0, 1, 8, 16, 24, 32, 40, 48
HELD_SLOT = HEAD_OF + HEADS
IN_SMEM = pl.BlockSpec(memory_space=pltpu.SMEM)
ANYWHERE = pl.BlockSpec(memory_space=pl.ANY)
IN_HBM = pl.BlockSpec(memory_space=pltpu.HBM)


LIGHT = pl.CostEstimate(flops=1000, bytes_accessed=1000, transcendentals=0)


def call(kernel, in_specs, limit=16, after=(), light=False, aliases=None, **kwargs):
    count = len(after)

    def waiting(*refs):
        kernel(*refs[count:])

    specs = [IN_HBM] * count + list(in_specs)
    run = pl.pallas_call(
        waiting,
        in_specs=specs,
        compiler_params=pltpu.CompilerParams(vmem_limit_bytes=limit * MIB),
        cost_estimate=LIGHT if light else None,
        input_output_aliases={count + i: out for i, out in (aliases or {}).items()},
        **kwargs,
    )
    label = getattr(kernel, "func", kernel).__name__

    def named(*operands):
        with jax.named_scope(label):
            placed = [
                pltpu.with_memory_space_constraint(value, pltpu.HBM) if spec is IN_HBM else value
                for value, spec in zip((*after, *operands), specs)
            ]
            return run(*placed)

    return named


def shaped(shape, dtype):
    return jax.ShapeDtypeStruct(shape, dtype)


def in_hbm(shape, dtype):
    return pltpu.HBM(shape, dtype)


def full(shape):
    return pl.BlockSpec(shape, lambda i: (0,) * len(shape))


TOKEN = full((8, 128))
TOKEN_SHAPE = in_hbm((8, 128), F32)


def mark(token_ref):
    token_ref[...] = jnp.zeros((8, 128), F32)


def fetch(pieces, target, sems):
    rows = target.shape[0] // len(pieces)
    copies = []
    for i, piece in enumerate(pieces):
        copies.append(
            pltpu.make_async_copy(
                piece.at[pl.ds(0, rows), :], target.at[pl.ds(i * rows, rows), :], sems.at[i]
            )
        )
    for copy in copies:
        copy.start()
    return copies


def load(ref, columns, targets, sems, rows=None):
    copies = []
    for i, target in enumerate(targets):
        width = target.shape[1]
        at = pl.ds(columns + i * width, width)
        copies.append(pltpu.make_async_copy(ref.at[:, at], target, sems.at[i]))
        copies[i].start()
    return copies


def held_rows(count):
    return [pltpu.VMEM((BLOCK, D), F32)] * count + [pltpu.SemaphoreType.DMA((count,))]


def weights_of(count):
    return [pltpu.VMEM((D, UNITS), BF16)] * count + [pltpu.SemaphoreType.DMA((count,))]


UNITS = 640


def pieces_of(count, rows=BLOCK, columns=D):
    return [pltpu.VMEM((count * rows, columns), BF16), pltpu.SemaphoreType.DMA((count,))]


def take_in(meta_ref, own_ref, got_ref, copies_of):
    for flag, ref in ((1, own_ref), (0, got_ref)):

        @pl.when(meta_ref[SAME] == flag)
        def _():
            copies = copies_of(ref)
            for copy in copies:
                copy.start()
            for copy in copies:
                copy.wait()


def hold_grads_kernel(meta_ref, own_ref, got_ref, held_ref, first_ref, sum_ref, token_ref, sems):
    def copies_of(ref):
        return [
            pltpu.make_async_copy(
                ref.at[rows_at(meta_ref, HELD + i), :],
                held_ref.at[pl.ds(i * BLOCK, BLOCK), :],
                sems.at[i],
            )
            for i in range(8)
        ]

    take_in(meta_ref, own_ref, got_ref, copies_of)
    first = held_ref[:BLOCK, :].astype(F32)
    first_ref[...] = first
    sum_ref[...] = jnp.sum(first, axis=0, keepdims=True)
    mark(token_ref)


def hold_grads(meta, own, got):
    return call(
        hold_grads_kernel,
        [IN_SMEM, IN_HBM, IN_HBM],
        light=True,
        grid=(1,),
        out_specs=[full((SEQ, D)), full((BLOCK, D)), full((1, D)), TOKEN],
        out_shape=(
            in_hbm((SEQ, D), BF16),
            in_hbm((BLOCK, D), F32),
            shaped((1, D), F32),
            TOKEN_SHAPE,
        ),
        scratch_shapes=[pltpu.SemaphoreType.DMA((8,))],
    )(meta, own, got)


def first_norm_kernel(
    meta_ref, own_ref, got_ref, gain_ref, shift_ref, normed_ref, first_ref, token_ref, x_ref, sems
):
    def copies_of(ref):
        return [
            pltpu.make_async_copy(ref.at[pl.ds(i * 256, 256), :], x_ref.at[pl.ds(i * 256, 256), :], sems.at[i])
            for i in range(4)
        ]

    take_in(meta_ref, own_ref, got_ref, copies_of)
    for i in range(4):
        at = pl.ds(i * 256, 256)
        unit = normal(x_ref[at, :].astype(F32))[0]
        normed_ref[at, :] = (unit * gain_ref[...] + shift_ref[...]).astype(BF16)
    first_ref[...] = x_ref[rows_at(meta_ref, HELD), :].astype(F32)
    mark(token_ref)


def first_norm(meta, own, got, gain, shift):
    return call(
        first_norm_kernel,
        [IN_SMEM, IN_HBM, IN_HBM, full((1, D)), full((1, D))],
        grid=(1,),
        out_specs=[full((SEQ, D)), full((BLOCK, D)), TOKEN],
        out_shape=(in_hbm((SEQ, D), BF16), in_hbm((BLOCK, D), F32), TOKEN_SHAPE),
        scratch_shapes=pieces_of(4, 256),
    )(meta, own, got, gain, shift)


def later(values, after):
    count = len(values)

    def later_kernel(*refs):
        pass

    return call(
        later_kernel,
        [IN_HBM] * count,
        after=after,
        out_specs=[IN_HBM] * count,
        out_shape=[in_hbm(value.shape, value.dtype) for value in values],
        aliases={i: i for i in range(count)},
    )(*values)


def spread_out(value, rows, after):
    def spread_out_kernel(value_ref, out_ref):
        for i in range(16):
            out_ref[i] = value_ref[:rows, :]

    shape = (16, rows, value.shape[1])
    return call(
        spread_out_kernel,
        [full(value.shape)],
        grid=(1,),
        out_specs=full(shape),
        out_shape=in_hbm(shape, value.dtype),
        after=after,
    )(value)


def rows_at(meta_ref, index):
    return pl.ds(pl.multiple_of(meta_ref[index] * BLOCK, BLOCK), BLOCK)


def nt(a, b):
    return lax.dot_general(a, b, (((1,), (1,)), ((), ())), preferred_element_type=F32)


def tn(a, b):
    return lax.dot_general(a, b, (((0,), (0,)), ((), ())), preferred_element_type=F32)


QB = 256


def allowed_at(start_ref, at, keys):
    key = lax.broadcasted_iota(jnp.int32, (keys, QB), 0)
    query = lax.broadcasted_iota(jnp.int32, (keys, QB), 1) + at
    return (key >= start_ref[:, at : at + QB]) & (key <= query)


def attend_forward_kernel(meta_ref, start_ref, qkv_ref, *refs):
    pieces = refs[:4]
    turned_ref, lse_ref, token_ref, own_ref, sems = refs[4:]
    mark(token_ref)
    heads = []
    for h in range(3):
        lo = h * HEAD_DIM
        q = qkv_ref[:, lo : lo + HEAD_DIM] * jnp.asarray(SCALE, BF16)
        k = qkv_ref[:, LOCAL + lo : LOCAL + lo + HEAD_DIM]
        v = qkv_ref[:, 2 * LOCAL + lo : 2 * LOCAL + lo + HEAD_DIM]
        heads.append((q, k, v.astype(F32).T.astype(BF16)))
    for block in range(SEQ // QB):
        at = block * QB
        keys = at + QB
        allowed = allowed_at(start_ref, at, keys)
        parts = []
        for h, (q, k, vt) in enumerate(heads):
            scores = nt(k[:keys], q[at : at + QB])
            scores = jnp.where(allowed, scores, -1e30)
            top = jnp.max(scores, axis=0, keepdims=True)
            weights = jnp.exp(scores - top)
            total = jnp.sum(weights, axis=0, keepdims=True)
            turned = (
                jnp.dot(vt[:, :keys], weights.astype(BF16), preferred_element_type=F32) / total
            )
            lse_ref[h : h + 1, at : at + QB] = top + jnp.log(total)
            turned_ref[h * HEAD_DIM : (h + 1) * HEAD_DIM, at : at + QB] = turned
            parts.append(turned)
        out = jnp.concatenate(parts, axis=0).T.astype(BF16)
        own_ref[at : at + QB, :] = jnp.where(meta_ref[CORE] == 0, out[:, :160], out[:, 32:])
    copies = [
        pltpu.make_async_copy(
            own_ref.at[rows_at(meta_ref, TO_BLOCK + j), :],
            pieces[j // 2].at[pl.ds(j % 2 * BLOCK, BLOCK), :],
            sems.at[j],
        )
        for j in range(8)
    ]
    for copy in copies:
        copy.start()
    for copy in copies:
        copy.wait()


def attend_forward(meta, start, qkv):
    results = call(
        attend_forward_kernel,
        grid=(1,),
        in_specs=[IN_SMEM, full((1, SEQ)), full((SEQ, 3 * LOCAL))],
        out_specs=[ANYWHERE] * 4
        + [full((LOCAL, SEQ)), full((8, SEQ)), TOKEN],
        out_shape=[in_hbm((2 * BLOCK, 160), BF16)] * 4
        + [shaped((LOCAL, SEQ), F32), shaped((8, SEQ), F32), TOKEN_SHAPE],
        scratch_shapes=[pltpu.VMEM((SEQ, 160), BF16), pltpu.SemaphoreType.DMA((8,))],
    )(meta, start, qkv)
    return results[:4], results[4], results[5], results[6]


WIDE = LOCAL + 160


def attend_backward_kernel(meta_ref, start_ref, qkv_ref, turned_ref, lse_ref, *refs):
    pieces = refs[:8]
    out_ref, own_ref, sum_ref, mid_ref, grad_ref, sems, dk_ref, dv_ref = refs[8:]
    copies = [
        pltpu.make_async_copy(
            pieces[j].at[pl.ds(j % 2 * BLOCK, BLOCK), :],
            grad_ref.at[rows_at(meta_ref, FROM_BLOCK + j), :],
            sems.at[j],
        )
        for j in range(8)
    ]
    for copy in copies:
        copy.start()
    for copy in copies:
        copy.wait()
    mid_ref[...] = grad_ref[:, LOCAL:]
    for h in range(3):
        lo = h * HEAD_DIM
        q = qkv_ref[:, lo : lo + HEAD_DIM] * jnp.asarray(SCALE, BF16)
        k = qkv_ref[:, LOCAL + lo : LOCAL + lo + HEAD_DIM]
        v = qkv_ref[:, 2 * LOCAL + lo : 2 * LOCAL + lo + HEAD_DIM]
        g = grad_ref[:, lo : lo + HEAD_DIM]
        kt = k.astype(F32).T.astype(BF16)
        delta = jnp.sum(
            g.astype(F32).T * turned_ref[lo : lo + HEAD_DIM, :], axis=0, keepdims=True
        )
        for block in reversed(range(SEQ // QB)):
            at = block * QB
            keys = at + QB
            allowed = allowed_at(start_ref, at, keys)
            q_part, g_part = q[at : at + QB], g[at : at + QB]
            scores = nt(k[:keys], q_part)
            probs = jnp.where(
                allowed, jnp.exp(scores - lse_ref[h : h + 1, at : at + QB]), 0.0
            )
            grad_probs = nt(v[:keys], g_part)
            grad_scores = (probs * (grad_probs - delta[:, at : at + QB])).astype(BF16)
            dv = jnp.dot(probs.astype(BF16), g_part, preferred_element_type=F32)
            dk = jnp.dot(grad_scores, q_part, preferred_element_type=F32)
            dq = jnp.dot(kt[:, :keys], grad_scores, preferred_element_type=F32) * SCALE
            out_ref[at : at + QB, lo : lo + HEAD_DIM] = dq.T.astype(BF16)
            if keys == SEQ:
                dk_ref[...] = dk
                dv_ref[...] = dv
            else:
                dk_ref[:keys, :] += dk
                dv_ref[:keys, :] += dv
        out_ref[:, LOCAL + lo : LOCAL + lo + HEAD_DIM] = dk_ref[...].astype(BF16)
        out_ref[:, 2 * LOCAL + lo : 2 * LOCAL + lo + HEAD_DIM] = dv_ref[...].astype(BF16)
    for i in range(3):
        part = out_ref[:, i * LOCAL : (i + 1) * LOCAL]
        own = jnp.where(meta_ref[CORE] == 0, part[:, :160], part[:, 32:])
        own_ref[:, i * 160 : (i + 1) * 160] = own
        sum_ref[:, i * 160 : (i + 1) * 160] = jnp.sum(own.astype(F32), axis=0, keepdims=True)


def gelu(v):
    inner = 0.7978845608028654 * (v + 0.044715 * v * v * v)
    return 0.5 * v * (1.0 + jnp.tanh(inner))


def gelu_slope(v):
    t = jnp.tanh(0.7978845608028654 * (v + 0.044715 * v * v * v))
    return 0.5 * (1.0 + t) + 0.5 * v * (1.0 - t * t) * 0.7978845608028654 * (
        1.0 + 3 * 0.044715 * v * v
    )


HALF = 512
def up_down_kernel(
    a, b, c, d, w_ref, bias_ref, hidden_ref, act_ref, out_ref, *refs
):
    x_ref, sems, y_ref, done, up_ref, down_ref, w_sems = refs
    copies = fetch((a, b, c, d), x_ref, sems)
    weights = load(w_ref, 0, (up_ref, down_ref), w_sems)
    outs = []
    for i in range(2):
        at = pl.ds(i * 256, 256)
        copies[2 * i].wait()
        copies[2 * i + 1].wait()
        if not i:
            weights[0].wait()
        hidden = jnp.dot(x_ref[at, :], up_ref[...], preferred_element_type=F32) + bias_ref[...]
        hidden_ref[at, :] = hidden
        act = gelu(hidden).astype(BF16)
        act_ref[at, :] = act
        if not i:
            weights[1].wait()
        y_ref[at, :] = nt(act, down_ref[...]).astype(BF16)
        outs.append(pltpu.make_async_copy(y_ref.at[at, :], out_ref.at[at, :], done.at[i]))
        outs[i].start()
    for copy in outs:
        copy.wait()


def up_down(pieces, weights, bias):
    return call(
        up_down_kernel,
        grid=(1,),
        in_specs=[IN_HBM] * 5 + [full((1, UNITS))],
        out_specs=[full((HALF, UNITS)), full((HALF, UNITS)), ANYWHERE],
        scratch_shapes=pieces_of(4) + pieces_of(2, 256) + weights_of(2),
        out_shape=(
            in_hbm((HALF, UNITS), F32),
            in_hbm((HALF, UNITS), BF16),
            shaped((HALF, D), BF16),
        ),
    )(*pieces, weights, bias)


def up_down_back_kernel(a, b, c, d, w_ref, hidden_ref, low_ref, sum_ref, out_ref, *refs):
    g_ref, sems, y_ref, done, down_ref, up_ref, w_sems, kept_ref, kept_sems = refs
    copies = fetch((a, b, c, d), g_ref, sems)
    kept = pltpu.make_async_copy(hidden_ref, kept_ref, kept_sems.at[0])
    kept.start()
    weights = load(w_ref, UNITS, (down_ref,), w_sems)
    weights.append(pltpu.make_async_copy(w_ref.at[:, pl.ds(0, UNITS)], up_ref, w_sems.at[1]))
    weights[1].start()
    outs = []
    total = jnp.zeros((1, UNITS), F32)
    for i in range(2):
        at = pl.ds(i * 256, 256)
        copies[2 * i].wait()
        copies[2 * i + 1].wait()
        if not i:
            weights[0].wait()
            kept.wait()
        grad = jnp.dot(g_ref[at, :], down_ref[...], preferred_element_type=F32)
        grad = grad * gelu_slope(kept_ref[at, :])
        total += jnp.sum(grad, axis=0, keepdims=True)
        low = grad.astype(BF16)
        low_ref[at, :] = low
        if not i:
            weights[1].wait()
        y_ref[at, :] = nt(low, up_ref[...]).astype(BF16)
        outs.append(pltpu.make_async_copy(y_ref.at[at, :], out_ref.at[at, :], done.at[i]))
        outs[i].start()
    sum_ref[...] = total
    for copy in outs:
        copy.wait()


def up_down_back(pieces, weights, hidden):
    return call(
        up_down_back_kernel,
        grid=(1,),
        in_specs=[IN_HBM] * 4 + [ANYWHERE, IN_HBM],
        out_specs=[full((HALF, UNITS)), full((1, UNITS)), ANYWHERE],
        scratch_shapes=pieces_of(4)
        + pieces_of(2, 256)
        + weights_of(2)
        + [pltpu.VMEM((HALF, UNITS), F32), pltpu.SemaphoreType.DMA((1,))],
        out_shape=(
            in_hbm((HALF, UNITS), BF16),
            shaped((1, UNITS), F32),
            shaped((HALF, D), BF16),
        ),
    )(*pieces, weights, hidden)


def up_down_both_kernel(first, meta_ref, a, b, c, d, grad_ref, w_ref, bias_ref, *refs):
    if not first:
        refs = refs[1:]
    act_ref, low_ref, sum_ref, back_ref, out_ref = refs[:5]
    x_ref, sems, g_ref, g_sems, back, back_done, out, out_done = refs[5:13]
    up_ref, down_ref, w_sems = refs[13:]
    copies = fetch((a, b, c, d), x_ref, sems)
    weights = load(w_ref, 0, (up_ref, down_ref), w_sems)
    grads = [grad_ref.at[pl.ds((first + 2 * i) * BLOCK, 256), :] for i in range(2)]
    grads = fetch(grads, g_ref, g_sems)
    total = jnp.zeros((1, UNITS), F32)
    done = []
    for i in range(2):
        at = pl.ds(i * 256, 256)
        copies[2 * i].wait()
        copies[2 * i + 1].wait()
        grads[i].wait()
        if not i:
            weights[0].wait()
        hidden = jnp.dot(x_ref[at, :], up_ref[...], preferred_element_type=F32) + bias_ref[...]
        act = gelu(hidden).astype(BF16)
        act_ref[at, :] = act
        if not i:
            weights[1].wait()
        grad = jnp.dot(g_ref[at, :], down_ref[...], preferred_element_type=F32)
        grad = grad * gelu_slope(hidden)
        total += jnp.sum(grad, axis=0, keepdims=True)
        low = grad.astype(BF16)
        low_ref[at, :] = low
        back[at, :] = nt(low, up_ref[...]).astype(BF16)
        done.append(pltpu.make_async_copy(back.at[at, :], back_ref.at[at, :], back_done.at[i]))
        done[-1].start()
        out[at, :] = nt(act, down_ref[...]).astype(BF16)
        for k in range(2 * i, 2 * i + 2):
            rows = rows_at(meta_ref, HELD + first + k)
            done.append(
                pltpu.make_async_copy(
                    out.at[pl.ds(k * BLOCK, BLOCK), :], out_ref.at[rows, :], out_done.at[k]
                )
            )
            done[-1].start()
    sum_ref[...] = total
    for copy in done:
        copy.wait()


def up_down_both(meta, pieces, grads, first, weights, bias, outs=None):
    extra = [] if outs is None else [outs]
    return call(
        functools.partial(up_down_both_kernel, first),
        [IN_SMEM] + [IN_HBM] * 6 + [full((1, UNITS))] + [IN_HBM] * len(extra),
        aliases={8: 4} if extra else None,
        grid=(1,),
        out_specs=[full((HALF, UNITS)), full((HALF, UNITS)), full((1, UNITS)), ANYWHERE, ANYWHERE],
        out_shape=(
            in_hbm((HALF, UNITS), BF16),
            in_hbm((HALF, UNITS), BF16),
            shaped((1, UNITS), F32),
            shaped((HALF, D), BF16),
            in_hbm((SEQ, D), BF16),
        ),
        scratch_shapes=pieces_of(4)
        + pieces_of(2, 256) * 2
        + pieces_of(4)
        + weights_of(2),
    )(meta, *pieces, grads, weights, bias, *extra)


def unit_grads_kernel(x_count, g_count, extra, *refs):
    xs, gs = refs[:x_count], refs[x_count : x_count + g_count]
    halves = refs[x_count + g_count : x_count + g_count + 4]
    refs = refs[x_count + g_count + 4 :]
    if extra:
        heads_ref, refs = refs[0], refs[1:]
    out_ref, token_ref, x_ref, x_sems, g_ref, g_sems, low_ref, low_sems, act_ref, act_sems = refs[:10]
    if extra:
        rest = pltpu.make_async_copy(
            heads_ref, out_ref.at[:, pl.ds(2 * UNITS, UNITS)], refs[10].at[0]
        )
        rest.start()
    ups = fetch(xs, x_ref, x_sems) + fetch(halves[:2], low_ref, low_sems)
    downs = fetch(gs, g_ref, g_sems) + fetch(halves[2:], act_ref, act_sems)
    for copies, left, right, column in (
        (ups, x_ref, low_ref, 0),
        (downs, g_ref, act_ref, UNITS),
    ):
        for copy in copies:
            copy.wait()
        for t in range(5):
            at = pl.ds(t * 256, 256)
            out_ref[at, column : column + UNITS] = tn(left[:, at], right[...]).astype(BF16)
    if extra:
        out_ref[:, 3 * UNITS :] = jnp.zeros((D, 128), BF16)
        rest.wait()
    mark(token_ref)


def unit_grads(pieces, lows, grads, acts, after, heads=None):
    extra = [] if heads is None else [heads]
    columns = 2 * UNITS + (UNITS + 128 if extra else 0)
    return call(
        functools.partial(unit_grads_kernel, len(pieces), len(grads), bool(extra)),
        [IN_HBM] * (len(pieces) + len(grads) + 4 + len(extra)),
        limit=28,
        after=after,
        light=True,
        grid=(1,),
        out_specs=[full((D, columns)), TOKEN],
        out_shape=(in_hbm((D, columns), BF16), TOKEN_SHAPE),
        scratch_shapes=pieces_of(len(pieces), SEQ // len(pieces))
        + pieces_of(len(grads), SEQ // len(grads))
        + pieces_of(2, HALF, UNITS) * 2
        + [pltpu.SemaphoreType.DMA((1,))],
    )(*pieces, *grads, *lows, *acts, *extra)


def head_grads_kernel(layer, *refs):
    ins, (out_ref, token_ref), refs = refs[:4], refs[4:6], refs[6:]
    held, sems = refs[:4], refs[4]
    copies = [pltpu.make_async_copy(ins[i], held[i], sems.at[i]) for i in (0, 1, 3)]
    for d in range(8):
        copies.append(
            pltpu.make_async_copy(
                ins[2].at[pl.ds((LAYERS * d + layer) * BLOCK, BLOCK), :],
                held[2].at[pl.ds(d * BLOCK, BLOCK), :],
                sems.at[4 + d],
            )
        )
    for copy in copies:
        copy.start()
    for copy in copies:
        copy.wait()
    normed_ref, own_ref, heads_ref, mid_ref = held
    for t in range(5):
        at = pl.ds(t * 256, 256)
        one = tn(normed_ref[:, at], own_ref[...]).astype(BF16)
        two = tn(heads_ref[:, at], mid_ref[...]).astype(BF16)
        out_ref[at, :] = jnp.concatenate([one, two], axis=1)
    mark(token_ref)


def head_grads(normed, own, heads, mid, layer, after):
    return call(
        functools.partial(head_grads_kernel, layer),
        [IN_HBM] * 4,
        limit=20,
        after=after,
        light=True,
        grid=(1,),
        out_specs=[full((D, UNITS)), TOKEN],
        out_shape=(in_hbm((D, UNITS), BF16), TOKEN_SHAPE),
        scratch_shapes=[pltpu.VMEM((SEQ, n), BF16) for n in (D, 480, D, 160)]
        + [pltpu.SemaphoreType.DMA((12,))],
    )(normed, own, heads, mid)


def add_cores_kernel(near_ref, far_ref, *refs):
    outs, token_ref, (one, one_sems, two, two_sems, sums, done) = refs[:4], refs[4], refs[5:]
    mark(token_ref)
    at = [pl.ds(i * BLOCK, BLOCK) for i in range(4)]
    order = (3, 1, 2, 0)
    ins = {}
    for i in order:
        ins[i] = (
            pltpu.make_async_copy(near_ref.at[at[i], :], one.at[at[i], :], one_sems.at[i]),
            pltpu.make_async_copy(far_ref.at[at[i], :], two.at[at[i], :], two_sems.at[i]),
        )
        ins[i][0].start()
        ins[i][1].start()
    copies = []
    for i in order:
        ins[i][0].wait()
        ins[i][1].wait()
        sums[at[i], :] = (one[at[i], :].astype(F32) + two[at[i], :].astype(F32)).astype(BF16)
        copies.append(pltpu.make_async_copy(sums.at[at[i], :], outs[i], done.at[i]))
        copies[-1].start()
    for copy in copies:
        copy.wait()


def add_cores(near, far, after=()):
    return call(
        add_cores_kernel,
        after=after,
        grid=(1,),
        in_specs=[ANYWHERE] * 2,
        out_specs=[ANYWHERE] * 4 + [TOKEN],
        out_shape=[in_hbm((BLOCK, D), BF16)] * 4 + [TOKEN_SHAPE],
        scratch_shapes=pieces_of(4) * 3,
    )(near, far)


def project_kernel(column, meta_ref, *refs):
    pieces = refs[:8]
    full_ref, bias_ref, qkv_ref, normed_ref, x_ref, sems, w_ref, w_sems = refs[8:]
    copies = fetch(pieces, x_ref, sems)
    load(full_ref, column * UNITS, (w_ref,), w_sems)[0].wait()
    for i in range(0, 8, 2):
        copies[i].wait()
        copies[i + 1].wait()
        x = x_ref[i * BLOCK : (i + 2) * BLOCK, :]
        qkv = jnp.dot(x, w_ref[:, : 3 * LOCAL], preferred_element_type=F32) + bias_ref[...]
        qkv = qkv.astype(BF16)
        for k in range(2):
            at = rows_at(meta_ref, HELD + i + k)
            normed_ref[at, :] = x[k * BLOCK : (k + 1) * BLOCK]
            qkv_ref[at, :] = qkv[k * BLOCK : (k + 1) * BLOCK]


def columns_of(at):
    return pl.BlockSpec((D, UNITS), lambda i: (0, at))


def project_first_kernel(x_ref, w_ref, bias_ref, qkv_ref):
    qkv = jnp.dot(x_ref[...], w_ref[:, : 3 * LOCAL], preferred_element_type=F32)
    qkv_ref[...] = (qkv + bias_ref[...]).astype(BF16)


def project_first(normed, weights, bias):
    return call(
        project_first_kernel,
        grid=(4,),
        in_specs=[pl.BlockSpec((256, D), lambda i: (i, 0)), columns_of(0), full((1, 3 * LOCAL))],
        out_specs=pl.BlockSpec((256, 3 * LOCAL), lambda i: (i, 0)),
        out_shape=shaped((SEQ, 3 * LOCAL), BF16),
    )(normed, weights, bias)


def gathered_rows_kernel(step_ref, *refs):
    pieces, wide_ref, out_ref, held, sems = refs[:8], refs[8], refs[9], refs[10], refs[11]
    copies = [
        pltpu.make_async_copy(
            piece.at[pl.ds(BLOCK, EXTRA), :], held.at[i], sems.at[i]
        )
        for i, piece in enumerate(pieces)
    ]
    for copy in copies:
        copy.start()
    for copy in copies:
        copy.wait()
    out_ref[:, : 3 * LOCAL] = wide_ref[...]
    out_ref[:, 3 * LOCAL : UNITS] = jnp.zeros((80, UNITS - 3 * LOCAL), BF16)
    for f in range(8):
        rows = held[step_ref[f]].astype(F32)
        parts = [rows[:10, j * 160 : (j + 1) * 160] for j in range(8)]
        at = UNITS + f * 160
        out_ref[:, at : at + 160] = jnp.concatenate(parts, axis=0).astype(BF16)


def gathered_rows(steps, pieces, wide):
    return call(
        gathered_rows_kernel,
        grid=(1,),
        light=True,
        in_specs=[IN_SMEM] + [IN_HBM] * 8 + [full((80, 3 * LOCAL))],
        out_specs=full((80, UNITS + D)),
        out_shape=in_hbm((80, UNITS + D), BF16),
        scratch_shapes=[pltpu.VMEM((8, EXTRA, D), BF16), pltpu.SemaphoreType.DMA((8,))],
    )(steps, *pieces, wide)


EXTRA = 16


def turn_kernel(one_ref, two_ref, terms_ref, out_ref):
    out_ref[:, D:] = terms_ref[...]
    for i in range(10):
        at = pl.ds(i * 128, 128)
        rows = jnp.concatenate(
            [one_ref[at, 64:].astype(F32), two_ref[at, :96].astype(F32)], axis=1
        )
        out_ref[:, at] = rows.T.astype(BF16)


def turn(weights, terms):
    first = 3 * LOCAL // 128
    return call(
        turn_kernel,
        grid=(1,),
        in_specs=[
            pl.BlockSpec((D, 128), lambda i: (0, first)),
            pl.BlockSpec((D, 128), lambda i: (0, first + 1)),
            full((160, 128)),
        ],
        out_specs=full((160, D + 128)),
        out_shape=in_hbm((160, D + 128), BF16),
    )(weights, weights, terms)


def project_attend_kernel(column, meta_ref, *refs):
    ins, (start_ref, qkv_ref, normed_ref), refs = refs[:10], refs[10:13], refs[13:]
    project_kernel(column, meta_ref, *ins, qkv_ref, normed_ref, *refs[7:11])
    attend_forward_kernel(meta_ref, start_ref, qkv_ref, *refs[:7], *refs[11:])


def project_attend(meta, pieces, weights, at, bias, start):
    results = call(
        functools.partial(project_attend_kernel, at),
        limit=24,
        grid=(1,),
        in_specs=[IN_SMEM] + [IN_HBM] * 9 + [full((1, 3 * LOCAL)), full((1, SEQ))],
        out_specs=[full((SEQ, 3 * LOCAL)), full((SEQ, D))]
        + [ANYWHERE] * 4
        + [full((LOCAL, SEQ)), full((8, SEQ)), TOKEN],
        out_shape=[in_hbm((SEQ, 3 * LOCAL), BF16), in_hbm((SEQ, D), BF16)]
        + [in_hbm((2 * BLOCK, 160), BF16)] * 4
        + [in_hbm((LOCAL, SEQ), F32), in_hbm((8, SEQ), F32), TOKEN_SHAPE],
        scratch_shapes=pieces_of(8)
        + weights_of(1)
        + [pltpu.VMEM((SEQ, 160), BF16), pltpu.SemaphoreType.DMA((8,))],
    )(meta, *pieces, weights, bias, start)
    return results[0], results[1], results[2:6], results[6], results[7]


def project_back(meta_ref, grad_ref, w_ref, y_ref, out_ref, done, first):
    column = lax.broadcasted_iota(jnp.int32, (1, 3 * LOCAL), 1)
    twice = jnp.zeros((1, 3 * LOCAL), jnp.int32)
    for i in range(3):
        at = column - i * LOCAL
        twice += jnp.where((at >= 0) & (at < HEAD_DIM), 1, 0)
    counted = twice * meta_ref[CORE] == 0
    outs = []
    for i in range(2):
        x = jnp.concatenate(
            [grad_ref[rows_at(meta_ref, HELD + first + 2 * i + k), :] for k in range(2)],
            axis=0,
        )
        x = jnp.where(counted, x.astype(F32), 0.0).astype(BF16)
        at = pl.ds(i * 256, 256)
        y_ref[at, :] = nt(x, w_ref[:, : 3 * LOCAL]).astype(BF16)
        outs.append(pltpu.make_async_copy(y_ref.at[at, :], out_ref.at[at, :], done.at[i]))
        outs[i].start()
    return outs


def attend_project_back_kernel(column_at, meta_ref, start_ref, qkv_ref, turned_ref, lse_ref, *refs):
    pieces, full_ref = refs[:8], refs[8]
    own_ref, sum_ref, mid_ref, far_ref, near_ref = refs[9:14]
    out_ref, grad_ref, sems, dk_ref, dv_ref, w_ref, w_sems = refs[14:21]
    far, far_done, near, near_done = refs[21:]
    weights = load(full_ref, column_at * UNITS, (w_ref,), w_sems)
    attend_backward_kernel(
        meta_ref,
        start_ref,
        qkv_ref,
        turned_ref,
        lse_ref,
        *pieces,
        out_ref,
        own_ref,
        sum_ref,
        mid_ref,
        grad_ref,
        sems,
        dk_ref,
        dv_ref,
    )
    weights[0].wait()
    copies = project_back(meta_ref, out_ref, w_ref, far, far_ref, far_done, 4)
    copies += project_back(meta_ref, out_ref, w_ref, near, near_ref, near_done, 0)
    for copy in copies:
        copy.wait()


def attend_project_back(meta, start, qkv, turned, lse, pieces, weights, column_at):
    return call(
        functools.partial(attend_project_back_kernel, column_at),
        limit=28,
        grid=(1,),
        in_specs=[
            IN_SMEM,
            full((1, SEQ)),
            full((SEQ, 3 * LOCAL)),
            full((LOCAL, SEQ)),
            full((8, SEQ)),
        ]
        + [IN_HBM] * 9,
        out_specs=[full((SEQ, 480)), full((1, 480)), full((SEQ, 160)), ANYWHERE, ANYWHERE],
        out_shape=(
            in_hbm((SEQ, 480), BF16),
            shaped((1, 480), F32),
            in_hbm((SEQ, 160), BF16),
            shaped((HALF, D), BF16),
            shaped((HALF, D), BF16),
        ),
        scratch_shapes=[
            pltpu.VMEM((SEQ, 3 * LOCAL), BF16),
            pltpu.VMEM((SEQ, WIDE), BF16),
            pltpu.SemaphoreType.DMA((8,)),
            pltpu.VMEM((SEQ, HEAD_DIM), F32),
            pltpu.VMEM((SEQ, HEAD_DIM), F32),
        ]
        + weights_of(1)
        + pieces_of(2, 256) * 2,
    )(meta, start, qkv, turned, lse, *pieces, weights)


def normal(v):
    mean = jnp.mean(v, axis=-1, keepdims=True)
    centred = v - mean
    variance = jnp.mean(centred * centred, axis=-1, keepdims=True)
    scale = lax.rsqrt(variance + 1e-05)
    return centred * scale, scale


def four(pieces, held_ref, sems):
    copies = fetch(pieces, held_ref, sems)
    for copy in copies:
        copy.wait()
    a, b, c, d = (held_ref[i * BLOCK : (i + 1) * BLOCK, :].astype(F32) for i in range(4))
    return (a + b) + (c + d)


def send_out(value, held_ref, out, sem):
    held_ref[...] = value
    copy = pltpu.make_async_copy(held_ref, out, sem)
    copy.start()
    return copy


def join_norm_kernel(
    a, b, c, d, old_ref, bias_ref, gain_ref, shift_ref, new_ref, low_ref, *refs
):
    x_ref, sems, y_ref, done, held_ref, held_sems = refs
    old = pltpu.make_async_copy(old_ref, held_ref, held_sems.at[0])
    old.start()
    total = four((a, b, c, d), x_ref, sems)
    old.wait()
    new = held_ref[...] + total + bias_ref[...]
    low = (normal(new)[0] * gain_ref[...] + shift_ref[...]).astype(BF16)
    copy = send_out(low, y_ref, low_ref, done.at[0])
    new_ref[...] = new
    copy.wait()


def join_norm(parts, old, bias, gain, shift, after=()):
    return call(
        join_norm_kernel,
        after=after,
        grid=(1,),
        in_specs=[IN_HBM] * 5 + [full((1, D))] * 3,
        out_specs=[full((BLOCK, D)), ANYWHERE],
        out_shape=(in_hbm((BLOCK, D), F32), in_hbm((BLOCK, D), BF16)),
        scratch_shapes=pieces_of(4) + pieces_of(1) + held_rows(1),
    )(*parts, old, bias, gain, shift)


def join_heads_kernel(turned, meta_ref, *refs):
    pieces, refs = refs[:8], refs[8:]
    w_refs, refs = (refs[:8], refs[8:]) if turned else (refs[:1], refs[1:])
    old_ref, gain_ref, shift_ref, more_ref, new_ref, low_ref, heads_ref, bias_ref = refs[:8]
    slots, sems, ordered, y_ref, done, held_ref, held_sems = refs[8:15]
    *w_held, w_sems = refs[15:17] if turned else refs[15:18]
    old = pltpu.make_async_copy(old_ref, held_ref, held_sems.at[0])
    old.start()
    copies = [
        pltpu.make_async_copy(
            pieces[j].at[pl.ds(j % 2 * BLOCK, BLOCK), :],
            slots.at[meta_ref[FROM_SLOT + j]],
            sems.at[j],
        )
        for j in range(8)
    ]
    for copy in copies:
        copy.start()
    weights = load_halves(meta_ref, w_refs, w_held, w_sems)
    if turned:
        terms_ref, terms_sems = refs[17:]
        for i, ref in enumerate(w_refs):
            at = pl.ds(pl.multiple_of(meta_ref[HELD_SLOT + i] * 160, 160), 160)
            copies.append(
                pltpu.make_async_copy(
                    ref.at[:, pl.ds(D, 128)], terms_ref.at[at, :], terms_sems.at[i]
                )
            )
            copies[-1].start()
    for copy in copies:
        copy.wait()
    if turned:
        terms = terms_ref[...].astype(F32).T
        terms = [
            (terms[l : l + 1] + terms[l + 2 : l + 3]) + terms[l + 4 : l + 5] for l in range(LAYERS)
        ]
        bias_ref[...] = jnp.concatenate(terms + [jnp.zeros((6, D), F32)], axis=0)
        bias = terms[0]
    else:
        bias = more_ref[1:2, :]
        bias_ref[...] = more_ref[...]
    for chip in range(4):
        five = jnp.concatenate([slots[2 * chip], slots[2 * chip + 1]], axis=1)
        for i in range(5):
            ordered[5 * chip + i] = five[:, i * HEAD_DIM : (i + 1) * HEAD_DIM]
    x = jnp.concatenate([ordered[meta_ref[HEAD_OF + r]] for r in range(HEADS)], axis=1)
    product = nt if turned else lambda a, b: jnp.dot(a, b, preferred_element_type=F32)
    for copy in weights:
        copy.wait()
    branch = [product(x, ref[...]) for ref in w_held]
    branch = branch[0] if turned else jnp.concatenate(branch, axis=1)
    old.wait()
    new = held_ref[...] + branch + bias
    low = (normal(new)[0] * gain_ref[...] + shift_ref[...]).astype(BF16)
    if turned:
        y_ref[BLOCK:, :] = more_ref[...]
    y_ref[:BLOCK, :] = low
    copy = pltpu.make_async_copy(y_ref, low_ref, done.at[0])
    copy.start()
    new_ref[...] = new
    heads_ref[...] = x
    copy.wait()


def load_halves(meta_ref, refs, targets, sems):
    if len(refs) == 1:
        return load(refs[0], UNITS, targets, sems)
    copies = []
    for i, ref in enumerate(refs):
        at = pl.ds(pl.multiple_of(meta_ref[HELD_SLOT + i] * 160, 160), 160)
        copies.append(
            pltpu.make_async_copy(ref.at[:, pl.ds(0, D)], targets[0].at[at, :], sems.at[i])
        )
        copies[i].start()
    return copies


def halves_of(turned):
    if turned:
        return [pltpu.VMEM((D, D), BF16), pltpu.SemaphoreType.DMA((8,))]
    return [pltpu.VMEM((D, UNITS), BF16)] * 2 + [pltpu.SemaphoreType.DMA((2,))]


def join_heads(meta, pieces, weights, turned, old, gain, shift, more):
    rows = BLOCK + EXTRA if turned else BLOCK
    return call(
        functools.partial(join_heads_kernel, turned),
        grid=(1,),
        in_specs=[IN_SMEM]
        + [IN_HBM] * (9 + len(weights))
        + [full((1, D))] * 2
        + [full(more.shape)],
        out_specs=[full((BLOCK, D)), ANYWHERE, full((BLOCK, D)), full((8, D))],
        out_shape=(
            in_hbm((BLOCK, D), F32),
            in_hbm((rows, D), BF16),
            in_hbm((BLOCK, D), BF16),
            shaped((8, D), F32),
        ),
        scratch_shapes=[
            pltpu.VMEM((8, BLOCK, 160), BF16),
            pltpu.SemaphoreType.DMA((8,)),
            pltpu.VMEM((HEADS, BLOCK, HEAD_DIM), BF16),
        ]
        + pieces_of(1, rows)
        + held_rows(1)
        + halves_of(turned)
        + ([pltpu.VMEM((D, 128), BF16), pltpu.SemaphoreType.DMA((8,))] if turned else []),
    )(meta, *pieces, *weights, old, gain, shift, more)


def norm_back_math(dy, x, old, gain):
    unit, scale = normal(x)
    slope = dy * gain
    mean_one = jnp.mean(slope, axis=-1, keepdims=True)
    mean_two = jnp.mean(slope * unit, axis=-1, keepdims=True)
    new = old + scale * (slope - mean_one - unit * mean_two)
    sums = jnp.concatenate(
        [
            jnp.sum(dy * unit, axis=0, keepdims=True),
            jnp.sum(dy, axis=0, keepdims=True),
            jnp.sum(new, axis=0, keepdims=True),
            jnp.zeros((5, D), F32),
        ],
        axis=0,
    )
    return new, sums


def hold_rows(refs, targets, sems):
    copies = []
    for i, (ref, target) in enumerate(zip(refs, targets)):
        copies.append(pltpu.make_async_copy(ref, target, sems.at[i]))
        copies[i].start()
    return copies


def norm_back_kernel(
    a, b, c, d, x_ref, old_ref, gain_ref, new_ref, low_ref, sums_ref, token_ref, *refs
):
    mark(token_ref)
    p_ref, sems, y_ref, done, x_held, old_held, held_sems = refs
    held = hold_rows((x_ref, old_ref), (x_held, old_held), held_sems)
    total = four((a, b, c, d), p_ref, sems)
    for copy in held:
        copy.wait()
    new, sums = norm_back_math(total, x_held[...], old_held[...], gain_ref[...])
    copy = send_out(new.astype(BF16), y_ref, low_ref, done.at[0])
    new_ref[...] = new
    sums_ref[...] = sums
    copy.wait()


def finish_kernel(sum_ref, first_ref, old_ref, bias_ref, out_ref):
    out_ref[:BLOCK, :] = first_ref[...].astype(BF16)
    last = old_ref[...] + sum_ref[...].astype(F32) + bias_ref[...]
    out_ref[BLOCK:, :] = last.astype(BF16)


def finish(total, first, old, bias):
    return call(
        finish_kernel,
        [full((BLOCK, D))] * 3 + [full((1, D))],
        light=True,
        grid=(1,),
        out_specs=full((2 * BLOCK, D)),
        out_shape=in_hbm((2 * BLOCK, D), BF16),
    )(total, first, old, bias)


def norm_back(parts, x, old, gain, after):
    return call(
        norm_back_kernel,
        after=after,
        grid=(1,),
        in_specs=[IN_HBM] * 6 + [full((1, D))],
        out_specs=[full((BLOCK, D)), ANYWHERE, full((8, D)), TOKEN],
        out_shape=(
            in_hbm((BLOCK, D), F32),
            in_hbm((BLOCK, D), BF16),
            shaped((8, D), F32),
            TOKEN_SHAPE,
        ),
        scratch_shapes=pieces_of(4) + pieces_of(1) + held_rows(2),
    )(*parts, x, old, gain)


def norm_back_heads_kernel(turned, meta_ref, a, b, c, d, x_ref, old_ref, gain_ref, *refs):
    w_refs, refs = (refs[:8], refs[8:]) if turned else (refs[:1], refs[1:])
    new_ref, low_ref, sums_ref = refs[:3]
    pieces, token_ref, refs = refs[3:7], refs[7], refs[8:]
    slots, sent, ordered, p_ref, sems, y_ref, done, x_held, old_held, held_sems = refs[:10]
    *w_held, w_sems = refs[10:]
    mark(token_ref)
    held = hold_rows((x_ref, old_ref), (x_held, old_held), held_sems)
    total = four((a, b, c, d), p_ref, sems)
    weights = load_halves(meta_ref, w_refs, w_held, w_sems)
    for copy in held:
        copy.wait()
    new, sums = norm_back_math(total, x_held[...], old_held[...], gain_ref[...])
    new_ref[...] = new
    low = new.astype(BF16)
    copies = [send_out(low, y_ref, low_ref, done.at[0])]
    sums_ref[...] = sums
    for copy in weights:
        copy.wait()
    if turned:
        grads = jnp.dot(low, w_held[0][...], preferred_element_type=F32)
    else:
        grads = nt(low[:, :UNITS], w_held[0][...]) + nt(low[:, UNITS:], w_held[1][...])
    for r in range(HEADS):
        ordered[meta_ref[HEAD_OF + r]] = grads[:, r * HEAD_DIM : (r + 1) * HEAD_DIM].astype(BF16)
    for f in range(8):
        h = 5 * (f // 2) + 2 * (f % 2)
        slots[f, :, :LOCAL] = jnp.concatenate([ordered[h + i] for i in range(3)], axis=1)
        slots[f, :, LOCAL:] = low[:, f * 160 : (f + 1) * 160]
    for j in range(8):
        target = pieces[j // 2].at[pl.ds(j % 2 * BLOCK, BLOCK), :]
        copies.append(
            pltpu.make_async_copy(slots.at[meta_ref[TO_SLOT + j]], target, sent.at[j])
        )
        copies[-1].start()
    for copy in copies:
        copy.wait()


def norm_back_heads(meta, parts, x, old, gain, weights, turned, after):
    results = call(
        functools.partial(norm_back_heads_kernel, turned),
        after=after,
        grid=(1,),
        in_specs=[IN_SMEM] + [IN_HBM] * 6 + [full((1, D))] + [IN_HBM] * len(weights),
        out_specs=[full((BLOCK, D)), ANYWHERE, full((8, D))] + [ANYWHERE] * 4 + [TOKEN],
        out_shape=[in_hbm((BLOCK, D), F32), in_hbm((BLOCK, D), BF16), shaped((8, D), F32)]
        + [in_hbm((2 * BLOCK, WIDE), BF16)] * 4
        + [TOKEN_SHAPE],
        scratch_shapes=[
            pltpu.VMEM((8, BLOCK, WIDE), BF16),
            pltpu.SemaphoreType.DMA((8,)),
            pltpu.VMEM((HEADS, BLOCK, HEAD_DIM), BF16),
        ]
        + pieces_of(4)
        + pieces_of(1)
        + held_rows(2)
        + halves_of(turned),
    )(meta, *parts, x, old, gain, *weights)
    return results[0], results[2], results[3:7], results[7]


def on_device(
    stream_in,
    segments,
    head_table,
    query_key_value,
    attention_out,
    expand_weight,
    contract_weight,
    norm_gain,
    norm_bias,
    attention_bias,
    expand_bias,
    contract_bias,
    cotangent,
):
    row = lax.axis_index("row")
    col = lax.axis_index("col")
    core = row % 2
    z = row // 4
    y = col % 4
    x = ((row // 2) % 2) * 2 + col // 4
    first = core == 0
    sequence = z * 4 + x

    to_devices = [(core ^ dc, (y + dy) % 4) for dy, dc in STEPS]
    from_devices = [(core ^ dc, (y - dy) % 4) for dy, dc in STEPS]
    held = [core * 4 + (y - k) % 4 for k in HOPS] + [(1 - core) * 4 + (y - k) % 4 for k in HOPS]
    meta = (
        [core, (core == x % 2).astype(jnp.int32)]
        + [core] * 6
        + [c * 4 + at for c, at in to_devices]
        + [2 * at + c for c, at in to_devices]
        + [c * 4 + at for c, at in from_devices]
        + [2 * at + c for c, at in from_devices]
        + held
    )
    slot_heads = head_table.reshape(-1)
    filled = (slot_heads < HEADS).astype(jnp.int32)
    places24 = jnp.arange(24, dtype=jnp.int32)
    order = jnp.sum(jnp.where(places24[None, :] < places24[:, None], filled[None, :], 0), axis=1)
    head_ids = jnp.arange(HEADS, dtype=jnp.int32)
    ranked = (order[None, :] == head_ids[:, None]) & (slot_heads[None, :] < HEADS)
    head_of_rank = jnp.sum(jnp.where(ranked, slot_heads[None, :], 0), axis=1)
    held_slots = [2 * ((y - k) % 4) + c for c in (core, 1 - core) for k in HOPS]
    meta = jnp.concatenate([jnp.stack(meta), head_of_rank, jnp.stack(held_slots)])
    meta = meta.astype(jnp.int32)

    def spread_core(own, axis=-1):
        half = HEAD_DIM // 2
        low = lax.slice_in_dim(own, 0, half, axis=axis)
        high = lax.slice_in_dim(own, own.shape[axis] - half, own.shape[axis], axis=axis)
        got = send(jnp.where(first, high, low), CORES)
        return jnp.where(
            first,
            jnp.concatenate([own, got], axis=axis),
            jnp.concatenate([got, own], axis=axis),
        )

    packed_a = [
        jnp.concatenate([query_key_value[l, i] for i in range(3)] + [attention_out[l]], axis=1)
        for l in range(LAYERS)
    ]
    packed_b = [
        jnp.concatenate([expand_weight[l], contract_weight[l].T], axis=1) for l in range(LAYERS)
    ]

    def three(value):
        parts = []
        for _ in range(3):
            parts.append(value.astype(BF16))
            value = value - parts[-1].astype(F32)
        return jnp.concatenate(parts, axis=0)

    def added(rows):
        rows = rows.astype(F32).reshape(3, LAYERS, -1)
        return (rows[0] + rows[1]) + rows[2]

    none = jnp.zeros((LAYERS, 160), F32)
    head_bias = jnp.concatenate(
        [attention_bias[:, 0], none, attention_bias[:, 1], attention_bias[:, 2]], axis=1
    )
    packed_a[0] = jnp.concatenate(
        [packed_a[0], three(head_bias), three(expand_bias), jnp.zeros((4, UNITS), BF16)], axis=0
    )
    packed_a[0] = jnp.concatenate(
        [packed_a[0], jnp.pad(attention_out[1], ((0, 16), (0, 0)))], axis=1
    )
    shards = jnp.concatenate(
        [jnp.pad(value, ((0, 16), (0, 0))) for value in packed_b]
        + [packed_a[0], jnp.pad(packed_a[1][:, :480], ((0, 16), (0, 0)))],
        axis=1,
    )
    stream_got = send(stream_in, CORES)
    (shards,) = later((shards,), (stream_got,))
    shards = send(shards, TO_FEATURE)
    def gain_of(l, i):
        return norm_gain[l, i].reshape(1, D), norm_bias[l, i].reshape(1, D)

    normed, stream, token = first_norm(meta, stream_in, stream_got, *gain_of(0, 0))
    (shards,) = later((shards,), (token,))
    moved_a = shards[:, 2 * D : 2 * D + 800]
    moved_heads = shards[:80, 2 * D + 800 :]

    def widen_heads(own):
        return spread_core(own.reshape(-1, 3, 160)).reshape(-1, 3 * LOCAL)

    def widen(moved):
        return jnp.concatenate([widen_heads(moved[:, :480]), moved[:, 480:UNITS]], axis=1)

    def gather_plane(value):
        return lax.all_gather(value, AXES, axis=0, tiled=True, axis_index_groups=PLANES)

    wide_a = widen(moved_a)
    first_a = lax.all_to_all(
        spread_out(wide_a, 80, (token,)), AXES, 0, 0, tiled=True, axis_index_groups=PLANES
    ).reshape(D, 736)

    terms = jnp.pad(wide_a[80:86, 3 * LOCAL :], ((0, 122), (0, 0))).T
    qkv_bias = added(wide_a[80:86, : 3 * LOCAL]).reshape(LAYERS, 1, 3 * LOCAL)
    up_bias = added(moved_a[86:92, :UNITS]).reshape(LAYERS, 1, UNITS)
    block = turn(first_a, terms)
    (moved_first,) = later((shards[:80, :D],), (block,))
    first_b = gather_plane(moved_first)
    wide_late = widen_heads(moved_heads)
    more = moved_a[:80, UNITS:].reshape(8, 10, 160).transpose(1, 0, 2).reshape(10, D)
    more = jnp.pad(more, ((0, EXTRA - 10), (0, 0)))
    step_of_feature = jnp.sum(
        jnp.where(
            jnp.stack([2 * ((y - k) % 4) + c for c in (core, 1 - core) for k in HOPS])[None, :]
            == jnp.arange(8)[:, None],
            jnp.arange(8)[None, :],
            0,
        ),
        axis=1,
    )

    w_in = [(first_a, 0)]
    w_units = [first_b]

    def exchange(pieces):
        near = [send(piece, along_y(k)) if k else piece for piece, k in zip(pieces, HOPS)]
        return [value for piece in near for value in (piece, send(piece, CORES))]

    def gather_pieces(block):
        near = [block] + [send(block, along_y(k)) for k in HOPS[1:]]
        return near + [send(value, CORES) for value in near]

    seg = lax.dynamic_slice_in_dim(segments, sequence * SEQ, SEQ)
    start = jnp.sum((seg[:, None] < seg[None, :]).astype(jnp.int32), axis=0, keepdims=True)
    def gather_tokens(value):
        return lax.all_gather(value, AXES, axis=0, tiled=True, axis_index_groups=BY_TOKEN)

    def sum_parts(far, near, after=()):
        *parts, token = add_cores(near, send(far, CORES), after)
        return [send(part, along_y(-k)) if k else part for part, k in zip(parts, HOPS)], token

    def scatter_plane(value):
        return lax.psum_scatter(
            value, AXES, scatter_dimension=0, tiled=True, axis_index_groups=PLANES
        )

    def to_result(value):
        value = send(value, HOME)
        layers = value.shape[0] // BLOCK
        blocks = jnp.moveaxis(value.reshape(layers, BLOCK, 8, 160), 2, 0)
        blocks = lax.all_to_all(blocks, "col", 0, 0, tiled=True)
        return jnp.moveaxis(blocks, 0, 1).reshape(layers, SEQ, 160)

    grad_held, grad, grad_sum, held_token = hold_grads(meta, cotangent, send(cotangent, CORES))
    pieces = None
    kept = []
    for l in range(LAYERS):
        first_layer = l == 0
        if first_layer:
            qkv = project_first(normed, first_a, qkv_bias[l])
            turned_out = [block] + [send(block, along_y(k)) for k in HOPS[1:]]
            pieces, turned, lse, token = attend_forward(meta, start, qkv)
        else:
            qkv, normed, pieces, turned, lse = project_attend(
                meta, pieces, *w_in[l], qkv_bias[l], start
            )
        pieces = exchange(pieces)
        if first_layer:
            turned_out = later(turned_out, (pieces[1],))
            turned_out = [*turned_out] + [send(value, CORES) for value in turned_out]
        if first_layer:
            w_heads = turned_out
        else:
            w_heads = [late]
        gain, shift = gain_of(l, 1)
        mid, low, heads, more = join_heads(
            meta, pieces, w_heads, first_layer, stream, gain, shift, more
        )
        pieces = gather_pieces(low)
        if first_layer:
            rows = gathered_rows(step_of_feature.astype(jnp.int32), pieces, wide_late)
            late = gather_plane(rows)
            w_in.append((late, 0))
            (moved_units,) = later((shards[:80, D : 2 * D],), (rows,))
            w_units.append(gather_plane(moved_units))
        bias = contract_bias[l].reshape(1, D)
        state = (stream, mid, normed, pieces, w_heads, qkv, turned, lse, heads)
        if first_layer:
            far = up_down(pieces[4:], w_units[l], up_bias[l])
            near = up_down(pieces[:4], w_units[l], up_bias[l])
            kept.append(state + (far, near))
            parts, _ = sum_parts(far[2], near[2])
            gain, shift = gain_of(l + 1, 0)
            stream, low = join_norm(parts, mid, bias, gain, shift, (held_token,))
            pieces = gather_pieces(low)
        else:
            both_heads = jnp.concatenate([kept[0][8], heads], axis=0)
            (both_heads,) = later((both_heads,), (pieces[1], pieces[2], pieces[3]))
            all_heads = gather_tokens(both_heads)
            far = up_down_both(meta, pieces[4:], grad_held, 4, w_units[l], up_bias[l])
            near = up_down_both(meta, pieces[:4], grad_held, 0, w_units[l], up_bias[l], far[4])
            kept.append(state + (far, near))
            last = (near[4], mid, bias)

    grad_pieces = None
    wide_sums = [None] * LAYERS
    plane_sums = [None] * LAYERS
    for l in reversed(range(LAYERS)):
        stream, mid, normed, pieces, w_heads, qkv, turned, lse, _, far, near = kept[l]
        if l:
            act_far, low_far, sum_far, back_far, _ = far
            act_near, low_near, sum_near, back_near, _ = near
        else:
            low_far, sum_far, back_far = up_down_back(grad_pieces[4:], w_units[l], far[0])
            low_near, sum_near, back_near = up_down_back(grad_pieces[:4], w_units[l], near[0])
            act_far, act_near = far[1], near[1]
        parts, token = sum_parts(back_far, back_near)
        units, token = unit_grads(
            pieces,
            (low_near, low_far),
            (grad_held,) if l else grad_pieces,
            (act_near, act_far),
            (token, all_heads) if l else (token, last_rows),
            None if l else heads,
        )
        mid_grad, sums_two, pieces, token = norm_back_heads(
            meta,
            parts,
            mid,
            grad,
            gain_of(l, 1)[0],
            w_heads,
            l == 0,
            (token,) if l else (token, units_one),
        )
        if l:
            last_sum, last_mid, last_bias = last
            units, last_sum = later((units, last_sum), (token,))
            last_sum = lax.psum_scatter(
                last_sum, AXES, scatter_dimension=0, tiled=True, axis_index_groups=BY_TOKEN
            )
            last_rows = finish(last_sum, stream, last_mid, last_bias)
            units_one = scatter_plane(units)
        else:
            (units,) = later((units,), (token,))
            units_both = scatter_plane(units)
        grad_own, qkv_sum, mid_all, back_far, back_near = attend_project_back(
            meta, start, qkv, turned, lse, exchange(pieces), *w_in[l]
        )
        parts, token = sum_parts(back_far, back_near)
        heads, token = head_grads(normed, grad_own, all_heads, mid_all, l, (token,))
        after = (token,)
        if not l:
            heads_zero = lax.all_to_all(
                heads.reshape(16, 80, UNITS), AXES, 0, 0, tiled=True, axis_index_groups=PLANES
            )
            after = (token, heads_zero)
        grad_new, next_low, sums_one, token = norm_back(
            parts, stream, mid_grad, gain_of(l, 0)[0], after
        )
        wide_sums[l] = jnp.concatenate([sums_one[:2], sums_two[:3], grad_sum], axis=0)
        plane_sums[l] = jnp.concatenate(
            [
                qkv_sum[:, :160],
                qkv_sum[:, 320:],
                sum_far + sum_near,
                jnp.zeros((1, D - 960), F32),
            ],
            axis=1,
        )
        if l:
            grad_sum = sums_one[2:3]
            grad_pieces = gather_pieces(next_low)
        grad = grad_new
    heads_added = jnp.sum(heads_zero.astype(F32), axis=0).astype(BF16)
    results = to_result(jnp.concatenate([last_rows, next_low], axis=0))
    activations = results[:LAYERS]
    grad_stream = results[LAYERS].astype(F32)


    back = jnp.concatenate([units_one, units_both, heads_added], axis=1)
    back = send(back, FROM_FEATURE)
    units_one, units_both = back[:, : 2 * UNITS], back[:, 2 * UNITS : 4 * UNITS]
    heads_one, heads_zero = back[:, 4 * UNITS : 5 * UNITS], back[:, 5 * UNITS + 128 :]
    unit_back = jnp.stack([units_both, units_one]).astype(F32)
    head_back = jnp.stack([heads_zero, heads_one]).astype(F32)
    grad_query_key_value = head_back[:, :, :480].reshape(LAYERS, 80, 3, 160).transpose(0, 2, 1, 3)
    grad_attention_out = head_back[:, :, 480:]
    grad_expand = unit_back[:, :, :UNITS]
    grad_contract = unit_back[:, :, UNITS:].transpose(0, 2, 1)

    def sum_four(value, perms):
        one, two, three = (send(value, perm) for perm in perms)
        return (value + two) + (one + three)

    wide = jnp.concatenate(wide_sums, axis=0)
    wide = sum_four(wide + send(wide, CORES), [along_y(k) for k in (1, 2, 3)])
    (sums,) = later((jnp.concatenate([wide] + plane_sums, axis=0),), (back,))
    sums = sum_four(sums, [along_plane(0, k) for k in (1, 2, 3)])
    sums = sum_four(sums, [along_plane(k, 0) for k in (1, 2, 3)])
    wide = sums[:12].reshape(LAYERS, 6, D)
    plane = send(sums[12:], FROM_FEATURE)
    grad_norm_gain = jnp.stack([wide[:, 0], wide[:, 2]], axis=1)
    grad_norm_bias = jnp.stack([wide[:, 1], wide[:, 3]], axis=1)
    out_sums = lax.dynamic_slice_in_dim(wide[:, 4], col * 160, 160, 1)
    grad_attention_bias = jnp.stack([plane[:, :160], plane[:, 160:320], out_sums], axis=1)
    grad_expand_bias = plane[:, 320:960]
    grad_contract_bias = wide[:, 5]
    return (
        activations,
        grad_stream,
        grad_query_key_value,
        grad_attention_out,
        grad_expand,
        grad_contract,
        grad_norm_gain,
        grad_norm_bias,
        grad_attention_bias,
        grad_expand_bias,
        grad_contract_bias,
    )


def solution(mesh):
    placed = (
        P("row", None),
        P(),
        P(),
        P(None, None, "row", "col"),
        P(None, "row", "col"),
        P(None, "row", "col"),
        P(None, "col", "row"),
        P(),
        P(),
        P(None, None, "col"),
        P(None, "col"),
        P(),
        P("row", None),
    )
    return jax.shard_map(
        on_device,
        mesh=mesh,
        in_specs=placed,
        out_specs=(
            P(None, "row", "col"),
            P("row", "col"),
            P(None, None, "row", "col"),
            P(None, "row", "col"),
            P(None, "row", "col"),
            P(None, "col", "row"),
            P(),
            P(),
            P(None, None, "col"),
            P(None, "col"),
            P(),
        ),
        check_vma=False,
    )
```

```python
import functools

import jax
import jax.numpy as jnp
from jax import lax
from jax.experimental import pallas as pl
from jax.experimental.pallas import tpu as pltpu
from jax.sharding import PartitionSpec as P

D = 1280
HEADS = 20
HEAD_DIM = 64
SEQ = 1024
LAYERS = 2
BLOCK = 128
LOCAL = 3 * HEAD_DIM
SCALE = HEAD_DIM ** (-0.5)
AXES = ("row", "col")
BF16 = jnp.bfloat16
F32 = jnp.float32
MIB = 1024 * 1024


def device(z, x, core, y):
    return (z * 4 + (x // 2) * 2 + core) * 8 + (x % 2) * 4 + y


def pairs(target):
    out = []
    for z in range(4):
        for x in range(4):
            for core in range(2):
                for y in range(4):
                    out.append((device(z, x, core, y), device(*target(z, x, core, y))))
    return out


def along_y(k):
    return pairs(lambda z, x, core, y: (z, x, core, (y + k) % 4))


def along_plane(dz, dx):
    return pairs(lambda z, x, core, y: ((z + dz) % 4, (x + dx) % 4, core, y))


def to_feature(z, x, core, y):
    block = (x % 2) * 4 + y
    return (z, (x // 2) * 2 + core, block % 2, block // 2)


CORES = pairs(lambda z, x, core, y: (z, x, 1 - core, y))
TO_FEATURE = pairs(to_feature)
FROM_FEATURE = [(b, a) for a, b in TO_FEATURE]
HOME = pairs(lambda z, x, core, y: (z, (x // 2) * 2 + core, x % 2, y))
PLANES = [
    [device(z, x, core, y) for z in range(4) for x in range(4)]
    for y in range(4)
    for core in range(2)
]
BY_FEATURE = [
    [device(z, x, core, y) for y in range(4) for core in range(2)]
    for z in range(4)
    for x in range(4)
]
BY_TOKEN = [
    [device(z, x, core, y) for core in range(2) for y in range(4)]
    for z in range(4)
    for x in range(4)
]
STEPS = [(dy, dc) for dy in (0, 1, 3, 2) for dc in (0, 1)]
HOPS = (0, 1, 3, 2)


NAMES = {tuple(CORES): "cores", tuple(TO_FEATURE): "to_feature", tuple(FROM_FEATURE): "from_feature"}


def send(value, perm):
    with jax.named_scope("send_" + NAMES.get(tuple(perm), "far")):
        return lax.ppermute(value, AXES, perm)


CORE, SAME, TO_BLOCK, TO_SLOT, FROM_BLOCK, FROM_SLOT, HELD, HEAD_OF = 0, 1, 8, 16, 24, 32, 40, 48
HELD_SLOT = HEAD_OF + HEADS
IN_SMEM = pl.BlockSpec(memory_space=pltpu.SMEM)
ANYWHERE = pl.BlockSpec(memory_space=pl.ANY)
IN_HBM = pl.BlockSpec(memory_space=pltpu.HBM)


LIGHT = pl.CostEstimate(flops=1000, bytes_accessed=1000, transcendentals=0)


def call(kernel, in_specs, limit=16, after=(), light=False, aliases=None, **kwargs):
    count = len(after)

    def waiting(*refs):
        kernel(*refs[count:])

    specs = [IN_HBM] * count + list(in_specs)
    run = pl.pallas_call(
        waiting,
        in_specs=specs,
        compiler_params=pltpu.CompilerParams(vmem_limit_bytes=limit * MIB),
        cost_estimate=LIGHT if light else None,
        input_output_aliases={count + i: out for i, out in (aliases or {}).items()},
        **kwargs,
    )
    label = getattr(kernel, "func", kernel).__name__

    def named(*operands):
        with jax.named_scope(label):
            placed = [
                pltpu.with_memory_space_constraint(value, pltpu.HBM) if spec is IN_HBM else value
                for value, spec in zip((*after, *operands), specs)
            ]
            return run(*placed)

    return named


def shaped(shape, dtype):
    return jax.ShapeDtypeStruct(shape, dtype)


def in_hbm(shape, dtype):
    return pltpu.HBM(shape, dtype)


def full(shape):
    return pl.BlockSpec(shape, lambda i: (0,) * len(shape))


TOKEN = full((8, 128))
TOKEN_SHAPE = in_hbm((8, 128), F32)


def mark(token_ref):
    token_ref[...] = jnp.zeros((8, 128), F32)


def fetch(pieces, target, sems):
    rows = target.shape[0] // len(pieces)
    copies = []
    for i, piece in enumerate(pieces):
        copies.append(
            pltpu.make_async_copy(
                piece.at[pl.ds(0, rows), :], target.at[pl.ds(i * rows, rows), :], sems.at[i]
            )
        )
    for copy in copies:
        copy.start()
    return copies


def load(ref, columns, targets, sems, rows=None):
    copies = []
    for i, target in enumerate(targets):
        width = target.shape[1]
        at = pl.ds(columns + i * width, width)
        copies.append(pltpu.make_async_copy(ref.at[:, at], target, sems.at[i]))
        copies[i].start()
    return copies


def held_rows(count):
    return [pltpu.VMEM((BLOCK, D), F32)] * count + [pltpu.SemaphoreType.DMA((count,))]


def weights_of(count):
    return [pltpu.VMEM((D, UNITS), BF16)] * count + [pltpu.SemaphoreType.DMA((count,))]


UNITS = 640


def pieces_of(count, rows=BLOCK, columns=D):
    return [pltpu.VMEM((count * rows, columns), BF16), pltpu.SemaphoreType.DMA((count,))]


def take_in(meta_ref, own_ref, got_ref, copies_of):
    for flag, ref in ((1, own_ref), (0, got_ref)):

        @pl.when(meta_ref[SAME] == flag)
        def _():
            copies = copies_of(ref)
            for copy in copies:
                copy.start()
            for copy in copies:
                copy.wait()


def hold_grads_kernel(meta_ref, own_ref, got_ref, held_ref, first_ref, sum_ref, token_ref, sems):
    def copies_of(ref):
        return [
            pltpu.make_async_copy(
                ref.at[rows_at(meta_ref, HELD + i), :],
                held_ref.at[pl.ds(i * BLOCK, BLOCK), :],
                sems.at[i],
            )
            for i in range(8)
        ]

    take_in(meta_ref, own_ref, got_ref, copies_of)
    first = held_ref[:BLOCK, :].astype(F32)
    first_ref[...] = first
    sum_ref[...] = jnp.sum(first, axis=0, keepdims=True)
    mark(token_ref)


def hold_grads(meta, own, got):
    return call(
        hold_grads_kernel,
        [IN_SMEM, IN_HBM, IN_HBM],
        light=True,
        grid=(1,),
        out_specs=[full((SEQ, D)), full((BLOCK, D)), full((1, D)), TOKEN],
        out_shape=(
            in_hbm((SEQ, D), BF16),
            in_hbm((BLOCK, D), F32),
            shaped((1, D), F32),
            TOKEN_SHAPE,
        ),
        scratch_shapes=[pltpu.SemaphoreType.DMA((8,))],
    )(meta, own, got)


def first_norm_kernel(
    meta_ref, own_ref, got_ref, gain_ref, shift_ref, normed_ref, first_ref, token_ref, x_ref, sems
):
    def copies_of(ref):
        return [
            pltpu.make_async_copy(ref.at[pl.ds(i * 256, 256), :], x_ref.at[pl.ds(i * 256, 256), :], sems.at[i])
            for i in range(4)
        ]

    take_in(meta_ref, own_ref, got_ref, copies_of)
    for i in range(4):
        at = pl.ds(i * 256, 256)
        unit = normal(x_ref[at, :].astype(F32))[0]
        normed_ref[at, :] = (unit * gain_ref[...] + shift_ref[...]).astype(BF16)
    first_ref[...] = x_ref[rows_at(meta_ref, HELD), :].astype(F32)
    mark(token_ref)


def first_norm(meta, own, got, gain, shift):
    return call(
        first_norm_kernel,
        [IN_SMEM, IN_HBM, IN_HBM, full((1, D)), full((1, D))],
        grid=(1,),
        out_specs=[full((SEQ, D)), full((BLOCK, D)), TOKEN],
        out_shape=(in_hbm((SEQ, D), BF16), in_hbm((BLOCK, D), F32), TOKEN_SHAPE),
        scratch_shapes=pieces_of(4, 256),
    )(meta, own, got, gain, shift)


def later(values, after):
    count = len(values)

    def later_kernel(*refs):
        pass

    return call(
        later_kernel,
        [IN_HBM] * count,
        after=after,
        out_specs=[IN_HBM] * count,
        out_shape=[in_hbm(value.shape, value.dtype) for value in values],
        aliases={i: i for i in range(count)},
    )(*values)


def spread_out(value, rows, after):
    def spread_out_kernel(value_ref, out_ref):
        for i in range(16):
            out_ref[i] = value_ref[:rows, :]

    shape = (16, rows, value.shape[1])
    return call(
        spread_out_kernel,
        [full(value.shape)],
        grid=(1,),
        out_specs=full(shape),
        out_shape=in_hbm(shape, value.dtype),
        after=after,
    )(value)


def rows_at(meta_ref, index):
    return pl.ds(pl.multiple_of(meta_ref[index] * BLOCK, BLOCK), BLOCK)


def nt(a, b):
    return lax.dot_general(a, b, (((1,), (1,)), ((), ())), preferred_element_type=F32)


def tn(a, b):
    return lax.dot_general(a, b, (((0,), (0,)), ((), ())), preferred_element_type=F32)


QB = 256


def allowed_at(start_ref, at, keys):
    key = lax.broadcasted_iota(jnp.int32, (keys, QB), 0)
    query = lax.broadcasted_iota(jnp.int32, (keys, QB), 1) + at
    return (key >= start_ref[:, at : at + QB]) & (key <= query)


def attend_forward_kernel(meta_ref, start_ref, qkv_ref, *refs):
    pieces = refs[:4]
    turned_ref, lse_ref, token_ref, own_ref, sems = refs[4:]
    mark(token_ref)
    heads = []
    for h in range(3):
        lo = h * HEAD_DIM
        q = qkv_ref[:, lo : lo + HEAD_DIM] * jnp.asarray(SCALE, BF16)
        k = qkv_ref[:, LOCAL + lo : LOCAL + lo + HEAD_DIM]
        v = qkv_ref[:, 2 * LOCAL + lo : 2 * LOCAL + lo + HEAD_DIM]
        heads.append((q, k, v.astype(F32).T.astype(BF16)))
    for block in range(SEQ // QB):
        at = block * QB
        keys = at + QB
        allowed = allowed_at(start_ref, at, keys)
        parts = []
        for h, (q, k, vt) in enumerate(heads):
            scores = nt(k[:keys], q[at : at + QB])
            scores = jnp.where(allowed, scores, -1e30)
            top = jnp.max(scores, axis=0, keepdims=True)
            weights = jnp.exp(scores - top)
            total = jnp.sum(weights, axis=0, keepdims=True)
            turned = (
                jnp.dot(vt[:, :keys], weights.astype(BF16), preferred_element_type=F32) / total
            )
            lse_ref[h : h + 1, at : at + QB] = top + jnp.log(total)
            turned_ref[h * HEAD_DIM : (h + 1) * HEAD_DIM, at : at + QB] = turned
            parts.append(turned)
        out = jnp.concatenate(parts, axis=0).T.astype(BF16)
        own_ref[at : at + QB, :] = jnp.where(meta_ref[CORE] == 0, out[:, :160], out[:, 32:])
    copies = [
        pltpu.make_async_copy(
            own_ref.at[rows_at(meta_ref, TO_BLOCK + j), :],
            pieces[j // 2].at[pl.ds(j % 2 * BLOCK, BLOCK), :],
            sems.at[j],
        )
        for j in range(8)
    ]
    for copy in copies:
        copy.start()
    for copy in copies:
        copy.wait()


def attend_forward(meta, start, qkv):
    results = call(
        attend_forward_kernel,
        grid=(1,),
        in_specs=[IN_SMEM, full((1, SEQ)), full((SEQ, 3 * LOCAL))],
        out_specs=[ANYWHERE] * 4
        + [full((LOCAL, SEQ)), full((8, SEQ)), TOKEN],
        out_shape=[in_hbm((2 * BLOCK, 160), BF16)] * 4
        + [shaped((LOCAL, SEQ), F32), shaped((8, SEQ), F32), TOKEN_SHAPE],
        scratch_shapes=[pltpu.VMEM((SEQ, 160), BF16), pltpu.SemaphoreType.DMA((8,))],
    )(meta, start, qkv)
    return results[:4], results[4], results[5], results[6]


WIDE = LOCAL + 160


def attend_backward_kernel(meta_ref, start_ref, qkv_ref, turned_ref, lse_ref, *refs):
    pieces = refs[:8]
    out_ref, own_ref, sum_ref, mid_ref, grad_ref, sems, dk_ref, dv_ref = refs[8:]
    copies = [
        pltpu.make_async_copy(
            pieces[j].at[pl.ds(j % 2 * BLOCK, BLOCK), :],
            grad_ref.at[rows_at(meta_ref, FROM_BLOCK + j), :],
            sems.at[j],
        )
        for j in range(8)
    ]
    for copy in copies:
        copy.start()
    for copy in copies:
        copy.wait()
    mid_ref[...] = grad_ref[:, LOCAL:]
    for h in range(3):
        lo = h * HEAD_DIM
        q = qkv_ref[:, lo : lo + HEAD_DIM] * jnp.asarray(SCALE, BF16)
        k = qkv_ref[:, LOCAL + lo : LOCAL + lo + HEAD_DIM]
        v = qkv_ref[:, 2 * LOCAL + lo : 2 * LOCAL + lo + HEAD_DIM]
        g = grad_ref[:, lo : lo + HEAD_DIM]
        kt = k.astype(F32).T.astype(BF16)
        delta = jnp.sum(
            g.astype(F32).T * turned_ref[lo : lo + HEAD_DIM, :], axis=0, keepdims=True
        )
        for block in reversed(range(SEQ // QB)):
            at = block * QB
            keys = at + QB
            allowed = allowed_at(start_ref, at, keys)
            q_part, g_part = q[at : at + QB], g[at : at + QB]
            scores = nt(k[:keys], q_part)
            probs = jnp.where(
                allowed, jnp.exp(scores - lse_ref[h : h + 1, at : at + QB]), 0.0
            )
            grad_probs = nt(v[:keys], g_part)
            grad_scores = (probs * (grad_probs - delta[:, at : at + QB])).astype(BF16)
            dv = jnp.dot(probs.astype(BF16), g_part, preferred_element_type=F32)
            dk = jnp.dot(grad_scores, q_part, preferred_element_type=F32)
            dq = jnp.dot(kt[:, :keys], grad_scores, preferred_element_type=F32) * SCALE
            out_ref[at : at + QB, lo : lo + HEAD_DIM] = dq.T.astype(BF16)
            if keys == SEQ:
                dk_ref[...] = dk
                dv_ref[...] = dv
            else:
                dk_ref[:keys, :] += dk
                dv_ref[:keys, :] += dv
        out_ref[:, LOCAL + lo : LOCAL + lo + HEAD_DIM] = dk_ref[...].astype(BF16)
        out_ref[:, 2 * LOCAL + lo : 2 * LOCAL + lo + HEAD_DIM] = dv_ref[...].astype(BF16)
    for i in range(3):
        part = out_ref[:, i * LOCAL : (i + 1) * LOCAL]
        own = jnp.where(meta_ref[CORE] == 0, part[:, :160], part[:, 32:])
        own_ref[:, i * 160 : (i + 1) * 160] = own
        sum_ref[:, i * 160 : (i + 1) * 160] = jnp.sum(own.astype(F32), axis=0, keepdims=True)


def gelu(v):
    inner = 0.7978845608028654 * (v + 0.044715 * v * v * v)
    return 0.5 * v * (1.0 + jnp.tanh(inner))


def gelu_slope(v):
    t = jnp.tanh(0.7978845608028654 * (v + 0.044715 * v * v * v))
    return 0.5 * (1.0 + t) + 0.5 * v * (1.0 - t * t) * 0.7978845608028654 * (
        1.0 + 3 * 0.044715 * v * v
    )


HALF = 512
def up_down_kernel(
    a, b, c, d, w_ref, bias_ref, hidden_ref, act_ref, out_ref, *refs
):
    x_ref, sems, y_ref, done, up_ref, down_ref, w_sems = refs
    copies = fetch((a, b, c, d), x_ref, sems)
    weights = load(w_ref, 0, (up_ref, down_ref), w_sems)
    outs = []
    for i in range(2):
        at = pl.ds(i * 256, 256)
        copies[2 * i].wait()
        copies[2 * i + 1].wait()
        if not i:
            weights[0].wait()
        hidden = jnp.dot(x_ref[at, :], up_ref[...], preferred_element_type=F32) + bias_ref[...]
        hidden_ref[at, :] = hidden
        act = gelu(hidden).astype(BF16)
        act_ref[at, :] = act
        if not i:
            weights[1].wait()
        y_ref[at, :] = nt(act, down_ref[...]).astype(BF16)
        outs.append(pltpu.make_async_copy(y_ref.at[at, :], out_ref.at[at, :], done.at[i]))
        outs[i].start()
    for copy in outs:
        copy.wait()


def up_down(pieces, weights, bias):
    return call(
        up_down_kernel,
        grid=(1,),
        in_specs=[IN_HBM] * 5 + [full((1, UNITS))],
        out_specs=[full((HALF, UNITS)), full((HALF, UNITS)), ANYWHERE],
        scratch_shapes=pieces_of(4) + pieces_of(2, 256) + weights_of(2),
        out_shape=(
            in_hbm((HALF, UNITS), F32),
            in_hbm((HALF, UNITS), BF16),
            shaped((HALF, D), BF16),
        ),
    )(*pieces, weights, bias)


def up_down_back_kernel(a, b, c, d, w_ref, hidden_ref, low_ref, sum_ref, out_ref, *refs):
    g_ref, sems, y_ref, done, down_ref, up_ref, w_sems, kept_ref, kept_sems = refs
    copies = fetch((a, b, c, d), g_ref, sems)
    kept = pltpu.make_async_copy(hidden_ref, kept_ref, kept_sems.at[0])
    kept.start()
    weights = load(w_ref, UNITS, (down_ref,), w_sems)
    weights.append(pltpu.make_async_copy(w_ref.at[:, pl.ds(0, UNITS)], up_ref, w_sems.at[1]))
    weights[1].start()
    outs = []
    total = jnp.zeros((1, UNITS), F32)
    for i in range(2):
        at = pl.ds(i * 256, 256)
        copies[2 * i].wait()
        copies[2 * i + 1].wait()
        if not i:
            weights[0].wait()
            kept.wait()
        grad = jnp.dot(g_ref[at, :], down_ref[...], preferred_element_type=F32)
        grad = grad * gelu_slope(kept_ref[at, :])
        total += jnp.sum(grad, axis=0, keepdims=True)
        low = grad.astype(BF16)
        low_ref[at, :] = low
        if not i:
            weights[1].wait()
        y_ref[at, :] = nt(low, up_ref[...]).astype(BF16)
        outs.append(pltpu.make_async_copy(y_ref.at[at, :], out_ref.at[at, :], done.at[i]))
        outs[i].start()
    sum_ref[...] = total
    for copy in outs:
        copy.wait()


def up_down_back(pieces, weights, hidden):
    return call(
        up_down_back_kernel,
        grid=(1,),
        in_specs=[IN_HBM] * 4 + [ANYWHERE, IN_HBM],
        out_specs=[full((HALF, UNITS)), full((1, UNITS)), ANYWHERE],
        scratch_shapes=pieces_of(4)
        + pieces_of(2, 256)
        + weights_of(2)
        + [pltpu.VMEM((HALF, UNITS), F32), pltpu.SemaphoreType.DMA((1,))],
        out_shape=(
            in_hbm((HALF, UNITS), BF16),
            shaped((1, UNITS), F32),
            shaped((HALF, D), BF16),
        ),
    )(*pieces, weights, hidden)


def up_down_both_kernel(first, meta_ref, a, b, c, d, grad_ref, w_ref, bias_ref, *refs):
    if not first:
        refs = refs[1:]
    act_ref, low_ref, sum_ref, back_ref, out_ref = refs[:5]
    x_ref, sems, g_ref, g_sems, back, back_done, out, out_done = refs[5:13]
    up_ref, down_ref, w_sems = refs[13:]
    copies = fetch((a, b, c, d), x_ref, sems)
    weights = load(w_ref, 0, (up_ref, down_ref), w_sems)
    grads = [grad_ref.at[pl.ds((first + 2 * i) * BLOCK, 256), :] for i in range(2)]
    grads = fetch(grads, g_ref, g_sems)
    total = jnp.zeros((1, UNITS), F32)
    done = []
    for i in range(2):
        at = pl.ds(i * 256, 256)
        copies[2 * i].wait()
        copies[2 * i + 1].wait()
        grads[i].wait()
        if not i:
            weights[0].wait()
        hidden = jnp.dot(x_ref[at, :], up_ref[...], preferred_element_type=F32) + bias_ref[...]
        act = gelu(hidden).astype(BF16)
        act_ref[at, :] = act
        if not i:
            weights[1].wait()
        grad = jnp.dot(g_ref[at, :], down_ref[...], preferred_element_type=F32)
        grad = grad * gelu_slope(hidden)
        total += jnp.sum(grad, axis=0, keepdims=True)
        low = grad.astype(BF16)
        low_ref[at, :] = low
        back[at, :] = nt(low, up_ref[...]).astype(BF16)
        done.append(pltpu.make_async_copy(back.at[at, :], back_ref.at[at, :], back_done.at[i]))
        done[-1].start()
        out[at, :] = nt(act, down_ref[...]).astype(BF16)
        for k in range(2 * i, 2 * i + 2):
            rows = rows_at(meta_ref, HELD + first + k)
            done.append(
                pltpu.make_async_copy(
                    out.at[pl.ds(k * BLOCK, BLOCK), :], out_ref.at[rows, :], out_done.at[k]
                )
            )
            done[-1].start()
    sum_ref[...] = total
    for copy in done:
        copy.wait()


def up_down_both(meta, pieces, grads, first, weights, bias, outs=None):
    extra = [] if outs is None else [outs]
    return call(
        functools.partial(up_down_both_kernel, first),
        [IN_SMEM] + [IN_HBM] * 6 + [full((1, UNITS))] + [IN_HBM] * len(extra),
        aliases={8: 4} if extra else None,
        grid=(1,),
        out_specs=[full((HALF, UNITS)), full((HALF, UNITS)), full((1, UNITS)), ANYWHERE, ANYWHERE],
        out_shape=(
            in_hbm((HALF, UNITS), BF16),
            in_hbm((HALF, UNITS), BF16),
            shaped((1, UNITS), F32),
            shaped((HALF, D), BF16),
            in_hbm((SEQ, D), BF16),
        ),
        scratch_shapes=pieces_of(4)
        + pieces_of(2, 256) * 2
        + pieces_of(4)
        + weights_of(2),
    )(meta, *pieces, grads, weights, bias, *extra)


def unit_grads_kernel(x_count, g_count, extra, *refs):
    xs, gs = refs[:x_count], refs[x_count : x_count + g_count]
    halves = refs[x_count + g_count : x_count + g_count + 4]
    refs = refs[x_count + g_count + 4 :]
    if extra:
        heads_ref, refs = refs[0], refs[1:]
    out_ref, token_ref, x_ref, x_sems, g_ref, g_sems, low_ref, low_sems, act_ref, act_sems = refs[:10]
    if extra:
        rest = pltpu.make_async_copy(
            heads_ref, out_ref.at[:, pl.ds(2 * UNITS, UNITS)], refs[10].at[0]
        )
        rest.start()
    ups = fetch(xs, x_ref, x_sems) + fetch(halves[:2], low_ref, low_sems)
    downs = fetch(gs, g_ref, g_sems) + fetch(halves[2:], act_ref, act_sems)
    for copies, left, right, column in (
        (ups, x_ref, low_ref, 0),
        (downs, g_ref, act_ref, UNITS),
    ):
        for copy in copies:
            copy.wait()
        for t in range(5):
            at = pl.ds(t * 256, 256)
            out_ref[at, column : column + UNITS] = tn(left[:, at], right[...]).astype(BF16)
    if extra:
        out_ref[:, 3 * UNITS :] = jnp.zeros((D, 128), BF16)
        rest.wait()
    mark(token_ref)


def unit_grads(pieces, lows, grads, acts, after, heads=None):
    extra = [] if heads is None else [heads]
    columns = 2 * UNITS + (UNITS + 128 if extra else 0)
    return call(
        functools.partial(unit_grads_kernel, len(pieces), len(grads), bool(extra)),
        [IN_HBM] * (len(pieces) + len(grads) + 4 + len(extra)),
        limit=28,
        after=after,
        light=True,
        grid=(1,),
        out_specs=[full((D, columns)), TOKEN],
        out_shape=(in_hbm((D, columns), BF16), TOKEN_SHAPE),
        scratch_shapes=pieces_of(len(pieces), SEQ // len(pieces))
        + pieces_of(len(grads), SEQ // len(grads))
        + pieces_of(2, HALF, UNITS) * 2
        + [pltpu.SemaphoreType.DMA((1,))],
    )(*pieces, *grads, *lows, *acts, *extra)


def head_grads_kernel(layer, *refs):
    ins, (out_ref, token_ref), refs = refs[:4], refs[4:6], refs[6:]
    held, sems = refs[:4], refs[4]
    copies = [pltpu.make_async_copy(ins[i], held[i], sems.at[i]) for i in (0, 1, 3)]
    for d in range(8):
        copies.append(
            pltpu.make_async_copy(
                ins[2].at[pl.ds((LAYERS * d + layer) * BLOCK, BLOCK), :],
                held[2].at[pl.ds(d * BLOCK, BLOCK), :],
                sems.at[4 + d],
            )
        )
    for copy in copies:
        copy.start()
    for copy in copies:
        copy.wait()
    normed_ref, own_ref, heads_ref, mid_ref = held
    for t in range(5):
        at = pl.ds(t * 256, 256)
        one = tn(normed_ref[:, at], own_ref[...]).astype(BF16)
        two = tn(heads_ref[:, at], mid_ref[...]).astype(BF16)
        out_ref[at, :] = jnp.concatenate([one, two], axis=1)
    mark(token_ref)


def head_grads(normed, own, heads, mid, layer, after):
    return call(
        functools.partial(head_grads_kernel, layer),
        [IN_HBM] * 4,
        limit=20,
        after=after,
        light=True,
        grid=(1,),
        out_specs=[full((D, UNITS)), TOKEN],
        out_shape=(in_hbm((D, UNITS), BF16), TOKEN_SHAPE),
        scratch_shapes=[pltpu.VMEM((SEQ, n), BF16) for n in (D, 480, D, 160)]
        + [pltpu.SemaphoreType.DMA((12,))],
    )(normed, own, heads, mid)


def add_cores_kernel(near_ref, far_ref, *refs):
    outs, token_ref, (one, one_sems, two, two_sems, sums, done) = refs[:4], refs[4], refs[5:]
    mark(token_ref)
    at = [pl.ds(i * BLOCK, BLOCK) for i in range(4)]
    order = (3, 1, 2, 0)
    ins = {}
    for i in order:
        ins[i] = (
            pltpu.make_async_copy(near_ref.at[at[i], :], one.at[at[i], :], one_sems.at[i]),
            pltpu.make_async_copy(far_ref.at[at[i], :], two.at[at[i], :], two_sems.at[i]),
        )
        ins[i][0].start()
        ins[i][1].start()
    copies = []
    for i in order:
        ins[i][0].wait()
        ins[i][1].wait()
        sums[at[i], :] = (one[at[i], :].astype(F32) + two[at[i], :].astype(F32)).astype(BF16)
        copies.append(pltpu.make_async_copy(sums.at[at[i], :], outs[i], done.at[i]))
        copies[-1].start()
    for copy in copies:
        copy.wait()


def add_cores(near, far, after=()):
    return call(
        add_cores_kernel,
        after=after,
        grid=(1,),
        in_specs=[ANYWHERE] * 2,
        out_specs=[ANYWHERE] * 4 + [TOKEN],
        out_shape=[in_hbm((BLOCK, D), BF16)] * 4 + [TOKEN_SHAPE],
        scratch_shapes=pieces_of(4) * 3,
    )(near, far)


def project_kernel(column, meta_ref, *refs):
    pieces = refs[:8]
    full_ref, bias_ref, qkv_ref, normed_ref, x_ref, sems, w_ref, w_sems = refs[8:]
    copies = fetch(pieces, x_ref, sems)
    load(full_ref, column * UNITS, (w_ref,), w_sems)[0].wait()
    for i in range(0, 8, 2):
        copies[i].wait()
        copies[i + 1].wait()
        x = x_ref[i * BLOCK : (i + 2) * BLOCK, :]
        qkv = jnp.dot(x, w_ref[:, : 3 * LOCAL], preferred_element_type=F32) + bias_ref[...]
        qkv = qkv.astype(BF16)
        for k in range(2):
            at = rows_at(meta_ref, HELD + i + k)
            normed_ref[at, :] = x[k * BLOCK : (k + 1) * BLOCK]
            qkv_ref[at, :] = qkv[k * BLOCK : (k + 1) * BLOCK]


def columns_of(at):
    return pl.BlockSpec((D, UNITS), lambda i: (0, at))


def project_first_kernel(x_ref, w_ref, bias_ref, qkv_ref):
    qkv = jnp.dot(x_ref[...], w_ref[:, : 3 * LOCAL], preferred_element_type=F32)
    qkv_ref[...] = (qkv + bias_ref[...]).astype(BF16)


def project_first(normed, weights, bias):
    return call(
        project_first_kernel,
        grid=(4,),
        in_specs=[pl.BlockSpec((256, D), lambda i: (i, 0)), columns_of(0), full((1, 3 * LOCAL))],
        out_specs=pl.BlockSpec((256, 3 * LOCAL), lambda i: (i, 0)),
        out_shape=shaped((SEQ, 3 * LOCAL), BF16),
    )(normed, weights, bias)


def gathered_rows_kernel(step_ref, *refs):
    pieces, wide_ref, out_ref, held, sems = refs[:8], refs[8], refs[9], refs[10], refs[11]
    copies = [
        pltpu.make_async_copy(
            piece.at[pl.ds(BLOCK, EXTRA), :], held.at[i], sems.at[i]
        )
        for i, piece in enumerate(pieces)
    ]
    for copy in copies:
        copy.start()
    for copy in copies:
        copy.wait()
    out_ref[:, : 3 * LOCAL] = wide_ref[...]
    out_ref[:, 3 * LOCAL : UNITS] = jnp.zeros((80, UNITS - 3 * LOCAL), BF16)
    for f in range(8):
        rows = held[step_ref[f]].astype(F32)
        parts = [rows[:10, j * 160 : (j + 1) * 160] for j in range(8)]
        at = UNITS + f * 160
        out_ref[:, at : at + 160] = jnp.concatenate(parts, axis=0).astype(BF16)


def gathered_rows(steps, pieces, wide):
    return call(
        gathered_rows_kernel,
        grid=(1,),
        light=True,
        in_specs=[IN_SMEM] + [IN_HBM] * 8 + [full((80, 3 * LOCAL))],
        out_specs=full((80, UNITS + D)),
        out_shape=in_hbm((80, UNITS + D), BF16),
        scratch_shapes=[pltpu.VMEM((8, EXTRA, D), BF16), pltpu.SemaphoreType.DMA((8,))],
    )(steps, *pieces, wide)


EXTRA = 16


def turn_kernel(one_ref, two_ref, terms_ref, out_ref):
    out_ref[:, D:] = terms_ref[...]
    for i in range(10):
        at = pl.ds(i * 128, 128)
        rows = jnp.concatenate(
            [one_ref[at, 64:].astype(F32), two_ref[at, :96].astype(F32)], axis=1
        )
        out_ref[:, at] = rows.T.astype(BF16)


def turn(weights, terms):
    first = 3 * LOCAL // 128
    return call(
        turn_kernel,
        grid=(1,),
        in_specs=[
            pl.BlockSpec((D, 128), lambda i: (0, first)),
            pl.BlockSpec((D, 128), lambda i: (0, first + 1)),
            full((160, 128)),
        ],
        out_specs=full((160, D + 128)),
        out_shape=in_hbm((160, D + 128), BF16),
    )(weights, weights, terms)


def project_attend_kernel(column, meta_ref, *refs):
    ins, (start_ref, qkv_ref, normed_ref), refs = refs[:10], refs[10:13], refs[13:]
    project_kernel(column, meta_ref, *ins, qkv_ref, normed_ref, *refs[7:11])
    attend_forward_kernel(meta_ref, start_ref, qkv_ref, *refs[:7], *refs[11:])


def project_attend(meta, pieces, weights, at, bias, start):
    results = call(
        functools.partial(project_attend_kernel, at),
        limit=24,
        grid=(1,),
        in_specs=[IN_SMEM] + [IN_HBM] * 9 + [full((1, 3 * LOCAL)), full((1, SEQ))],
        out_specs=[full((SEQ, 3 * LOCAL)), full((SEQ, D))]
        + [ANYWHERE] * 4
        + [full((LOCAL, SEQ)), full((8, SEQ)), TOKEN],
        out_shape=[in_hbm((SEQ, 3 * LOCAL), BF16), in_hbm((SEQ, D), BF16)]
        + [in_hbm((2 * BLOCK, 160), BF16)] * 4
        + [in_hbm((LOCAL, SEQ), F32), in_hbm((8, SEQ), F32), TOKEN_SHAPE],
        scratch_shapes=pieces_of(8)
        + weights_of(1)
        + [pltpu.VMEM((SEQ, 160), BF16), pltpu.SemaphoreType.DMA((8,))],
    )(meta, *pieces, weights, bias, start)
    return results[0], results[1], results[2:6], results[6], results[7]


def project_back(meta_ref, grad_ref, w_ref, y_ref, out_ref, done, first):
    column = lax.broadcasted_iota(jnp.int32, (1, 3 * LOCAL), 1)
    twice = jnp.zeros((1, 3 * LOCAL), jnp.int32)
    for i in range(3):
        at = column - i * LOCAL
        twice += jnp.where((at >= 0) & (at < HEAD_DIM), 1, 0)
    counted = twice * meta_ref[CORE] == 0
    outs = []
    for i in range(2):
        x = jnp.concatenate(
            [grad_ref[rows_at(meta_ref, HELD + first + 2 * i + k), :] for k in range(2)],
            axis=0,
        )
        x = jnp.where(counted, x.astype(F32), 0.0).astype(BF16)
        at = pl.ds(i * 256, 256)
        y_ref[at, :] = nt(x, w_ref[:, : 3 * LOCAL]).astype(BF16)
        outs.append(pltpu.make_async_copy(y_ref.at[at, :], out_ref.at[at, :], done.at[i]))
        outs[i].start()
    return outs


def attend_project_back_kernel(column_at, meta_ref, start_ref, qkv_ref, turned_ref, lse_ref, *refs):
    pieces, full_ref = refs[:8], refs[8]
    own_ref, sum_ref, mid_ref, far_ref, near_ref = refs[9:14]
    out_ref, grad_ref, sems, dk_ref, dv_ref, w_ref, w_sems = refs[14:21]
    far, far_done, near, near_done = refs[21:]
    weights = load(full_ref, column_at * UNITS, (w_ref,), w_sems)
    attend_backward_kernel(
        meta_ref,
        start_ref,
        qkv_ref,
        turned_ref,
        lse_ref,
        *pieces,
        out_ref,
        own_ref,
        sum_ref,
        mid_ref,
        grad_ref,
        sems,
        dk_ref,
        dv_ref,
    )
    weights[0].wait()
    copies = project_back(meta_ref, out_ref, w_ref, far, far_ref, far_done, 4)
    copies += project_back(meta_ref, out_ref, w_ref, near, near_ref, near_done, 0)
    for copy in copies:
        copy.wait()


def attend_project_back(meta, start, qkv, turned, lse, pieces, weights, column_at):
    return call(
        functools.partial(attend_project_back_kernel, column_at),
        limit=28,
        grid=(1,),
        in_specs=[
            IN_SMEM,
            full((1, SEQ)),
            full((SEQ, 3 * LOCAL)),
            full((LOCAL, SEQ)),
            full((8, SEQ)),
        ]
        + [IN_HBM] * 9,
        out_specs=[full((SEQ, 480)), full((1, 480)), full((SEQ, 160)), ANYWHERE, ANYWHERE],
        out_shape=(
            in_hbm((SEQ, 480), BF16),
            shaped((1, 480), F32),
            in_hbm((SEQ, 160), BF16),
            shaped((HALF, D), BF16),
            shaped((HALF, D), BF16),
        ),
        scratch_shapes=[
            pltpu.VMEM((SEQ, 3 * LOCAL), BF16),
            pltpu.VMEM((SEQ, WIDE), BF16),
            pltpu.SemaphoreType.DMA((8,)),
            pltpu.VMEM((SEQ, HEAD_DIM), F32),
            pltpu.VMEM((SEQ, HEAD_DIM), F32),
        ]
        + weights_of(1)
        + pieces_of(2, 256) * 2,
    )(meta, start, qkv, turned, lse, *pieces, weights)


def normal(v):
    mean = jnp.mean(v, axis=-1, keepdims=True)
    centred = v - mean
    variance = jnp.mean(centred * centred, axis=-1, keepdims=True)
    scale = lax.rsqrt(variance + 1e-05)
    return centred * scale, scale


def four(pieces, held_ref, sems):
    copies = fetch(pieces, held_ref, sems)
    for copy in copies:
        copy.wait()
    a, b, c, d = (held_ref[i * BLOCK : (i + 1) * BLOCK, :].astype(F32) for i in range(4))
    return (a + b) + (c + d)


def send_out(value, held_ref, out, sem):
    held_ref[...] = value
    copy = pltpu.make_async_copy(held_ref, out, sem)
    copy.start()
    return copy


def join_norm_kernel(
    a, b, c, d, old_ref, bias_ref, gain_ref, shift_ref, new_ref, low_ref, *refs
):
    x_ref, sems, y_ref, done, held_ref, held_sems = refs
    old = pltpu.make_async_copy(old_ref, held_ref, held_sems.at[0])
    old.start()
    total = four((a, b, c, d), x_ref, sems)
    old.wait()
    new = held_ref[...] + total + bias_ref[...]
    low = (normal(new)[0] * gain_ref[...] + shift_ref[...]).astype(BF16)
    copy = send_out(low, y_ref, low_ref, done.at[0])
    new_ref[...] = new
    copy.wait()


def join_norm(parts, old, bias, gain, shift, after=()):
    return call(
        join_norm_kernel,
        after=after,
        grid=(1,),
        in_specs=[IN_HBM] * 5 + [full((1, D))] * 3,
        out_specs=[full((BLOCK, D)), ANYWHERE],
        out_shape=(in_hbm((BLOCK, D), F32), in_hbm((BLOCK, D), BF16)),
        scratch_shapes=pieces_of(4) + pieces_of(1) + held_rows(1),
    )(*parts, old, bias, gain, shift)


def join_heads_kernel(turned, meta_ref, *refs):
    pieces, refs = refs[:8], refs[8:]
    w_refs, refs = (refs[:8], refs[8:]) if turned else (refs[:1], refs[1:])
    old_ref, gain_ref, shift_ref, more_ref, new_ref, low_ref, heads_ref, bias_ref = refs[:8]
    slots, sems, ordered, y_ref, done, held_ref, held_sems = refs[8:15]
    *w_held, w_sems = refs[15:17] if turned else refs[15:18]
    old = pltpu.make_async_copy(old_ref, held_ref, held_sems.at[0])
    old.start()
    copies = [
        pltpu.make_async_copy(
            pieces[j].at[pl.ds(j % 2 * BLOCK, BLOCK), :],
            slots.at[meta_ref[FROM_SLOT + j]],
            sems.at[j],
        )
        for j in range(8)
    ]
    for copy in copies:
        copy.start()
    weights = load_halves(meta_ref, w_refs, w_held, w_sems)
    if turned:
        terms_ref, terms_sems = refs[17:]
        for i, ref in enumerate(w_refs):
            at = pl.ds(pl.multiple_of(meta_ref[HELD_SLOT + i] * 160, 160), 160)
            copies.append(
                pltpu.make_async_copy(
                    ref.at[:, pl.ds(D, 128)], terms_ref.at[at, :], terms_sems.at[i]
                )
            )
            copies[-1].start()
    for copy in copies:
        copy.wait()
    if turned:
        terms = terms_ref[...].astype(F32).T
        terms = [
            (terms[l : l + 1] + terms[l + 2 : l + 3]) + terms[l + 4 : l + 5] for l in range(LAYERS)
        ]
        bias_ref[...] = jnp.concatenate(terms + [jnp.zeros((6, D), F32)], axis=0)
        bias = terms[0]
    else:
        bias = more_ref[1:2, :]
        bias_ref[...] = more_ref[...]
    for chip in range(4):
        five = jnp.concatenate([slots[2 * chip], slots[2 * chip + 1]], axis=1)
        for i in range(5):
            ordered[5 * chip + i] = five[:, i * HEAD_DIM : (i + 1) * HEAD_DIM]
    x = jnp.concatenate([ordered[meta_ref[HEAD_OF + r]] for r in range(HEADS)], axis=1)
    product = nt if turned else lambda a, b: jnp.dot(a, b, preferred_element_type=F32)
    for copy in weights:
        copy.wait()
    branch = [product(x, ref[...]) for ref in w_held]
    branch = branch[0] if turned else jnp.concatenate(branch, axis=1)
    old.wait()
    new = held_ref[...] + branch + bias
    low = (normal(new)[0] * gain_ref[...] + shift_ref[...]).astype(BF16)
    if turned:
        y_ref[BLOCK:, :] = more_ref[...]
    y_ref[:BLOCK, :] = low
    copy = pltpu.make_async_copy(y_ref, low_ref, done.at[0])
    copy.start()
    new_ref[...] = new
    heads_ref[...] = x
    copy.wait()


def load_halves(meta_ref, refs, targets, sems):
    if len(refs) == 1:
        return load(refs[0], UNITS, targets, sems)
    copies = []
    for i, ref in enumerate(refs):
        at = pl.ds(pl.multiple_of(meta_ref[HELD_SLOT + i] * 160, 160), 160)
        copies.append(
            pltpu.make_async_copy(ref.at[:, pl.ds(0, D)], targets[0].at[at, :], sems.at[i])
        )
        copies[i].start()
    return copies


def halves_of(turned):
    if turned:
        return [pltpu.VMEM((D, D), BF16), pltpu.SemaphoreType.DMA((8,))]
    return [pltpu.VMEM((D, UNITS), BF16)] * 2 + [pltpu.SemaphoreType.DMA((2,))]


def join_heads(meta, pieces, weights, turned, old, gain, shift, more):
    rows = BLOCK + EXTRA if turned else BLOCK
    return call(
        functools.partial(join_heads_kernel, turned),
        grid=(1,),
        in_specs=[IN_SMEM]
        + [IN_HBM] * (9 + len(weights))
        + [full((1, D))] * 2
        + [full(more.shape)],
        out_specs=[full((BLOCK, D)), ANYWHERE, full((BLOCK, D)), full((8, D))],
        out_shape=(
            in_hbm((BLOCK, D), F32),
            in_hbm((rows, D), BF16),
            in_hbm((BLOCK, D), BF16),
            shaped((8, D), F32),
        ),
        scratch_shapes=[
            pltpu.VMEM((8, BLOCK, 160), BF16),
            pltpu.SemaphoreType.DMA((8,)),
            pltpu.VMEM((HEADS, BLOCK, HEAD_DIM), BF16),
        ]
        + pieces_of(1, rows)
        + held_rows(1)
        + halves_of(turned)
        + ([pltpu.VMEM((D, 128), BF16), pltpu.SemaphoreType.DMA((8,))] if turned else []),
    )(meta, *pieces, *weights, old, gain, shift, more)


def norm_back_math(dy, x, old, gain):
    unit, scale = normal(x)
    slope = dy * gain
    mean_one = jnp.mean(slope, axis=-1, keepdims=True)
    mean_two = jnp.mean(slope * unit, axis=-1, keepdims=True)
    new = old + scale * (slope - mean_one - unit * mean_two)
    sums = jnp.concatenate(
        [
            jnp.sum(dy * unit, axis=0, keepdims=True),
            jnp.sum(dy, axis=0, keepdims=True),
            jnp.sum(new, axis=0, keepdims=True),
            jnp.zeros((5, D), F32),
        ],
        axis=0,
    )
    return new, sums


def hold_rows(refs, targets, sems):
    copies = []
    for i, (ref, target) in enumerate(zip(refs, targets)):
        copies.append(pltpu.make_async_copy(ref, target, sems.at[i]))
        copies[i].start()
    return copies


def norm_back_kernel(
    a, b, c, d, x_ref, old_ref, gain_ref, new_ref, low_ref, sums_ref, token_ref, *refs
):
    mark(token_ref)
    p_ref, sems, y_ref, done, x_held, old_held, held_sems = refs
    held = hold_rows((x_ref, old_ref), (x_held, old_held), held_sems)
    total = four((a, b, c, d), p_ref, sems)
    for copy in held:
        copy.wait()
    new, sums = norm_back_math(total, x_held[...], old_held[...], gain_ref[...])
    copy = send_out(new.astype(BF16), y_ref, low_ref, done.at[0])
    new_ref[...] = new
    sums_ref[...] = sums
    copy.wait()


def finish_kernel(sum_ref, first_ref, old_ref, bias_ref, out_ref):
    out_ref[:BLOCK, :] = first_ref[...].astype(BF16)
    last = old_ref[...] + sum_ref[...].astype(F32) + bias_ref[...]
    out_ref[BLOCK:, :] = last.astype(BF16)


def finish(total, first, old, bias):
    return call(
        finish_kernel,
        [full((BLOCK, D))] * 3 + [full((1, D))],
        light=True,
        grid=(1,),
        out_specs=full((2 * BLOCK, D)),
        out_shape=in_hbm((2 * BLOCK, D), BF16),
    )(total, first, old, bias)


def norm_back(parts, x, old, gain, after):
    return call(
        norm_back_kernel,
        after=after,
        grid=(1,),
        in_specs=[IN_HBM] * 6 + [full((1, D))],
        out_specs=[full((BLOCK, D)), ANYWHERE, full((8, D)), TOKEN],
        out_shape=(
            in_hbm((BLOCK, D), F32),
            in_hbm((BLOCK, D), BF16),
            shaped((8, D), F32),
            TOKEN_SHAPE,
        ),
        scratch_shapes=pieces_of(4) + pieces_of(1) + held_rows(2),
    )(*parts, x, old, gain)


def norm_back_heads_kernel(turned, meta_ref, a, b, c, d, x_ref, old_ref, gain_ref, *refs):
    w_refs, refs = (refs[:8], refs[8:]) if turned else (refs[:1], refs[1:])
    new_ref, low_ref, sums_ref = refs[:3]
    pieces, token_ref, refs = refs[3:7], refs[7], refs[8:]
    slots, sent, ordered, p_ref, sems, y_ref, done, x_held, old_held, held_sems = refs[:10]
    *w_held, w_sems = refs[10:]
    mark(token_ref)
    held = hold_rows((x_ref, old_ref), (x_held, old_held), held_sems)
    total = four((a, b, c, d), p_ref, sems)
    weights = load_halves(meta_ref, w_refs, w_held, w_sems)
    for copy in held:
        copy.wait()
    new, sums = norm_back_math(total, x_held[...], old_held[...], gain_ref[...])
    new_ref[...] = new
    low = new.astype(BF16)
    copies = [send_out(low, y_ref, low_ref, done.at[0])]
    sums_ref[...] = sums
    for copy in weights:
        copy.wait()
    if turned:
        grads = jnp.dot(low, w_held[0][...], preferred_element_type=F32)
    else:
        grads = nt(low[:, :UNITS], w_held[0][...]) + nt(low[:, UNITS:], w_held[1][...])
    for r in range(HEADS):
        ordered[meta_ref[HEAD_OF + r]] = grads[:, r * HEAD_DIM : (r + 1) * HEAD_DIM].astype(BF16)
    for f in range(8):
        h = 5 * (f // 2) + 2 * (f % 2)
        slots[f, :, :LOCAL] = jnp.concatenate([ordered[h + i] for i in range(3)], axis=1)
        slots[f, :, LOCAL:] = low[:, f * 160 : (f + 1) * 160]
    for j in range(8):
        target = pieces[j // 2].at[pl.ds(j % 2 * BLOCK, BLOCK), :]
        copies.append(
            pltpu.make_async_copy(slots.at[meta_ref[TO_SLOT + j]], target, sent.at[j])
        )
        copies[-1].start()
    for copy in copies:
        copy.wait()


def norm_back_heads(meta, parts, x, old, gain, weights, turned, after):
    results = call(
        functools.partial(norm_back_heads_kernel, turned),
        after=after,
        grid=(1,),
        in_specs=[IN_SMEM] + [IN_HBM] * 6 + [full((1, D))] + [IN_HBM] * len(weights),
        out_specs=[full((BLOCK, D)), ANYWHERE, full((8, D))] + [ANYWHERE] * 4 + [TOKEN],
        out_shape=[in_hbm((BLOCK, D), F32), in_hbm((BLOCK, D), BF16), shaped((8, D), F32)]
        + [in_hbm((2 * BLOCK, WIDE), BF16)] * 4
        + [TOKEN_SHAPE],
        scratch_shapes=[
            pltpu.VMEM((8, BLOCK, WIDE), BF16),
            pltpu.SemaphoreType.DMA((8,)),
            pltpu.VMEM((HEADS, BLOCK, HEAD_DIM), BF16),
        ]
        + pieces_of(4)
        + pieces_of(1)
        + held_rows(2)
        + halves_of(turned),
    )(meta, *parts, x, old, gain, *weights)
    return results[0], results[2], results[3:7], results[7]


def on_device(
    stream_in,
    segments,
    head_table,
    query_key_value,
    attention_out,
    expand_weight,
    contract_weight,
    norm_gain,
    norm_bias,
    attention_bias,
    expand_bias,
    contract_bias,
    cotangent,
):
    row = lax.axis_index("row")
    col = lax.axis_index("col")
    core = row % 2
    z = row // 4
    y = col % 4
    x = ((row // 2) % 2) * 2 + col // 4
    first = core == 0
    sequence = z * 4 + x

    to_devices = [(core ^ dc, (y + dy) % 4) for dy, dc in STEPS]
    from_devices = [(core ^ dc, (y - dy) % 4) for dy, dc in STEPS]
    held = [core * 4 + (y - k) % 4 for k in HOPS] + [(1 - core) * 4 + (y - k) % 4 for k in HOPS]
    meta = (
        [core, (core == x % 2).astype(jnp.int32)]
        + [core] * 6
        + [c * 4 + at for c, at in to_devices]
        + [2 * at + c for c, at in to_devices]
        + [c * 4 + at for c, at in from_devices]
        + [2 * at + c for c, at in from_devices]
        + held
    )
    slot_heads = head_table.reshape(-1)
    filled = (slot_heads < HEADS).astype(jnp.int32)
    places24 = jnp.arange(24, dtype=jnp.int32)
    order = jnp.sum(jnp.where(places24[None, :] < places24[:, None], filled[None, :], 0), axis=1)
    head_ids = jnp.arange(HEADS, dtype=jnp.int32)
    ranked = (order[None, :] == head_ids[:, None]) & (slot_heads[None, :] < HEADS)
    head_of_rank = jnp.sum(jnp.where(ranked, slot_heads[None, :], 0), axis=1)
    held_slots = [2 * ((y - k) % 4) + c for c in (core, 1 - core) for k in HOPS]
    meta = jnp.concatenate([jnp.stack(meta), head_of_rank, jnp.stack(held_slots)])
    meta = meta.astype(jnp.int32)

    def spread_core(own, axis=-1):
        half = HEAD_DIM // 2
        low = lax.slice_in_dim(own, 0, half, axis=axis)
        high = lax.slice_in_dim(own, own.shape[axis] - half, own.shape[axis], axis=axis)
        got = send(jnp.where(first, high, low), CORES)
        return jnp.where(
            first,
            jnp.concatenate([own, got], axis=axis),
            jnp.concatenate([got, own], axis=axis),
        )

    packed_a = [
        jnp.concatenate([query_key_value[l, i] for i in range(3)] + [attention_out[l]], axis=1)
        for l in range(LAYERS)
    ]
    packed_b = [
        jnp.concatenate([expand_weight[l], contract_weight[l].T], axis=1) for l in range(LAYERS)
    ]

    def three(value):
        parts = []
        for _ in range(3):
            parts.append(value.astype(BF16))
            value = value - parts[-1].astype(F32)
        return jnp.concatenate(parts, axis=0)

    def added(rows):
        rows = rows.astype(F32).reshape(3, LAYERS, -1)
        return (rows[0] + rows[1]) + rows[2]

    none = jnp.zeros((LAYERS, 160), F32)
    head_bias = jnp.concatenate(
        [attention_bias[:, 0], none, attention_bias[:, 1], attention_bias[:, 2]], axis=1
    )
    packed_a[0] = jnp.concatenate(
        [packed_a[0], three(head_bias), three(expand_bias), jnp.zeros((4, UNITS), BF16)], axis=0
    )
    packed_a[0] = jnp.concatenate(
        [packed_a[0], jnp.pad(attention_out[1], ((0, 16), (0, 0)))], axis=1
    )
    shards = jnp.concatenate(
        [jnp.pad(value, ((0, 16), (0, 0))) for value in packed_b]
        + [packed_a[0], jnp.pad(packed_a[1][:, :480], ((0, 16), (0, 0)))],
        axis=1,
    )
    stream_got = send(stream_in, CORES)
    (shards,) = later((shards,), (stream_got,))
    shards = send(shards, TO_FEATURE)
    def gain_of(l, i):
        return norm_gain[l, i].reshape(1, D), norm_bias[l, i].reshape(1, D)

    normed, stream, token = first_norm(meta, stream_in, stream_got, *gain_of(0, 0))
    (shards,) = later((shards,), (token,))
    moved_a = shards[:, 2 * D : 2 * D + 800]
    moved_heads = shards[:80, 2 * D + 800 :]

    def widen_heads(own):
        return spread_core(own.reshape(-1, 3, 160)).reshape(-1, 3 * LOCAL)

    def widen(moved):
        return jnp.concatenate([widen_heads(moved[:, :480]), moved[:, 480:UNITS]], axis=1)

    def gather_plane(value):
        return lax.all_gather(value, AXES, axis=0, tiled=True, axis_index_groups=PLANES)

    wide_a = widen(moved_a)
    first_a = lax.all_to_all(
        spread_out(wide_a, 80, (token,)), AXES, 0, 0, tiled=True, axis_index_groups=PLANES
    ).reshape(D, 736)

    terms = jnp.pad(wide_a[80:86, 3 * LOCAL :], ((0, 122), (0, 0))).T
    qkv_bias = added(wide_a[80:86, : 3 * LOCAL]).reshape(LAYERS, 1, 3 * LOCAL)
    up_bias = added(moved_a[86:92, :UNITS]).reshape(LAYERS, 1, UNITS)
    block = turn(first_a, terms)
    (moved_first,) = later((shards[:80, :D],), (block,))
    first_b = gather_plane(moved_first)
    wide_late = widen_heads(moved_heads)
    more = moved_a[:80, UNITS:].reshape(8, 10, 160).transpose(1, 0, 2).reshape(10, D)
    more = jnp.pad(more, ((0, EXTRA - 10), (0, 0)))
    step_of_feature = jnp.sum(
        jnp.where(
            jnp.stack([2 * ((y - k) % 4) + c for c in (core, 1 - core) for k in HOPS])[None, :]
            == jnp.arange(8)[:, None],
            jnp.arange(8)[None, :],
            0,
        ),
        axis=1,
    )

    w_in = [(first_a, 0)]
    w_units = [first_b]

    def exchange(pieces):
        near = [send(piece, along_y(k)) if k else piece for piece, k in zip(pieces, HOPS)]
        return [value for piece in near for value in (piece, send(piece, CORES))]

    def gather_pieces(block):
        near = [block] + [send(block, along_y(k)) for k in HOPS[1:]]
        return near + [send(value, CORES) for value in near]

    seg = lax.dynamic_slice_in_dim(segments, sequence * SEQ, SEQ)
    start = jnp.sum((seg[:, None] < seg[None, :]).astype(jnp.int32), axis=0, keepdims=True)
    def gather_tokens(value):
        return lax.all_gather(value, AXES, axis=0, tiled=True, axis_index_groups=BY_TOKEN)

    def sum_parts(far, near, after=()):
        *parts, token = add_cores(near, send(far, CORES), after)
        return [send(part, along_y(-k)) if k else part for part, k in zip(parts, HOPS)], token

    def scatter_plane(value):
        return lax.psum_scatter(
            value, AXES, scatter_dimension=0, tiled=True, axis_index_groups=PLANES
        )

    def to_result(value, until=()):
        value = send(value, HOME)
        if until:
            (value,) = later((value,), until)
        layers = value.shape[0] // BLOCK
        blocks = jnp.moveaxis(value.reshape(layers, BLOCK, 8, 160), 2, 0)
        blocks = lax.all_to_all(blocks, "col", 0, 0, tiled=True)
        return jnp.moveaxis(blocks, 0, 1).reshape(layers, SEQ, 160)

    grad_held, grad, grad_sum, held_token = hold_grads(meta, cotangent, send(cotangent, CORES))
    pieces = None
    kept = []
    for l in range(LAYERS):
        first_layer = l == 0
        if first_layer:
            qkv = project_first(normed, first_a, qkv_bias[l])
            turned_out = [block] + [send(block, along_y(k)) for k in HOPS[1:]]
            pieces, turned, lse, token = attend_forward(meta, start, qkv)
        else:
            qkv, normed, pieces, turned, lse = project_attend(
                meta, pieces, *w_in[l], qkv_bias[l], start
            )
        pieces = exchange(pieces)
        if first_layer:
            turned_out = later(turned_out, (pieces[1],))
            turned_out = [*turned_out] + [send(value, CORES) for value in turned_out]
        if first_layer:
            w_heads = turned_out
        else:
            w_heads = [late]
        gain, shift = gain_of(l, 1)
        mid, low, heads, more = join_heads(
            meta, pieces, w_heads, first_layer, stream, gain, shift, more
        )
        pieces = gather_pieces(low)
        if first_layer:
            rows = gathered_rows(step_of_feature.astype(jnp.int32), pieces, wide_late)
            late = gather_plane(rows)
            w_in.append((late, 0))
            (moved_units,) = later((shards[:80, D : 2 * D],), (rows,))
            w_units.append(gather_plane(moved_units))
        bias = contract_bias[l].reshape(1, D)
        state = (stream, mid, normed, pieces, w_heads, qkv, turned, lse, heads)
        if first_layer:
            far = up_down(pieces[4:], w_units[l], up_bias[l])
            near = up_down(pieces[:4], w_units[l], up_bias[l])
            kept.append(state + (far, near))
            parts, _ = sum_parts(far[2], near[2])
            gain, shift = gain_of(l + 1, 0)
            stream, low = join_norm(parts, mid, bias, gain, shift, (held_token,))
            pieces = gather_pieces(low)
        else:
            both_heads = jnp.concatenate([kept[0][8], heads], axis=0)
            (both_heads,) = later((both_heads,), (pieces[1], pieces[2], pieces[3]))
            all_heads = gather_tokens(both_heads)
            far = up_down_both(meta, pieces[4:], grad_held, 4, w_units[l], up_bias[l])
            near = up_down_both(meta, pieces[:4], grad_held, 0, w_units[l], up_bias[l], far[4])
            kept.append(state + (far, near))
            last = (near[4], mid, bias)

    grad_pieces = None
    wide_sums = [None] * LAYERS
    plane_sums = [None] * LAYERS
    for l in reversed(range(LAYERS)):
        stream, mid, normed, pieces, w_heads, qkv, turned, lse, _, far, near = kept[l]
        if l:
            act_far, low_far, sum_far, back_far, _ = far
            act_near, low_near, sum_near, back_near, _ = near
        else:
            low_far, sum_far, back_far = up_down_back(grad_pieces[4:], w_units[l], far[0])
            low_near, sum_near, back_near = up_down_back(grad_pieces[:4], w_units[l], near[0])
            act_far, act_near = far[1], near[1]
        parts, token = sum_parts(back_far, back_near)
        units, token = unit_grads(
            pieces,
            (low_near, low_far),
            (grad_held,) if l else grad_pieces,
            (act_near, act_far),
            (token,) if l else (token, last_rows),
            None if l else heads,
        )
        mid_grad, sums_two, pieces, token = norm_back_heads(
            meta,
            parts,
            mid,
            grad,
            gain_of(l, 1)[0],
            w_heads,
            l == 0,
            (token, all_heads) if l else (token, units_one),
        )
        if l:
            last_sum, last_mid, last_bias = last
            units, last_sum = later((units, last_sum), (token,))
            last_sum = lax.psum_scatter(
                last_sum, AXES, scatter_dimension=0, tiled=True, axis_index_groups=BY_TOKEN
            )
            last_rows = finish(last_sum, stream, last_mid, last_bias)
            units_one = scatter_plane(units)
        else:
            (units,) = later((units,), (token,))
            units_both = scatter_plane(units)
        grad_own, qkv_sum, mid_all, back_far, back_near = attend_project_back(
            meta, start, qkv, turned, lse, exchange(pieces), *w_in[l]
        )
        parts, token = sum_parts(back_far, back_near)
        heads, token = head_grads(normed, grad_own, all_heads, mid_all, l, (token,))
        grad_new, next_low, sums_one, token = norm_back(
            parts, stream, mid_grad, gain_of(l, 0)[0], (token,)
        )
        wide_sums[l] = jnp.concatenate([sums_one[:2], sums_two[:3], grad_sum], axis=0)
        plane_sums[l] = jnp.concatenate(
            [
                qkv_sum[:, :160],
                qkv_sum[:, 320:],
                sum_far + sum_near,
                jnp.zeros((1, D - 960), F32),
            ],
            axis=1,
        )
        if l:
            grad_sum = sums_one[2:3]
            grad_pieces = gather_pieces(next_low)
        grad = grad_new
    heads_zero = lax.all_to_all(
        heads.reshape(16, 80, UNITS), AXES, 0, 0, tiled=True, axis_index_groups=PLANES
    )
    heads_added = jnp.sum(heads_zero.astype(F32), axis=0).astype(BF16)
    results = to_result(jnp.concatenate([last_rows, next_low], axis=0), (heads_zero,))
    activations = results[:LAYERS]
    grad_stream = results[LAYERS].astype(F32)


    back = jnp.concatenate([units_one, units_both, heads_added], axis=1)
    back = send(back, FROM_FEATURE)
    units_one, units_both = back[:, : 2 * UNITS], back[:, 2 * UNITS : 4 * UNITS]
    heads_one, heads_zero = back[:, 4 * UNITS : 5 * UNITS], back[:, 5 * UNITS + 128 :]
    unit_back = jnp.stack([units_both, units_one]).astype(F32)
    head_back = jnp.stack([heads_zero, heads_one]).astype(F32)
    grad_query_key_value = head_back[:, :, :480].reshape(LAYERS, 80, 3, 160).transpose(0, 2, 1, 3)
    grad_attention_out = head_back[:, :, 480:]
    grad_expand = unit_back[:, :, :UNITS]
    grad_contract = unit_back[:, :, UNITS:].transpose(0, 2, 1)

    def sum_four(value, perms):
        one, two, three = (send(value, perm) for perm in perms)
        return (value + two) + (one + three)

    wide = jnp.concatenate(wide_sums, axis=0)
    wide = sum_four(wide + send(wide, CORES), [along_y(k) for k in (1, 2, 3)])
    sums = jnp.concatenate([wide] + plane_sums, axis=0)
    sums = sum_four(sums, [along_plane(0, k) for k in (1, 2, 3)])
    sums = sum_four(sums, [along_plane(k, 0) for k in (1, 2, 3)])
    wide = sums[:12].reshape(LAYERS, 6, D)
    plane = send(sums[12:], FROM_FEATURE)
    grad_norm_gain = jnp.stack([wide[:, 0], wide[:, 2]], axis=1)
    grad_norm_bias = jnp.stack([wide[:, 1], wide[:, 3]], axis=1)
    out_sums = lax.dynamic_slice_in_dim(wide[:, 4], col * 160, 160, 1)
    grad_attention_bias = jnp.stack([plane[:, :160], plane[:, 160:320], out_sums], axis=1)
    grad_expand_bias = plane[:, 320:960]
    grad_contract_bias = wide[:, 5]
    return (
        activations,
        grad_stream,
        grad_query_key_value,
        grad_attention_out,
        grad_expand,
        grad_contract,
        grad_norm_gain,
        grad_norm_bias,
        grad_attention_bias,
        grad_expand_bias,
        grad_contract_bias,
    )


def solution(mesh):
    placed = (
        P("row", None),
        P(),
        P(),
        P(None, None, "row", "col"),
        P(None, "row", "col"),
        P(None, "row", "col"),
        P(None, "col", "row"),
        P(),
        P(),
        P(None, None, "col"),
        P(None, "col"),
        P(),
        P("row", None),
    )
    return jax.shard_map(
        on_device,
        mesh=mesh,
        in_specs=placed,
        out_specs=(
            P(None, "row", "col"),
            P("row", "col"),
            P(None, None, "row", "col"),
            P(None, "row", "col"),
            P(None, "row", "col"),
            P(None, "col", "row"),
            P(),
            P(),
            P(None, None, "col"),
            P(None, "col"),
            P(),
        ),
        check_vma=False,
    )
```
